32 devices in a mesh: lon: 8 (over y, x, core), lat: 4 (over z).
Axes of the slice: x: 2, y: 2, z: 4, core: 2. Of those that a mesh axis runs over, the one named last changes fastest.
Arguments:
- concentration: float32 [72, 8, 64, 1024], P(None, None, 'lat', 'lon'), may hold values from -0.3 to 0.3
- adjoint: float32 [72, 8, 64, 1024], P(None, None, 'lat', 'lon'), may hold values from -4 to 4
- wind_east: float32 [72, 64, 1024], P(None, 'lat', 'lon'), may hold values from -0.45 to 0.45
- wind_north: float32 [72, 64, 1024], P(None, 'lat', 'lon'), may hold values from -0.45 to 0.45
- mixing: float32 [72, 64, 1024], P(None, 'lat', 'lon'), may hold values from 0.01 to 100
- sound_col: int32 [1, 32, 1024], P(None, ('lon', 'lat')), may hold values from -1 to 2047, as said below
- kernel: float32 [72, 32, 1024], P(None, ('lon', 'lat')), may hold values from 0.5 to 3
- observed: float32 [1, 32, 1024], P(None, ('lon', 'lat')), may hold values from -12 to 12
- obs_error: float32 [1, 32, 1024], P(None, ('lon', 'lat')), may hold values from 1 to 3
Outputs:
- adjoint_out: float32 [72, 8, 64, 1024], P(None, None, 'lat', 'lon')
- residual: float32 [1, 32, 1024], P(None, ('lon', 'lat'))
The draws below stay inside these ranges and needn't reach their ends.
Inputs may be any that keep to these rules, and one draw needn't show every extreme that they name: `sound_col`: each entry is a column index inside the brick of its slot (slots b * 32 to b * 32 + 31 of an owner belong to brick b in lon-major order), or -1 for an empty slot; for each owner and brick the used slots come first. In every draw some brick receives 32 soundings from every owner.
All inputs are finite; a program needn't handle non-finite values.
Results may differ from the reference program's by a relative error of at most 0.00022.
Values sent between devices are 32-bit elements; how exact they have to be, the bound alone decides.
No kernel may reach another device: no remote copies, remote signals or barrier semaphores. Data moves between devices by JAX's collectives and lax.ppermute only.
A program may use at most 192 MiB of HBM per device.

```python
import math
import jax
import jax.numpy as jnp
from jax import lax

VERTICAL_LEVELS = 72
TR = 8
CX = 128
CY = 16
CAP = 32
BRICKS = 32
SLOTS = 1024
NX = 1024
NY = 64
N_LAT = 4


def draw_sound_col(key, part):
    key_count, key_busy, key_full, key_cols = jax.random.split(jax.random.fold_in(key, 11), 4)
    loaded = jax.random.randint(key_count, (BRICKS, BRICKS), 0, CAP + 1)
    busyness = jnp.left_shift(jnp.int32(1), jax.random.randint(key_busy, (1, BRICKS), 0, 4))
    counts = jnp.minimum(loaded * busyness // 4, CAP)
    fullest = jax.random.randint(key_full, (), 0, BRICKS)
    brick_index = jnp.arange(BRICKS)[None, :]
    counts = jnp.where(brick_index == fullest, CAP, counts)
    columns = jax.random.randint(key_cols, (BRICKS, BRICKS, CAP), 0, CY * CX)
    slot_index = jnp.arange(CAP)[None, None, :]
    picked = jnp.where(slot_index < counts[:, :, None], columns, -1)
    return picked.reshape(1, BRICKS, BRICKS * CAP).astype(jnp.int32)


def draw_mixing(key, part):
    key_kind, key_weak, key_strong, key_level_set, key_cut = jax.random.split(jax.random.fold_in(key, 23), 5)
    share = 0.5
    strong_low = 20.0
    strong = jax.random.uniform(key_kind, (1, NY, NX), jnp.float32) < share
    weak_values = jnp.exp(jax.random.uniform(key_weak, (VERTICAL_LEVELS, NY, NX), jnp.float32, jnp.log(0.05), jnp.log(3.0)))
    strong_values = jnp.exp(jax.random.uniform(key_strong, (VERTICAL_LEVELS, NY, NX), jnp.float32, jnp.log(strong_low), jnp.log(100.0)))
    base = jnp.where(strong, strong_values, weak_values)
    group_levels = jax.random.randint(key_level_set, (3,), 0, VERTICAL_LEVELS)
    level_position = jnp.arange(VERTICAL_LEVELS)[:, None]
    sounding_group = jnp.any(level_position == group_levels[None, :], axis=1).reshape(VERTICAL_LEVELS, 1, 1)
    level_cutoff = jax.random.uniform(key_cut, (1, NY, NX), jnp.float32, 0.2, 0.5)
    weight_factor = jnp.where(sounding_group, level_cutoff, 1.0)
    return (base * weight_factor).astype(jnp.float32)


def draw_adjoint(key, part):
    key_rough, key_common = jax.random.split(jax.random.fold_in(key, 37), 2)
    rough = 0.8 * jax.random.normal(key_rough, (VERTICAL_LEVELS, TR, NY, NX), jnp.float32)
    common = 0.6 * jax.random.normal(key_common, (1, TR, NY, NX), jnp.float32)
    return jnp.clip(rough + common, -4.0, 4.0).astype(jnp.float32)


def levels(own_key, extent, cuts, low, largest):
    factor_of = 1.0
    for axis_at, shards_of in cuts:
        draws = jax.random.uniform(jax.random.fold_in(jax.random.fold_in(own_key, 6), axis_at), (shards_of,), jnp.float32, low / len(cuts), largest / len(cuts))
        factor_of = factor_of * jnp.repeat(jnp.exp(draws), extent[axis_at] // shards_of).reshape((-1,) + (1,) * (len(extent) - 1 - axis_at))
    return factor_of


def centred(rng, dims, width, limit, shards=(), held_as=jnp.bfloat16):
    drawn = width * jax.random.normal(rng, dims, jnp.float32)
    if shards:
        drawn = drawn * levels(rng, dims, shards, -0.22, 0.18)
    return jnp.clip(drawn, -limit, limit).astype(held_as)


def setup_inputs(seed: int = 0) -> dict:
    seeds = jax.random.split(jax.random.key(seed), 10)
    return {
        "concentration": centred(seeds[0], (VERTICAL_LEVELS, TR, NY, NX), 0.05, 0.3, ((2, 4), (3, 8)), jnp.float32),
        "adjoint": draw_adjoint(jax.random.fold_in(seeds[9], 71), 0),
        "wind_east": jnp.clip(jax.random.uniform(seeds[2], (VERTICAL_LEVELS, NY, NX), jnp.float32, -0.45, 0.45) * levels(seeds[2], (VERTICAL_LEVELS, NY, NX), ((1, 4), (2, 8)), -0.4, 0.0), -0.45, 0.45),
        "wind_north": jnp.clip(jax.random.uniform(seeds[3], (VERTICAL_LEVELS, NY, NX), jnp.float32, -0.45, 0.45) * levels(seeds[3], (VERTICAL_LEVELS, NY, NX), ((1, 4), (2, 8)), -0.4, 0.0), -0.45, 0.45),
        "mixing": draw_mixing(jax.random.fold_in(seeds[9], 71), 0),
        "sound_col": draw_sound_col(jax.random.fold_in(seeds[9], 71), 0),
        "kernel": jnp.clip(jnp.exp(math.log(3.0) - 1.7917595 * jax.random.uniform(seeds[6], (VERTICAL_LEVELS, BRICKS, SLOTS), jnp.float32) ** levels(seeds[6], (VERTICAL_LEVELS, BRICKS, SLOTS), ((1, 32),), -0.2, 0.2)), 0.5, 3.0),
        "observed": centred(seeds[7], (1, BRICKS, SLOTS), 2.0, 12.0, ((1, 32),), jnp.float32),
        "obs_error": jnp.clip(jnp.exp(math.log(3.0) - 1.0986123 * jax.random.uniform(seeds[8], (1, BRICKS, SLOTS), jnp.float32) ** levels(seeds[8], (1, BRICKS, SLOTS), ((1, 32),), -0.2, 0.2)), 1.0, 3.0),
    }


def advect(padded, east_wind, north_wind):
    centre = padded[..., 1:-1, 1:-1]
    eastern = padded[..., 1:-1, 2:]
    western = padded[..., 1:-1, :-2]
    northern = padded[..., 2:, 1:-1]
    southern = padded[..., :-2, 1:-1]
    out_east = jnp.maximum(east_wind[:, 1:-1, 1:-1], 0.0)[:, None]
    in_west = jnp.minimum(east_wind[:, 1:-1, :-2], 0.0)[:, None]
    out_north = jnp.maximum(north_wind[:, 1:-1, 1:-1], 0.0)[:, None]
    in_south = jnp.minimum(north_wind[:, :-2, 1:-1], 0.0)[:, None]
    staying = 1.0 - out_east + in_west - out_north + in_south
    return centre * staying + out_east * eastern - in_west * western + out_north * northern - in_south * southern


def diffuse(field, mixing):
    level_count = field.shape[0]
    level_position = lax.broadcasted_iota(jnp.int32, mixing.shape, 0)
    upward = jnp.where(level_position < level_count - 1, mixing, 0.0)
    downward = jnp.concatenate([jnp.zeros_like(upward[:1]), upward[:-1]], axis=0)
    middle = 1.0 + upward + downward

    def sweep_down(running, inputs):
        weight_factor, solved = running
        below_term, centre_term, above_term, source = inputs
        pivot_term = centre_term - below_term * weight_factor
        next_factor = above_term / pivot_term
        next_value = (source + below_term[None] * solved) / pivot_term[None]
        return (next_factor, next_value), (next_factor, next_value)

    initial = (jnp.zeros_like(mixing[0]), jnp.zeros_like(field[0]))
    ignored, (factors, values) = lax.scan(sweep_down, initial, (downward, middle, upward, field))

    def sweep_up(running, inputs):
        weight_factor, solved = inputs
        result = solved + weight_factor[None] * running
        return result, result

    ignored, finished = lax.scan(sweep_up, jnp.zeros_like(field[0]), (factors, values), reverse=True)
    return finished


def pad_rims(field):
    wrapped = jnp.concatenate([field[..., -1:], field, field[..., :1]], axis=-1)
    widths = [(0, 0)] * (field.ndim - 2) + [(1, 1), (0, 0)]
    return jnp.pad(wrapped, widths)


def reference(concentration, adjoint, wind_east, wind_north, mixing, sound_col, kernel, observed, obs_error):
    profile_sum = jnp.sum(concentration, axis=1).reshape(VERTICAL_LEVELS, NY * NX)
    columns = sound_col[0]
    brick_index = lax.broadcasted_iota(jnp.int32, columns.shape, 1) // CAP
    cell_index = jnp.maximum(columns, 0)
    grid_row = (brick_index % N_LAT) * CY + cell_index // CX
    grid_col = (brick_index // N_LAT) * CX + cell_index % CX
    flat_index = (grid_row * NX + grid_col).reshape(-1).astype(jnp.int32)
    sampled = profile_sum[:, flat_index].reshape(VERTICAL_LEVELS, BRICKS, SLOTS)
    modelled = jnp.sum(kernel * sampled, axis=0, keepdims=True)
    residual = jnp.where(sound_col >= 0, (modelled - observed) / obs_error, 0.0)
    weights = kernel * (residual / obs_error)
    forcing_cols = jnp.zeros((VERTICAL_LEVELS, NY * NX), jnp.float32).at[:, flat_index].add(weights.reshape(VERTICAL_LEVELS, -1))
    started = adjoint + forcing_cols.reshape(VERTICAL_LEVELS, 1, NY, NX)
    east_pad = pad_rims(wind_east)
    north_pad = pad_rims(wind_north)

    def two_steps(tracer_field):
        single = tracer_field[:, None]
        stepped = diffuse(advect(pad_rims(single), east_pad, north_pad), mixing)
        finished = diffuse(advect(pad_rims(stepped), east_pad, north_pad), mixing)
        return finished[:, 0]

    adjoint_out = jnp.moveaxis(lax.map(two_steps, jnp.moveaxis(started, 1, 0)), 0, 1)
    return adjoint_out, residual
```

```python
import functools

import jax
import jax.numpy as jnp
from jax import lax
from jax.experimental import pallas as pl
from jax.experimental.pallas import tpu as pltpu
from jax.sharding import PartitionSpec as P

LANES = 128
SUB = 8
MIB = 1 << 20


def rim_chunks(level_count):
    chunks = -(-level_count // 63)
    return chunks, -(-level_count // chunks)


def lane_iota():
    return lax.broadcasted_iota(jnp.int32, (SUB, LANES), 1)


def sub_iota():
    return lax.broadcasted_iota(jnp.int32, (SUB, LANES), 0)


def call(body, out_shapes, scratch, vmem_mib, flops, bytes_accessed, name):
    return pl.pallas_call(
        body,
        out_shape=out_shapes,
        scratch_shapes=scratch,
        compiler_params=pltpu.CompilerParams(vmem_limit_bytes=vmem_mib * MIB),
        cost_estimate=pl.CostEstimate(
            flops=flops, bytes_accessed=bytes_accessed, transcendentals=0
        ),
        name=name,
    )


def f32(*shape):
    return jax.ShapeDtypeStruct(shape, jnp.float32)


def put_rim(value, lane, q, chunk, rows, east_ref, west_ref):
    turned = pltpu.roll(value, 2 * q + 2, 1)
    east_ref[chunk, rows, :] = jnp.where(lane == 2 * q + 1, turned, east_ref[chunk, rows, :])
    if west_ref is not None:
        west_ref[chunk, rows, :] = jnp.where(lane == 2 * q + 2, turned, west_ref[chunk, rows, :])


def put_rows(field_ref, north_ref, south_ref, row_count, count):
    def body(i, carry):
        start = pl.multiple_of(i * SUB, SUB)
        first = start * row_count
        if south_ref is not None:
            south_ref[pl.ds(start, SUB), :] = field_ref[pl.ds(first, SUB, stride=row_count), :]
        if north_ref is not None:
            north_ref[pl.ds(start, SUB), :] = field_ref[
                pl.ds(first + row_count - 1, SUB, stride=row_count), :
            ]
        return carry

    lax.fori_loop(0, count // SUB, body, 0)


def first_rims(levels, tracers, rows, chunks, per_chunk, field, east, north, e_ref, w_ref, s_ref, n_ref):
    lane = lane_iota()
    e_ref[...] = jnp.zeros(e_ref.shape, jnp.float32)
    w_ref[...] = jnp.zeros(w_ref.shape, jnp.float32)
    plane = tracers * rows
    for chunk in range(chunks):
        def body(q, carry, chunk=chunk):
            k = chunk * per_chunk + q
            for r in range(0, plane, SUB):
                at = pl.multiple_of(k * plane + r, SUB)
                put_rim(field[pl.ds(at, SUB), :], lane, q, chunk, pl.ds(r, SUB), e_ref, w_ref)
            for r in range(0, rows, SUB):
                at = pl.multiple_of(k * rows + r, SUB)
                put_rim(east[pl.ds(at, SUB), :], lane, q, chunk, pl.ds(plane + r, SUB), e_ref, None)
            return carry

        lax.fori_loop(0, min(per_chunk, levels - chunk * per_chunk), body, 0)
    put_rows(field, n_ref.at[pl.ds(0, levels * tracers)], s_ref, rows, levels * tracers)
    put_rows(north, n_ref.at[pl.ds(levels * tracers, levels)], None, rows, levels)


def coefficients(levels, rows, per_chunk, east, north, mixing, east_rim, south_rim, *outs):
    stay, from_e, from_w, from_n, from_s, below, above = outs
    lane, sub = lane_iota(), sub_iota()
    halves = rows // SUB

    def body(k, carry):
        chunk, q = k // per_chunk, k % per_chunk
        has_up = (k < levels - 1).astype(jnp.float32)
        new = []
        tops = []
        for h in range(halves):
            at = pl.multiple_of(k * rows + h * SUB, SUB)
            blk = pl.ds(at, SUB)
            down, factor = carry[h]
            up = mixing[blk, :] * has_up
            pivot = 1.0 + up + down - down * factor
            inv = 1.0 / pivot
            next_factor = up * inv
            e = east[blk, :]
            n = north[blk, :]
            rim = pltpu.roll(east_rim[chunk, pl.ds(h * SUB, SUB), :], LANES - 1 - 2 * q, 1)
            w_in = jnp.minimum(jnp.where(lane == 0, rim, pltpu.roll(e, 1, 1)), 0.0)
            if h == 0:
                edge = south_rim[pl.ds(k, 1), :]
            else:
                edge = tops[h - 1]
            tops.append(n[SUB - 1 : SUB, :])
            s_in = jnp.minimum(
                jnp.where(sub == 0, jnp.broadcast_to(edge, (SUB, LANES)), pltpu.roll(n, 1, 0)), 0.0
            )
            e_out = jnp.maximum(e, 0.0)
            n_out = jnp.maximum(n, 0.0)
            stay[blk, :] = (1.0 - e_out + w_in - n_out + s_in) * inv
            from_e[blk, :] = e_out * inv
            from_w[blk, :] = -(w_in * inv)
            from_n[blk, :] = n_out * inv
            from_s[blk, :] = -(s_in * inv)
            below[blk, :] = down * inv
            above[blk, :] = next_factor
            new.append((up, next_factor))
        return tuple(new)

    zero = jnp.zeros((SUB, LANES), jnp.float32)
    lax.fori_loop(0, levels, body, tuple((zero, zero) for _ in range(halves)))


def step(levels, tracers, rows, chunks, per_chunk, rims_out, spread, *refs):
    refs = list(refs)
    field, east_in, west_in, north_in, south_in = refs[:5]
    stay, from_e, from_w, from_n, from_s, below, above = refs[5:12]
    refs = refs[12:]
    base = refs.pop(0) if spread else None
    out = refs.pop(0)
    if rims_out:
        e_ref, w_ref, s_ref, n_ref = refs[:4]
        refs = refs[4:]
    rim = refs.pop(0)
    solved = refs.pop(0) if spread else out
    lane, sub = lane_iota(), sub_iota()
    plane = tracers * rows
    halves = rows // SUB

    for chunk in range(chunks):
        for r in range(0, plane, SUB):
            rr = pl.ds(r, SUB)
            rim[chunk, rr, :] = jnp.where(
                lane % 2 == 1, east_in[chunk, rr, :], pltpu.roll(west_in[chunk, rr, :], LANES - 2, 1)
            )

    def forward(k, carry):
        chunk, q = k // per_chunk, k % per_chunk
        turn = LANES - 1 - 2 * q
        co = []
        for h in range(halves):
            blk = pl.ds(pl.multiple_of(k * rows + h * SUB, SUB), SUB)
            co.append(tuple(c[blk, :] for c in (stay, from_e, from_w, from_n, from_s, below)))
        new = []
        for t in range(tracers):
            edge_n = north_in[pl.ds(k * tracers + t, 1), :]
            edge_s = south_in[pl.ds(k * tracers + t, 1), :]
            for h in range(halves):
                r = t * rows + h * SUB
                at = k * plane + r
                cell = field[pl.ds(pl.multiple_of(at, SUB), SUB), :]
                side = pltpu.roll(rim[chunk, pl.ds(r, SUB), :], turn, 1)
                e = jnp.where(lane == LANES - 1, side, pltpu.roll(cell, LANES - 1, 1))
                w = jnp.where(lane == 0, side, pltpu.roll(cell, 1, 1))
                if h == halves - 1:
                    n = jnp.where(
                        sub == SUB - 1, jnp.broadcast_to(edge_n, (SUB, LANES)), pltpu.roll(cell, SUB - 1, 0)
                    )
                else:
                    n = field[pl.ds(at + 1, SUB), :]
                if h == 0:
                    s = jnp.where(sub == 0, jnp.broadcast_to(edge_s, (SUB, LANES)), pltpu.roll(cell, 1, 0))
                else:
                    s = field[pl.ds(at - 1, SUB), :]
                c0, ce, cw, cn, cs, a = co[h]
                value = (c0 * cell + ce * e) + (cw * w + cn * n) + (cs * s + a * carry[t * halves + h])
                solved[pl.ds(pl.multiple_of(at, SUB), SUB), :] = value
                new.append(value)
        return tuple(new)

    zero = jnp.zeros((SUB, LANES), jnp.float32)
    lax.fori_loop(0, levels, forward, (zero,) * (tracers * halves))

    if rims_out:
        e_ref[...] = jnp.zeros(e_ref.shape, jnp.float32)
        w_ref[...] = jnp.zeros(w_ref.shape, jnp.float32)

    def backward(i, carry):
        k = levels - 1 - i
        chunk, q = k // per_chunk, k % per_chunk
        new = []
        for h in range(halves):
            f = above[pl.ds(pl.multiple_of(k * rows + h * SUB, SUB), SUB), :]
            for t in range(tracers):
                r = t * rows + h * SUB
                blk = pl.ds(pl.multiple_of(k * plane + r, SUB), SUB)
                value = solved[blk, :] + f * carry[h * tracers + t]
                if not spread:
                    out[blk, :] = value
                if rims_out:
                    put_rim(value, lane, q, chunk, pl.ds(r, SUB), e_ref, w_ref)
                new.append(value)
            if spread:
                for t in range(spread):
                    blk = pl.ds(pl.multiple_of(k * rows * spread + t * rows + h * SUB, SUB), SUB)
                    out[blk, :] = base[blk, :] + new[-1]
        return tuple(new)

    lax.fori_loop(0, levels, backward, (zero,) * (tracers * halves))
    if rims_out:
        put_rows(out, n_ref, s_ref, rows, levels * tracers)


def pack(levels, lon_count, kernel, columns, observed, errors, out):
    per_level = columns.shape[0]
    width = per_level // lon_count
    for i in range(lon_count):
        for m in range(width):
            row = i * width + m
            lanes = pl.ds(m * LANES, LANES)
            out[i, pl.ds(0, levels), lanes] = kernel[pl.ds(row, levels, stride=per_level), :]
            out[i, pl.ds(levels, SUB), lanes] = jnp.concatenate(
                [
                    columns[pl.ds(row, 1), :].astype(jnp.float32),
                    observed[pl.ds(row, 1), :],
                    errors[pl.ds(row, 1), :],
                    jnp.zeros((SUB - 3, LANES), jnp.float32),
                ],
                axis=0,
            )


def repack(rows, lon_count, lat_count, cap, arrived, out):
    lane = lane_iota()
    per_vector = LANES // cap

    def body(b, carry):
        blk = pl.ds(pl.multiple_of(b * SUB, SUB), SUB)
        for j in range(lat_count):
            for col in range(lon_count // per_vector):
                made = None
                for g in range(per_vector):
                    i = col * per_vector + g
                    at = j * cap
                    piece = arrived[i, blk, pl.ds(at // LANES * LANES, LANES)]
                    shift = (g * cap - at % LANES) % LANES
                    if shift:
                        piece = pltpu.roll(piece, shift, 1)
                    made = piece if made is None else jnp.where(lane >= g * cap, piece, made)
                out[j, blk, pl.ds(col * LANES, LANES)] = made
        return carry

    lax.fori_loop(0, rows // SUB, body, 0)


def tracer_sum(concentration, high, low):
    total = jnp.sum(concentration[...], axis=1)
    total = total.reshape(total.shape[0] * total.shape[1], total.shape[2])
    top = total.astype(jnp.bfloat16)
    high[...] = top
    low[...] = (total - top.astype(jnp.float32)).astype(jnp.bfloat16)


def soundings(
    levels, rows, lon_count, lat_count, cap, chunks, per_chunk,
    arrived, high, low, forcing, e_ref, w_ref, s_ref, n_ref, back, table, scaled
):
    width = lon_count * cap
    blocks = levels // SUB
    row_index = lax.broadcasted_iota(jnp.int32, (rows, width), 0)
    cell_index = lax.broadcasted_iota(jnp.int32, (LANES, width), 0)

    def row_mask(j):
        col = arrived[j, pl.ds(levels, 1), :].astype(jnp.int32)
        return row_index == (col >> 7)

    for j in range(lat_count):
        col = arrived[j, pl.ds(levels, 1), :].astype(jnp.int32)
        lookup = jnp.where(cell_index == (col & (LANES - 1)), 1.0, 0.0).astype(jnp.bfloat16)
        table[j, :, :] = lookup

        def gather(b, total, j=j):
            blk = pl.ds(pl.multiple_of(b * SUB * rows, SUB * rows), SUB * rows)
            look = table[j, :, :]
            seen = jnp.dot(high[blk, :], look, preferred_element_type=jnp.float32)
            seen += jnp.dot(low[blk, :], look, preferred_element_type=jnp.float32)
            weight = arrived[j, pl.ds(pl.multiple_of(b * SUB, SUB), SUB), :]
            for kk in range(SUB):
                total += weight[kk : kk + 1, :] * seen[kk * rows : (kk + 1) * rows, :]
            return total

        total = lax.fori_loop(0, blocks, gather, jnp.zeros((rows, width), jnp.float32))
        modelled = jnp.sum(jnp.where(row_mask(j), total, 0.0), axis=0, keepdims=True)
        observed = arrived[j, pl.ds(levels + 1, 1), :]
        error = arrived[j, pl.ds(levels + 2, 1), :]
        residual = jnp.where(col >= 0, (modelled - observed) / error, 0.0)
        scaled[pl.ds(j, 1), :] = residual / error
        for i in range(lon_count):
            at = i * cap
            piece = residual[:, at // LANES * LANES : at // LANES * LANES + LANES]
            if at % LANES:
                piece = pltpu.roll(piece, LANES - at % LANES, 1)
            back[pl.ds(i * lat_count + j, 1), :] = piece

    def scatter(b, carry):
        total = jnp.zeros((SUB * rows, LANES), jnp.float32)
        for j in range(lat_count):
            weight = arrived[j, pl.ds(pl.multiple_of(b * SUB, SUB), SUB), :] * scaled[pl.ds(j, 1), :]
            top = weight.astype(jnp.bfloat16).astype(jnp.float32)
            mask = row_mask(j)
            for part in (top, weight - top):
                spread = jnp.concatenate(
                    [jnp.where(mask, part[kk : kk + 1, :], 0.0) for kk in range(SUB)], axis=0
                ).astype(jnp.bfloat16)
                total += lax.dot_general(
                    spread, table[j, :, :], (((1,), (1,)), ((), ())), preferred_element_type=jnp.float32
                )
        forcing[pl.ds(pl.multiple_of(b * SUB * rows, SUB * rows), SUB * rows), :] = total
        return carry

    lax.fori_loop(0, blocks, scatter, 0)

    lane = lane_iota()
    e_ref[...] = jnp.zeros(e_ref.shape, jnp.float32)
    w_ref[...] = jnp.zeros(w_ref.shape, jnp.float32)
    for chunk in range(chunks):
        def body(q, carry, chunk=chunk):
            for r in range(0, rows, SUB):
                at = pl.multiple_of((chunk * per_chunk + q) * rows + r, SUB)
                put_rim(forcing[pl.ds(at, SUB), :], lane, q, chunk, pl.ds(r, SUB), e_ref, w_ref)
            return carry

        lax.fori_loop(0, min(per_chunk, levels - chunk * per_chunk), body, 0)
    put_rows(forcing, n_ref, s_ref, rows, levels)


def unpack(lon_count, lat_count, cap, arrived, out):
    lane = lax.broadcasted_iota(jnp.int32, (1, LANES), 1)
    per_vector = LANES // cap
    for row in range(out.shape[0]):
        made = None
        for g in range(per_vector):
            piece = arrived[pl.ds(row * per_vector + g, 1), :]
            if g:
                piece = pltpu.roll(piece, g * cap, 1)
            made = piece if made is None else jnp.where(lane >= g * cap, piece, made)
        out[pl.ds(row, 1), :] = made


def shift(value, axis, by, ring):
    count = lax.axis_size(axis)
    if ring:
        pairs = [(i, (i + by) % count) for i in range(count)]
    else:
        pairs = [(i, i + by) for i in range(count) if 0 <= i + by < count]
    return lax.ppermute(value, axis, pairs)


def exchange(east_rim, west_rim, south_rim, north_rim):
    return (
        shift(east_rim, "lon", 1, True),
        shift(west_rim, "lon", -1, True),
        shift(south_rim, "lat", -1, False),
        shift(north_rim, "lat", 1, False),
    )


def per_device(
    concentration, adjoint, wind_east, wind_north, mixing, sound_col, kernel, observed, obs_error
):
    levels, tracers, rows, cols = adjoint.shape
    lon_count, lat_count = lax.axis_size("lon"), lax.axis_size("lat")
    slots = sound_col.shape[2]
    cap = slots // (lon_count * lat_count)
    chunks, per_chunk = rim_chunks(levels)
    plane = tracers * rows
    sent_rows = levels + SUB
    per_level = slots // LANES
    field_bytes = levels * plane * cols * 4

    def flat(x):
        return x.reshape(-1, LANES)

    packed = call(
        functools.partial(pack, levels, lon_count),
        f32(lon_count, sent_rows, lat_count * cap), (), 8, 10, 800000, "pack",
    )(flat(kernel), flat(sound_col), flat(observed), flat(obs_error))
    by_lon = lax.all_to_all(packed, "lon", split_axis=0, concat_axis=0, tiled=True)

    field = flat(adjoint)
    east, north, mix = flat(wind_east), flat(wind_north), flat(mixing)
    rims = call(
        functools.partial(first_rims, levels, tracers, rows, chunks, per_chunk),
        (
            f32(chunks, plane + rows, LANES), f32(chunks, plane, LANES),
            f32(levels * tracers, LANES), f32(levels * tracers + levels, LANES),
        ),
        (), 16, field_bytes, 2 * field_bytes, "first_rims",
    )(field, east, north)
    from_west, from_east, from_north, from_south = exchange(*rims)

    by_lat = call(
        functools.partial(repack, sent_rows, lon_count, lat_count, cap),
        f32(lat_count, sent_rows, lon_count * cap), (), 8, 10, 800000, "repack",
    )(by_lon)
    arrived = lax.all_to_all(by_lat, "lat", split_axis=0, concat_axis=0, tiled=True)

    level_block = SUB
    high, low = pl.pallas_call(
        tracer_sum,
        grid=(levels // level_block,),
        in_specs=[pl.BlockSpec((level_block, tracers, rows, cols), lambda i: (i, 0, 0, 0))],
        out_specs=[pl.BlockSpec((level_block * rows, cols), lambda i: (i, 0))] * 2,
        out_shape=[jax.ShapeDtypeStruct((levels * rows, cols), jnp.bfloat16)] * 2,
        compiler_params=pltpu.CompilerParams(vmem_limit_bytes=8 * MIB),
        cost_estimate=pl.CostEstimate(
            flops=field_bytes // 4, bytes_accessed=field_bytes, transcendentals=0
        ),
        name="tracer_sum",
    )(concentration)

    weights = call(
        functools.partial(coefficients, levels, rows, per_chunk),
        (f32(levels * rows, LANES),) * 7, (), 12, field_bytes * 2, field_bytes * 2, "coefficients",
    )(
        east, north, mix,
        lax.slice_in_dim(from_west, plane, plane + rows, axis=1),
        lax.slice_in_dim(from_south, levels * tracers, levels * tracers + levels, axis=0),
    )

    def rim_shapes(count):
        return (
            f32(chunks, count * rows, LANES), f32(chunks, count * rows, LANES),
            f32(levels * count, LANES), f32(levels * count, LANES),
        )

    def advance(value, rims, count, rims_out, base=None):
        spread = tracers if base is not None else 0
        out = f32(levels * (spread or count) * rows, LANES)
        scratch = [pltpu.VMEM((chunks, count * rows, LANES), jnp.float32)]
        if spread:
            scratch.append(pltpu.VMEM((levels * rows, LANES), jnp.float32))
        return call(
            functools.partial(step, levels, count, rows, chunks, per_chunk, rims_out, spread),
            (out,) + rim_shapes(count) if rims_out else out,
            scratch, 24, field_bytes * count, field_bytes * count // 2 + 4 * field_bytes // 8 * bool(spread),
            "step",
        )(value, *rims, *weights, *(() if base is None else (base,)))

    stepped, *rims = advance(field, (from_west, from_east, from_north, from_south), tracers, True)
    finished = advance(stepped, exchange(*rims), tracers, False)

    forcing, *rest = call(
        functools.partial(soundings, levels, rows, lon_count, lat_count, cap, chunks, per_chunk),
        (f32(levels * rows, LANES),) + rim_shapes(1) + (f32(lon_count * lat_count, LANES),),
        (
            pltpu.VMEM((lat_count, LANES, lon_count * cap), jnp.bfloat16),
            pltpu.VMEM((max(lat_count, SUB), lon_count * cap), jnp.float32),
        ),
        16, field_bytes * 8, field_bytes, "soundings",
    )(arrived, high, low)
    rims, back = rest[:4], rest[4]
    stepped_forcing, *rims = advance(forcing, exchange(*rims), 1, True)

    returned = lax.all_to_all(
        back.reshape(lon_count * lat_count, 1, LANES), ("lon", "lat"),
        split_axis=0, concat_axis=0, tiled=True,
    )
    residual = call(
        functools.partial(unpack, lon_count, lat_count, cap),
        f32(per_level, LANES), (), 4, 10, 10000, "unpack",
    )(returned.reshape(lon_count * lat_count, LANES))

    result = advance(stepped_forcing, exchange(*rims), 1, False, finished)
    return result.reshape(adjoint.shape), residual.reshape(sound_col.shape)


def solution(mesh):
    field = P(None, None, "lat", "lon")
    face = P(None, "lat", "lon")
    owned = P(None, ("lon", "lat"), None)
    return jax.shard_map(
        per_device,
        mesh=mesh,
        in_specs=(field, field, face, face, face, owned, owned, owned, owned),
        out_specs=(field, owned),
        check_vma=False,
    )
```

```python
import functools

import jax
import jax.numpy as jnp
from jax import lax
from jax.experimental import pallas as pl
from jax.experimental.pallas import tpu as pltpu
from jax.sharding import PartitionSpec as P

LANES = 128
SUB = 8
MIB = 1 << 20


def rim_chunks(level_count):
    chunks = -(-level_count // 63)
    return chunks, -(-level_count // chunks)


def lane_iota():
    return lax.broadcasted_iota(jnp.int32, (SUB, LANES), 1)


def sub_iota():
    return lax.broadcasted_iota(jnp.int32, (SUB, LANES), 0)


def call(body, out_shapes, scratch, vmem_mib, flops, bytes_accessed, name):
    return pl.pallas_call(
        body,
        out_shape=out_shapes,
        scratch_shapes=scratch,
        compiler_params=pltpu.CompilerParams(vmem_limit_bytes=vmem_mib * MIB),
        cost_estimate=pl.CostEstimate(
            flops=flops, bytes_accessed=bytes_accessed, transcendentals=0
        ),
        name=name,
    )


def sweep(levels, unroll, level, carry):
    while levels % unroll:
        unroll -= 1

    def body(i, carry):
        for u in range(unroll):
            carry = level(i * unroll + u, carry)
        return carry

    return lax.fori_loop(0, levels // unroll, body, carry)


def f32(*shape):
    return jax.ShapeDtypeStruct(shape, jnp.float32)


def put_rims(field, rows, levels, per_chunk, chunks, out, first, plane):
    lane = lane_iota()

    for chunk in range(chunks):
        count = min(per_chunk, levels - chunk * per_chunk)

        def body(i, carry, chunk=chunk, count=count):
            r = pl.multiple_of(i * SUB, SUB)
            made = jnp.zeros((SUB, LANES), jnp.float32)
            for q in range(count):
                at = pl.multiple_of((chunk * per_chunk + q) * plane + r, SUB)
                turned = pltpu.roll(field[pl.ds(at, SUB), :], 2 * q + 2, 1)
                made = jnp.where(lane >= 2 * q + 1, turned, made)
            out[chunk, pl.ds(pl.multiple_of(first + r, SUB), SUB), :] = made
            return carry

        lax.fori_loop(0, plane // SUB, body, 0)


def put_rows(field, north, south, rows, count):
    unroll = next(u for u in (9, 8, 4, 2, 1) if count // SUB % u == 0)

    def body(i, carry):
        for u in range(unroll):
            start = pl.multiple_of((i * unroll + u) * SUB, SUB)
            at = start * rows
            if south is not None:
                south[pl.ds(start, SUB), :] = field[pl.ds(at, SUB, stride=rows), :]
            north[pl.ds(start, SUB), :] = field[pl.ds(at + rows - 1, SUB, stride=rows), :]
        return carry

    lax.fori_loop(0, count // SUB // unroll, body, 0)


def first_rims(levels, tracers, rows, chunks, per_chunk, field, east, north, side, s_ref, n_ref):
    plane = tracers * rows
    put_rims(field, rows, levels, per_chunk, chunks, side, 0, plane)
    put_rims(east, rows, levels, per_chunk, chunks, side, plane, rows)
    put_rows(field, n_ref.at[pl.ds(0, levels * tracers)], s_ref, rows, levels * tracers)
    put_rows(north, n_ref.at[pl.ds(levels * tracers, levels)], None, rows, levels)


def coefficients(levels, rows, per_chunk, east, north, mixing, east_rim, south_rim, *outs):
    stay, from_e, from_w, from_n, from_s, below, above = outs
    lane, sub = lane_iota(), sub_iota()
    halves = rows // SUB

    def level(k, carry):
        chunk, q = k // per_chunk, k % per_chunk
        has_up = (k < levels - 1).astype(jnp.float32)
        new = []
        tops = []
        for h in range(halves):
            at = pl.multiple_of(k * rows + h * SUB, SUB)
            blk = pl.ds(at, SUB)
            down, factor = carry[h]
            up = mixing[blk, :] * has_up
            pivot = 1.0 + up + down - down * factor
            inv = 1.0 / pivot
            next_factor = up * inv
            e = east[blk, :]
            n = north[blk, :]
            rim = pltpu.roll(east_rim[chunk, pl.ds(h * SUB, SUB), :], LANES - 1 - 2 * q, 1)
            w_in = jnp.minimum(jnp.where(lane == 0, rim, pltpu.roll(e, 1, 1)), 0.0)
            if h == 0:
                edge = south_rim[pl.ds(k, 1), :]
            else:
                edge = tops[h - 1]
            tops.append(n[SUB - 1 : SUB, :])
            s_in = jnp.minimum(
                jnp.where(sub == 0, jnp.broadcast_to(edge, (SUB, LANES)), pltpu.roll(n, 1, 0)), 0.0
            )
            e_out = jnp.maximum(e, 0.0)
            n_out = jnp.maximum(n, 0.0)
            stay[blk, :] = (1.0 - e_out + w_in - n_out + s_in) * inv
            from_e[blk, :] = e_out * inv
            from_w[blk, :] = -(w_in * inv)
            from_n[blk, :] = n_out * inv
            from_s[blk, :] = -(s_in * inv)
            below[blk, :] = down * inv
            above[blk, :] = next_factor
            new.append((up, next_factor))
        return tuple(new)

    zero = jnp.zeros((SUB, LANES), jnp.float32)
    sweep(levels, 8, level, tuple((zero, zero) for _ in range(halves)))


def step(levels, tracers, rows, chunks, per_chunk, rims_out, spread, *refs):
    refs = list(refs)
    field, east_in, west_in, north_in, south_in = refs[:5]
    stay, from_e, from_w, from_n, from_s, below, above = refs[5:12]
    refs = refs[12:]
    base = refs.pop(0) if spread else None
    out = refs.pop(0)
    if rims_out:
        side_ref, s_ref, n_ref = refs[:3]
        refs = refs[3:]
    rim = refs.pop(0)
    solved = refs.pop(0) if spread else out
    lane, sub = lane_iota(), sub_iota()
    plane = tracers * rows
    halves = rows // SUB

    for chunk in range(chunks):
        for r in range(0, plane, SUB):
            rr = pl.ds(r, SUB)
            rim[chunk, rr, :] = jnp.where(
                lane % 2 == 1, east_in[chunk, rr, :], pltpu.roll(west_in[chunk, rr, :], LANES - 2, 1)
            )

    def forward(k, carry):
        chunk, q = k // per_chunk, k % per_chunk
        turn = LANES - 1 - 2 * q
        co = []
        for h in range(halves):
            blk = pl.ds(pl.multiple_of(k * rows + h * SUB, SUB), SUB)
            co.append(tuple(c[blk, :] for c in (stay, from_e, from_w, from_n, from_s, below)))
        new = []
        for t in range(tracers):
            edge_n = north_in[pl.ds(k * tracers + t, 1), :]
            edge_s = south_in[pl.ds(k * tracers + t, 1), :]
            for h in range(halves):
                r = t * rows + h * SUB
                at = k * plane + r
                cell = field[pl.ds(pl.multiple_of(at, SUB), SUB), :]
                side = pltpu.roll(rim[chunk, pl.ds(r, SUB), :], turn, 1)
                e = jnp.where(lane == LANES - 1, side, pltpu.roll(cell, LANES - 1, 1))
                w = jnp.where(lane == 0, side, pltpu.roll(cell, 1, 1))
                if h == halves - 1:
                    n = jnp.where(
                        sub == SUB - 1, jnp.broadcast_to(edge_n, (SUB, LANES)), pltpu.roll(cell, SUB - 1, 0)
                    )
                else:
                    n = field[pl.ds(at + 1, SUB), :]
                if h == 0:
                    s = jnp.where(sub == 0, jnp.broadcast_to(edge_s, (SUB, LANES)), pltpu.roll(cell, 1, 0))
                else:
                    s = field[pl.ds(at - 1, SUB), :]
                c0, ce, cw, cn, cs, a = co[h]
                value = (c0 * cell + ce * e) + (cw * w + cn * n) + (cs * s + a * carry[t * halves + h])
                solved[pl.ds(pl.multiple_of(at, SUB), SUB), :] = value
                new.append(value)
        return tuple(new)

    zero = jnp.zeros((SUB, LANES), jnp.float32)
    unroll = 2 if tracers > 1 else 8
    sweep(levels, unroll, forward, (zero,) * (tracers * halves))

    def backward(i, carry):
        k = levels - 1 - i
        new = []
        for h in range(halves):
            f = above[pl.ds(pl.multiple_of(k * rows + h * SUB, SUB), SUB), :]
            for t in range(tracers):
                r = t * rows + h * SUB
                blk = pl.ds(pl.multiple_of(k * plane + r, SUB), SUB)
                value = solved[blk, :] + f * carry[h * tracers + t]
                if not spread:
                    out[blk, :] = value
                new.append(value)
            if spread:
                for t in range(spread):
                    blk = pl.ds(pl.multiple_of(k * rows * spread + t * rows + h * SUB, SUB), SUB)
                    out[blk, :] = base[blk, :] + new[-1]
        return tuple(new)

    sweep(levels, unroll, backward, (zero,) * (tracers * halves))
    if rims_out:
        put_rims(out, rows, levels, per_chunk, chunks, side_ref, 0, plane)
        put_rows(out, n_ref, s_ref, rows, levels * tracers)


def pack(levels, lon_count, kernel, columns, observed, errors, out):
    per_level = columns.shape[0]
    width = per_level // lon_count
    for i in range(lon_count):
        for m in range(width):
            row = i * width + m
            lanes = pl.ds(m * LANES, LANES)
            out[i, pl.ds(0, levels), lanes] = kernel[pl.ds(row, levels, stride=per_level), :]
            out[i, pl.ds(levels, SUB), lanes] = jnp.concatenate(
                [
                    columns[pl.ds(row, 1), :].astype(jnp.float32),
                    observed[pl.ds(row, 1), :],
                    errors[pl.ds(row, 1), :],
                    jnp.zeros((SUB - 3, LANES), jnp.float32),
                ],
                axis=0,
            )


def repack(rows, lon_count, lat_count, cap, arrived, out):
    lane = lane_iota()
    per_vector = LANES // cap

    def body(b, carry):
        blk = pl.ds(pl.multiple_of(b * SUB, SUB), SUB)
        for j in range(lat_count):
            for col in range(lon_count // per_vector):
                made = None
                for g in range(per_vector):
                    i = col * per_vector + g
                    at = j * cap
                    piece = arrived[i, blk, pl.ds(at // LANES * LANES, LANES)]
                    shift = (g * cap - at % LANES) % LANES
                    if shift:
                        piece = pltpu.roll(piece, shift, 1)
                    made = piece if made is None else jnp.where(lane >= g * cap, piece, made)
                out[j, blk, pl.ds(col * LANES, LANES)] = made
        return carry

    lax.fori_loop(0, rows // SUB, body, 0)


def tracer_sum(concentration, out):
    total = jnp.sum(concentration[...], axis=1)
    levels, rows, cols = total.shape
    for h in range(rows // SUB):
        part = total[:, h * SUB : (h + 1) * SUB, :].reshape(levels * SUB, cols)
        top = part.astype(jnp.bfloat16)
        lanes = pl.ds(h * cols, cols)
        out[0, :, lanes] = top
        out[1, :, lanes] = (part - top.astype(jnp.float32)).astype(jnp.bfloat16)


def soundings(
    levels, rows, lon_count, lat_count, cap, chunks, per_chunk, block,
    arrived, sums, forcing, side_ref, s_ref, n_ref, back, table, scaled
):
    width = lon_count * cap
    halves = rows // SUB
    keys = halves * LANES
    sub_index = lax.broadcasted_iota(jnp.int32, (SUB, width), 0)
    key_index = lax.broadcasted_iota(jnp.int32, (keys, width), 0)
    turned_index = lax.broadcasted_iota(jnp.int32, (LANES, keys), 1)

    def columns(j):
        return arrived[j, pl.ds(levels, 1), :].astype(jnp.int32)

    def key_of(col):
        return (col >> 10) * LANES + (col & (LANES - 1))

    def mask_of(j):
        return sub_index == ((columns(j) >> 7) & (SUB - 1))

    for j in range(lat_count):
        col = columns(j)
        key = key_of(col)
        look = jnp.where(key_index == key, 1.0, 0.0).astype(jnp.bfloat16)
        for c in range(width // LANES):
            piece = key[:, c * LANES : (c + 1) * LANES].astype(jnp.float32)
            across = jnp.broadcast_to(piece, (LANES, LANES)).T.astype(jnp.int32)
            across = jnp.concatenate([across] * halves, axis=1)
            table[j, pl.ds(c * LANES, LANES), :] = jnp.where(turned_index == across, 1.0, 0.0).astype(
                jnp.bfloat16
            )
        total = jnp.zeros((SUB, width), jnp.float32)
        for b in range(levels // block):
            blk = pl.ds(b * block * SUB, block * SUB)
            seen = jnp.dot(sums[0, blk, :], look, preferred_element_type=jnp.float32)
            seen += jnp.dot(sums[1, blk, :], look, preferred_element_type=jnp.float32)
            weight = arrived[j, pl.ds(b * block, block), :]
            for k in range(block):
                total += weight[k : k + 1, :] * seen[k * SUB : (k + 1) * SUB, :]
        modelled = jnp.sum(jnp.where(mask_of(j), total, 0.0), axis=0, keepdims=True)
        observed = arrived[j, pl.ds(levels + 1, 1), :]
        error = arrived[j, pl.ds(levels + 2, 1), :]
        residual = jnp.where(col >= 0, (modelled - observed) / error, 0.0)
        scaled[pl.ds(j, 1), :] = residual / error
        for i in range(lon_count):
            at = i * cap
            piece = residual[:, at // LANES * LANES : at // LANES * LANES + LANES]
            if at % LANES:
                piece = pltpu.roll(piece, LANES - at % LANES, 1)
            back[pl.ds(i * lat_count + j, 1), :] = piece

    for b in range(levels // block):
        total = jnp.zeros((block * SUB, keys), jnp.float32)
        for j in range(lat_count):
            weight = arrived[j, pl.ds(b * block, block), :] * scaled[pl.ds(j, 1), :]
            top = weight.astype(jnp.bfloat16).astype(jnp.float32)
            mask = mask_of(j)
            for part in (top, weight - top):
                spread = jnp.concatenate(
                    [jnp.where(mask, part[k : k + 1, :], 0.0) for k in range(block)], axis=0
                ).astype(jnp.bfloat16)
                total += jnp.dot(spread, table[j, :, :], preferred_element_type=jnp.float32)
        for k in range(block):
            for h in range(halves):
                forcing[pl.ds((b * block + k) * rows + h * SUB, SUB), :] = total[
                    k * SUB : (k + 1) * SUB, h * LANES : (h + 1) * LANES
                ]

    put_rims(forcing, rows, levels, per_chunk, chunks, side_ref, 0, rows)
    put_rows(forcing, n_ref, s_ref, rows, levels)


def unpack(lon_count, lat_count, cap, arrived, out):
    lane = lax.broadcasted_iota(jnp.int32, (1, LANES), 1)
    per_vector = LANES // cap
    for row in range(out.shape[0]):
        made = None
        for g in range(per_vector):
            piece = arrived[pl.ds(row * per_vector + g, 1), :]
            if g:
                piece = pltpu.roll(piece, g * cap, 1)
            made = piece if made is None else jnp.where(lane >= g * cap, piece, made)
        out[pl.ds(row, 1), :] = made


def shift(value, axis, by, ring):
    count = lax.axis_size(axis)
    if ring:
        pairs = [(i, (i + by) % count) for i in range(count)]
    else:
        pairs = [(i, i + by) for i in range(count) if 0 <= i + by < count]
    return lax.ppermute(value, axis, pairs)


def exchange(side_rim, south_rim, north_rim):
    return (
        shift(side_rim, "lon", 1, True),
        shift(side_rim, "lon", -1, True),
        shift(south_rim, "lat", -1, False),
        shift(north_rim, "lat", 1, False),
    )


def per_device(
    concentration, adjoint, wind_east, wind_north, mixing, sound_col, kernel, observed, obs_error
):
    levels, tracers, rows, cols = adjoint.shape
    lon_count, lat_count = lax.axis_size("lon"), lax.axis_size("lat")
    slots = sound_col.shape[2]
    cap = slots // (lon_count * lat_count)
    chunks, per_chunk = rim_chunks(levels)
    plane = tracers * rows
    sent_rows = levels + SUB
    per_level = slots // LANES
    field_bytes = levels * plane * cols * 4

    def flat(x):
        return x.reshape(-1, LANES)

    packed = call(
        functools.partial(pack, levels, lon_count),
        f32(lon_count, sent_rows, lat_count * cap), (), 2, 10, 800000, "pack",
    )(flat(kernel), flat(sound_col), flat(observed), flat(obs_error))
    by_lon = lax.all_to_all(packed, "lon", split_axis=0, concat_axis=0, tiled=True)

    field = flat(adjoint)
    east, north, mix = flat(wind_east), flat(wind_north), flat(mixing)
    rims = call(
        functools.partial(first_rims, levels, tracers, rows, chunks, per_chunk),
        (
            f32(chunks, plane + rows, LANES),
            f32(levels * tracers, LANES), f32(levels * tracers + levels, LANES),
        ),
        (), 2, field_bytes, 2 * field_bytes, "first_rims",
    )(field, east, north)
    from_west, from_east, from_north, from_south = exchange(*rims)

    by_lat = call(
        functools.partial(repack, sent_rows, lon_count, lat_count, cap),
        f32(lat_count, sent_rows, lon_count * cap), (), 2, 10, 800000, "repack",
    )(by_lon)
    arrived = lax.all_to_all(by_lat, "lat", split_axis=0, concat_axis=0, tiled=True)

    sums = call(
        tracer_sum,
        jax.ShapeDtypeStruct((2, levels * SUB, rows // SUB * cols), jnp.bfloat16),
        (), 4, field_bytes // 4, field_bytes, "tracer_sum",
    )(concentration)

    weights = call(
        functools.partial(coefficients, levels, rows, per_chunk),
        (f32(levels * rows, LANES),) * 7, (), 2, field_bytes * 2, field_bytes * 2, "coefficients",
    )(
        east, north, mix,
        lax.slice_in_dim(from_west, plane, plane + rows, axis=1),
        lax.slice_in_dim(from_south, levels * tracers, levels * tracers + levels, axis=0),
    )

    def rim_shapes(count):
        return (
            f32(chunks, count * rows, LANES),
            f32(levels * count, LANES), f32(levels * count, LANES),
        )

    def advance(value, rims, count, rims_out, base=None):
        spread = tracers if base is not None else 0
        out = f32(levels * (spread or count) * rows, LANES)
        scratch = [pltpu.VMEM((chunks, count * rows, LANES), jnp.float32)]
        if spread:
            scratch.append(pltpu.VMEM((levels * rows, LANES), jnp.float32))
        return call(
            functools.partial(step, levels, count, rows, chunks, per_chunk, rims_out, spread),
            (out,) + rim_shapes(count) if rims_out else out,
            scratch, 8 if spread else 2, field_bytes * count, field_bytes * count // 2 + 4 * field_bytes // 8 * bool(spread),
            "step",
        )(value, *rims, *weights, *(() if base is None else (base,)))

    stepped, *rims = advance(field, (from_west, from_east, from_north, from_south), tracers, True)
    finished = advance(stepped, exchange(*rims), tracers, False)

    block = next(u for u in (24, 16, 8) if levels % u == 0)
    forcing, *rest = call(
        functools.partial(soundings, levels, rows, lon_count, lat_count, cap, chunks, per_chunk, block),
        (f32(levels * rows, LANES),) + rim_shapes(1) + (f32(lon_count * lat_count, LANES),),
        (
            pltpu.VMEM((lat_count, lon_count * cap, rows // SUB * LANES), jnp.bfloat16),
            pltpu.VMEM((max(lat_count, SUB), lon_count * cap), jnp.float32),
        ),
        8, field_bytes * 8, field_bytes, "soundings",
    )(arrived, sums)
    rims, back = rest[:3], rest[3]
    stepped_forcing, *rims = advance(forcing, exchange(*rims), 1, True)

    returned = lax.all_to_all(
        back.reshape(lon_count * lat_count, 1, LANES), ("lon", "lat"),
        split_axis=0, concat_axis=0, tiled=True,
    )
    residual = call(
        functools.partial(unpack, lon_count, lat_count, cap),
        f32(per_level, LANES), (), 2, 10, 10000, "unpack",
    )(returned.reshape(lon_count * lat_count, LANES))

    result = advance(stepped_forcing, exchange(*rims), 1, False, finished)
    return result.reshape(adjoint.shape), residual.reshape(sound_col.shape)


def solution(mesh):
    field = P(None, None, "lat", "lon")
    face = P(None, "lat", "lon")
    owned = P(None, ("lon", "lat"), None)
    return jax.shard_map(
        per_device,
        mesh=mesh,
        in_specs=(field, field, face, face, face, owned, owned, owned, owned),
        out_specs=(field, owned),
        check_vma=False,
    )
```

```python
import functools

import jax
import jax.numpy as jnp
from jax import lax
from jax.experimental import pallas as pl
from jax.experimental.pallas import tpu as pltpu
from jax.sharding import PartitionSpec as P

LANES = 128
SUB = 8
MIB = 1 << 20
ANY = pl.BlockSpec(memory_space=pl.ANY)
VMEM = pl.BlockSpec(memory_space=pltpu.VMEM)


def rim_chunks(levels):
    chunks = -(-levels // 63)
    return chunks, -(-levels // chunks)


def lane_iota():
    return lax.broadcasted_iota(jnp.int32, (SUB, LANES), 1)


def sub_iota():
    return lax.broadcasted_iota(jnp.int32, (SUB, LANES), 0)


def largest(count, *choices):
    return next(u for u in choices if count % u == 0)


def f32(*shape):
    return jax.ShapeDtypeStruct(shape, jnp.float32)


def vmem(*shape):
    return pltpu.VMEM(shape, jnp.float32)


def call(body, ins, outs, out_specs, scratch, mib, flops, size, name):
    return pl.pallas_call(
        body,
        in_specs=ins,
        out_specs=out_specs,
        out_shape=outs,
        scratch_shapes=scratch,
        compiler_params=pltpu.CompilerParams(vmem_limit_bytes=mib * MIB),
        cost_estimate=pl.CostEstimate(flops=flops, bytes_accessed=size, transcendentals=0),
        name=name,
    )


def put_rims(field, offset, levels, per_chunk, chunks, out, first, plane):
    lane = lane_iota()
    group = largest(plane // SUB, 4, 2, 1)
    for chunk in range(chunks):
        count = min(per_chunk, levels - chunk * per_chunk)

        def body(i, carry, chunk=chunk, count=count):
            r = pl.multiple_of(i * SUB * group, SUB * group)
            made = [jnp.zeros((SUB, LANES), jnp.float32)] * group
            for q in range(count):
                for g in range(group):
                    at = pl.multiple_of((chunk * per_chunk + q) * plane + offset + r + g * SUB, SUB)
                    turned = pltpu.roll(field[pl.ds(at, SUB), :], 2 * q + 2, 1)
                    made[g] = jnp.where(lane >= 2 * q + 1, turned, made[g])
            for g in range(group):
                out[chunk, pl.ds(pl.multiple_of(first + r + g * SUB, SUB), SUB), :] = made[g]
            return carry

        lax.fori_loop(0, plane // SUB // group, body, 0)


def put_rows(field, offset, north, south, rows, count):
    unroll = largest(count // SUB, 9, 8, 4, 2, 1)

    def body(i, carry):
        for u in range(unroll):
            start = pl.multiple_of((i * unroll + u) * SUB, SUB)
            at = start * rows + offset
            if south is not None:
                south[pl.ds(start, SUB), :] = field[pl.ds(at, SUB, stride=rows), :]
            north[pl.ds(start, SUB), :] = field[pl.ds(at + rows - 1, SUB, stride=rows), :]
        return carry

    lax.fori_loop(0, count // SUB // unroll, body, 0)


def first_rims(levels, tracers, rows, chunks, per_chunk, field, east, north, side, s_ref, n_ref, f, e, n, sems):
    plane = tracers * rows
    half = chunks * 2
    size = levels * plane // half
    wind_copies = [
        pltpu.make_async_copy(east, e, sems.at[half]),
        pltpu.make_async_copy(north, n, sems.at[half + 1]),
    ]
    copies = [
        pltpu.make_async_copy(field.at[pl.ds(i * size, size)], f.at[pl.ds(i * size, size)], sems.at[i])
        for i in range(half)
    ]
    for copy in wind_copies + copies:
        copy.start()
    wind_copies[0].wait()
    put_rims(e, 0, levels, per_chunk, chunks, side, plane, rows)
    wind_copies[1].wait()
    put_rows(n, 0, n_ref.at[pl.ds(levels * tracers, levels)], None, rows, levels)
    for copy in copies:
        copy.wait()
    put_rims(f, 0, levels, per_chunk, chunks, side, 0, plane)
    put_rows(f, 0, n_ref.at[pl.ds(0, levels * tracers)], s_ref, rows, levels * tracers)


def step(levels, tracers, rows, chunks, per_chunk, unroll, first, *refs):
    refs = list(refs)
    field, east, north, mixing, west0, south0 = refs[:6]
    west_in, east_in, north_in, south_in = refs[6:10]
    refs = refs[10:]
    if first:
        forcing, f_west, f_east, f_north, f_south = refs[:5]
        refs = refs[5:]
    out = refs.pop(0)
    if first:
        side_ref, s_ref, n_ref = refs[:3]
        refs = refs[3:]
    buf, e_buf, n_buf, m_buf, above, rim, sems = refs

    plane = tracers * rows
    halves = rows // SUB
    lane, sub = lane_iota(), sub_iota()
    blocks = levels // unroll
    flat = buf.reshape((levels * tracers + 2) * rows, LANES)
    south_flag = (lax.axis_index("lat") > 0).astype(jnp.float32)
    north_flag = (lax.axis_index("lat") < lax.axis_size("lat") - 1).astype(jnp.float32)
    north_mask = jnp.where(sub == SUB - 1, north_flag, 1.0)

    def load(b):
        at = b * unroll * tracers
        return pltpu.make_async_copy(
            field.at[pl.ds(at, unroll * tracers)], buf.at[pl.ds(at + 1, unroll * tracers)], sems.at[b]
        )

    def store(b):
        at = b * unroll * tracers
        return pltpu.make_async_copy(
            buf.at[pl.ds(at + 1, unroll * tracers)], out.at[pl.ds(at, unroll * tracers)], sems.at[b]
        )

    winds = [
        pltpu.make_async_copy(source, target, sems.at[blocks + i])
        for i, (source, target) in enumerate(((east, e_buf), (north, n_buf), (mixing, m_buf)))
    ]
    for copy in winds:
        copy.start()
    for b in range(blocks):
        load(b).start()

    def meet(target, from_west, from_east, source, count):
        for chunk in range(chunks):
            for r in range(0, count, SUB):
                a, b = pl.ds(target + r, SUB), pl.ds(source + r, SUB)
                turned = pltpu.roll(from_east[chunk, b, :], LANES - 2, 1)
                rim[chunk, a, :] = jnp.where(lane % 2 == 1, from_west[chunk, b, :], turned)

    meet(0, west_in, east_in, 0, plane)
    if first:
        meet(plane, f_west, f_east, 0, rows)
    for copy in winds:
        copy.wait()

    def stencil(source, at, rim_row, chunk, turn, edge_n, edge_s, co):
        values = []
        for h in range(halves):
            here = at + h * SUB
            cell = source[pl.ds(pl.multiple_of(here, SUB), SUB), :]
            side = pltpu.roll(rim[chunk, pl.ds(rim_row + h * SUB, SUB), :], turn, 1)
            e = jnp.where(lane == LANES - 1, side, pltpu.roll(cell, LANES - 1, 1))
            w = jnp.where(lane == 0, side, pltpu.roll(cell, 1, 1))
            if h == halves - 1:
                n = jnp.where(sub == SUB - 1, edge_n, pltpu.roll(cell, SUB - 1, 0))
            else:
                n = source[pl.ds(here + 1, SUB), :]
            s = source[pl.ds(here - 1, SUB), :]
            if h == 0:
                s = jnp.where(sub == 0, edge_s, s)
            c0, ce, cw, cn, cs = co[h][:5]
            values.append((c0 * cell + ce * e) + (cw * w + cn * n) + cs * s)
        return values

    def forward(k, carry):
        chunk, q = k // per_chunk, k % per_chunk
        turn = LANES - 1 - 2 * q
        has_up = (k < levels - 1).astype(jnp.float32)
        solved, pivots = carry
        co, new_pivots, edge = [], [], None
        for h in range(halves):
            blk = pl.ds(pl.multiple_of(k * rows + h * SUB, SUB), SUB)
            down, factor = pivots[h]
            up = m_buf[blk, :] * has_up
            inv = 1.0 / (1.0 + up + down - down * factor)
            factor = up * inv
            new_pivots.append((up, factor))
            above[blk, :] = factor
            e, n = e_buf[blk, :], n_buf[blk, :]
            side = pltpu.roll(west0[chunk, pl.ds(plane + h * SUB, SUB), :], turn, 1)
            w_in = jnp.minimum(jnp.where(lane == 0, side, pltpu.roll(e, 1, 1)), 0.0)
            if h == 0:
                edge = south0[pl.ds(levels * tracers + k, 1), :] * south_flag
            s_in = jnp.minimum(jnp.where(sub == 0, edge, pltpu.roll(n, 1, 0)), 0.0)
            edge = n[SUB - 1 : SUB, :]
            e_out, n_out = jnp.maximum(e, 0.0), jnp.maximum(n, 0.0)
            from_n = n_out * inv
            if h == halves - 1:
                from_n = from_n * north_mask
            stay = (1.0 - e_out + w_in - n_out + s_in) * inv
            co.append((stay, e_out * inv, -(w_in * inv), from_n, -(s_in * inv), down * inv))
        extra = None
        if first:
            extra = stencil(
                forcing, k * rows + SUB, plane, chunk, turn,
                f_north[pl.ds(k, 1), :], f_south[pl.ds(k, 1), :], co,
            )
        new = []
        for t in range(tracers):
            at = (k + 1) * plane - plane + (t + 1) * rows
            values = stencil(
                flat, at, t * rows, chunk, turn,
                north_in[pl.ds(k * tracers + t, 1), :], south_in[pl.ds(k * tracers + t, 1), :], co,
            )
            for h in range(halves):
                value = values[h] + co[h][5] * solved[t * halves + h]
                if first:
                    value = value + extra[h]
                new.append(value)
                flat[pl.ds(pl.multiple_of(at + h * SUB, SUB), SUB), :] = value
        return tuple(new), tuple(new_pivots)

    def forward_block(b, carry):
        load(b).wait()
        for u in range(unroll):
            carry = forward(b * unroll + u, carry)
        return carry

    zero = jnp.zeros((SUB, LANES), jnp.float32)
    zeros = (zero,) * (tracers * halves)
    lax.fori_loop(0, blocks, forward_block, (zeros, ((zero, zero),) * halves))

    def backward(k, carry):
        new = []
        for h in range(halves):
            f = above[pl.ds(pl.multiple_of(k * rows + h * SUB, SUB), SUB), :]
            for t in range(tracers):
                blk = pl.ds(pl.multiple_of(k * plane + (t + 1) * rows + h * SUB, SUB), SUB)
                value = flat[blk, :] + f * carry[h * tracers + t]
                flat[blk, :] = value
                new.append(value)
        return tuple(new)

    def backward_block(i, carry):
        b = blocks - 1 - i
        for u in reversed(range(unroll)):
            carry = backward(b * unroll + u, carry)
        store(b).start()
        return carry

    lax.fori_loop(0, blocks, backward_block, zeros)
    if first:
        put_rims(flat, rows, levels, per_chunk, chunks, side_ref, 0, plane)
        put_rows(flat, rows, n_ref, s_ref, rows, levels * tracers)
    for b in range(blocks):
        store(b).wait()


def pack(levels, group_rows, cap, kernel, columns, observed, errors, out, k_buf, c_buf, o_buf, e_buf, wide, sems):
    lane = lane_iota()
    copies = [
        pltpu.make_async_copy(source, target, sems.at[i])
        for i, (source, target) in enumerate(
            ((columns, c_buf), (observed, o_buf), (errors, e_buf), (kernel, k_buf))
        )
    ]
    for copy in copies:
        copy.start()
    for copy in copies:
        copy.wait()
    per_level = columns.shape[0]
    groups = LANES // cap
    pad = groups * group_rows - levels - 3

    def body(i, carry):
        one = pl.ds(i, 1)
        tail = [c_buf[one, :].astype(jnp.float32), o_buf[one, :], e_buf[one, :]]
        wide[pl.ds(0, levels), :] = k_buf[pl.ds(i, levels, stride=per_level), :]
        wide[pl.ds(levels, pad + 3), :] = jnp.concatenate(
            tail + [jnp.zeros((pad, LANES), jnp.float32)], axis=0
        )
        for j in range(groups):
            for m in range(group_rows // SUB):
                made = None
                for g in range(groups):
                    piece = wide[pl.ds(g * group_rows + m * SUB, SUB), :]
                    if g != j:
                        piece = pltpu.roll(piece, (g - j) * cap % LANES, 1)
                    made = piece if made is None else jnp.where(lane >= g * cap, piece, made)
                out[i * groups + j, pl.ds(m * SUB, SUB), :] = made
        return carry

    lax.fori_loop(0, per_level, body, 0)


def tracer_sum(block, concentration, out, buf, sems):
    levels, tracers, rows, cols = buf.shape

    def load(b):
        return pltpu.make_async_copy(
            concentration.at[pl.ds(b * block, block)], buf.at[pl.ds(b * block, block)], sems.at[b]
        )

    for b in range(levels // block):
        load(b).start()

    def body(b, carry):
        load(b).wait()
        for h in range(rows // SUB):
            tops, rests = [], []
            for k in range(block):
                part = jnp.sum(buf[b * block + k, :, pl.ds(h * SUB, SUB), :], axis=0)
                top = part.astype(jnp.bfloat16).astype(jnp.float32)
                tops.append(top)
                rests.append(part - top)
            at = pl.ds(pl.multiple_of(b * block * SUB, block * SUB), block * SUB)
            lanes = pl.ds(h * cols, cols)
            out[0, at, lanes] = jnp.concatenate(tops, axis=0).astype(jnp.bfloat16)
            out[1, at, lanes] = jnp.concatenate(rests, axis=0).astype(jnp.bfloat16)
        return carry

    lax.fori_loop(0, levels // block, body, 0)


def soundings(
    levels, rows, group_rows, cap, chunks, per_chunk, block,
    received, sums, forcing, side_ref, s_ref, n_ref, back, arrived, table, scaled
):
    lane = lane_iota()
    parts, _, width = arrived.shape
    halves = rows // SUB
    keys = halves * LANES
    groups = LANES // cap
    senders = width // cap

    def unpack(c, carry):
        part, col = c // (width // LANES), c % (width // LANES)
        for g in range(groups):
            for m in range(group_rows // SUB):
                made = None
                for p in range(groups):
                    piece = received[c * groups + p, pl.ds(m * SUB, SUB), :]
                    if p != g:
                        piece = pltpu.roll(piece, (p - g) * cap % LANES, 1)
                    made = piece if made is None else jnp.where(lane >= p * cap, piece, made)
                lanes = pl.ds(pl.multiple_of(col * LANES, LANES), LANES)
                arrived[part, pl.ds(g * group_rows + m * SUB, SUB), lanes] = made
        return carry

    lax.fori_loop(0, parts * width // LANES, unpack, 0)

    sub_index = lax.broadcasted_iota(jnp.int32, (SUB, width), 0)
    key_index = lax.broadcasted_iota(jnp.int32, (keys, width), 0)
    turned_index = lax.broadcasted_iota(jnp.int32, (LANES, keys), 1)

    def columns(j):
        return arrived[j, pl.ds(levels, 1), :].astype(jnp.int32)

    def key_of(col):
        return (col >> 10) * LANES + (col & (LANES - 1))

    def mask_of(j):
        return sub_index == ((columns(j) >> 7) & (SUB - 1))

    for j in range(parts):
        col = columns(j)
        key = key_of(col)
        look = jnp.where(key_index == key, 1.0, 0.0).astype(jnp.bfloat16)
        for c in range(width // LANES):
            piece = key[:, c * LANES : (c + 1) * LANES].astype(jnp.float32)
            across = jnp.broadcast_to(piece, (LANES, LANES)).T.astype(jnp.int32)
            across = jnp.concatenate([across] * halves, axis=1)
            table[j, pl.ds(c * LANES, LANES), :] = jnp.where(turned_index == across, 1.0, 0.0).astype(
                jnp.bfloat16
            )
        total = jnp.zeros((SUB, width), jnp.float32)
        for b in range(levels // block):
            blk = pl.ds(b * block * SUB, block * SUB)
            seen = jnp.dot(sums[0, blk, :], look, preferred_element_type=jnp.float32)
            seen += jnp.dot(sums[1, blk, :], look, preferred_element_type=jnp.float32)
            weight = arrived[j, pl.ds(b * block, block), :]
            for k in range(block):
                total += weight[k : k + 1, :] * seen[k * SUB : (k + 1) * SUB, :]
        modelled = jnp.sum(jnp.where(mask_of(j), total, 0.0), axis=0, keepdims=True)
        observed = arrived[j, pl.ds(levels + 1, 1), :]
        error = arrived[j, pl.ds(levels + 2, 1), :]
        residual = jnp.where(col >= 0, (modelled - observed) / error, 0.0)
        scaled[pl.ds(j, 1), :] = residual / error
        for i in range(senders):
            at = i * cap
            piece = residual[:, at // LANES * LANES : at // LANES * LANES + LANES]
            if at % LANES:
                piece = pltpu.roll(piece, LANES - at % LANES, 1)
            back[pl.ds(j * senders + i, 1), :] = piece

    zeros = jnp.zeros((SUB, LANES), jnp.float32)
    forcing[pl.ds(0, SUB), :] = zeros
    forcing[pl.ds(levels * rows + SUB, SUB), :] = zeros
    for b in range(levels // block):
        total = jnp.zeros((block * SUB, keys), jnp.float32)
        for j in range(parts):
            weight = arrived[j, pl.ds(b * block, block), :] * scaled[pl.ds(j, 1), :]
            top = weight.astype(jnp.bfloat16).astype(jnp.float32)
            mask = mask_of(j)
            for part in (top, weight - top):
                spread = jnp.concatenate(
                    [jnp.where(mask, part[k : k + 1, :], 0.0) for k in range(block)], axis=0
                ).astype(jnp.bfloat16)
                total += jnp.dot(spread, table[j, :, :], preferred_element_type=jnp.float32)
        for k in range(block):
            for h in range(halves):
                forcing[pl.ds((b * block + k) * rows + (h + 1) * SUB, SUB), :] = total[
                    k * SUB : (k + 1) * SUB, h * LANES : (h + 1) * LANES
                ]

    put_rims(forcing, SUB, levels, per_chunk, chunks, side_ref, 0, rows)
    put_rows(forcing, SUB, n_ref, s_ref, rows, levels)


def unpack_residual(cap, arrived, out):
    lane = lax.broadcasted_iota(jnp.int32, (1, LANES), 1)
    groups = LANES // cap
    for row in range(out.shape[0]):
        made = None
        for g in range(groups):
            piece = arrived[pl.ds(row * groups + g, 1), :]
            if g:
                piece = pltpu.roll(piece, g * cap, 1)
            made = piece if made is None else jnp.where(lane >= g * cap, piece, made)
        out[pl.ds(row, 1), :] = made


def shift(value, axis, by):
    count = lax.axis_size(axis)
    return lax.ppermute(value, axis, [(i, (i + by) % count) for i in range(count)])


def exchange(side_rim, south_rim, north_rim):
    return (
        shift(side_rim, "lon", 1),
        shift(side_rim, "lon", -1),
        shift(south_rim, "lat", -1),
        shift(north_rim, "lat", 1),
    )


def per_device(
    concentration, adjoint, wind_east, wind_north, mixing, sound_col, kernel, observed, obs_error
):
    levels, tracers, rows, cols = adjoint.shape
    bricks = lax.axis_size("lon") * lax.axis_size("lat")
    slots = sound_col.shape[2]
    cap = slots // bricks
    chunks, per_chunk = rim_chunks(levels)
    plane = tracers * rows
    per_level = slots // LANES
    groups = LANES // cap
    group_rows = -(-(levels + 3) // (groups * SUB)) * SUB
    field_bytes = levels * plane * cols * 4
    dma = pltpu.SemaphoreType.DMA

    def flat(x):
        return x.reshape(-1, LANES)

    packed = call(
        functools.partial(pack, levels, group_rows, cap),
        [ANY] * 4, f32(bricks, group_rows, LANES), VMEM,
        (
            vmem(levels * per_level, LANES), pltpu.VMEM((per_level, LANES), jnp.int32),
            vmem(per_level, LANES), vmem(per_level, LANES), vmem(groups * group_rows, LANES), dma((4,)),
        ),
        4, 10, 800000, "pack",
    )(flat(kernel), flat(sound_col), flat(observed), flat(obs_error))
    received = lax.all_to_all(packed, ("lon", "lat"), split_axis=0, concat_axis=0, tiled=True)

    field = adjoint.reshape(levels * tracers, rows, LANES)
    east, north, mix = flat(wind_east), flat(wind_north), flat(mixing)
    rims = call(
        functools.partial(first_rims, levels, tracers, rows, chunks, per_chunk),
        [ANY] * 3,
        (f32(chunks, plane + rows, LANES), f32(levels * tracers, LANES), f32(levels * tracers + levels, LANES)),
        (VMEM,) * 3,
        (vmem(levels * plane, LANES), vmem(levels * rows, LANES), vmem(levels * rows, LANES), dma((chunks * 2 + 2,))),
        10, field_bytes, 2 * field_bytes, "first_rims",
    )(flat(adjoint), east, north)
    start_rims = exchange(*rims)

    block = largest(levels, 24, 16, 8)
    sum_block = largest(levels, 12, 8)
    sums = call(
        functools.partial(tracer_sum, sum_block),
        [ANY], jax.ShapeDtypeStruct((2, levels * SUB, rows // SUB * cols), jnp.bfloat16), VMEM,
        (vmem(levels, tracers, rows, cols), dma((levels // sum_block,))),
        10, field_bytes // 4, field_bytes, "tracer_sum",
    )(concentration)

    width = largest(slots, 2 * LANES, LANES)
    parts = slots // width
    forcing, *rims, back = call(
        functools.partial(soundings, levels, rows, group_rows, cap, chunks, per_chunk, block),
        [VMEM] * 2,
        (
            f32(levels * rows + 2 * SUB, LANES), f32(chunks, rows, LANES), f32(levels, LANES), f32(levels, LANES),
            f32(bricks, LANES),
        ),
        (VMEM,) * 5,
        (
            vmem(parts, groups * group_rows, width),
            pltpu.VMEM((parts, width, rows // SUB * LANES), jnp.bfloat16),
            vmem(max(parts, SUB), width),
        ),
        16, field_bytes * 8, field_bytes, "soundings",
    )(received, sums)
    forcing_rims = exchange(*rims)

    unroll = largest(levels, 4, 3, 2, 1)

    def advance(value, first, *operands):
        outs, specs = (f32(*value.shape),), (ANY,)
        if first:
            outs += (f32(chunks, plane, LANES), f32(levels * tracers, LANES), f32(levels * tracers, LANES))
            specs += (VMEM,) * 3
        return call(
            functools.partial(step, levels, tracers, rows, chunks, per_chunk, unroll, first),
            [ANY] * 4 + [VMEM] * (2 + len(operands)), outs, specs,
            (
                vmem(levels * tracers + 2, rows, LANES), vmem(levels * rows, LANES), vmem(levels * rows, LANES),
                vmem(levels * rows, LANES), vmem(levels * rows, LANES), vmem(chunks, plane + rows, LANES),
                dma((levels // unroll + 3,)),
            ),
            12, field_bytes * 8, field_bytes * 2, "step",
        )(value, east, north, mix, start_rims[0], start_rims[3], *operands)

    stepped, *rims = advance(field, True, *start_rims, forcing, *forcing_rims)
    (result,) = advance(stepped, False, *exchange(*rims))

    returned = lax.all_to_all(
        back.reshape(bricks, 1, LANES), ("lon", "lat"), split_axis=0, concat_axis=0, tiled=True
    )
    residual = call(
        functools.partial(unpack_residual, cap), [VMEM], f32(per_level, LANES), VMEM, (), 2, 10, 10000, "residual",
    )(returned.reshape(bricks, LANES))
    return result.reshape(adjoint.shape), residual.reshape(sound_col.shape)


def solution(mesh):
    field = P(None, None, "lat", "lon")
    face = P(None, "lat", "lon")
    owned = P(None, ("lon", "lat"), None)
    return jax.shard_map(
        per_device,
        mesh=mesh,
        in_specs=(field, field, face, face, face, owned, owned, owned, owned),
        out_specs=(field, owned),
        check_vma=False,
    )
```

```python
import functools

import jax
import jax.numpy as jnp
from jax import lax
from jax.experimental import pallas as pl
from jax.experimental.pallas import tpu as pltpu
from jax.sharding import PartitionSpec as P

LANES = 128
SUB = 8
MIB = 1 << 20
HBM = pl.BlockSpec(memory_space=pltpu.HBM)
VMEM = pl.BlockSpec(memory_space=pltpu.VMEM)


def rim_chunks(levels):
    chunks = -(-levels // 63)
    return chunks, -(-levels // chunks)


def lane_iota():
    return lax.broadcasted_iota(jnp.int32, (SUB, LANES), 1)


def sub_iota():
    return lax.broadcasted_iota(jnp.int32, (SUB, LANES), 0)


def largest(count, *choices):
    return next(u for u in choices if count % u == 0)


def f32(*shape):
    return jax.ShapeDtypeStruct(shape, jnp.float32)


def vmem(*shape):
    return pltpu.VMEM(shape, jnp.float32)


def call(body, ins, outs, out_specs, scratch, mib, flops, size, name):
    return pl.pallas_call(
        body,
        in_specs=ins,
        out_specs=out_specs,
        out_shape=outs,
        scratch_shapes=scratch,
        compiler_params=pltpu.CompilerParams(vmem_limit_bytes=mib * MIB),
        cost_estimate=pl.CostEstimate(flops=flops, bytes_accessed=size, transcendentals=0),
        name=name,
    )


def put_rims(field, offset, levels, per_chunk, chunk, out, first, plane):
    lane = lane_iota()
    group = largest(plane // SUB, 4, 2, 1)
    count = min(per_chunk, levels - chunk * per_chunk)

    def body(i, carry):
        r = pl.multiple_of(i * SUB * group, SUB * group)
        made = [jnp.zeros((SUB, LANES), jnp.float32)] * group
        for q in range(count):
            for g in range(group):
                at = pl.multiple_of((chunk * per_chunk + q) * plane + offset + r + g * SUB, SUB)
                turned = pltpu.roll(field[pl.ds(at, SUB), :], 2 * q + 2, 1)
                made[g] = jnp.where(lane >= 2 * q + 1, turned, made[g])
        for g in range(group):
            out[chunk, pl.ds(pl.multiple_of(first + r + g * SUB, SUB), SUB), :] = made[g]
        return carry

    lax.fori_loop(0, plane // SUB // group, body, 0)


def put_rows(field, offset, a_ref, b_ref, rows, begin, end):
    unroll = largest((end - begin) // SUB, 9, 8, 4, 2, 1)
    odd = lax.axis_index("lat") % 2
    in_a = (1 - odd) * (rows - 1)
    in_b = odd * (rows - 1)

    def body(i, carry):
        for u in range(unroll):
            start = pl.multiple_of(begin + (i * unroll + u) * SUB, SUB)
            at = start * rows + offset
            a_ref[pl.ds(start, SUB), :] = field[pl.ds(at + in_a, SUB, stride=rows), :]
            b_ref[pl.ds(start, SUB), :] = field[pl.ds(at + in_b, SUB, stride=rows), :]
        return carry

    lax.fori_loop(0, (end - begin) // SUB // unroll, body, 0)


def first_rims(levels, tracers, rows, chunks, per_chunk, field, east, north, side, a_ref, b_ref, f, e, n, sems):
    plane = tracers * rows
    wind_copies = [
        pltpu.make_async_copy(east, e, sems.at[chunks]),
        pltpu.make_async_copy(north, n, sems.at[chunks + 1]),
    ]
    copies = []
    for i in range(chunks):
        part = pl.ds(i * per_chunk * plane, min(per_chunk, levels - i * per_chunk) * plane)
        copies.append(pltpu.make_async_copy(field.at[part], f.at[part], sems.at[i]))
    for copy in wind_copies + copies:
        copy.start()
    wind_copies[0].wait()
    for i in range(chunks):
        put_rims(e, 0, levels, per_chunk, i, side, plane, rows)
    wind_copies[1].wait()
    winds = pl.ds(levels * tracers, levels)
    put_rows(n, 0, a_ref.at[winds], b_ref.at[winds], rows, 0, levels)
    for i in range(chunks):
        copies[i].wait()
        put_rims(f, 0, levels, per_chunk, i, side, 0, plane)
        put_rows(
            f, 0, a_ref, b_ref, rows, i * per_chunk * tracers, min((i + 1) * per_chunk, levels) * tracers
        )


def coefficients(levels, tracers, rows, per_chunk, unroll, east, north, mixing, west0, a0, b0, *refs):
    outs, (e_buf, n_buf, m_buf, sems) = refs[:7], refs[7:]
    plane = tracers * rows
    halves = rows // SUB
    lane, sub = lane_iota(), sub_iota()
    copies = [
        pltpu.make_async_copy(source, target, sems.at[i])
        for i, (source, target) in enumerate(((east, e_buf), (north, n_buf), (mixing, m_buf)))
    ]
    for copy in copies:
        copy.start()
    for copy in copies:
        copy.wait()
    place = lax.axis_index("lat")
    even = jnp.full((1, LANES), place, jnp.int32) % 2 == 0
    south_flag = (place > 0).astype(jnp.float32)
    north_flag = (place < lax.axis_size("lat") - 1).astype(jnp.float32)
    north_mask = jnp.where(sub == SUB - 1, north_flag, 1.0)

    def level(k, pivots):
        chunk, q = k // per_chunk, k % per_chunk
        has_up = (k < levels - 1).astype(jnp.float32)
        new, edge = [], None
        for h in range(halves):
            blk = pl.ds(pl.multiple_of(k * rows + h * SUB, SUB), SUB)
            down, factor = pivots[h]
            up = m_buf[blk, :] * has_up
            inv = 1.0 / (1.0 + up + down - down * factor)
            factor = up * inv
            new.append((up, factor))
            e, n = e_buf[blk, :], n_buf[blk, :]
            side = pltpu.roll(west0[chunk, pl.ds(plane + h * SUB, SUB), :], LANES - 1 - 2 * q, 1)
            w_in = jnp.minimum(jnp.where(lane == 0, side, pltpu.roll(e, 1, 1)), 0.0)
            if h == 0:
                row = pl.ds(levels * tracers + k, 1)
                edge = jnp.where(even, b0[row, :], a0[row, :]) * south_flag
            s_in = jnp.minimum(jnp.where(sub == 0, edge, pltpu.roll(n, 1, 0)), 0.0)
            edge = n[SUB - 1 : SUB, :]
            e_out, n_out = jnp.maximum(e, 0.0), jnp.maximum(n, 0.0)
            from_n = n_out * inv
            if h == halves - 1:
                from_n = from_n * north_mask
            stay = (1.0 - e_out + w_in - n_out + s_in) * inv
            values = (stay, e_out * inv, -(w_in * inv), from_n, -(s_in * inv), down * inv, factor)
            for out, value in zip(outs, values):
                out[blk, :] = value
        return tuple(new)

    def body(b, carry):
        for u in range(unroll):
            carry = level(b * unroll + u, carry)
        return carry

    zero = jnp.zeros((SUB, LANES), jnp.float32)
    lax.fori_loop(0, levels // unroll, body, ((zero, zero),) * halves)


def step(levels, tracers, rows, chunks, per_chunk, unroll, first, *refs):
    refs = list(refs)
    field, weights, (west_in, east_in, a_in, b_in) = refs[0], refs[1:7], refs[8:12]
    above = refs[7]
    refs = refs[12:]
    if first:
        forcing, f_west, f_east, f_a, f_b = refs[:5]
        refs = refs[5:]
    out = refs.pop(0)
    if first:
        side_ref, a_ref, b_ref = refs[:3]
        refs = refs[3:]
    buf, rim, edges, sems = refs

    plane = tracers * rows
    halves = rows // SUB
    lane, sub = lane_iota(), sub_iota()
    blocks = levels // unroll
    flat = buf.reshape((levels * tracers + 2) * rows, LANES)

    def load(b):
        at = b * unroll * tracers
        return pltpu.make_async_copy(
            field.at[pl.ds(at, unroll * tracers)], buf.at[pl.ds(at + 1, unroll * tracers)], sems.at[b]
        )

    def store(b):
        at = b * unroll * tracers
        return pltpu.make_async_copy(
            buf.at[pl.ds(at + 1, unroll * tracers)], out.at[pl.ds(at, unroll * tracers)], sems.at[b]
        )

    for b in range(blocks):
        load(b).start()

    def meet(target, from_west, from_east, count):
        for chunk in range(chunks):
            for r in range(0, count, SUB):
                a, b = pl.ds(target + r, SUB), pl.ds(r, SUB)
                turned = pltpu.roll(from_east[chunk, b, :], LANES - 2, 1)
                rim[chunk, a, :] = jnp.where(lane % 2 == 1, from_west[chunk, b, :], turned)

    even = jnp.full((SUB, LANES), lax.axis_index("lat"), jnp.int32) % 2 == 0

    def pair(target, from_a, from_b, count):
        repeat = largest(count // SUB, 9, 8, 4, 2, 1)

        def body(i, carry):
            for u in range(repeat):
                at = pl.multiple_of((i * repeat + u) * SUB, SUB)
                a, b = from_a[pl.ds(at, SUB), :], from_b[pl.ds(at, SUB), :]
                edges[0, pl.ds(target + at, SUB), :] = jnp.where(even, a, b)
                edges[1, pl.ds(target + at, SUB), :] = jnp.where(even, b, a)
            return carry

        lax.fori_loop(0, count // SUB // repeat, body, 0)

    meet(0, west_in, east_in, plane)
    pair(0, a_in, b_in, levels * tracers)
    if first:
        meet(plane, f_west, f_east, rows)
        pair(levels * tracers, f_a, f_b, levels)

    def stencil(source, at, rim_row, chunk, turn, edge_n, edge_s, co):
        values = []
        for h in range(halves):
            here = at + h * SUB
            cell = source[pl.ds(pl.multiple_of(here, SUB), SUB), :]
            side = pltpu.roll(rim[chunk, pl.ds(rim_row + h * SUB, SUB), :], turn, 1)
            e = jnp.where(lane == LANES - 1, side, pltpu.roll(cell, LANES - 1, 1))
            w = jnp.where(lane == 0, side, pltpu.roll(cell, 1, 1))
            if h == halves - 1:
                n = jnp.where(sub == SUB - 1, edge_n, pltpu.roll(cell, SUB - 1, 0))
            else:
                n = source[pl.ds(here + 1, SUB), :]
            s = source[pl.ds(here - 1, SUB), :]
            if h == 0:
                s = jnp.where(sub == 0, edge_s, s)
            c0, ce, cw, cn, cs = co[h][:5]
            values.append((c0 * cell + ce * e) + (cw * w + cn * n) + cs * s)
        return values

    def edge(side, row):
        return edges[side, pl.ds(row, 1), :]

    def forward(k, solved):
        chunk, q = k // per_chunk, k % per_chunk
        turn = LANES - 1 - 2 * q
        co = []
        for h in range(halves):
            blk = pl.ds(pl.multiple_of(k * rows + h * SUB, SUB), SUB)
            co.append([weight[blk, :] for weight in weights])
        if first:
            row = levels * tracers + k
            extra = stencil(
                forcing, k * rows + SUB, plane, chunk, turn, edge(0, row), edge(1, row), co
            )
        new = []
        for t in range(tracers):
            at = k * plane + (t + 1) * rows
            row = k * tracers + t
            values = stencil(flat, at, t * rows, chunk, turn, edge(0, row), edge(1, row), co)
            for h in range(halves):
                value = values[h]
                if first:
                    value = value + extra[h]
                value = value + co[h][5] * solved[t * halves + h]
                new.append(value)
                flat[pl.ds(pl.multiple_of(at + h * SUB, SUB), SUB), :] = value
        return tuple(new)

    def forward_block(b, carry):
        load(b).wait()
        for u in range(unroll):
            carry = forward(b * unroll + u, carry)
        return carry

    zero = jnp.zeros((SUB, LANES), jnp.float32)
    zeros = (zero,) * (tracers * halves)
    lax.fori_loop(0, blocks, forward_block, zeros)

    def backward(k, carry):
        new = []
        for h in range(halves):
            f = above[pl.ds(pl.multiple_of(k * rows + h * SUB, SUB), SUB), :]
            for t in range(tracers):
                blk = pl.ds(pl.multiple_of(k * plane + (t + 1) * rows + h * SUB, SUB), SUB)
                value = flat[blk, :] + f * carry[h * tracers + t]
                flat[blk, :] = value
                new.append(value)
        return tuple(new)

    def backward_block(i, carry):
        b = blocks - 1 - i
        for u in reversed(range(unroll)):
            carry = backward(b * unroll + u, carry)
        store(b).start()
        return carry

    lax.fori_loop(0, blocks, backward_block, zeros)
    if first:
        for chunk in range(chunks):
            put_rims(flat, rows, levels, per_chunk, chunk, side_ref, 0, plane)
        put_rows(flat, rows, a_ref, b_ref, rows, 0, levels * tracers)
    for b in range(blocks):
        store(b).wait()


def pack(levels, group_rows, cap, kernel, columns, observed, errors, out, k_buf, c_buf, o_buf, e_buf, wide, sems):
    lane = lane_iota()
    copies = [
        pltpu.make_async_copy(source, target, sems.at[i])
        for i, (source, target) in enumerate(
            ((columns, c_buf), (observed, o_buf), (errors, e_buf), (kernel, k_buf))
        )
    ]
    for copy in copies:
        copy.start()
    for copy in copies:
        copy.wait()
    per_level = columns.shape[0]
    groups = LANES // cap
    pad = groups * group_rows - levels - 3

    def body(i, carry):
        one = pl.ds(i, 1)
        tail = [c_buf[one, :].astype(jnp.float32), o_buf[one, :], e_buf[one, :]]
        wide[pl.ds(0, levels), :] = k_buf[pl.ds(i, levels, stride=per_level), :]
        wide[pl.ds(levels, pad + 3), :] = jnp.concatenate(
            tail + [jnp.zeros((pad, LANES), jnp.float32)], axis=0
        )
        for j in range(groups):
            for m in range(group_rows // SUB):
                made = None
                for g in range(groups):
                    piece = wide[pl.ds(g * group_rows + m * SUB, SUB), :]
                    if g != j:
                        piece = pltpu.roll(piece, (g - j) * cap % LANES, 1)
                    made = piece if made is None else jnp.where(lane >= g * cap, piece, made)
                out[i * groups + j, pl.ds(m * SUB, SUB), :] = made
        return carry

    lax.fori_loop(0, per_level, body, 0)


def tracer_sum(block, concentration, out, buf, sems):
    levels, tracers, rows, cols = buf.shape

    def load(b):
        return pltpu.make_async_copy(
            concentration.at[pl.ds(b * block, block)], buf.at[pl.ds(b * block, block)], sems.at[b]
        )

    for b in range(levels // block):
        load(b).start()

    def body(b, carry):
        load(b).wait()
        for h in range(rows // SUB):
            tops, rests = [], []
            for k in range(block):
                part = jnp.sum(buf[b * block + k, :, pl.ds(h * SUB, SUB), :], axis=0)
                top = part.astype(jnp.bfloat16).astype(jnp.float32)
                tops.append(top)
                rests.append(part - top)
            at = pl.ds(pl.multiple_of(b * block * SUB, block * SUB), block * SUB)
            lanes = pl.ds(h * cols, cols)
            out[0, at, lanes] = jnp.concatenate(tops, axis=0).astype(jnp.bfloat16)
            out[1, at, lanes] = jnp.concatenate(rests, axis=0).astype(jnp.bfloat16)
        return carry

    lax.fori_loop(0, levels // block, body, 0)


def soundings(
    levels, rows, group_rows, cap, chunks, per_chunk, block,
    received, sums, forcing, side_ref, a_ref, b_ref, back, arrived, table, scaled
):
    lane = lane_iota()
    parts, _, width = arrived.shape
    halves = rows // SUB
    keys = halves * LANES
    groups = LANES // cap

    def unpack(c, carry):
        part, col = c // (width // LANES), c % (width // LANES)
        for g in range(groups):
            for m in range(group_rows // SUB):
                made = None
                for p in range(groups):
                    piece = received[c * groups + p, pl.ds(m * SUB, SUB), :]
                    if p != g:
                        piece = pltpu.roll(piece, (p - g) * cap % LANES, 1)
                    made = piece if made is None else jnp.where(lane >= p * cap, piece, made)
                lanes = pl.ds(pl.multiple_of(col * LANES, LANES), LANES)
                arrived[part, pl.ds(g * group_rows + m * SUB, SUB), lanes] = made
        return carry

    lax.fori_loop(0, parts * width // LANES, unpack, 0)

    sub_index = lax.broadcasted_iota(jnp.int32, (SUB, width), 0)
    key_index = lax.broadcasted_iota(jnp.int32, (keys, width), 0)
    turned_index = lax.broadcasted_iota(jnp.int32, (LANES, keys), 1)

    def columns(j):
        return arrived[j, pl.ds(levels, 1), :].astype(jnp.int32)

    def key_of(col):
        return (col >> 10) * LANES + (col & (LANES - 1))

    def mask_of(j):
        return sub_index == ((columns(j) >> 7) & (SUB - 1))

    for j in range(parts):
        col = columns(j)
        key = key_of(col)
        look = jnp.where(key_index == key, 1.0, 0.0).astype(jnp.bfloat16)
        for c in range(width // LANES):
            piece = key[:, c * LANES : (c + 1) * LANES].astype(jnp.float32)
            across = jnp.broadcast_to(piece, (LANES, LANES)).T.astype(jnp.int32)
            across = jnp.concatenate([across] * halves, axis=1)
            table[j, pl.ds(c * LANES, LANES), :] = jnp.where(turned_index == across, 1.0, 0.0).astype(
                jnp.bfloat16
            )
        total = jnp.zeros((SUB, width), jnp.float32)
        for b in range(levels // block):
            blk = pl.ds(b * block * SUB, block * SUB)
            seen = jnp.dot(sums[0, blk, :], look, preferred_element_type=jnp.float32)
            seen += jnp.dot(sums[1, blk, :], look, preferred_element_type=jnp.float32)
            weight = arrived[j, pl.ds(b * block, block), :]
            for k in range(block):
                total += weight[k : k + 1, :] * seen[k * SUB : (k + 1) * SUB, :]
        modelled = jnp.sum(jnp.where(mask_of(j), total, 0.0), axis=0, keepdims=True)
        observed = arrived[j, pl.ds(levels + 1, 1), :]
        error = arrived[j, pl.ds(levels + 2, 1), :]
        residual = jnp.where(col >= 0, (modelled - observed) / error, 0.0)
        scaled[pl.ds(j, 1), :] = residual / error
        for c in range(width // LANES):
            back[pl.ds(j * (width // LANES) + c, 1), :] = residual[:, c * LANES : (c + 1) * LANES]

    zeros = jnp.zeros((SUB, LANES), jnp.float32)
    forcing[pl.ds(0, SUB), :] = zeros
    forcing[pl.ds(levels * rows + SUB, SUB), :] = zeros
    for b in range(levels // block):
        total = jnp.zeros((block * SUB, keys), jnp.float32)
        for j in range(parts):
            weight = arrived[j, pl.ds(b * block, block), :] * scaled[pl.ds(j, 1), :]
            top = weight.astype(jnp.bfloat16).astype(jnp.float32)
            mask = mask_of(j)
            for part in (top, weight - top):
                spread = jnp.concatenate(
                    [jnp.where(mask, part[k : k + 1, :], 0.0) for k in range(block)], axis=0
                ).astype(jnp.bfloat16)
                total += jnp.dot(spread, table[j, :, :], preferred_element_type=jnp.float32)
        for k in range(block):
            for h in range(halves):
                forcing[pl.ds((b * block + k) * rows + (h + 1) * SUB, SUB), :] = total[
                    k * SUB : (k + 1) * SUB, h * LANES : (h + 1) * LANES
                ]

    for chunk in range(chunks):
        put_rims(forcing, SUB, levels, per_chunk, chunk, side_ref, 0, rows)
    put_rows(forcing, SUB, a_ref, b_ref, rows, 0, levels)


def unpack_residual(cap, gathered, out):
    lane = lax.broadcasted_iota(jnp.int32, (1, LANES), 1)
    groups = LANES // cap
    me = lax.axis_index("lon") * lax.axis_size("lat") + lax.axis_index("lat")
    mine, place = me // groups, me % groups
    for row in range(out.shape[0]):
        made = None
        for g in range(groups):
            piece = gathered[row * groups + g, pl.ds(mine, 1), :]
            piece = pltpu.roll(piece, (g - place + groups) % groups * cap, 1)
            made = piece if made is None else jnp.where(lane >= g * cap, piece, made)
        out[pl.ds(row, 1), :] = made


def exchange(side_rim, a_rim, b_rim):
    lons, lats = lax.axis_size("lon"), lax.axis_size("lat")

    def partner(j, odd):
        other = j + 1 if j % 2 == odd else j - 1
        return other if 0 <= other < lats else j

    return (
        lax.ppermute(side_rim, "lon", [(i, (i + 1) % lons) for i in range(lons)]),
        lax.ppermute(side_rim, "lon", [((i + 1) % lons, i) for i in range(lons)]),
        lax.ppermute(a_rim, "lat", [(j, partner(j, 0)) for j in range(lats)]),
        lax.ppermute(b_rim, "lat", [(j, partner(j, 1)) for j in range(lats)]),
    )


def per_device(
    concentration, adjoint, wind_east, wind_north, mixing, sound_col, kernel, observed, obs_error
):
    levels, tracers, rows, cols = adjoint.shape
    bricks = lax.axis_size("lon") * lax.axis_size("lat")
    slots = sound_col.shape[2]
    cap = slots // bricks
    chunks, per_chunk = rim_chunks(levels)
    plane = tracers * rows
    per_level = slots // LANES
    groups = LANES // cap
    group_rows = -(-(levels + 3) // (groups * SUB)) * SUB
    field_bytes = levels * plane * cols * 4
    dma = pltpu.SemaphoreType.DMA

    def flat(x):
        return x.reshape(-1, LANES)

    packed = call(
        functools.partial(pack, levels, group_rows, cap),
        [HBM] * 4, f32(bricks, group_rows, LANES), VMEM,
        (
            vmem(levels * per_level, LANES), pltpu.VMEM((per_level, LANES), jnp.int32),
            vmem(per_level, LANES), vmem(per_level, LANES), vmem(groups * group_rows, LANES), dma((4,)),
        ),
        4, 10, 800000, "pack",
    )(flat(kernel), flat(sound_col), flat(observed), flat(obs_error))
    received = lax.all_to_all(packed, ("lon", "lat"), split_axis=0, concat_axis=0, tiled=True)

    field = adjoint.reshape(levels * tracers, rows, LANES)
    east, north, mix = flat(wind_east), flat(wind_north), flat(mixing)
    rims = call(
        functools.partial(first_rims, levels, tracers, rows, chunks, per_chunk),
        [HBM] * 3,
        (f32(chunks, plane + rows, LANES),) + (f32(levels * tracers + levels, LANES),) * 2,
        (VMEM,) * 3,
        (vmem(levels * plane, LANES), vmem(levels * rows, LANES), vmem(levels * rows, LANES), dma((chunks + 2,))),
        10, field_bytes, 2 * field_bytes, "first_rims",
    )(flat(adjoint), east, north)
    start_rims = exchange(*rims)

    block = largest(levels, 24, 16, 8)
    sum_block = largest(levels, 12, 8)
    sums = call(
        functools.partial(tracer_sum, sum_block),
        [HBM], jax.ShapeDtypeStruct((2, levels * SUB, rows // SUB * cols), jnp.bfloat16), VMEM,
        (vmem(levels, tracers, rows, cols), dma((levels // sum_block,))),
        10, field_bytes // 4, field_bytes, "tracer_sum",
    )(concentration)

    width = largest(slots, 2 * LANES, LANES)
    parts = slots // width
    forcing, *rims, back = call(
        functools.partial(soundings, levels, rows, group_rows, cap, chunks, per_chunk, block),
        [VMEM] * 2,
        (
            f32(levels * rows + 2 * SUB, LANES), f32(chunks, rows, LANES), f32(levels, LANES), f32(levels, LANES),
            f32(per_level, LANES),
        ),
        (VMEM,) * 5,
        (
            vmem(parts, groups * group_rows, width),
            pltpu.VMEM((parts, width, rows // SUB * LANES), jnp.bfloat16),
            vmem(max(parts, SUB), width),
        ),
        6, field_bytes * 8, field_bytes, "soundings",
    )(received, sums)
    forcing_rims = exchange(*rims)

    unroll = largest(levels, 8, 4, 3, 2, 1)
    weights = call(
        functools.partial(coefficients, levels, tracers, rows, per_chunk, unroll),
        [HBM] * 3 + [VMEM] * 3, (f32(levels * rows, LANES),) * 7, (VMEM,) * 7,
        (vmem(levels * rows, LANES),) * 3 + (dma((3,)),),
        4, field_bytes, field_bytes, "coefficients",
    )(east, north, mix, start_rims[0], start_rims[2], start_rims[3])

    def advance(value, first, *operands):
        outs, specs = (f32(*value.shape),), (HBM,)
        if first:
            outs += (f32(chunks, plane, LANES), f32(levels * tracers, LANES), f32(levels * tracers, LANES))
            specs += (VMEM,) * 3
        return call(
            functools.partial(step, levels, tracers, rows, chunks, per_chunk, unroll, first),
            [HBM] + [VMEM] * (7 + len(operands)), outs, specs,
            (
                vmem(levels * tracers + 2, rows, LANES), vmem(chunks, plane + rows, LANES),
                vmem(2, levels * tracers + levels, LANES), dma((levels // unroll,)),
            ),
            8, field_bytes * 8, field_bytes * 2, "step",
        )(value, *weights, *operands)

    stepped, *rims = advance(field, True, *start_rims, forcing, *forcing_rims)
    (result,) = advance(stepped, False, *exchange(*rims))

    gathered = lax.all_gather(back, ("lon", "lat"))
    residual = call(
        functools.partial(unpack_residual, cap), [VMEM], f32(per_level, LANES), VMEM, (), 2, 10, 10000, "residual",
    )(gathered)
    return result.reshape(adjoint.shape), residual.reshape(sound_col.shape)


def solution(mesh):
    field = P(None, None, "lat", "lon")
    face = P(None, "lat", "lon")
    owned = P(None, ("lon", "lat"), None)
    return jax.shard_map(
        per_device,
        mesh=mesh,
        in_specs=(field, field, face, face, face, owned, owned, owned, owned),
        out_specs=(field, owned),
        check_vma=False,
    )
```

```python
import functools

import jax
import jax.numpy as jnp
from jax import lax
from jax.experimental import pallas as pl
from jax.experimental.pallas import tpu as pltpu
from jax.sharding import PartitionSpec as P

LANES = 128
SUB = 8
MIB = 1 << 20
HBM = pl.BlockSpec(memory_space=pltpu.HBM)
VMEM = pl.BlockSpec(memory_space=pltpu.VMEM)


def rim_chunks(levels):
    chunks = -(-levels // 63)
    return chunks, -(-levels // chunks)


def lane_iota():
    return lax.broadcasted_iota(jnp.int32, (SUB, LANES), 1)


def sub_iota():
    return lax.broadcasted_iota(jnp.int32, (SUB, LANES), 0)


def largest(count, *choices):
    return next(u for u in choices if count % u == 0)


def in_hbm(x):
    return pltpu.with_memory_space_constraint(x, pltpu.HBM)


def f32(*shape):
    return jax.ShapeDtypeStruct(shape, jnp.float32)


def vmem(*shape):
    return pltpu.VMEM(shape, jnp.float32)


def call(body, ins, outs, out_specs, scratch, mib, flops, size, name):
    return pl.pallas_call(
        body,
        in_specs=ins,
        out_specs=out_specs,
        out_shape=outs,
        scratch_shapes=scratch,
        compiler_params=pltpu.CompilerParams(vmem_limit_bytes=mib * MIB),
        cost_estimate=pl.CostEstimate(flops=flops, bytes_accessed=size, transcendentals=0),
        name=name,
    )


def put_rims(field, offset, levels, per_chunk, chunk, out, first, plane):
    lane = lane_iota()
    group = largest(plane // SUB, 4, 2, 1)
    count = min(per_chunk, levels - chunk * per_chunk)

    def body(i, carry):
        r = pl.multiple_of(i * SUB * group, SUB * group)
        made = [jnp.zeros((SUB, LANES), jnp.float32)] * group
        for q in range(count):
            for g in range(group):
                at = pl.multiple_of((chunk * per_chunk + q) * plane + offset + r + g * SUB, SUB)
                turned = pltpu.roll(field[pl.ds(at, SUB), :], 2 * q + 2, 1)
                made[g] = jnp.where(lane >= 2 * q + 1, turned, made[g])
        for g in range(group):
            out[chunk, pl.ds(pl.multiple_of(first + r + g * SUB, SUB), SUB), :] = made[g]
        return carry

    lax.fori_loop(0, plane // SUB // group, body, 0)


def put_rows(field, offset, a_ref, b_ref, rows, begin, end):
    unroll = largest((end - begin) // SUB, 9, 8, 4, 2, 1)
    odd = lax.axis_index("lat") % 2
    in_a = (1 - odd) * (rows - 1)
    in_b = odd * (rows - 1)

    def body(i, carry):
        for u in range(unroll):
            start = pl.multiple_of(begin + (i * unroll + u) * SUB, SUB)
            at = start * rows + offset
            a_ref[pl.ds(start, SUB), :] = field[pl.ds(at + in_a, SUB, stride=rows), :]
            b_ref[pl.ds(start, SUB), :] = field[pl.ds(at + in_b, SUB, stride=rows), :]
        return carry

    lax.fori_loop(0, (end - begin) // SUB // unroll, body, 0)


def first_rims(levels, tracers, rows, chunks, per_chunk, field, east, north, side, a_ref, b_ref, f, e, n, sems):
    plane = tracers * rows
    wind_copies = [
        pltpu.make_async_copy(east, e, sems.at[chunks]),
        pltpu.make_async_copy(north, n, sems.at[chunks + 1]),
    ]
    copies = []
    for i in range(chunks):
        part = pl.ds(i * per_chunk * plane, min(per_chunk, levels - i * per_chunk) * plane)
        copies.append(pltpu.make_async_copy(field.at[part], f.at[part], sems.at[i]))
    for copy in wind_copies + copies:
        copy.start()
    wind_copies[0].wait()
    for i in range(chunks):
        put_rims(e, 0, levels, per_chunk, i, side, plane, rows)
    wind_copies[1].wait()
    winds = pl.ds(levels * tracers, levels)
    put_rows(n, 0, a_ref.at[winds], b_ref.at[winds], rows, 0, levels)
    for i in range(chunks):
        copies[i].wait()
        put_rims(f, 0, levels, per_chunk, i, side, 0, plane)
        put_rows(
            f, 0, a_ref, b_ref, rows, i * per_chunk * tracers, min((i + 1) * per_chunk, levels) * tracers
        )


def coefficients(levels, tracers, rows, per_chunk, unroll, east, north, mixing, west0, a0, b0, *refs):
    outs, (e_buf, n_buf, m_buf, sems) = refs[:7], refs[7:]
    plane = tracers * rows
    halves = rows // SUB
    lane, sub = lane_iota(), sub_iota()
    copies = [
        pltpu.make_async_copy(source, target, sems.at[i])
        for i, (source, target) in enumerate(((east, e_buf), (north, n_buf), (mixing, m_buf)))
    ]
    for copy in copies:
        copy.start()
    for copy in copies:
        copy.wait()
    place = lax.axis_index("lat")
    even = jnp.full((1, LANES), place, jnp.int32) % 2 == 0
    south_flag = (place > 0).astype(jnp.float32)
    north_flag = (place < lax.axis_size("lat") - 1).astype(jnp.float32)
    north_mask = jnp.where(sub == SUB - 1, north_flag, 1.0)

    def level(k, pivots):
        chunk, q = k // per_chunk, k % per_chunk
        has_up = (k < levels - 1).astype(jnp.float32)
        new, edge = [], None
        for h in range(halves):
            blk = pl.ds(pl.multiple_of(k * rows + h * SUB, SUB), SUB)
            down, factor = pivots[h]
            up = m_buf[blk, :] * has_up
            inv = 1.0 / (1.0 + up + down - down * factor)
            factor = up * inv
            new.append((up, factor))
            e, n = e_buf[blk, :], n_buf[blk, :]
            side = pltpu.roll(west0[chunk, pl.ds(plane + h * SUB, SUB), :], LANES - 1 - 2 * q, 1)
            w_in = jnp.minimum(jnp.where(lane == 0, side, pltpu.roll(e, 1, 1)), 0.0)
            if h == 0:
                row = pl.ds(levels * tracers + k, 1)
                edge = jnp.where(even, b0[row, :], a0[row, :]) * south_flag
            s_in = jnp.minimum(jnp.where(sub == 0, edge, pltpu.roll(n, 1, 0)), 0.0)
            edge = n[SUB - 1 : SUB, :]
            e_out, n_out = jnp.maximum(e, 0.0), jnp.maximum(n, 0.0)
            from_n = n_out * inv
            if h == halves - 1:
                from_n = from_n * north_mask
            stay = (1.0 - e_out + w_in - n_out + s_in) * inv
            values = (stay, e_out * inv, -(w_in * inv), from_n, -(s_in * inv), down * inv, factor)
            for out, value in zip(outs, values):
                out[blk, :] = value
        return tuple(new)

    def body(b, carry):
        for u in range(unroll):
            carry = level(b * unroll + u, carry)
        return carry

    zero = jnp.zeros((SUB, LANES), jnp.float32)
    lax.fori_loop(0, levels // unroll, body, ((zero, zero),) * halves)


def step(levels, tracers, rows, chunks, per_chunk, unroll, first, *refs):
    refs = list(refs)
    field, weights, (west_in, east_in, a_in, b_in) = refs[0], refs[1:7], refs[8:12]
    above = refs[7]
    refs = refs[12:]
    if first:
        forcing, f_west, f_east, f_a, f_b = refs[:5]
        refs = refs[5:]
    out = refs.pop(0)
    if first:
        side_ref, a_ref, b_ref = refs[:3]
        refs = refs[3:]
    buf, rim, edges, sems = refs

    plane = tracers * rows
    halves = rows // SUB
    lane, sub = lane_iota(), sub_iota()
    blocks = levels // unroll
    flat = buf.reshape((levels * tracers + 2) * rows, LANES)

    def load(b):
        at = b * unroll * tracers
        return pltpu.make_async_copy(
            field.at[pl.ds(at, unroll * tracers)], buf.at[pl.ds(at + 1, unroll * tracers)], sems.at[b]
        )

    def store(b):
        at = b * unroll * tracers
        return pltpu.make_async_copy(
            buf.at[pl.ds(at + 1, unroll * tracers)], out.at[pl.ds(at, unroll * tracers)], sems.at[b]
        )

    for b in range(blocks):
        load(b).start()

    def meet(target, from_west, from_east, count):
        for chunk in range(chunks):
            for r in range(0, count, SUB):
                a, b = pl.ds(target + r, SUB), pl.ds(r, SUB)
                turned = pltpu.roll(from_east[chunk, b, :], LANES - 2, 1)
                rim[chunk, a, :] = jnp.where(lane % 2 == 1, from_west[chunk, b, :], turned)

    even = jnp.full((SUB, LANES), lax.axis_index("lat"), jnp.int32) % 2 == 0

    def pair(target, from_a, from_b, count):
        repeat = largest(count // SUB, 9, 8, 4, 2, 1)

        def body(i, carry):
            for u in range(repeat):
                at = pl.multiple_of((i * repeat + u) * SUB, SUB)
                a, b = from_a[pl.ds(at, SUB), :], from_b[pl.ds(at, SUB), :]
                edges[0, pl.ds(target + at, SUB), :] = jnp.where(even, a, b)
                edges[1, pl.ds(target + at, SUB), :] = jnp.where(even, b, a)
            return carry

        lax.fori_loop(0, count // SUB // repeat, body, 0)

    meet(0, west_in, east_in, plane)
    pair(0, a_in, b_in, levels * tracers)
    if first:
        meet(plane, f_west, f_east, rows)
        pair(levels * tracers, f_a, f_b, levels)

    def stencil(source, at, rim_row, chunk, turn, row, h, co):
        here = at + h * SUB
        cell = source[pl.ds(pl.multiple_of(here, SUB), SUB), :]
        side = pltpu.roll(rim[chunk, pl.ds(rim_row + h * SUB, SUB), :], turn, 1)
        e = jnp.where(lane == LANES - 1, side, pltpu.roll(cell, LANES - 1, 1))
        w = jnp.where(lane == 0, side, pltpu.roll(cell, 1, 1))
        if h == halves - 1:
            n = jnp.where(sub == SUB - 1, edges[0, pl.ds(row, 1), :], pltpu.roll(cell, SUB - 1, 0))
        else:
            n = source[pl.ds(here + 1, SUB), :]
        if h == 0:
            s = jnp.where(sub == 0, edges[1, pl.ds(row, 1), :], pltpu.roll(cell, 1, 0))
        else:
            s = source[pl.ds(here - 1, SUB), :]
        c0, ce, cw, cn, cs = co[:5]
        return (c0 * cell + ce * e) + (cw * w + cn * n) + cs * s

    def forward(k, solved):
        chunk, q = k // per_chunk, k % per_chunk
        turn = LANES - 1 - 2 * q
        new = []
        for h in range(halves):
            blk = pl.ds(pl.multiple_of(k * rows + h * SUB, SUB), SUB)
            co = [weight[blk, :] for weight in weights]
            extra = None
            if first:
                extra = stencil(forcing, k * rows + SUB, plane, chunk, turn, levels * tracers + k, h, co)
            for t in range(tracers):
                at = k * plane + (t + 1) * rows
                value = stencil(flat, at, t * rows, chunk, turn, k * tracers + t, h, co)
                if first:
                    value = value + extra
                new.append(value + co[5] * solved[h * tracers + t])
        for h in range(halves):
            for t in range(tracers):
                at = k * plane + (t + 1) * rows + h * SUB
                flat[pl.ds(pl.multiple_of(at, SUB), SUB), :] = new[h * tracers + t]
        return tuple(new)

    def forward_block(b, carry):
        load(b).wait()
        for u in range(unroll):
            carry = forward(b * unroll + u, carry)
        return carry

    zero = jnp.zeros((SUB, LANES), jnp.float32)
    zeros = (zero,) * (tracers * halves)
    lax.fori_loop(0, blocks, forward_block, zeros)

    def backward(k, carry):
        new = []
        for h in range(halves):
            f = above[pl.ds(pl.multiple_of(k * rows + h * SUB, SUB), SUB), :]
            for t in range(tracers):
                blk = pl.ds(pl.multiple_of(k * plane + (t + 1) * rows + h * SUB, SUB), SUB)
                value = flat[blk, :] + f * carry[h * tracers + t]
                flat[blk, :] = value
                new.append(value)
        return tuple(new)

    def backward_block(i, carry):
        b = blocks - 1 - i
        for u in reversed(range(unroll)):
            carry = backward(b * unroll + u, carry)
        store(b).start()
        return carry

    lax.fori_loop(0, blocks, backward_block, zeros)
    if first:
        for chunk in range(chunks):
            put_rims(flat, rows, levels, per_chunk, chunk, side_ref, 0, plane)
        put_rows(flat, rows, a_ref, b_ref, rows, 0, levels * tracers)
    for b in range(blocks):
        store(b).wait()


def pack(levels, group_rows, cap, kernel, columns, observed, errors, out, k_buf, c_buf, o_buf, e_buf, wide, sems):
    lane = lane_iota()
    copies = [
        pltpu.make_async_copy(source, target, sems.at[i])
        for i, (source, target) in enumerate(
            ((columns, c_buf), (observed, o_buf), (errors, e_buf), (kernel, k_buf))
        )
    ]
    for copy in copies:
        copy.start()
    for copy in copies:
        copy.wait()
    per_level = columns.shape[0]
    groups = LANES // cap
    pad = groups * group_rows - levels - 3

    def body(i, carry):
        one = pl.ds(i, 1)
        tail = [c_buf[one, :].astype(jnp.float32), o_buf[one, :], e_buf[one, :]]
        wide[pl.ds(0, levels), :] = k_buf[pl.ds(i, levels, stride=per_level), :]
        wide[pl.ds(levels, pad + 3), :] = jnp.concatenate(
            tail + [jnp.zeros((pad, LANES), jnp.float32)], axis=0
        )
        for j in range(groups):
            for m in range(group_rows // SUB):
                made = None
                for g in range(groups):
                    piece = wide[pl.ds(g * group_rows + m * SUB, SUB), :]
                    if g != j:
                        piece = pltpu.roll(piece, (g - j) * cap % LANES, 1)
                    made = piece if made is None else jnp.where(lane >= g * cap, piece, made)
                out[i * groups + j, pl.ds(m * SUB, SUB), :] = made
        return carry

    lax.fori_loop(0, per_level, body, 0)


def tracer_sum(block, concentration, out, buf, sems):
    levels, tracers, rows, cols = buf.shape

    def load(b):
        return pltpu.make_async_copy(
            concentration.at[pl.ds(b * block, block)], buf.at[pl.ds(b * block, block)], sems.at[b]
        )

    for b in range(levels // block):
        load(b).start()

    def body(b, carry):
        load(b).wait()
        for h in range(rows // SUB):
            tops, rests = [], []
            for k in range(block):
                part = jnp.sum(buf[b * block + k, :, pl.ds(h * SUB, SUB), :], axis=0)
                top = part.astype(jnp.bfloat16).astype(jnp.float32)
                tops.append(top)
                rests.append(part - top)
            at = pl.ds(pl.multiple_of(b * block * SUB, block * SUB), block * SUB)
            lanes = pl.ds(h * cols, cols)
            out[0, at, lanes] = jnp.concatenate(tops, axis=0).astype(jnp.bfloat16)
            out[1, at, lanes] = jnp.concatenate(rests, axis=0).astype(jnp.bfloat16)
        return carry

    lax.fori_loop(0, levels // block, body, 0)


def soundings(
    levels, rows, group_rows, cap, chunks, per_chunk, block,
    received, sums, forcing, side_ref, a_ref, b_ref, back, arrived, table, scaled
):
    lane = lane_iota()
    parts, _, width = arrived.shape
    halves = rows // SUB
    keys = halves * LANES
    groups = LANES // cap

    def unpack(c, carry):
        part, col = c // (width // LANES), c % (width // LANES)
        for g in range(groups):
            for m in range(group_rows // SUB):
                made = None
                for p in range(groups):
                    piece = received[c * groups + p, pl.ds(m * SUB, SUB), :]
                    if p != g:
                        piece = pltpu.roll(piece, (p - g) * cap % LANES, 1)
                    made = piece if made is None else jnp.where(lane >= p * cap, piece, made)
                lanes = pl.ds(pl.multiple_of(col * LANES, LANES), LANES)
                arrived[part, pl.ds(g * group_rows + m * SUB, SUB), lanes] = made
        return carry

    lax.fori_loop(0, parts * width // LANES, unpack, 0)

    sub_index = lax.broadcasted_iota(jnp.int32, (SUB, width), 0)
    key_index = lax.broadcasted_iota(jnp.int32, (keys, width), 0)
    turned_index = lax.broadcasted_iota(jnp.int32, (LANES, keys), 1)

    def columns(j):
        return arrived[j, pl.ds(levels, 1), :].astype(jnp.int32)

    def key_of(col):
        return (col >> 10) * LANES + (col & (LANES - 1))

    def mask_of(j):
        return sub_index == ((columns(j) >> 7) & (SUB - 1))

    for j in range(parts):
        col = columns(j)
        key = key_of(col)
        look = jnp.where(key_index == key, 1.0, 0.0).astype(jnp.bfloat16)
        for c in range(width // LANES):
            piece = key[:, c * LANES : (c + 1) * LANES].astype(jnp.float32)
            across = jnp.broadcast_to(piece, (LANES, LANES)).T.astype(jnp.int32)
            across = jnp.concatenate([across] * halves, axis=1)
            table[j, pl.ds(c * LANES, LANES), :] = jnp.where(turned_index == across, 1.0, 0.0).astype(
                jnp.bfloat16
            )
        total = jnp.zeros((SUB, width), jnp.float32)
        for b in range(levels // block):
            blk = pl.ds(b * block * SUB, block * SUB)
            seen = jnp.dot(sums[0, blk, :], look, preferred_element_type=jnp.float32)
            seen += jnp.dot(sums[1, blk, :], look, preferred_element_type=jnp.float32)
            weight = arrived[j, pl.ds(b * block, block), :]
            for k in range(block):
                total += weight[k : k + 1, :] * seen[k * SUB : (k + 1) * SUB, :]
        modelled = jnp.sum(jnp.where(mask_of(j), total, 0.0), axis=0, keepdims=True)
        observed = arrived[j, pl.ds(levels + 1, 1), :]
        error = arrived[j, pl.ds(levels + 2, 1), :]
        residual = jnp.where(col >= 0, (modelled - observed) / error, 0.0)
        scaled[pl.ds(j, 1), :] = residual / error
        for i in range(width // cap):
            at = i * cap
            piece = residual[:, at // LANES * LANES : at // LANES * LANES + LANES]
            if at % LANES:
                piece = pltpu.roll(piece, LANES - at % LANES, 1)
            back[pl.ds(j * (width // cap) + i, 1), :] = piece

    zeros = jnp.zeros((SUB, LANES), jnp.float32)
    forcing[pl.ds(0, SUB), :] = zeros
    forcing[pl.ds(levels * rows + SUB, SUB), :] = zeros
    for b in range(levels // block):
        total = jnp.zeros((block * SUB, keys), jnp.float32)
        for j in range(parts):
            weight = arrived[j, pl.ds(b * block, block), :] * scaled[pl.ds(j, 1), :]
            top = weight.astype(jnp.bfloat16).astype(jnp.float32)
            mask = mask_of(j)
            for part in (top, weight - top):
                spread = jnp.concatenate(
                    [jnp.where(mask, part[k : k + 1, :], 0.0) for k in range(block)], axis=0
                ).astype(jnp.bfloat16)
                total += jnp.dot(spread, table[j, :, :], preferred_element_type=jnp.float32)
        for k in range(block):
            for h in range(halves):
                forcing[pl.ds((b * block + k) * rows + (h + 1) * SUB, SUB), :] = total[
                    k * SUB : (k + 1) * SUB, h * LANES : (h + 1) * LANES
                ]

    for chunk in range(chunks):
        put_rims(forcing, SUB, levels, per_chunk, chunk, side_ref, 0, rows)
    put_rows(forcing, SUB, a_ref, b_ref, rows, 0, levels)


def unpack_residual(cap, arrived, out):
    lane = lax.broadcasted_iota(jnp.int32, (1, LANES), 1)
    groups = LANES // cap
    for row in range(out.shape[0]):
        made = None
        for g in range(groups):
            piece = arrived[pl.ds(row * groups + g, 1), :]
            if g:
                piece = pltpu.roll(piece, g * cap, 1)
            made = piece if made is None else jnp.where(lane >= g * cap, piece, made)
        out[pl.ds(row, 1), :] = made


def exchange(side_rim, a_rim, b_rim):
    lons, lats = lax.axis_size("lon"), lax.axis_size("lat")

    def partner(j, odd):
        other = j + 1 if j % 2 == odd else j - 1
        return other if 0 <= other < lats else j

    return (
        lax.ppermute(side_rim, "lon", [(i, (i + 1) % lons) for i in range(lons)]),
        lax.ppermute(side_rim, "lon", [((i + 1) % lons, i) for i in range(lons)]),
        lax.ppermute(a_rim, "lat", [(j, partner(j, 0)) for j in range(lats)]),
        lax.ppermute(b_rim, "lat", [(j, partner(j, 1)) for j in range(lats)]),
    )


def per_device(
    concentration, adjoint, wind_east, wind_north, mixing, sound_col, kernel, observed, obs_error
):
    levels, tracers, rows, cols = adjoint.shape
    bricks = lax.axis_size("lon") * lax.axis_size("lat")
    slots = sound_col.shape[2]
    cap = slots // bricks
    chunks, per_chunk = rim_chunks(levels)
    plane = tracers * rows
    per_level = slots // LANES
    groups = LANES // cap
    group_rows = -(-(levels + 3) // (groups * SUB)) * SUB
    field_bytes = levels * plane * cols * 4
    dma = pltpu.SemaphoreType.DMA

    def flat(x):
        return x.reshape(-1, LANES)

    packed = call(
        functools.partial(pack, levels, group_rows, cap),
        [HBM] * 4, f32(bricks, group_rows, LANES), VMEM,
        (
            vmem(levels * per_level, LANES), pltpu.VMEM((per_level, LANES), jnp.int32),
            vmem(per_level, LANES), vmem(per_level, LANES), vmem(groups * group_rows, LANES), dma((4,)),
        ),
        4, 10, 800000, "pack",
    )(*(in_hbm(flat(x)) for x in (kernel, sound_col, observed, obs_error)))
    received = lax.all_to_all(packed, ("lon", "lat"), split_axis=0, concat_axis=0, tiled=True)

    field = adjoint.reshape(levels * tracers, rows, LANES)
    east, north, mix = (in_hbm(flat(x)) for x in (wind_east, wind_north, mixing))
    rims = call(
        functools.partial(first_rims, levels, tracers, rows, chunks, per_chunk),
        [HBM] * 3,
        (f32(chunks, plane + rows, LANES),) + (f32(levels * tracers + levels, LANES),) * 2,
        (VMEM,) * 3,
        (vmem(levels * plane, LANES), vmem(levels * rows, LANES), vmem(levels * rows, LANES), dma((chunks + 2,))),
        10, field_bytes, 2 * field_bytes, "first_rims",
    )(in_hbm(flat(adjoint)), east, north)
    start_rims = exchange(*rims)

    block = largest(levels, 24, 16, 8)
    sum_block = largest(levels, 12, 8)
    sums = call(
        functools.partial(tracer_sum, sum_block),
        [HBM], jax.ShapeDtypeStruct((2, levels * SUB, rows // SUB * cols), jnp.bfloat16), VMEM,
        (vmem(levels, tracers, rows, cols), dma((levels // sum_block,))),
        10, field_bytes // 4, field_bytes, "tracer_sum",
    )(concentration)

    width = largest(slots, 2 * LANES, LANES)
    parts = slots // width
    forcing, *rims, back = call(
        functools.partial(soundings, levels, rows, group_rows, cap, chunks, per_chunk, block),
        [VMEM] * 2,
        (
            f32(levels * rows + 2 * SUB, LANES), f32(chunks, rows, LANES), f32(levels, LANES), f32(levels, LANES),
            f32(bricks, LANES),
        ),
        (VMEM,) * 5,
        (
            vmem(parts, groups * group_rows, width),
            pltpu.VMEM((parts, width, rows // SUB * LANES), jnp.bfloat16),
            vmem(max(parts, SUB), width),
        ),
        10, field_bytes * 8, field_bytes, "soundings",
    )(received, sums)
    forcing_rims = exchange(*rims)

    unroll = largest(levels, 8, 4, 3, 2, 1)
    weights = call(
        functools.partial(coefficients, levels, tracers, rows, per_chunk, unroll),
        [HBM] * 3 + [VMEM] * 3, (f32(levels * rows, LANES),) * 7, (VMEM,) * 7,
        (vmem(levels * rows, LANES),) * 3 + (dma((3,)),),
        4, field_bytes, field_bytes, "coefficients",
    )(east, north, mix, start_rims[0], start_rims[2], start_rims[3])

    def advance(value, first, *operands):
        outs, specs = (f32(*value.shape),), (HBM,)
        if first:
            outs += (f32(chunks, plane, LANES), f32(levels * tracers, LANES), f32(levels * tracers, LANES))
            specs += (VMEM,) * 3
        return call(
            functools.partial(step, levels, tracers, rows, chunks, per_chunk, unroll, first),
            [HBM] + [VMEM] * (7 + len(operands)), outs, specs,
            (
                vmem(levels * tracers + 2, rows, LANES), vmem(chunks, plane + rows, LANES),
                vmem(2, levels * tracers + levels, LANES), dma((levels // unroll,)),
            ),
            8, field_bytes * 8, field_bytes * 2, "step",
        )(value, *weights, *operands)

    stepped, *rims = advance(in_hbm(field), True, *start_rims, forcing, *forcing_rims)
    (result,) = advance(stepped, False, *exchange(*rims))

    returned = lax.all_to_all(
        back.reshape(bricks, 1, LANES), ("lon", "lat"), split_axis=0, concat_axis=0, tiled=True
    )
    result, returned = lax.optimization_barrier((result, returned))
    residual = call(
        functools.partial(unpack_residual, cap), [VMEM], f32(per_level, LANES), VMEM, (), 2, 10, 10000, "residual",
    )(returned.reshape(bricks, LANES))
    return result.reshape(adjoint.shape), residual.reshape(sound_col.shape)


def solution(mesh):
    field = P(None, None, "lat", "lon")
    face = P(None, "lat", "lon")
    owned = P(None, ("lon", "lat"), None)
    return jax.shard_map(
        per_device,
        mesh=mesh,
        in_specs=(field, field, face, face, face, owned, owned, owned, owned),
        out_specs=(field, owned),
        check_vma=False,
    )
```

```python
import functools

import jax
import jax.numpy as jnp
from jax import lax
from jax.experimental import pallas as pl
from jax.experimental.pallas import tpu as pltpu
from jax.sharding import PartitionSpec as P

LANES = 128
SUB = 8
MIB = 1 << 20
ANY = pl.BlockSpec(memory_space=pl.ANY)
HBM = pl.BlockSpec(memory_space=pltpu.HBM)
VMEM = pl.BlockSpec(memory_space=pltpu.VMEM)


def rim_chunks(levels, unroll):
    per_chunk = 63 // unroll * unroll
    chunks = -(-levels // per_chunk)
    return chunks, -(-levels // (chunks * unroll)) * unroll


def lane_iota():
    return lax.broadcasted_iota(jnp.int32, (SUB, LANES), 1)


def sub_iota():
    return lax.broadcasted_iota(jnp.int32, (SUB, LANES), 0)


def largest(count, *choices):
    return next(u for u in choices if count % u == 0)


def in_hbm(x):
    return pltpu.with_memory_space_constraint(x, pltpu.HBM)


def hbm(*shape):
    return pltpu.HBM(shape, jnp.float32)


def f32(*shape):
    return jax.ShapeDtypeStruct(shape, jnp.float32)


def vmem(*shape):
    return pltpu.VMEM(shape, jnp.float32)


def call(body, ins, outs, out_specs, scratch, mib, flops, size, name):
    return pl.pallas_call(
        body,
        in_specs=ins,
        out_specs=out_specs,
        out_shape=outs,
        scratch_shapes=scratch,
        compiler_params=pltpu.CompilerParams(vmem_limit_bytes=mib * MIB),
        cost_estimate=pl.CostEstimate(flops=flops, bytes_accessed=size, transcendentals=0),
        name=name,
    )


def put_rims(field, offset, levels, per_chunk, chunk, out, first, plane):
    lane = lane_iota()
    group = largest(plane // SUB, 4, 2, 1)
    count = min(per_chunk, levels - chunk * per_chunk)

    def body(i, carry):
        r = pl.multiple_of(i * SUB * group, SUB * group)
        made = [jnp.zeros((SUB, LANES), jnp.float32)] * group
        for q in range(count):
            for g in range(group):
                at = pl.multiple_of((chunk * per_chunk + q) * plane + offset + r + g * SUB, SUB)
                turned = pltpu.roll(field[pl.ds(at, SUB), :], 2 * q + 2, 1)
                made[g] = jnp.where(lane >= 2 * q + 1, turned, made[g])
        for g in range(group):
            out[chunk, pl.ds(pl.multiple_of(first + r + g * SUB, SUB), SUB), :] = made[g]
        return carry

    lax.fori_loop(0, plane // SUB // group, body, 0)


def put_rows(field, offset, a_ref, b_ref, rows, begin, end):
    unroll = largest((end - begin) // SUB, 9, 8, 4, 2, 1)
    odd = lax.axis_index("lat") % 2
    in_a = (1 - odd) * (rows - 1)
    in_b = odd * (rows - 1)

    def body(i, carry):
        for u in range(unroll):
            start = pl.multiple_of(begin + (i * unroll + u) * SUB, SUB)
            at = start * rows + offset
            a_ref[pl.ds(start, SUB), :] = field[pl.ds(at + in_a, SUB, stride=rows), :]
            b_ref[pl.ds(start, SUB), :] = field[pl.ds(at + in_b, SUB, stride=rows), :]
        return carry

    lax.fori_loop(0, (end - begin) // SUB // unroll, body, 0)


def first_rims(levels, tracers, rows, chunks, per_chunk, field, east, north, side, a_ref, b_ref, f, e, n, sems):
    plane = tracers * rows
    wind_copies = [
        pltpu.make_async_copy(east, e, sems.at[chunks]),
        pltpu.make_async_copy(north, n, sems.at[chunks + 1]),
    ]
    copies = []
    for i in range(chunks):
        part = pl.ds(i * per_chunk * plane, min(per_chunk, levels - i * per_chunk) * plane)
        copies.append(pltpu.make_async_copy(field.at[part], f.at[part], sems.at[i]))
    for copy in wind_copies + copies:
        copy.start()
    wind_copies[0].wait()
    for i in range(chunks):
        put_rims(e, 0, levels, per_chunk, i, side, plane, rows)
    wind_copies[1].wait()
    winds = pl.ds(levels * tracers, levels)
    put_rows(n, 0, a_ref.at[winds], b_ref.at[winds], rows, 0, levels)
    for i in range(chunks):
        copies[i].wait()
        put_rims(f, 0, levels, per_chunk, i, side, 0, plane)
        put_rows(
            f, 0, a_ref, b_ref, rows, i * per_chunk * tracers, min((i + 1) * per_chunk, levels) * tracers
        )


def coefficients(levels, tracers, rows, per_chunk, unroll, east, north, mixing, west0, a0, b0, *refs):
    outs, (e_buf, n_buf, m_buf, w_rim, a_rim, b_rim, sems) = refs[:7], refs[7:]
    plane = tracers * rows
    halves = rows // SUB
    lane, sub = lane_iota(), sub_iota()
    copies = [
        pltpu.make_async_copy(source, target, sems.at[i])
        for i, (source, target) in enumerate(
            (
                (east, e_buf), (north, n_buf), (mixing, m_buf), (west0.at[:, pl.ds(plane, rows)], w_rim),
                (a0.at[pl.ds(levels * tracers, levels)], a_rim), (b0.at[pl.ds(levels * tracers, levels)], b_rim),
            )
        )
    ]
    for copy in copies:
        copy.start()
    for copy in copies:
        copy.wait()
    place = lax.axis_index("lat")
    even = jnp.full((1, LANES), place, jnp.int32) % 2 == 0
    south_flag = (place > 0).astype(jnp.float32)
    north_flag = (place < lax.axis_size("lat") - 1).astype(jnp.float32)
    north_mask = jnp.where(sub == SUB - 1, north_flag, 1.0)

    def level(k, pivots):
        chunk, q = k // per_chunk, k % per_chunk
        has_up = (k < levels - 1).astype(jnp.float32)
        new, edge = [], None
        for h in range(halves):
            blk = pl.ds(pl.multiple_of(k * rows + h * SUB, SUB), SUB)
            down, factor = pivots[h]
            up = m_buf[blk, :] * has_up
            inv = 1.0 / (1.0 + up + down - down * factor)
            factor = up * inv
            new.append((up, factor))
            e, n = e_buf[blk, :], n_buf[blk, :]
            side = pltpu.roll(w_rim[chunk, pl.ds(h * SUB, SUB), :], LANES - 1 - 2 * q, 1)
            w_in = jnp.minimum(jnp.where(lane == 0, side, pltpu.roll(e, 1, 1)), 0.0)
            if h == 0:
                row = pl.ds(k, 1)
                edge = jnp.where(even, b_rim[row, :], a_rim[row, :]) * south_flag
            s_in = jnp.minimum(jnp.where(sub == 0, edge, pltpu.roll(n, 1, 0)), 0.0)
            edge = n[SUB - 1 : SUB, :]
            e_out, n_out = jnp.maximum(e, 0.0), jnp.maximum(n, 0.0)
            from_n = n_out * inv
            if h == halves - 1:
                from_n = from_n * north_mask
            stay = (1.0 - e_out + w_in - n_out + s_in) * inv
            values = (stay, e_out * inv, -(w_in * inv), from_n, -(s_in * inv), down * inv, factor)
            for out, value in zip(outs, values):
                out[blk, :] = value
        return tuple(new)

    def body(b, carry):
        for u in range(unroll):
            carry = level(b * unroll + u, carry)
        return carry

    zero = jnp.zeros((SUB, LANES), jnp.float32)
    lax.fori_loop(0, levels // unroll, body, ((zero, zero),) * halves)


def step(levels, tracers, rows, chunks, per_chunk, unroll, first, *refs):
    refs = list(refs)
    weights, (field, above_in, *rims_in) = refs[:6], refs[6:12]
    refs = refs[12:]
    if first:
        forcing, f_west, f_east, f_a, f_b = refs[:5]
        refs = refs[5:]
    out = refs.pop(0)
    if first:
        side_ref, a_ref, b_ref = refs[:3]
        refs = refs[3:]
    buf, above, west_buf, east_buf, a_buf, b_buf, rim, edges, sems = refs

    plane = tracers * rows
    halves = rows // SUB
    lane, sub = lane_iota(), sub_iota()
    blocks = levels // unroll
    flat = buf.reshape((levels * tracers + 2) * rows, LANES)

    def load(b):
        at = b * unroll * tracers
        return pltpu.make_async_copy(
            field.at[pl.ds(at, unroll * tracers)], buf.at[pl.ds(at + 1, unroll * tracers)], sems.at[b]
        )

    def store(b):
        at = b * unroll * tracers
        return pltpu.make_async_copy(
            buf.at[pl.ds(at + 1, unroll * tracers)], out.at[pl.ds(at, unroll * tracers)], sems.at[b]
        )

    columns, latitudes = pl.ds(0, plane), pl.ds(0, levels * tracers)
    rim_copies = [
        pltpu.make_async_copy(source, target, sems.at[blocks + i])
        for i, (source, target) in enumerate(
            (
                (rims_in[0].at[:, columns], west_buf), (rims_in[1].at[:, columns], east_buf),
                (rims_in[2].at[latitudes], a_buf), (rims_in[3].at[latitudes], b_buf),
            )
        )
    ]
    above_copy = pltpu.make_async_copy(above_in, above, sems.at[blocks + 4])
    load(0).start()
    for copy in rim_copies:
        copy.start()
    for b in range(1, blocks):
        load(b).start()
    above_copy.start()

    def meet(target, from_west, from_east, count):
        for chunk in range(chunks):
            for r in range(0, count, SUB):
                a, b = pl.ds(target + r, SUB), pl.ds(r, SUB)
                turned = pltpu.roll(from_east[chunk, b, :], LANES - 2, 1)
                rim[chunk, a, :] = jnp.where(lane % 2 == 1, from_west[chunk, b, :], turned)

    even = jnp.full((SUB, LANES), lax.axis_index("lat"), jnp.int32) % 2 == 0

    def pair(target, from_a, from_b, count):
        repeat = largest(count // SUB, 9, 8, 4, 2, 1)

        def body(i, carry):
            for u in range(repeat):
                at = pl.multiple_of((i * repeat + u) * SUB, SUB)
                a, b = from_a[pl.ds(at, SUB), :], from_b[pl.ds(at, SUB), :]
                edges[0, pl.ds(target + at, SUB), :] = jnp.where(even, a, b)
                edges[1, pl.ds(target + at, SUB), :] = jnp.where(even, b, a)
            return carry

        lax.fori_loop(0, count // SUB // repeat, body, 0)

    if first:
        meet(plane, f_west, f_east, rows)
        pair(levels * tracers, f_a, f_b, levels)
    for copy in rim_copies:
        copy.wait()
    meet(0, west_buf, east_buf, plane)
    pair(0, a_buf, b_buf, levels * tracers)

    def stencil(source, at, rim_row, chunk, turn, row, h, co):
        here = at + h * SUB
        cell = source[pl.ds(pl.multiple_of(here, SUB), SUB), :]
        side = pltpu.roll(rim[chunk, pl.ds(rim_row + h * SUB, SUB), :], turn, 1)
        e = jnp.where(lane == LANES - 1, side, pltpu.roll(cell, LANES - 1, 1))
        w = jnp.where(lane == 0, side, pltpu.roll(cell, 1, 1))
        n = source[pl.ds(here + 1, SUB), :]
        s = source[pl.ds(here - 1, SUB), :]
        if h == halves - 1:
            n = jnp.where(sub == SUB - 1, edges[0, pl.ds(row, 1), :], n)
        if h == 0:
            s = jnp.where(sub == 0, edges[1, pl.ds(row, 1), :], s)
        c0, ce, cw, cn, cs = co[:5]
        return (c0 * cell + ce * e) + (cw * w + cn * n) + cs * s

    def forward(k, chunk, q, solved):
        turn = LANES - 1 - 2 * q
        co, extra, new = [], [], []
        for h in range(halves):
            blk = pl.ds(pl.multiple_of(k * rows + h * SUB, SUB), SUB)
            co.append([weight[blk, :] for weight in weights])
            if first:
                row = levels * tracers + k
                extra.append(stencil(forcing, k * rows + SUB, plane, chunk, turn, row, h, co[h]))
        for t in range(tracers):
            at = k * plane + (t + 1) * rows
            values = [
                stencil(flat, at, t * rows, chunk, turn, k * tracers + t, h, co[h]) for h in range(halves)
            ]
            for h in range(halves):
                value = values[h] + extra[h] if first else values[h]
                value = value + co[h][5] * solved[t * halves + h]
                new.append(value)
                flat[pl.ds(pl.multiple_of(at + h * SUB, SUB), SUB), :] = value
        return tuple(new)

    def forward_block(b, carry):
        @pl.when(b < blocks - 1)
        def _():
            load(b + 1).wait()

        chunk, q = b * unroll // per_chunk, b * unroll % per_chunk
        for u in range(unroll):
            carry = forward(b * unroll + u, chunk, q + u, carry)
        return carry

    zero = jnp.zeros((SUB, LANES), jnp.float32)
    zeros = (zero,) * (tracers * halves)
    load(0).wait()
    lax.fori_loop(0, blocks, forward_block, zeros)
    above_copy.wait()

    def backward(k, carry):
        new = []
        for h in range(halves):
            f = above[pl.ds(pl.multiple_of(k * rows + h * SUB, SUB), SUB), :]
            for t in range(tracers):
                blk = pl.ds(pl.multiple_of(k * plane + (t + 1) * rows + h * SUB, SUB), SUB)
                value = flat[blk, :] + f * carry[h * tracers + t]
                flat[blk, :] = value
                new.append(value)
        return tuple(new)

    def backward_block(i, carry):
        b = blocks - 1 - i
        for u in reversed(range(unroll)):
            carry = backward(b * unroll + u, carry)
        store(b).start()
        return carry

    lax.fori_loop(0, blocks, backward_block, zeros)
    if first:
        for chunk in range(chunks):
            put_rims(flat, rows, levels, per_chunk, chunk, side_ref, 0, plane)
        put_rows(flat, rows, a_ref, b_ref, rows, 0, levels * tracers)
    for b in range(blocks):
        store(b).wait()


def pack(levels, group_rows, cap, kernel, columns, observed, errors, out, k_buf, c_buf, o_buf, e_buf, wide, sems):
    lane = lane_iota()
    copies = [
        pltpu.make_async_copy(source, target, sems.at[i])
        for i, (source, target) in enumerate(
            ((columns, c_buf), (observed, o_buf), (errors, e_buf), (kernel, k_buf))
        )
    ]
    for copy in copies:
        copy.start()
    for copy in copies:
        copy.wait()
    per_level = columns.shape[0]
    groups = LANES // cap
    pad = groups * group_rows - levels - 3

    together = wide.shape[0]

    def body(start, carry):
        for n in range(together):
            i = start * together + n
            one = pl.ds(i, 1)
            tail = [c_buf[one, :].astype(jnp.float32), o_buf[one, :], e_buf[one, :]]
            wide[n, pl.ds(0, levels), :] = k_buf[pl.ds(i, levels, stride=per_level), :]
            wide[n, pl.ds(levels, pad + 3), :] = jnp.concatenate(
                tail + [jnp.zeros((pad, LANES), jnp.float32)], axis=0
            )
        for n in range(together):
            i = start * together + n
            for j in range(groups):
                for m in range(group_rows // SUB):
                    made = None
                    for g in range(groups):
                        piece = wide[n, pl.ds(g * group_rows + m * SUB, SUB), :]
                        if g != j:
                            piece = pltpu.roll(piece, (g - j) * cap % LANES, 1)
                        made = piece if made is None else jnp.where(lane >= g * cap, piece, made)
                    out[i * groups + j, pl.ds(m * SUB, SUB), :] = made
        return carry

    lax.fori_loop(0, per_level // together, body, 0)


def tracer_sum(block, concentration, out, buf, sems):
    levels, tracers, rows, cols = buf.shape

    def load(b):
        return pltpu.make_async_copy(
            concentration.at[pl.ds(b * block, block)], buf.at[pl.ds(b * block, block)], sems.at[b]
        )

    for b in range(levels // block):
        load(b).start()

    def body(b, carry):
        load(b).wait()
        for h in range(rows // SUB):
            tops, rests = [], []
            for k in range(block):
                part = jnp.sum(buf[b * block + k, :, pl.ds(h * SUB, SUB), :], axis=0)
                top = part.astype(jnp.bfloat16).astype(jnp.float32)
                tops.append(top)
                rests.append(part - top)
            at = pl.ds(pl.multiple_of(b * block * SUB, block * SUB), block * SUB)
            lanes = pl.ds(h * cols, cols)
            out[0, at, lanes] = jnp.concatenate(tops, axis=0).astype(jnp.bfloat16)
            out[1, at, lanes] = jnp.concatenate(rests, axis=0).astype(jnp.bfloat16)
        return carry

    lax.fori_loop(0, levels // block, body, 0)


def soundings(
    levels, rows, group_rows, cap, chunks, per_chunk, block,
    received, sums, forcing, side_ref, a_ref, b_ref, back, arrived, table, scaled
):
    lane = lane_iota()
    parts, _, width = arrived.shape
    halves = rows // SUB
    keys = halves * LANES
    groups = LANES // cap

    def unpack(c, carry):
        part, col = c // (width // LANES), c % (width // LANES)
        for g in range(groups):
            for m in range(group_rows // SUB):
                made = None
                for p in range(groups):
                    piece = received[c * groups + p, pl.ds(m * SUB, SUB), :]
                    if p != g:
                        piece = pltpu.roll(piece, (p - g) * cap % LANES, 1)
                    made = piece if made is None else jnp.where(lane >= p * cap, piece, made)
                lanes = pl.ds(pl.multiple_of(col * LANES, LANES), LANES)
                arrived[part, pl.ds(g * group_rows + m * SUB, SUB), lanes] = made
        return carry

    lax.fori_loop(0, parts * width // LANES, unpack, 0)

    sub_index = lax.broadcasted_iota(jnp.int32, (SUB, width), 0)
    key_index = lax.broadcasted_iota(jnp.int32, (keys, width), 0)
    turned_index = lax.broadcasted_iota(jnp.int32, (LANES, keys), 1)

    def columns(j):
        return arrived[j, pl.ds(levels, 1), :].astype(jnp.int32)

    def key_of(col):
        return (col >> 10) * LANES + (col & (LANES - 1))

    def mask_of(j):
        return sub_index == ((columns(j) >> 7) & (SUB - 1))

    for j in range(parts):
        col = columns(j)
        key = key_of(col)
        look = jnp.where(key_index == key, 1.0, 0.0).astype(jnp.bfloat16)
        for c in range(width // LANES):
            piece = key[:, c * LANES : (c + 1) * LANES].astype(jnp.float32)
            across = jnp.broadcast_to(piece, (LANES, LANES)).T.astype(jnp.int32)
            across = jnp.concatenate([across] * halves, axis=1)
            table[j, pl.ds(c * LANES, LANES), :] = jnp.where(turned_index == across, 1.0, 0.0).astype(
                jnp.bfloat16
            )
        total = jnp.zeros((SUB, width), jnp.float32)
        for b in range(levels // block):
            blk = pl.ds(b * block * SUB, block * SUB)
            seen = jnp.dot(sums[0, blk, :], look, preferred_element_type=jnp.float32)
            seen += jnp.dot(sums[1, blk, :], look, preferred_element_type=jnp.float32)
            weight = arrived[j, pl.ds(b * block, block), :]
            for k in range(block):
                total += weight[k : k + 1, :] * seen[k * SUB : (k + 1) * SUB, :]
        modelled = jnp.sum(jnp.where(mask_of(j), total, 0.0), axis=0, keepdims=True)
        observed = arrived[j, pl.ds(levels + 1, 1), :]
        error = arrived[j, pl.ds(levels + 2, 1), :]
        residual = jnp.where(col >= 0, (modelled - observed) / error, 0.0)
        scaled[pl.ds(j, 1), :] = residual / error
        for i in range(width // cap):
            at = i * cap
            piece = residual[:, at // LANES * LANES : at // LANES * LANES + LANES]
            if at % LANES:
                piece = pltpu.roll(piece, LANES - at % LANES, 1)
            back[pl.ds(j * (width // cap) + i, 1), :] = piece

    zeros = jnp.zeros((SUB, LANES), jnp.float32)
    forcing[pl.ds(0, SUB), :] = zeros
    forcing[pl.ds(levels * rows + SUB, SUB), :] = zeros
    for b in range(levels // block):
        total = jnp.zeros((block * SUB, keys), jnp.float32)
        for j in range(parts):
            weight = arrived[j, pl.ds(b * block, block), :] * scaled[pl.ds(j, 1), :]
            top = weight.astype(jnp.bfloat16).astype(jnp.float32)
            mask = mask_of(j)
            for part in (top, weight - top):
                spread = jnp.concatenate(
                    [jnp.where(mask, part[k : k + 1, :], 0.0) for k in range(block)], axis=0
                ).astype(jnp.bfloat16)
                total += jnp.dot(spread, table[j, :, :], preferred_element_type=jnp.float32)
        for k in range(block):
            for h in range(halves):
                forcing[pl.ds((b * block + k) * rows + (h + 1) * SUB, SUB), :] = total[
                    k * SUB : (k + 1) * SUB, h * LANES : (h + 1) * LANES
                ]

    for chunk in range(chunks):
        put_rims(forcing, SUB, levels, per_chunk, chunk, side_ref, 0, rows)
    put_rows(forcing, SUB, a_ref, b_ref, rows, 0, levels)


def unpack_residual(cap, arrived, out):
    lane = lax.broadcasted_iota(jnp.int32, (1, LANES), 1)
    groups = LANES // cap
    for row in range(out.shape[0]):
        made = None
        for g in range(groups):
            piece = arrived[pl.ds(row * groups + g, 1), :]
            if g:
                piece = pltpu.roll(piece, g * cap, 1)
            made = piece if made is None else jnp.where(lane >= g * cap, piece, made)
        out[pl.ds(row, 1), :] = made


def exchange(side_rim, a_rim, b_rim):
    lons, lats = lax.axis_size("lon"), lax.axis_size("lat")

    def partner(j, odd):
        other = j + 1 if j % 2 == odd else j - 1
        return other if 0 <= other < lats else j

    return (
        lax.ppermute(side_rim, "lon", [(i, (i + 1) % lons) for i in range(lons)]),
        lax.ppermute(side_rim, "lon", [((i + 1) % lons, i) for i in range(lons)]),
        lax.ppermute(a_rim, "lat", [(j, partner(j, 0)) for j in range(lats)]),
        lax.ppermute(b_rim, "lat", [(j, partner(j, 1)) for j in range(lats)]),
    )


def per_device(
    concentration, adjoint, wind_east, wind_north, mixing, sound_col, kernel, observed, obs_error
):
    levels, tracers, rows, cols = adjoint.shape
    bricks = lax.axis_size("lon") * lax.axis_size("lat")
    slots = sound_col.shape[2]
    cap = slots // bricks
    unroll = largest(levels, 8, 4, 3, 2, 1)
    chunks, per_chunk = rim_chunks(levels, unroll)
    plane = tracers * rows
    per_level = slots // LANES
    groups = LANES // cap
    group_rows = -(-(levels + 3) // (groups * SUB)) * SUB
    field_bytes = levels * plane * cols * 4
    dma = pltpu.SemaphoreType.DMA

    def flat(x):
        return x.reshape(-1, LANES)

    packed = call(
        functools.partial(pack, levels, group_rows, cap),
        [HBM] * 4, f32(bricks, group_rows, LANES), VMEM,
        (
            vmem(levels * per_level, LANES), pltpu.VMEM((per_level, LANES), jnp.int32),
            vmem(per_level, LANES), vmem(per_level, LANES),
            vmem(largest(per_level, 8, 4, 2, 1), groups * group_rows, LANES), dma((4,)),
        ),
        4, 10, 800000, "pack",
    )(*(in_hbm(flat(x)) for x in (kernel, sound_col, observed, obs_error)))
    received = lax.all_to_all(packed, ("lon", "lat"), split_axis=0, concat_axis=0, tiled=True)

    field = adjoint.reshape(levels * tracers, rows, LANES)
    east, north, mix = (in_hbm(flat(x)) for x in (wind_east, wind_north, mixing))
    rims = call(
        functools.partial(first_rims, levels, tracers, rows, chunks, per_chunk),
        [HBM] * 3,
        (f32(chunks, plane + rows, LANES),) + (f32(levels * tracers + levels, LANES),) * 2,
        (VMEM,) * 3,
        (vmem(levels * plane, LANES), vmem(levels * rows, LANES), vmem(levels * rows, LANES), dma((chunks + 2,))),
        10, field_bytes, 2 * field_bytes, "first_rims",
    )(in_hbm(flat(adjoint)), east, north)
    start_rims = exchange(*rims)

    block = largest(levels, 24, 16, 8)
    sum_block = largest(levels, 12, 8)
    sums = call(
        functools.partial(tracer_sum, sum_block),
        [HBM], jax.ShapeDtypeStruct((2, levels * SUB, rows // SUB * cols), jnp.bfloat16), VMEM,
        (vmem(levels, tracers, rows, cols), dma((levels // sum_block,))),
        10, field_bytes // 4, field_bytes, "tracer_sum",
    )(concentration)

    width = largest(slots, 2 * LANES, LANES)
    parts = slots // width
    forcing, *rims, back = call(
        functools.partial(soundings, levels, rows, group_rows, cap, chunks, per_chunk, block),
        [VMEM] * 2,
        (
            f32(levels * rows + 2 * SUB, LANES), f32(chunks, rows, LANES), f32(levels, LANES), f32(levels, LANES),
            hbm(bricks, LANES),
        ),
        (VMEM,) * 5,
        (
            vmem(parts, groups * group_rows, width),
            pltpu.VMEM((parts, width, rows // SUB * LANES), jnp.bfloat16),
            vmem(max(parts, SUB), width),
        ),
        10, field_bytes * 8, field_bytes, "soundings",
    )(received, sums)
    forcing_rims = exchange(*rims)

    *weights, above = call(
        functools.partial(coefficients, levels, tracers, rows, per_chunk, unroll),
        [HBM] * 3 + [ANY] * 3, (f32(levels * rows, LANES),) * 6 + (hbm(levels * rows, LANES),), (VMEM,) * 7,
        (vmem(levels * rows, LANES),) * 3
        + (vmem(chunks, rows, LANES), vmem(levels, LANES), vmem(levels, LANES), dma((6,))),
        4, field_bytes, field_bytes, "coefficients",
    )(east, north, mix, start_rims[0], start_rims[2], start_rims[3])

    def advance(value, rims, first, *operands):
        outs, specs = ((hbm if first else f32)(*value.shape),), (HBM,)
        if first:
            outs += (f32(chunks, plane, LANES), f32(levels * tracers, LANES), f32(levels * tracers, LANES))
            specs += (VMEM,) * 3
        return call(
            functools.partial(step, levels, tracers, rows, chunks, per_chunk, unroll, first),
            [VMEM] * 6 + [HBM] * 2 + [ANY] * 4 + [VMEM] * len(operands), outs, specs,
            (
                vmem(levels * tracers + 2, rows, LANES), vmem(levels * rows, LANES),
                vmem(chunks, plane, LANES), vmem(chunks, plane, LANES),
                vmem(levels * tracers, LANES), vmem(levels * tracers, LANES),
                vmem(chunks, plane + rows, LANES), vmem(2, levels * tracers + levels, LANES),
                dma((levels // unroll + 5,)),
            ),
            10, field_bytes * 8, field_bytes * 2, "step",
        )(*weights, in_hbm(value), in_hbm(above), *rims, *operands)

    stepped, *rims = advance(field, start_rims, True, forcing, *forcing_rims)
    (result,) = advance(stepped, exchange(*rims), False)

    returned = lax.all_to_all(
        back.reshape(bricks, 1, LANES), ("lon", "lat"), split_axis=0, concat_axis=0, tiled=True
    )
    result, returned = lax.optimization_barrier((result, returned))
    residual = call(
        functools.partial(unpack_residual, cap), [VMEM], f32(per_level, LANES), VMEM, (), 2, 10, 10000, "residual",
    )(returned.reshape(bricks, LANES))
    return result.reshape(adjoint.shape), residual.reshape(sound_col.shape)


def solution(mesh):
    field = P(None, None, "lat", "lon")
    face = P(None, "lat", "lon")
    owned = P(None, ("lon", "lat"), None)
    return jax.shard_map(
        per_device,
        mesh=mesh,
        in_specs=(field, field, face, face, face, owned, owned, owned, owned),
        out_specs=(field, owned),
        check_vma=False,
    )
```

```python
import functools

import jax
import jax.numpy as jnp
from jax import lax
from jax.experimental import pallas as pl
from jax.experimental.pallas import tpu as pltpu
from jax.sharding import PartitionSpec as P

LANES = 128
SUB = 8
MIB = 1 << 20
ANY = pl.BlockSpec(memory_space=pl.ANY)
HBM = pl.BlockSpec(memory_space=pltpu.HBM)
VMEM = pl.BlockSpec(memory_space=pltpu.VMEM)


def rim_chunks(levels, unroll):
    per_chunk = 63 // unroll * unroll
    chunks = -(-levels // per_chunk)
    return chunks, -(-levels // (chunks * unroll)) * unroll


def lane_iota():
    return lax.broadcasted_iota(jnp.int32, (SUB, LANES), 1)


def sub_iota():
    return lax.broadcasted_iota(jnp.int32, (SUB, LANES), 0)


def largest(count, *choices):
    return next(u for u in choices if count % u == 0)


def in_hbm(x):
    return pltpu.with_memory_space_constraint(x, pltpu.HBM)


def hbm(*shape):
    return pltpu.HBM(shape, jnp.float32)


def f32(*shape):
    return jax.ShapeDtypeStruct(shape, jnp.float32)


def vmem(*shape):
    return pltpu.VMEM(shape, jnp.float32)


def call(body, ins, outs, out_specs, scratch, mib, flops, size, name):
    return pl.pallas_call(
        body,
        in_specs=ins,
        out_specs=out_specs,
        out_shape=outs,
        scratch_shapes=scratch,
        compiler_params=pltpu.CompilerParams(vmem_limit_bytes=mib * MIB),
        cost_estimate=pl.CostEstimate(flops=flops, bytes_accessed=size, transcendentals=0),
        name=name,
    )


def put_rims(field, offset, levels, per_chunk, chunk, out, first, plane):
    lane = lane_iota()
    group = largest(plane // SUB, 4, 2, 1)
    count = min(per_chunk, levels - chunk * per_chunk)

    def body(i, carry):
        r = pl.multiple_of(i * SUB * group, SUB * group)
        made = [jnp.zeros((SUB, LANES), jnp.float32)] * group
        for q in range(count):
            for g in range(group):
                at = pl.multiple_of((chunk * per_chunk + q) * plane + offset + r + g * SUB, SUB)
                turned = pltpu.roll(field[pl.ds(at, SUB), :], 2 * q + 2, 1)
                made[g] = jnp.where(lane >= 2 * q + 1, turned, made[g])
        for g in range(group):
            out[chunk, pl.ds(pl.multiple_of(first + r + g * SUB, SUB), SUB), :] = made[g]
        return carry

    lax.fori_loop(0, plane // SUB // group, body, 0)


def put_rows(field, offset, a_ref, b_ref, rows, begin, end):
    unroll = largest((end - begin) // SUB, 9, 8, 4, 2, 1)
    odd = lax.axis_index("lat") % 2
    in_a = (1 - odd) * (rows - 1)
    in_b = odd * (rows - 1)

    def body(i, carry):
        for u in range(unroll):
            start = pl.multiple_of(begin + (i * unroll + u) * SUB, SUB)
            at = start * rows + offset
            a_ref[pl.ds(start, SUB), :] = field[pl.ds(at + in_a, SUB, stride=rows), :]
            b_ref[pl.ds(start, SUB), :] = field[pl.ds(at + in_b, SUB, stride=rows), :]
        return carry

    lax.fori_loop(0, (end - begin) // SUB // unroll, body, 0)


def first_rims(levels, tracers, rows, chunks, per_chunk, field, east, north, side, a_ref, b_ref, f, e, n, sems):
    plane = tracers * rows
    wind_copies = [
        pltpu.make_async_copy(east, e, sems.at[chunks]),
        pltpu.make_async_copy(north, n, sems.at[chunks + 1]),
    ]
    copies = []
    for i in range(chunks):
        part = pl.ds(i * per_chunk * plane, min(per_chunk, levels - i * per_chunk) * plane)
        copies.append(pltpu.make_async_copy(field.at[part], f.at[part], sems.at[i]))
    for copy in wind_copies + copies:
        copy.start()
    wind_copies[0].wait()
    for i in range(chunks):
        put_rims(e, 0, levels, per_chunk, i, side, plane, rows)
    wind_copies[1].wait()
    winds = pl.ds(levels * tracers, levels)
    put_rows(n, 0, a_ref.at[winds], b_ref.at[winds], rows, 0, levels)
    for i in range(chunks):
        copies[i].wait()
        put_rims(f, 0, levels, per_chunk, i, side, 0, plane)
        put_rows(
            f, 0, a_ref, b_ref, rows, i * per_chunk * tracers, min((i + 1) * per_chunk, levels) * tracers
        )


def meet(rim, target, from_west, from_east, count):
    lane = lane_iota()
    for chunk in range(rim.shape[0]):
        for r in range(0, count, SUB):
            rows = pl.ds(r, SUB)
            turned = pltpu.roll(from_east[chunk, rows, :], LANES - 2, 1)
            rim[chunk, pl.ds(target + r, SUB), :] = jnp.where(lane % 2 == 1, from_west[chunk, rows, :], turned)


def pair(edges, target, from_a, from_b, count):
    even = jnp.full((SUB, LANES), lax.axis_index("lat"), jnp.int32) % 2 == 0
    repeat = largest(count // SUB, 9, 8, 4, 2, 1)

    def body(i, carry):
        for u in range(repeat):
            at = pl.multiple_of((i * repeat + u) * SUB, SUB)
            a, b = from_a[pl.ds(at, SUB), :], from_b[pl.ds(at, SUB), :]
            edges[0, pl.ds(target + at, SUB), :] = jnp.where(even, a, b)
            edges[1, pl.ds(target + at, SUB), :] = jnp.where(even, b, a)
        return carry

    lax.fori_loop(0, count // SUB // repeat, body, 0)


def coefficients(
    levels, tracers, rows, per_chunk, unroll, east, north, mixing, west0, east0, a0, b0, *refs
):
    outs, (rim, edges), (e_buf, n_buf, m_buf, sems) = refs[:7], refs[7:9], refs[9:]
    plane = tracers * rows
    halves = rows // SUB
    lane, sub = lane_iota(), sub_iota()
    copies = [
        pltpu.make_async_copy(source, target, sems.at[i])
        for i, (source, target) in enumerate(((east, e_buf), (north, n_buf), (mixing, m_buf)))
    ]
    for copy in copies:
        copy.start()
    meet(rim, 0, west0, east0, plane)
    pair(edges, 0, a0, b0, levels * tracers)
    for copy in copies:
        copy.wait()
    place = lax.axis_index("lat")
    even = jnp.full((1, LANES), place, jnp.int32) % 2 == 0
    south_flag = (place > 0).astype(jnp.float32)
    north_flag = (place < lax.axis_size("lat") - 1).astype(jnp.float32)
    north_mask = jnp.where(sub == SUB - 1, north_flag, 1.0)

    def level(k, pivots):
        chunk, q = k // per_chunk, k % per_chunk
        has_up = (k < levels - 1).astype(jnp.float32)
        new, edge = [], None
        for h in range(halves):
            blk = pl.ds(pl.multiple_of(k * rows + h * SUB, SUB), SUB)
            down, factor = pivots[h]
            up = m_buf[blk, :] * has_up
            inv = 1.0 / (1.0 + up + down - down * factor)
            factor = up * inv
            new.append((up, factor))
            e, n = e_buf[blk, :], n_buf[blk, :]
            side = pltpu.roll(west0[chunk, pl.ds(plane + h * SUB, SUB), :], LANES - 1 - 2 * q, 1)
            w_in = jnp.minimum(jnp.where(lane == 0, side, pltpu.roll(e, 1, 1)), 0.0)
            if h == 0:
                row = pl.ds(levels * tracers + k, 1)
                edge = jnp.where(even, b0[row, :], a0[row, :]) * south_flag
            s_in = jnp.minimum(jnp.where(sub == 0, edge, pltpu.roll(n, 1, 0)), 0.0)
            edge = n[SUB - 1 : SUB, :]
            e_out, n_out = jnp.maximum(e, 0.0), jnp.maximum(n, 0.0)
            from_n = n_out * inv
            if h == halves - 1:
                from_n = from_n * north_mask
            stay = (1.0 - e_out + w_in - n_out + s_in) * inv
            values = (stay, e_out * inv, -(w_in * inv), from_n, -(s_in * inv), down * inv, factor)
            for out, value in zip(outs, values):
                out[blk, :] = value
        return tuple(new)

    def body(b, carry):
        for u in range(unroll):
            carry = level(b * unroll + u, carry)
        return carry

    zero = jnp.zeros((SUB, LANES), jnp.float32)
    lax.fori_loop(0, levels // unroll, body, ((zero, zero),) * halves)


def step(levels, tracers, rows, chunks, per_chunk, unroll, first, *refs):
    refs = list(refs)
    weights, (field, above_in) = refs[:6], refs[6:8]
    if first:
        rim, edges, forcing, f_west, f_east, f_a, f_b, out, side_ref, a_ref, b_ref = refs[8:19]
        buf, above, rim_now, f_rim, f_edges, sems = refs[19:]
    else:
        west_in, east_in, a_in, b_in, out = refs[8:13]
        buf, above, rim_now, west_buf, east_buf, a_buf, b_buf, rim, edges, sems = refs[13:]

    plane = tracers * rows
    halves = rows // SUB
    lane, sub = lane_iota(), sub_iota()
    blocks = levels // unroll
    flat = buf.reshape((levels * tracers + 2) * rows, LANES)

    def load(b):
        at = b * unroll * tracers
        return pltpu.make_async_copy(
            field.at[pl.ds(at, unroll * tracers)], buf.at[pl.ds(at + 1, unroll * tracers)], sems.at[b]
        )

    def store(b):
        at = b * unroll * tracers
        return pltpu.make_async_copy(
            buf.at[pl.ds(at + 1, unroll * tracers)], out.at[pl.ds(at, unroll * tracers)], sems.at[b]
        )

    rim_copies = []
    if not first:
        rim_copies = [
            pltpu.make_async_copy(source, target, sems.at[blocks + 1 + i])
            for i, (source, target) in enumerate(
                ((west_in, west_buf), (east_in, east_buf), (a_in, a_buf), (b_in, b_buf))
            )
        ]
    above_copy = pltpu.make_async_copy(above_in, above, sems.at[blocks])
    load(0).start()
    for copy in rim_copies:
        copy.start()
    for b in range(1, blocks):
        load(b).start()
    above_copy.start()

    if first:
        meet(f_rim, 0, f_west, f_east, rows)
        pair(f_edges, 0, f_a, f_b, levels)
    else:
        for copy in rim_copies:
            copy.wait()
        meet(rim, 0, west_buf, east_buf, plane)
        pair(edges, 0, a_buf, b_buf, levels * tracers)

    def stencil(cells, near, here, side, edge, row, h, co):
        at = here + h * SUB
        cell = cells[pl.ds(at, SUB), :]
        e = jnp.where(lane == LANES - 1, side, pltpu.roll(cell, LANES - 1, 1))
        w = jnp.where(lane == 0, side, pltpu.roll(cell, 1, 1))
        source, start = near
        n = source[pl.ds(start + at + 1, SUB), :]
        s = source[pl.ds(start + at - 1, SUB), :]
        if h == halves - 1:
            n = jnp.where(sub == SUB - 1, edge[0, pl.ds(row, 1), :], n)
        if h == 0:
            s = jnp.where(sub == 0, edge[1, pl.ds(row, 1), :], s)
        c0, ce, cw, cn, cs = co[:5]
        return (c0 * cell + ce * e) + (cw * w + cn * n) + cs * s

    def part(ref, b, size, offset=0):
        return ref.at[pl.ds(pl.multiple_of(b * unroll * size + offset, SUB), unroll * size)]

    def forward_block(b, solved):
        @pl.when(b < blocks - 1)
        def _():
            load(b + 1).wait()

        chunk, q = b * unroll // per_chunk, b * unroll % per_chunk
        turn = (LANES - 2 * q) % LANES
        for r in range(0, plane, SUB):
            rim_now[pl.ds(r, SUB), :] = pltpu.roll(rim[chunk, pl.ds(r, SUB), :], turn, 1)
        if first:
            for r in range(0, rows, SUB):
                rim_now[pl.ds(plane + r, SUB), :] = pltpu.roll(f_rim[chunk, pl.ds(r, SUB), :], turn, 1)

        def side(u, r):
            return pltpu.roll(rim_now[pl.ds(r, SUB), :], LANES - 1 - 2 * u, 1)

        cells = part(flat, b, plane, rows)
        near = (flat, b * unroll * plane + rows)
        edge = edges.at[:, pl.ds(pl.multiple_of(b * unroll * tracers, SUB), unroll * tracers)]
        co_parts = [part(weight, b, rows) for weight in weights]
        if first:
            f_cells = part(forcing, b, rows, SUB)
            f_near = (forcing, b * unroll * rows + SUB)
            f_edge = f_edges.at[:, pl.ds(pl.multiple_of(b * unroll, SUB), unroll)]
        for u in range(unroll):
            co, extra, new = [], [], []
            for h in range(halves):
                co.append([weight[pl.ds(u * rows + h * SUB, SUB), :] for weight in co_parts])
                if first:
                    extra.append(
                        stencil(f_cells, f_near, u * rows, side(u, plane + h * SUB), f_edge, u, h, co[h])
                    )
            for t in range(tracers):
                here = u * plane + t * rows
                values = [
                    stencil(
                        cells, near, here, side(u, t * rows + h * SUB), edge, u * tracers + t, h, co[h]
                    )
                    for h in range(halves)
                ]
                for h in range(halves):
                    value = values[h] + extra[h] if first else values[h]
                    value = value + co[h][5] * solved[t * halves + h]
                    new.append(value)
                    cells[pl.ds(here + h * SUB, SUB), :] = value
            solved = tuple(new)
        return solved

    zero = jnp.zeros((SUB, LANES), jnp.float32)
    zeros = (zero,) * (tracers * halves)
    load(0).wait()
    lax.fori_loop(0, blocks, forward_block, zeros)
    above_copy.wait()

    def backward_block(i, later):
        b = blocks - 1 - i
        cells = part(flat, b, plane, rows)
        factors = part(above, b, rows)
        for u in reversed(range(unroll)):
            new = []
            for h in range(halves):
                factor = factors[pl.ds(u * rows + h * SUB, SUB), :]
                for t in range(tracers):
                    blk = pl.ds(u * plane + t * rows + h * SUB, SUB)
                    value = cells[blk, :] + factor * later[h * tracers + t]
                    cells[blk, :] = value
                    new.append(value)
            later = tuple(new)
        store(b).start()
        return later

    lax.fori_loop(0, blocks, backward_block, zeros)
    if first:
        for chunk in range(chunks):
            put_rims(flat, rows, levels, per_chunk, chunk, side_ref, 0, plane)
        put_rows(flat, rows, a_ref, b_ref, rows, 0, levels * tracers)
    for b in range(blocks):
        store(b).wait()


def pack(levels, group_rows, cap, kernel, columns, observed, errors, out, k_buf, c_buf, o_buf, e_buf, wide, sems):
    lane = lane_iota()
    copies = [
        pltpu.make_async_copy(source, target, sems.at[i])
        for i, (source, target) in enumerate(
            ((columns, c_buf), (observed, o_buf), (errors, e_buf), (kernel, k_buf))
        )
    ]
    for copy in copies:
        copy.start()
    for copy in copies:
        copy.wait()
    per_level = columns.shape[0]
    groups = LANES // cap
    pad = groups * group_rows - levels - 3

    together = wide.shape[0]

    def body(start, carry):
        for n in range(together):
            i = start * together + n
            one = pl.ds(i, 1)
            tail = [c_buf[one, :].astype(jnp.float32), o_buf[one, :], e_buf[one, :]]
            wide[n, pl.ds(0, levels), :] = k_buf[pl.ds(i, levels, stride=per_level), :]
            wide[n, pl.ds(levels, pad + 3), :] = jnp.concatenate(
                tail + [jnp.zeros((pad, LANES), jnp.float32)], axis=0
            )
        for n in range(together):
            i = start * together + n
            for j in range(groups):
                for m in range(group_rows // SUB):
                    made = None
                    for g in range(groups):
                        piece = wide[n, pl.ds(g * group_rows + m * SUB, SUB), :]
                        if g != j:
                            piece = pltpu.roll(piece, (g - j) * cap % LANES, 1)
                        made = piece if made is None else jnp.where(lane >= g * cap, piece, made)
                    out[i * groups + j, pl.ds(m * SUB, SUB), :] = made
        return carry

    lax.fori_loop(0, per_level // together, body, 0)


def tracer_sum(block, concentration, out, buf, sems):
    levels, tracers, rows, cols = buf.shape

    def load(b):
        return pltpu.make_async_copy(
            concentration.at[pl.ds(b * block, block)], buf.at[pl.ds(b * block, block)], sems.at[b]
        )

    for b in range(levels // block):
        load(b).start()

    def body(b, carry):
        load(b).wait()
        for h in range(rows // SUB):
            tops, rests = [], []
            for k in range(block):
                part = jnp.sum(buf[b * block + k, :, pl.ds(h * SUB, SUB), :], axis=0)
                top = part.astype(jnp.bfloat16).astype(jnp.float32)
                tops.append(top)
                rests.append(part - top)
            at = pl.ds(pl.multiple_of(b * block * SUB, block * SUB), block * SUB)
            lanes = pl.ds(h * cols, cols)
            out[0, at, lanes] = jnp.concatenate(tops, axis=0).astype(jnp.bfloat16)
            out[1, at, lanes] = jnp.concatenate(rests, axis=0).astype(jnp.bfloat16)
        return carry

    lax.fori_loop(0, levels // block, body, 0)


def soundings(
    levels, rows, group_rows, cap, chunks, per_chunk, block,
    received, sums, forcing, side_ref, a_ref, b_ref, back, arrived, table, scaled
):
    lane = lane_iota()
    parts, _, width = arrived.shape
    halves = rows // SUB
    keys = halves * LANES
    groups = LANES // cap

    def unpack(c, carry):
        part, col = c // (width // LANES), c % (width // LANES)
        for g in range(groups):
            for m in range(group_rows // SUB):
                made = None
                for p in range(groups):
                    piece = received[c * groups + p, pl.ds(m * SUB, SUB), :]
                    if p != g:
                        piece = pltpu.roll(piece, (p - g) * cap % LANES, 1)
                    made = piece if made is None else jnp.where(lane >= p * cap, piece, made)
                lanes = pl.ds(pl.multiple_of(col * LANES, LANES), LANES)
                arrived[part, pl.ds(g * group_rows + m * SUB, SUB), lanes] = made
        return carry

    lax.fori_loop(0, parts * width // LANES, unpack, 0)

    sub_index = lax.broadcasted_iota(jnp.int32, (SUB, width), 0)
    key_index = lax.broadcasted_iota(jnp.int32, (keys, width), 0)
    turned_index = lax.broadcasted_iota(jnp.int32, (LANES, keys), 1)

    def columns(j):
        return arrived[j, pl.ds(levels, 1), :].astype(jnp.int32)

    def key_of(col):
        return (col >> 10) * LANES + (col & (LANES - 1))

    def mask_of(j):
        return sub_index == ((columns(j) >> 7) & (SUB - 1))

    for j in range(parts):
        col = columns(j)
        key = key_of(col)
        look = jnp.where(key_index == key, 1.0, 0.0).astype(jnp.bfloat16)
        for c in range(width // LANES):
            piece = key[:, c * LANES : (c + 1) * LANES].astype(jnp.float32)
            across = jnp.broadcast_to(piece, (LANES, LANES)).T.astype(jnp.int32)
            across = jnp.concatenate([across] * halves, axis=1)
            table[j, pl.ds(c * LANES, LANES), :] = jnp.where(turned_index == across, 1.0, 0.0).astype(
                jnp.bfloat16
            )
        total = jnp.zeros((SUB, width), jnp.float32)
        for b in range(levels // block):
            blk = pl.ds(b * block * SUB, block * SUB)
            seen = jnp.dot(sums[0, blk, :], look, preferred_element_type=jnp.float32)
            seen += jnp.dot(sums[1, blk, :], look, preferred_element_type=jnp.float32)
            weight = arrived[j, pl.ds(b * block, block), :]
            for k in range(block):
                total += weight[k : k + 1, :] * seen[k * SUB : (k + 1) * SUB, :]
        modelled = jnp.sum(jnp.where(mask_of(j), total, 0.0), axis=0, keepdims=True)
        observed = arrived[j, pl.ds(levels + 1, 1), :]
        error = arrived[j, pl.ds(levels + 2, 1), :]
        residual = jnp.where(col >= 0, (modelled - observed) / error, 0.0)
        scaled[pl.ds(j, 1), :] = residual / error
        for i in range(width // cap):
            at = i * cap
            piece = residual[:, at // LANES * LANES : at // LANES * LANES + LANES]
            if at % LANES:
                piece = pltpu.roll(piece, LANES - at % LANES, 1)
            back[pl.ds(j * (width // cap) + i, 1), :] = piece

    zeros = jnp.zeros((SUB, LANES), jnp.float32)
    forcing[pl.ds(0, SUB), :] = zeros
    forcing[pl.ds(levels * rows + SUB, SUB), :] = zeros
    for b in range(levels // block):
        total = jnp.zeros((block * SUB, keys), jnp.float32)
        for j in range(parts):
            weight = arrived[j, pl.ds(b * block, block), :] * scaled[pl.ds(j, 1), :]
            top = weight.astype(jnp.bfloat16).astype(jnp.float32)
            mask = mask_of(j)
            for part in (top, weight - top):
                spread = jnp.concatenate(
                    [jnp.where(mask, part[k : k + 1, :], 0.0) for k in range(block)], axis=0
                ).astype(jnp.bfloat16)
                total += jnp.dot(spread, table[j, :, :], preferred_element_type=jnp.float32)
        for k in range(block):
            for h in range(halves):
                forcing[pl.ds((b * block + k) * rows + (h + 1) * SUB, SUB), :] = total[
                    k * SUB : (k + 1) * SUB, h * LANES : (h + 1) * LANES
                ]

    for chunk in range(chunks):
        put_rims(forcing, SUB, levels, per_chunk, chunk, side_ref, 0, rows)
    put_rows(forcing, SUB, a_ref, b_ref, rows, 0, levels)


def unpack_residual(cap, arrived, out):
    lane = lax.broadcasted_iota(jnp.int32, (1, LANES), 1)
    groups = LANES // cap
    for row in range(out.shape[0]):
        made = None
        for g in range(groups):
            piece = arrived[pl.ds(row * groups + g, 1), :]
            if g:
                piece = pltpu.roll(piece, g * cap, 1)
            made = piece if made is None else jnp.where(lane >= g * cap, piece, made)
        out[pl.ds(row, 1), :] = made


def exchange(side_rim, a_rim, b_rim):
    lons, lats = lax.axis_size("lon"), lax.axis_size("lat")

    def partner(j, odd):
        other = j + 1 if j % 2 == odd else j - 1
        return other if 0 <= other < lats else j

    return (
        lax.ppermute(side_rim, "lon", [(i, (i + 1) % lons) for i in range(lons)]),
        lax.ppermute(side_rim, "lon", [((i + 1) % lons, i) for i in range(lons)]),
        lax.ppermute(a_rim, "lat", [(j, partner(j, 0)) for j in range(lats)]),
        lax.ppermute(b_rim, "lat", [(j, partner(j, 1)) for j in range(lats)]),
    )


def per_device(
    concentration, adjoint, wind_east, wind_north, mixing, sound_col, kernel, observed, obs_error
):
    levels, tracers, rows, cols = adjoint.shape
    bricks = lax.axis_size("lon") * lax.axis_size("lat")
    slots = sound_col.shape[2]
    cap = slots // bricks
    unroll = largest(levels, 8, 4, 3, 2, 1)
    chunks, per_chunk = rim_chunks(levels, unroll)
    plane = tracers * rows
    per_level = slots // LANES
    groups = LANES // cap
    group_rows = -(-(levels + 3) // (groups * SUB)) * SUB
    field_bytes = levels * plane * cols * 4
    dma = pltpu.SemaphoreType.DMA

    def flat(x):
        return x.reshape(-1, LANES)

    packed = call(
        functools.partial(pack, levels, group_rows, cap),
        [HBM] * 4, f32(bricks, group_rows, LANES), VMEM,
        (
            vmem(levels * per_level, LANES), pltpu.VMEM((per_level, LANES), jnp.int32),
            vmem(per_level, LANES), vmem(per_level, LANES),
            vmem(largest(per_level, 8, 4, 2, 1), groups * group_rows, LANES), dma((4,)),
        ),
        4, 10, 800000, "pack",
    )(*(in_hbm(flat(x)) for x in (kernel, sound_col, observed, obs_error)))
    received = lax.all_to_all(packed, ("lon", "lat"), split_axis=0, concat_axis=0, tiled=True)

    field = adjoint.reshape(levels * tracers, rows, LANES)
    east, north, mix = (in_hbm(flat(x)) for x in (wind_east, wind_north, mixing))
    rims = call(
        functools.partial(first_rims, levels, tracers, rows, chunks, per_chunk),
        [HBM] * 3,
        (f32(chunks, plane + rows, LANES),) + (f32(levels * tracers + levels, LANES),) * 2,
        (VMEM,) * 3,
        (vmem(levels * plane, LANES), vmem(levels * rows, LANES), vmem(levels * rows, LANES), dma((chunks + 2,))),
        10, field_bytes, 2 * field_bytes, "first_rims",
    )(in_hbm(flat(adjoint)), east, north)
    start_rims = exchange(*rims)

    block = largest(levels, 24, 16, 8)
    sum_block = largest(levels, 12, 8)
    sums = call(
        functools.partial(tracer_sum, sum_block),
        [HBM], jax.ShapeDtypeStruct((2, levels * SUB, rows // SUB * cols), jnp.bfloat16), VMEM,
        (vmem(levels, tracers, rows, cols), dma((levels // sum_block,))),
        10, field_bytes // 4, field_bytes, "tracer_sum",
    )(concentration)

    width = largest(slots, 2 * LANES, LANES)
    parts = slots // width
    forcing, *rims, back = call(
        functools.partial(soundings, levels, rows, group_rows, cap, chunks, per_chunk, block),
        [VMEM] * 2,
        (
            f32(levels * rows + 2 * SUB, LANES), f32(chunks, rows, LANES), f32(levels, LANES), f32(levels, LANES),
            hbm(bricks, LANES),
        ),
        (VMEM,) * 5,
        (
            vmem(parts, groups * group_rows, width),
            pltpu.VMEM((parts, width, rows // SUB * LANES), jnp.bfloat16),
            vmem(max(parts, SUB), width),
        ),
        10, field_bytes * 8, field_bytes, "soundings",
    )(received, sums)
    forcing_rims = exchange(*rims)

    rim_shape, edge_shape = (chunks, plane, LANES), (2, levels * tracers, LANES)
    *weights, above, rim0, edges0 = call(
        functools.partial(coefficients, levels, tracers, rows, per_chunk, unroll),
        [HBM] * 3 + [VMEM] * 4,
        (f32(levels * rows, LANES),) * 6 + (hbm(levels * rows, LANES), f32(*rim_shape), f32(*edge_shape)),
        (VMEM,) * 9,
        (vmem(levels * rows, LANES),) * 3 + (dma((3,)),),
        4, field_bytes, field_bytes, "coefficients",
    )(east, north, mix, *start_rims)

    def advance(value, first, specs, operands, scratch):
        outs, out_specs = ((hbm if first else f32)(*value.shape),), (HBM,)
        if first:
            outs += (f32(*rim_shape), f32(levels * tracers, LANES), f32(levels * tracers, LANES))
            out_specs += (VMEM,) * 3
        return call(
            functools.partial(step, levels, tracers, rows, chunks, per_chunk, unroll, first),
            [VMEM] * 6 + [HBM] * 2 + [specs] * len(operands), outs, out_specs,
            (vmem(levels * tracers + 2, rows, LANES), vmem(levels * rows, LANES), vmem(plane + rows, LANES))
            + scratch + (dma((levels // unroll + 5,)),),
            10, field_bytes * 8, field_bytes * 2, "step",
        )(*weights, in_hbm(value), in_hbm(above), *operands)

    stepped, *rims = advance(
        field, True, VMEM, (rim0, edges0, forcing, *forcing_rims),
        (vmem(chunks, rows, LANES), vmem(2, levels, LANES)),
    )
    (result,) = advance(
        stepped, False, ANY, exchange(*rims),
        (vmem(*rim_shape),) * 2 + (vmem(levels * tracers, LANES),) * 2 + (vmem(*rim_shape), vmem(*edge_shape)),
    )

    returned = lax.all_to_all(
        back.reshape(bricks, 1, LANES), ("lon", "lat"), split_axis=0, concat_axis=0, tiled=True
    )
    result, returned = lax.optimization_barrier((result, returned))
    residual = call(
        functools.partial(unpack_residual, cap), [VMEM], f32(per_level, LANES), VMEM, (), 2, 10, 10000, "residual",
    )(returned.reshape(bricks, LANES))
    return result.reshape(adjoint.shape), residual.reshape(sound_col.shape)


def solution(mesh):
    field = P(None, None, "lat", "lon")
    face = P(None, "lat", "lon")
    owned = P(None, ("lon", "lat"), None)
    return jax.shard_map(
        per_device,
        mesh=mesh,
        in_specs=(field, field, face, face, face, owned, owned, owned, owned),
        out_specs=(field, owned),
        check_vma=False,
    )
```

```python
import functools

import jax
import jax.numpy as jnp
from jax import lax
from jax.experimental import pallas as pl
from jax.experimental.pallas import tpu as pltpu
from jax.sharding import PartitionSpec as P

LANES = 128
SUB = 8
MIB = 1 << 20
ANY = pl.BlockSpec(memory_space=pl.ANY)
HBM = pl.BlockSpec(memory_space=pltpu.HBM)
VMEM = pl.BlockSpec(memory_space=pltpu.VMEM)


def rim_chunks(levels, unroll):
    per_chunk = 63 // unroll * unroll
    chunks = -(-levels // per_chunk)
    return chunks, -(-levels // (chunks * unroll)) * unroll


def lane_iota():
    return lax.broadcasted_iota(jnp.int32, (SUB, LANES), 1)


def sub_iota():
    return lax.broadcasted_iota(jnp.int32, (SUB, LANES), 0)


def largest(count, *choices):
    return next(u for u in choices if count % u == 0)


def in_hbm(x):
    return pltpu.with_memory_space_constraint(x, pltpu.HBM)


def hbm(*shape):
    return pltpu.HBM(shape, jnp.float32)


def f32(*shape):
    return jax.ShapeDtypeStruct(shape, jnp.float32)


def vmem(*shape):
    return pltpu.VMEM(shape, jnp.float32)


def call(body, ins, outs, out_specs, scratch, mib, flops, size, name):
    return pl.pallas_call(
        body,
        in_specs=ins,
        out_specs=out_specs,
        out_shape=outs,
        scratch_shapes=scratch,
        compiler_params=pltpu.CompilerParams(vmem_limit_bytes=mib * MIB),
        cost_estimate=pl.CostEstimate(flops=flops, bytes_accessed=size, transcendentals=0),
        name=name,
    )


def put_rims(field, offset, levels, per_chunk, chunk, out, first, plane):
    lane = lane_iota()
    group = largest(plane // SUB, 4, 2, 1)
    count = min(per_chunk, levels - chunk * per_chunk)

    def body(i, carry):
        r = pl.multiple_of(i * SUB * group, SUB * group)
        made = [jnp.zeros((SUB, LANES), jnp.float32)] * group
        for q in range(count):
            for g in range(group):
                at = pl.multiple_of((chunk * per_chunk + q) * plane + offset + r + g * SUB, SUB)
                turned = pltpu.roll(field[pl.ds(at, SUB), :], 2 * q + 2, 1)
                made[g] = jnp.where(lane >= 2 * q + 1, turned, made[g])
        for g in range(group):
            out[chunk, pl.ds(pl.multiple_of(first + r + g * SUB, SUB), SUB), :] = made[g]
        return carry

    lax.fori_loop(0, plane // SUB // group, body, 0)


def put_rows(field, offset, a_ref, b_ref, rows, begin, end):
    unroll = largest((end - begin) // SUB, 9, 8, 4, 2, 1)
    odd = lax.axis_index("lat") % 2
    in_a = (1 - odd) * (rows - 1)
    in_b = odd * (rows - 1)

    def body(i, carry):
        for u in range(unroll):
            start = pl.multiple_of(begin + (i * unroll + u) * SUB, SUB)
            at = start * rows + offset
            a_ref[pl.ds(start, SUB), :] = field[pl.ds(at + in_a, SUB, stride=rows), :]
            b_ref[pl.ds(start, SUB), :] = field[pl.ds(at + in_b, SUB, stride=rows), :]
        return carry

    lax.fori_loop(0, (end - begin) // SUB // unroll, body, 0)


def first_rims(levels, tracers, rows, chunks, per_chunk, field, east, north, side, a_ref, b_ref, f, e, n, sems):
    plane = tracers * rows
    wind_copies = [
        pltpu.make_async_copy(east, e, sems.at[chunks]),
        pltpu.make_async_copy(north, n, sems.at[chunks + 1]),
    ]
    copies = []
    for i in range(chunks):
        part = pl.ds(i * per_chunk * plane, min(per_chunk, levels - i * per_chunk) * plane)
        copies.append(pltpu.make_async_copy(field.at[part], f.at[part], sems.at[i]))
    for copy in wind_copies + copies:
        copy.start()
    wind_copies[0].wait()
    for i in range(chunks):
        put_rims(e, 0, levels, per_chunk, i, side, plane, rows)
    wind_copies[1].wait()
    winds = pl.ds(levels * tracers, levels)
    put_rows(n, 0, a_ref.at[winds], b_ref.at[winds], rows, 0, levels)
    for i in range(chunks):
        copies[i].wait()
        put_rims(f, 0, levels, per_chunk, i, side, 0, plane)
        put_rows(
            f, 0, a_ref, b_ref, rows, i * per_chunk * tracers, min((i + 1) * per_chunk, levels) * tracers
        )


def meet(rim, target, from_west, from_east, count):
    lane = lane_iota()
    for chunk in range(rim.shape[0]):
        for r in range(0, count, SUB):
            rows = pl.ds(r, SUB)
            turned = pltpu.roll(from_east[chunk, rows, :], LANES - 2, 1)
            rim[chunk, pl.ds(target + r, SUB), :] = jnp.where(lane % 2 == 1, from_west[chunk, rows, :], turned)


def pair(edges, target, from_a, from_b, count):
    even = jnp.full((SUB, LANES), lax.axis_index("lat"), jnp.int32) % 2 == 0
    repeat = largest(count // SUB, 9, 8, 4, 2, 1)

    def body(i, carry):
        for u in range(repeat):
            at = pl.multiple_of((i * repeat + u) * SUB, SUB)
            a, b = from_a[pl.ds(at, SUB), :], from_b[pl.ds(at, SUB), :]
            edges[0, pl.ds(target + at, SUB), :] = jnp.where(even, a, b)
            edges[1, pl.ds(target + at, SUB), :] = jnp.where(even, b, a)
        return carry

    lax.fori_loop(0, count // SUB // repeat, body, 0)


def coefficients(
    levels, tracers, rows, per_chunk, unroll, east, north, mixing, west0, east0, a0, b0, *refs
):
    weights, rim, edges, e_buf, n_buf, m_buf, sems = refs
    plane = tracers * rows
    halves = rows // SUB
    lane, sub = lane_iota(), sub_iota()
    copies = [
        pltpu.make_async_copy(source, target, sems.at[i])
        for i, (source, target) in enumerate(((east, e_buf), (north, n_buf), (mixing, m_buf)))
    ]
    for copy in copies:
        copy.start()
    meet(rim, 0, west0, east0, plane)
    pair(edges, 0, a0, b0, levels * tracers)
    for copy in copies:
        copy.wait()
    place = lax.axis_index("lat")
    even = jnp.full((1, LANES), place, jnp.int32) % 2 == 0
    south_flag = (place > 0).astype(jnp.float32)
    north_flag = (place < lax.axis_size("lat") - 1).astype(jnp.float32)
    north_mask = jnp.where(sub == SUB - 1, north_flag, 1.0)

    def level(k, pivots):
        chunk, q = k // per_chunk, k % per_chunk
        has_up = (k < levels - 1).astype(jnp.float32)
        new, edge = [], None
        for h in range(halves):
            blk = pl.ds(pl.multiple_of(k * rows + h * SUB, SUB), SUB)
            down, factor = pivots[h]
            up = m_buf[blk, :] * has_up
            inv = 1.0 / (1.0 + up + down - down * factor)
            factor = up * inv
            new.append((up, factor))
            e, n = e_buf[blk, :], n_buf[blk, :]
            side = pltpu.roll(west0[chunk, pl.ds(plane + h * SUB, SUB), :], LANES - 1 - 2 * q, 1)
            w_in = jnp.minimum(jnp.where(lane == 0, side, pltpu.roll(e, 1, 1)), 0.0)
            if h == 0:
                row = pl.ds(levels * tracers + k, 1)
                edge = jnp.where(even, b0[row, :], a0[row, :]) * south_flag
            s_in = jnp.minimum(jnp.where(sub == 0, edge, pltpu.roll(n, 1, 0)), 0.0)
            edge = n[SUB - 1 : SUB, :]
            e_out, n_out = jnp.maximum(e, 0.0), jnp.maximum(n, 0.0)
            from_n = n_out * inv
            if h == halves - 1:
                from_n = from_n * north_mask
            stay = (1.0 - e_out + w_in - n_out + s_in) * inv
            from_e, from_w = e_out * inv, -(w_in * inv)
            from_rim = jnp.where(lane == 0, from_w, jnp.where(lane == LANES - 1, from_e, 0.0))
            from_e = jnp.where(lane == LANES - 1, 0.0, from_e)
            from_w = jnp.where(lane == 0, 0.0, from_w)
            values = (stay, from_e, from_w, from_n, -(s_in * inv), from_rim, down * inv, factor)
            for i, value in enumerate(values):
                weights[i, blk, :] = value
        return tuple(new)

    def body(b, carry):
        for u in range(unroll):
            carry = level(b * unroll + u, carry)
        return carry

    zero = jnp.zeros((SUB, LANES), jnp.float32)
    lax.fori_loop(0, levels // unroll, body, ((zero, zero),) * halves)


def step(levels, tracers, rows, chunks, per_chunk, unroll, first, *refs):
    if first:
        field, weights, rim, edges, forcing, f_west, f_east, f_a, f_b = refs[:9]
        out, weights_out, side_ref, a_ref, b_ref = refs[9:14]
        buf, rim_now, f_rim, f_edges, sems = refs[14:]
    else:
        field, weights_in, west_in, east_in, a_in, b_in, out = refs[:7]
        buf, rim_now, weights, west_buf, east_buf, a_buf, b_buf, rim, edges, sems = refs[7:]

    plane = tracers * rows
    halves = rows // SUB
    lane, sub = lane_iota(), sub_iota()
    blocks = levels // unroll
    flat = buf.reshape((levels * tracers + 2) * rows, LANES)

    def load(b):
        at = b * unroll * tracers
        return pltpu.make_async_copy(
            field.at[pl.ds(at, unroll * tracers)], buf.at[pl.ds(at + 1, unroll * tracers)], sems.at[b]
        )

    def store(b):
        at = b * unroll * tracers
        return pltpu.make_async_copy(
            buf.at[pl.ds(at + 1, unroll * tracers)], out.at[pl.ds(at, unroll * tracers)], sems.at[b]
        )

    last = 2 * blocks
    above = weights.at[weights.shape[0] - 1]
    if first:
        keep = pltpu.make_async_copy(weights, weights_out, sems.at[last])
        for b in range(blocks):
            load(b).start()
        keep.start()
        meet(f_rim, 0, f_west, f_east, rows)
        pair(f_edges, 0, f_a, f_b, levels)
    else:
        rim_copies = [
            pltpu.make_async_copy(source, target, sems.at[last + 1 + i])
            for i, (source, target) in enumerate(
                ((west_in, west_buf), (east_in, east_buf), (a_in, a_buf), (b_in, b_buf))
            )
        ]
        above_copy = pltpu.make_async_copy(weights_in.at[weights.shape[0] - 1], above, sems.at[last])
        for copy in rim_copies:
            copy.start()

        def load_weights(b):
            planes, levels_of = pl.ds(0, weights.shape[0] - 1), pl.ds(b * unroll * rows, unroll * rows)
            return pltpu.make_async_copy(
                weights_in.at[planes, levels_of], weights.at[planes, levels_of], sems.at[blocks + b]
            )

        for b in range(blocks):
            load(b).start()
            load_weights(b).start()
        above_copy.start()
        for copy in rim_copies:
            copy.wait()
        meet(rim, 0, west_buf, east_buf, plane)
        pair(edges, 0, a_buf, b_buf, levels * tracers)

    def shifted(cells, near, here, edge, row):
        norths, souths = [], []
        if first:
            halfs = [cells[pl.ds(here + h * SUB, SUB), :] for h in range(halves)]
            ups = [pltpu.roll(half, SUB - 1, 0) for half in halfs] + [edge[0, pl.ds(row, 1), :]]
            downs = [edge[1, pl.ds(row, 1), :]] + [pltpu.roll(half, 1, 0) for half in halfs]
            for h in range(halves):
                norths.append(jnp.where(sub == SUB - 1, ups[h + 1], ups[h]))
                souths.append(jnp.where(sub == 0, downs[h], downs[h + 1]))
            return norths, souths
        source, start = near
        for h in range(halves):
            n = source[pl.ds(start + here + h * SUB + 1, SUB), :]
            s = source[pl.ds(start + here + h * SUB - 1, SUB), :]
            if h == halves - 1:
                n = jnp.where(sub == SUB - 1, edge[0, pl.ds(row, 1), :], n)
            if h == 0:
                s = jnp.where(sub == 0, edge[1, pl.ds(row, 1), :], s)
            norths.append(n)
            souths.append(s)
        return norths, souths

    def stencil(cells, near, here, side, edge, row, co):
        norths, souths = shifted(cells, near, here, edge, row)
        values = []
        for h in range(halves):
            cell = cells[pl.ds(here + h * SUB, SUB), :]
            c0, ce, cw, cn, cs, rims = co[h][:6]
            value = (c0 * cell + ce * pltpu.roll(cell, LANES - 1, 1)) + (
                cw * pltpu.roll(cell, 1, 1) + cn * norths[h]
            )
            values.append(value + (cs * souths[h] + rims * side(h)))
        return values

    def part(ref, b, size, offset=0):
        return ref.at[pl.ds(pl.multiple_of(b * unroll * size + offset, SUB), unroll * size)]

    def forward_block(b, solved):
        if first:
            load(b).wait()
        else:
            load_weights(b).wait()

            @pl.when(b < blocks - 1)
            def _():
                load(b + 1).wait()

        chunk, q = b * unroll // per_chunk, b * unroll % per_chunk
        turn = (LANES - 2 * q) % LANES
        for r in range(0, plane, SUB):
            rim_now[pl.ds(r, SUB), :] = pltpu.roll(rim[chunk, pl.ds(r, SUB), :], turn, 1)
        if first:
            for r in range(0, rows, SUB):
                rim_now[pl.ds(plane + r, SUB), :] = pltpu.roll(f_rim[chunk, pl.ds(r, SUB), :], turn, 1)

        def side(u, r):
            return lambda h: pltpu.roll(rim_now[pl.ds(r + h * SUB, SUB), :], LANES - 1 - 2 * u, 1)

        cells = part(flat, b, plane, rows)
        near = (flat, b * unroll * plane + rows)
        edge = edges.at[:, pl.ds(pl.multiple_of(b * unroll * tracers, SUB), unroll * tracers)]
        co_part = weights.at[:, pl.ds(pl.multiple_of(b * unroll * rows, SUB), unroll * rows)]
        if first:
            f_cells = part(forcing, b, rows, SUB)
            f_near = (forcing, b * unroll * rows + SUB)
            f_edge = f_edges.at[:, pl.ds(pl.multiple_of(b * unroll, SUB), unroll)]
        for u in range(unroll):
            co = [
                [co_part[i, pl.ds(u * rows + h * SUB, SUB), :] for i in range(weights.shape[0] - 1)]
                for h in range(halves)
            ]
            if first:
                extra = stencil(f_cells, f_near, u * rows, side(u, plane), f_edge, u, co)
            new = []
            for t in range(tracers):
                here = u * plane + t * rows
                values = stencil(cells, near, here, side(u, t * rows), edge, u * tracers + t, co)
                for h in range(halves):
                    value = values[h] + extra[h] if first else values[h]
                    value = value + co[h][6] * solved[t * halves + h]
                    new.append(value)
                    cells[pl.ds(here + h * SUB, SUB), :] = value
            solved = tuple(new)
        return solved

    zero = jnp.zeros((SUB, LANES), jnp.float32)
    zeros = (zero,) * (tracers * halves)
    if not first:
        load(0).wait()
    lax.fori_loop(0, blocks, forward_block, zeros)
    if not first:
        above_copy.wait()

    def backward_block(i, later):
        b = blocks - 1 - i
        cells = part(flat, b, plane, rows)
        factors = part(above, b, rows)
        for u in reversed(range(unroll)):
            new = []
            for h in range(halves):
                factor = factors[pl.ds(u * rows + h * SUB, SUB), :]
                for t in range(tracers):
                    blk = pl.ds(u * plane + t * rows + h * SUB, SUB)
                    value = cells[blk, :] + factor * later[h * tracers + t]
                    cells[blk, :] = value
                    new.append(value)
            later = tuple(new)
        store(b).start()
        return later

    lax.fori_loop(0, blocks, backward_block, zeros)
    if first:
        for chunk in range(chunks):
            put_rims(flat, rows, levels, per_chunk, chunk, side_ref, 0, plane)
        put_rows(flat, rows, a_ref, b_ref, rows, 0, levels * tracers)
        keep.wait()
    for b in range(blocks):
        store(b).wait()


def pack(levels, group_rows, cap, kernel, columns, observed, errors, out, k_buf, c_buf, o_buf, e_buf, wide, sems):
    lane = lane_iota()
    copies = [
        pltpu.make_async_copy(source, target, sems.at[i])
        for i, (source, target) in enumerate(
            ((columns, c_buf), (observed, o_buf), (errors, e_buf), (kernel, k_buf))
        )
    ]
    for copy in copies:
        copy.start()
    for copy in copies:
        copy.wait()
    per_level = columns.shape[0]
    groups = LANES // cap
    pad = groups * group_rows - levels - 3

    together = wide.shape[0]

    def body(start, carry):
        for n in range(together):
            i = start * together + n
            one = pl.ds(i, 1)
            tail = [c_buf[one, :].astype(jnp.float32), o_buf[one, :], e_buf[one, :]]
            wide[n, pl.ds(0, levels), :] = k_buf[pl.ds(i, levels, stride=per_level), :]
            wide[n, pl.ds(levels, pad + 3), :] = jnp.concatenate(
                tail + [jnp.zeros((pad, LANES), jnp.float32)], axis=0
            )
        for n in range(together):
            i = start * together + n
            for j in range(groups):
                for m in range(group_rows // SUB):
                    made = None
                    for g in range(groups):
                        piece = wide[n, pl.ds(g * group_rows + m * SUB, SUB), :]
                        if g != j:
                            piece = pltpu.roll(piece, (g - j) * cap % LANES, 1)
                        made = piece if made is None else jnp.where(lane >= g * cap, piece, made)
                    out[i * groups + j, pl.ds(m * SUB, SUB), :] = made
        return carry

    lax.fori_loop(0, per_level // together, body, 0)


def tracer_sum(block, concentration, out, buf, sems):
    levels, tracers, rows, cols = buf.shape

    def load(b):
        return pltpu.make_async_copy(
            concentration.at[pl.ds(b * block, block)], buf.at[pl.ds(b * block, block)], sems.at[b]
        )

    for b in range(levels // block):
        load(b).start()

    def body(b, carry):
        load(b).wait()
        for h in range(rows // SUB):
            tops, rests = [], []
            for k in range(block):
                part = jnp.sum(buf[b * block + k, :, pl.ds(h * SUB, SUB), :], axis=0)
                top = part.astype(jnp.bfloat16).astype(jnp.float32)
                tops.append(top)
                rests.append(part - top)
            at = pl.ds(pl.multiple_of(b * block * SUB, block * SUB), block * SUB)
            lanes = pl.ds(h * cols, cols)
            out[0, at, lanes] = jnp.concatenate(tops, axis=0).astype(jnp.bfloat16)
            out[1, at, lanes] = jnp.concatenate(rests, axis=0).astype(jnp.bfloat16)
        return carry

    lax.fori_loop(0, levels // block, body, 0)


def soundings(
    levels, rows, group_rows, cap, chunks, per_chunk, block,
    received, sums, forcing, side_ref, a_ref, b_ref, back, arrived, table, scaled
):
    lane = lane_iota()
    parts, _, width = arrived.shape
    halves = rows // SUB
    keys = halves * LANES
    groups = LANES // cap

    def unpack(c, carry):
        part, col = c // (width // LANES), c % (width // LANES)
        for g in range(groups):
            for m in range(group_rows // SUB):
                made = None
                for p in range(groups):
                    piece = received[c * groups + p, pl.ds(m * SUB, SUB), :]
                    if p != g:
                        piece = pltpu.roll(piece, (p - g) * cap % LANES, 1)
                    made = piece if made is None else jnp.where(lane >= p * cap, piece, made)
                lanes = pl.ds(pl.multiple_of(col * LANES, LANES), LANES)
                arrived[part, pl.ds(g * group_rows + m * SUB, SUB), lanes] = made
        return carry

    lax.fori_loop(0, parts * width // LANES, unpack, 0)

    sub_index = lax.broadcasted_iota(jnp.int32, (SUB, width), 0)
    key_index = lax.broadcasted_iota(jnp.int32, (keys, width), 0)
    turned_index = lax.broadcasted_iota(jnp.int32, (LANES, keys), 1)

    def columns(j):
        return arrived[j, pl.ds(levels, 1), :].astype(jnp.int32)

    def key_of(col):
        return (col >> 10) * LANES + (col & (LANES - 1))

    def mask_of(j):
        return sub_index == ((columns(j) >> 7) & (SUB - 1))

    for j in range(parts):
        col = columns(j)
        key = key_of(col)
        look = jnp.where(key_index == key, 1.0, 0.0).astype(jnp.bfloat16)
        for c in range(width // LANES):
            piece = key[:, c * LANES : (c + 1) * LANES].astype(jnp.float32)
            across = jnp.broadcast_to(piece, (LANES, LANES)).T.astype(jnp.int32)
            across = jnp.concatenate([across] * halves, axis=1)
            table[j, pl.ds(c * LANES, LANES), :] = jnp.where(turned_index == across, 1.0, 0.0).astype(
                jnp.bfloat16
            )
        total = jnp.zeros((SUB, width), jnp.float32)
        for b in range(levels // block):
            blk = pl.ds(b * block * SUB, block * SUB)
            seen = jnp.dot(sums[0, blk, :], look, preferred_element_type=jnp.float32)
            seen += jnp.dot(sums[1, blk, :], look, preferred_element_type=jnp.float32)
            weight = arrived[j, pl.ds(b * block, block), :]
            for k in range(block):
                total += weight[k : k + 1, :] * seen[k * SUB : (k + 1) * SUB, :]
        modelled = jnp.sum(jnp.where(mask_of(j), total, 0.0), axis=0, keepdims=True)
        observed = arrived[j, pl.ds(levels + 1, 1), :]
        error = arrived[j, pl.ds(levels + 2, 1), :]
        residual = jnp.where(col >= 0, (modelled - observed) / error, 0.0)
        scaled[pl.ds(j, 1), :] = residual / error
        for i in range(width // cap):
            at = i * cap
            piece = residual[:, at // LANES * LANES : at // LANES * LANES + LANES]
            if at % LANES:
                piece = pltpu.roll(piece, LANES - at % LANES, 1)
            back[pl.ds(j * (width // cap) + i, 1), :] = piece

    zeros = jnp.zeros((SUB, LANES), jnp.float32)
    forcing[pl.ds(0, SUB), :] = zeros
    forcing[pl.ds(levels * rows + SUB, SUB), :] = zeros
    for b in range(levels // block):
        total = jnp.zeros((block * SUB, keys), jnp.float32)
        for j in range(parts):
            weight = arrived[j, pl.ds(b * block, block), :] * scaled[pl.ds(j, 1), :]
            top = weight.astype(jnp.bfloat16).astype(jnp.float32)
            mask = mask_of(j)
            for part in (top, weight - top):
                spread = jnp.concatenate(
                    [jnp.where(mask, part[k : k + 1, :], 0.0) for k in range(block)], axis=0
                ).astype(jnp.bfloat16)
                total += jnp.dot(spread, table[j, :, :], preferred_element_type=jnp.float32)
        for k in range(block):
            for h in range(halves):
                forcing[pl.ds((b * block + k) * rows + (h + 1) * SUB, SUB), :] = total[
                    k * SUB : (k + 1) * SUB, h * LANES : (h + 1) * LANES
                ]

    for chunk in range(chunks):
        put_rims(forcing, SUB, levels, per_chunk, chunk, side_ref, 0, rows)
    put_rows(forcing, SUB, a_ref, b_ref, rows, 0, levels)


def unpack_residual(cap, arrived, out):
    lane = lax.broadcasted_iota(jnp.int32, (1, LANES), 1)
    groups = LANES // cap
    for row in range(out.shape[0]):
        made = None
        for g in range(groups):
            piece = arrived[pl.ds(row * groups + g, 1), :]
            if g:
                piece = pltpu.roll(piece, g * cap, 1)
            made = piece if made is None else jnp.where(lane >= g * cap, piece, made)
        out[pl.ds(row, 1), :] = made


def exchange(side_rim, a_rim, b_rim):
    lons, lats = lax.axis_size("lon"), lax.axis_size("lat")

    def partner(j, odd):
        other = j + 1 if j % 2 == odd else j - 1
        return other if 0 <= other < lats else j

    return (
        lax.ppermute(side_rim, "lon", [(i, (i + 1) % lons) for i in range(lons)]),
        lax.ppermute(side_rim, "lon", [((i + 1) % lons, i) for i in range(lons)]),
        lax.ppermute(a_rim, "lat", [(j, partner(j, 0)) for j in range(lats)]),
        lax.ppermute(b_rim, "lat", [(j, partner(j, 1)) for j in range(lats)]),
    )


def per_device(
    concentration, adjoint, wind_east, wind_north, mixing, sound_col, kernel, observed, obs_error
):
    levels, tracers, rows, cols = adjoint.shape
    bricks = lax.axis_size("lon") * lax.axis_size("lat")
    slots = sound_col.shape[2]
    cap = slots // bricks
    unroll = largest(levels, 8, 4, 3, 2, 1)
    chunks, per_chunk = rim_chunks(levels, unroll)
    plane = tracers * rows
    per_level = slots // LANES
    groups = LANES // cap
    group_rows = -(-(levels + 3) // (groups * SUB)) * SUB
    field_bytes = levels * plane * cols * 4
    dma = pltpu.SemaphoreType.DMA

    def flat(x):
        return x.reshape(-1, LANES)

    packed = call(
        functools.partial(pack, levels, group_rows, cap),
        [HBM] * 4, f32(bricks, group_rows, LANES), VMEM,
        (
            vmem(levels * per_level, LANES), pltpu.VMEM((per_level, LANES), jnp.int32),
            vmem(per_level, LANES), vmem(per_level, LANES),
            vmem(largest(per_level, 8, 4, 2, 1), groups * group_rows, LANES), dma((4,)),
        ),
        4, 10, 800000, "pack",
    )(*(in_hbm(flat(x)) for x in (kernel, sound_col, observed, obs_error)))
    received = lax.all_to_all(packed, ("lon", "lat"), split_axis=0, concat_axis=0, tiled=True)

    field = adjoint.reshape(levels * tracers, rows, LANES)
    east, north, mix = (in_hbm(flat(x)) for x in (wind_east, wind_north, mixing))
    rims = call(
        functools.partial(first_rims, levels, tracers, rows, chunks, per_chunk),
        [HBM] * 3,
        (f32(chunks, plane + rows, LANES),) + (f32(levels * tracers + levels, LANES),) * 2,
        (VMEM,) * 3,
        (vmem(levels * plane, LANES), vmem(levels * rows, LANES), vmem(levels * rows, LANES), dma((chunks + 2,))),
        10, field_bytes, 2 * field_bytes, "first_rims",
    )(in_hbm(flat(adjoint)), east, north)
    start_rims = exchange(*rims)

    block = largest(levels, 24, 16, 8)
    sum_block = largest(levels, 12, 8)
    sums = call(
        functools.partial(tracer_sum, sum_block),
        [HBM], jax.ShapeDtypeStruct((2, levels * SUB, rows // SUB * cols), jnp.bfloat16), VMEM,
        (vmem(levels, tracers, rows, cols), dma((levels // sum_block,))),
        10, field_bytes // 4, field_bytes, "tracer_sum",
    )(concentration)

    width = largest(slots, 2 * LANES, LANES)
    parts = slots // width
    forcing, *rims, back = call(
        functools.partial(soundings, levels, rows, group_rows, cap, chunks, per_chunk, block),
        [VMEM] * 2,
        (
            f32(levels * rows + 2 * SUB, LANES), f32(chunks, rows, LANES), f32(levels, LANES), f32(levels, LANES),
            hbm(bricks, LANES),
        ),
        (VMEM,) * 5,
        (
            vmem(parts, groups * group_rows, width),
            pltpu.VMEM((parts, width, rows // SUB * LANES), jnp.bfloat16),
            vmem(max(parts, SUB), width),
        ),
        10, field_bytes * 8, field_bytes, "soundings",
    )(received, sums)
    forcing_rims = exchange(*rims)

    rim_shape, edge_shape = (chunks, plane, LANES), (2, levels * tracers, LANES)
    weight_shape = (8, levels * rows, LANES)
    weights, rim0, edges0 = call(
        functools.partial(coefficients, levels, tracers, rows, per_chunk, unroll),
        [HBM] * 3 + [VMEM] * 4,
        (f32(*weight_shape), f32(*rim_shape), f32(*edge_shape)),
        (VMEM,) * 3,
        (vmem(levels * rows, LANES),) * 3 + (dma((3,)),),
        4, field_bytes, field_bytes, "coefficients",
    )(east, north, mix, *start_rims)

    def advance(first, specs, operands, outs, out_specs, scratch):
        return call(
            functools.partial(step, levels, tracers, rows, chunks, per_chunk, unroll, first),
            specs, outs, out_specs,
            (vmem(levels * tracers + 2, rows, LANES), vmem(plane + rows, LANES))
            + scratch + (dma((2 * (levels // unroll) + 5,)),),
            16, field_bytes * 8, field_bytes * 2, "step",
        )(*operands)

    edge_rows = f32(levels * tracers, LANES)
    stepped, kept, *rims = advance(
        True, [HBM] + [VMEM] * 8, (in_hbm(field), weights, rim0, edges0, forcing, *forcing_rims),
        (hbm(*field.shape), hbm(*weight_shape), f32(*rim_shape), edge_rows, edge_rows), (HBM,) * 2 + (VMEM,) * 3,
        (vmem(chunks, rows, LANES), vmem(2, levels, LANES)),
    )
    (result,) = advance(
        False, [HBM] * 2 + [ANY] * 4, (in_hbm(stepped), in_hbm(kept), *exchange(*rims)),
        (f32(*field.shape),), (HBM,),
        (vmem(*weight_shape),) + (vmem(*rim_shape),) * 2 + (vmem(levels * tracers, LANES),) * 2
        + (vmem(*rim_shape), vmem(*edge_shape)),
    )

    returned = lax.all_to_all(
        back.reshape(bricks, 1, LANES), ("lon", "lat"), split_axis=0, concat_axis=0, tiled=True
    )
    result, returned = lax.optimization_barrier((result, returned))
    residual = call(
        functools.partial(unpack_residual, cap), [VMEM], f32(per_level, LANES), VMEM, (), 2, 10, 10000, "residual",
    )(returned.reshape(bricks, LANES))
    return result.reshape(adjoint.shape), residual.reshape(sound_col.shape)


def solution(mesh):
    field = P(None, None, "lat", "lon")
    face = P(None, "lat", "lon")
    owned = P(None, ("lon", "lat"), None)
    return jax.shard_map(
        per_device,
        mesh=mesh,
        in_specs=(field, field, face, face, face, owned, owned, owned, owned),
        out_specs=(field, owned),
        check_vma=False,
    )
```

```python
import functools

import jax
import jax.numpy as jnp
from jax import lax
from jax.experimental import pallas as pl
from jax.experimental.pallas import tpu as pltpu
from jax.sharding import PartitionSpec as P

LANES = 128
SUB = 8
MIB = 1 << 20
ANY = pl.BlockSpec(memory_space=pl.ANY)
HBM = pl.BlockSpec(memory_space=pltpu.HBM)
VMEM = pl.BlockSpec(memory_space=pltpu.VMEM)


def rim_chunks(levels, unroll):
    per_chunk = 63 // unroll * unroll
    chunks = -(-levels // per_chunk)
    return chunks, -(-levels // (chunks * unroll)) * unroll


def lane_iota():
    return lax.broadcasted_iota(jnp.int32, (SUB, LANES), 1)


def sub_iota():
    return lax.broadcasted_iota(jnp.int32, (SUB, LANES), 0)


def largest(count, *choices):
    return next(u for u in choices if count % u == 0)


def in_hbm(x):
    return pltpu.with_memory_space_constraint(x, pltpu.HBM)


def hbm(*shape):
    return pltpu.HBM(shape, jnp.float32)


def f32(*shape):
    return jax.ShapeDtypeStruct(shape, jnp.float32)


def vmem(*shape):
    return pltpu.VMEM(shape, jnp.float32)


def call(body, ins, outs, out_specs, scratch, mib, flops, size, name):
    return pl.pallas_call(
        body,
        in_specs=ins,
        out_specs=out_specs,
        out_shape=outs,
        scratch_shapes=scratch,
        compiler_params=pltpu.CompilerParams(vmem_limit_bytes=mib * MIB),
        cost_estimate=pl.CostEstimate(flops=flops, bytes_accessed=size, transcendentals=0),
        name=name,
    )


def put_rims(field, offset, levels, per_chunk, chunk, out, first, plane):
    lane = lane_iota()
    group = largest(plane // SUB, 4, 2, 1)
    count = min(per_chunk, levels - chunk * per_chunk)

    def body(i, carry):
        r = pl.multiple_of(i * SUB * group, SUB * group)
        made = [jnp.zeros((SUB, LANES), jnp.float32)] * group
        for q in range(count):
            for g in range(group):
                at = pl.multiple_of((chunk * per_chunk + q) * plane + offset + r + g * SUB, SUB)
                turned = pltpu.roll(field[pl.ds(at, SUB), :], 2 * q + 2, 1)
                made[g] = jnp.where(lane >= 2 * q + 1, turned, made[g])
        for g in range(group):
            out[chunk, pl.ds(pl.multiple_of(first + r + g * SUB, SUB), SUB), :] = made[g]
        return carry

    lax.fori_loop(0, plane // SUB // group, body, 0)


def put_rows(field, offset, a_ref, b_ref, rows, begin, end):
    unroll = largest((end - begin) // SUB, 9, 8, 4, 2, 1)
    odd = lax.axis_index("lat") % 2
    in_a = (1 - odd) * (rows - 1)
    in_b = odd * (rows - 1)

    def body(i, carry):
        for u in range(unroll):
            start = pl.multiple_of(begin + (i * unroll + u) * SUB, SUB)
            at = start * rows + offset
            a_ref[pl.ds(start, SUB), :] = field[pl.ds(at + in_a, SUB, stride=rows), :]
            b_ref[pl.ds(start, SUB), :] = field[pl.ds(at + in_b, SUB, stride=rows), :]
        return carry

    lax.fori_loop(0, (end - begin) // SUB // unroll, body, 0)


def first_rims(levels, tracers, rows, chunks, per_chunk, field, east, north, side, a_ref, b_ref, f, e, n, sems):
    plane = tracers * rows
    wind_copies = [
        pltpu.make_async_copy(east, e, sems.at[chunks]),
        pltpu.make_async_copy(north, n, sems.at[chunks + 1]),
    ]
    copies = []
    for i in range(chunks):
        part = pl.ds(i * per_chunk * plane, min(per_chunk, levels - i * per_chunk) * plane)
        copies.append(pltpu.make_async_copy(field.at[part], f.at[part], sems.at[i]))
    for copy in wind_copies + copies:
        copy.start()
    wind_copies[0].wait()
    for i in range(chunks):
        put_rims(e, 0, levels, per_chunk, i, side, plane, rows)
    wind_copies[1].wait()
    winds = pl.ds(levels * tracers, levels)
    put_rows(n, 0, a_ref.at[winds], b_ref.at[winds], rows, 0, levels)
    for i in range(chunks):
        copies[i].wait()
        put_rims(f, 0, levels, per_chunk, i, side, 0, plane)
        put_rows(
            f, 0, a_ref, b_ref, rows, i * per_chunk * tracers, min((i + 1) * per_chunk, levels) * tracers
        )


def meet(rim, target, from_west, from_east, count):
    lane = lane_iota()
    for chunk in range(rim.shape[0]):
        for r in range(0, count, SUB):
            rows = pl.ds(r, SUB)
            turned = pltpu.roll(from_east[chunk, rows, :], LANES - 2, 1)
            rim[chunk, pl.ds(target + r, SUB), :] = jnp.where(lane % 2 == 1, from_west[chunk, rows, :], turned)


def pair(edges, target, from_a, from_b, count):
    even = jnp.full((SUB, LANES), lax.axis_index("lat"), jnp.int32) % 2 == 0
    repeat = largest(count // SUB, 9, 8, 4, 2, 1)

    def body(i, carry):
        for u in range(repeat):
            at = pl.multiple_of((i * repeat + u) * SUB, SUB)
            a, b = from_a[pl.ds(at, SUB), :], from_b[pl.ds(at, SUB), :]
            edges[0, pl.ds(target + at, SUB), :] = jnp.where(even, a, b)
            edges[1, pl.ds(target + at, SUB), :] = jnp.where(even, b, a)
        return carry

    lax.fori_loop(0, count // SUB // repeat, body, 0)


def coefficients(
    levels, tracers, rows, per_chunk, unroll, east, north, mixing, west0, east0, a0, b0, *refs
):
    weights, rim, edges, e_buf, n_buf, m_buf, sems = refs
    plane = tracers * rows
    halves = rows // SUB
    lane, sub = lane_iota(), sub_iota()
    copies = [
        pltpu.make_async_copy(source, target, sems.at[i])
        for i, (source, target) in enumerate(((east, e_buf), (north, n_buf), (mixing, m_buf)))
    ]
    for copy in copies:
        copy.start()
    meet(rim, 0, west0, east0, plane)
    pair(edges, 0, a0, b0, levels * tracers)
    for copy in copies:
        copy.wait()
    place = lax.axis_index("lat")
    even = jnp.full((1, LANES), place, jnp.int32) % 2 == 0
    south_flag = (place > 0).astype(jnp.float32)
    north_flag = (place < lax.axis_size("lat") - 1).astype(jnp.float32)
    north_mask = jnp.where(sub == SUB - 1, north_flag, 1.0)

    def level(k, pivots):
        chunk, q = k // per_chunk, k % per_chunk
        has_up = (k < levels - 1).astype(jnp.float32)
        new, edge = [], None
        for h in range(halves):
            blk = pl.ds(pl.multiple_of(k * rows + h * SUB, SUB), SUB)
            down, factor = pivots[h]
            up = m_buf[blk, :] * has_up
            inv = 1.0 / (1.0 + up + down - down * factor)
            factor = up * inv
            new.append((up, factor))
            e, n = e_buf[blk, :], n_buf[blk, :]
            side = pltpu.roll(west0[chunk, pl.ds(plane + h * SUB, SUB), :], LANES - 1 - 2 * q, 1)
            w_in = jnp.minimum(jnp.where(lane == 0, side, pltpu.roll(e, 1, 1)), 0.0)
            if h == 0:
                row = pl.ds(levels * tracers + k, 1)
                edge = jnp.where(even, b0[row, :], a0[row, :]) * south_flag
            s_in = jnp.minimum(jnp.where(sub == 0, edge, pltpu.roll(n, 1, 0)), 0.0)
            edge = n[SUB - 1 : SUB, :]
            e_out, n_out = jnp.maximum(e, 0.0), jnp.maximum(n, 0.0)
            from_n = n_out * inv
            if h == halves - 1:
                from_n = from_n * north_mask
            stay = (1.0 - e_out + w_in - n_out + s_in) * inv
            from_e, from_w = e_out * inv, -(w_in * inv)
            from_rim = jnp.where(lane == 0, from_w, jnp.where(lane == LANES - 1, from_e, 0.0))
            from_e = jnp.where(lane == LANES - 1, 0.0, from_e)
            from_w = jnp.where(lane == 0, 0.0, from_w)
            values = (stay, from_e, from_w, from_n, -(s_in * inv), from_rim, down * inv, factor)
            for i, value in enumerate(values):
                weights[i, blk, :] = value
        return tuple(new)

    def body(b, carry):
        for u in range(unroll):
            carry = level(b * unroll + u, carry)
        return carry

    zero = jnp.zeros((SUB, LANES), jnp.float32)
    lax.fori_loop(0, levels // unroll, body, ((zero, zero),) * halves)


def step(levels, tracers, rows, chunks, per_chunk, unroll, first, *refs):
    if first:
        field, weights, rim, edges, forcing, f_west, f_east, f_a, f_b = refs[:9]
        out, weights_out, side_ref, a_ref, b_ref = refs[9:14]
        buf, rim_now, f_rim, f_edges, sems = refs[14:]
    else:
        field, weights_in, west_in, east_in, a_in, b_in, out = refs[:7]
        buf, rim_now, weights, west_buf, east_buf, a_buf, b_buf, rim, edges, sems = refs[7:]

    plane = tracers * rows
    halves = rows // SUB
    lane, sub = lane_iota(), sub_iota()
    blocks = levels // unroll
    flat = buf.reshape((levels * tracers + 2) * rows, LANES)

    def load(b):
        at = b * unroll * tracers
        return pltpu.make_async_copy(
            field.at[pl.ds(at, unroll * tracers)], buf.at[pl.ds(at + 1, unroll * tracers)], sems.at[b]
        )

    def store(b):
        at = b * unroll * tracers
        return pltpu.make_async_copy(
            buf.at[pl.ds(at + 1, unroll * tracers)], out.at[pl.ds(at, unroll * tracers)], sems.at[b]
        )

    last = 2 * blocks
    above = weights.at[weights.shape[0] - 1]
    if first:
        keep = pltpu.make_async_copy(weights, weights_out, sems.at[last])
        for b in range(blocks):
            load(b).start()
        keep.start()
        meet(f_rim, 0, f_west, f_east, rows)
        pair(f_edges, 0, f_a, f_b, levels)
    else:
        rim_copies = [
            pltpu.make_async_copy(source, target, sems.at[last + 1 + i])
            for i, (source, target) in enumerate(
                ((west_in, west_buf), (east_in, east_buf), (a_in, a_buf), (b_in, b_buf))
            )
        ]
        above_copy = pltpu.make_async_copy(weights_in.at[weights.shape[0] - 1], above, sems.at[last])
        for copy in rim_copies:
            copy.start()

        def load_weights(b):
            planes, levels_of = pl.ds(0, weights.shape[0] - 1), pl.ds(b * unroll * rows, unroll * rows)
            return pltpu.make_async_copy(
                weights_in.at[planes, levels_of], weights.at[planes, levels_of], sems.at[blocks + b]
            )

        for b in range(blocks):
            load(b).start()
            load_weights(b).start()
        above_copy.start()
        for copy in rim_copies:
            copy.wait()
        meet(rim, 0, west_buf, east_buf, plane)
        pair(edges, 0, a_buf, b_buf, levels * tracers)

    def stencil(cells, here, side, edge, row, co):
        halfs = [cells[pl.ds(here + h * SUB, SUB), :] for h in range(halves)]
        ups = [pltpu.roll(half, SUB - 1, 0) for half in halfs] + [edge[0, pl.ds(row, 1), :]]
        downs = [edge[1, pl.ds(row, 1), :]] + [pltpu.roll(half, 1, 0) for half in halfs]
        values = []
        for h, cell in enumerate(halfs):
            n = jnp.where(sub == SUB - 1, ups[h + 1], ups[h])
            s = jnp.where(sub == 0, downs[h], downs[h + 1])
            c0, ce, cw, cn, cs, rims = co[h][:6]
            value = (c0 * cell + ce * pltpu.roll(cell, LANES - 1, 1)) + (cw * pltpu.roll(cell, 1, 1) + cn * n)
            values.append(value + (cs * s + rims * side(h)))
        return values

    def part(ref, b, size, offset=0):
        return ref.at[pl.ds(pl.multiple_of(b * unroll * size + offset, SUB), unroll * size)]

    def forward_block(b, solved):
        load(b).wait()
        if not first:
            load_weights(b).wait()

        chunk, q = b * unroll // per_chunk, b * unroll % per_chunk
        turn = (LANES - 2 * q) % LANES
        for r in range(0, plane, SUB):
            rim_now[pl.ds(r, SUB), :] = pltpu.roll(rim[chunk, pl.ds(r, SUB), :], turn, 1)
        if first:
            for r in range(0, rows, SUB):
                rim_now[pl.ds(plane + r, SUB), :] = pltpu.roll(f_rim[chunk, pl.ds(r, SUB), :], turn, 1)

        def side(u, r):
            return lambda h: pltpu.roll(rim_now[pl.ds(r + h * SUB, SUB), :], LANES - 1 - 2 * u, 1)

        cells = part(flat, b, plane, rows)
        edge = edges.at[:, pl.ds(pl.multiple_of(b * unroll * tracers, SUB), unroll * tracers)]
        co_part = weights.at[:, pl.ds(pl.multiple_of(b * unroll * rows, SUB), unroll * rows)]
        if first:
            f_cells = part(forcing, b, rows, SUB)
            f_edge = f_edges.at[:, pl.ds(pl.multiple_of(b * unroll, SUB), unroll)]
        for u in range(unroll):
            co = [
                [co_part[i, pl.ds(u * rows + h * SUB, SUB), :] for i in range(weights.shape[0] - 1)]
                for h in range(halves)
            ]
            if first:
                extra = stencil(f_cells, u * rows, side(u, plane), f_edge, u, co)
            new = []
            for t in range(tracers):
                here = u * plane + t * rows
                values = stencil(cells, here, side(u, t * rows), edge, u * tracers + t, co)
                for h in range(halves):
                    value = values[h] + extra[h] if first else values[h]
                    value = value + co[h][6] * solved[t * halves + h]
                    new.append(value)
                    cells[pl.ds(here + h * SUB, SUB), :] = value
            solved = tuple(new)
        return solved

    zero = jnp.zeros((SUB, LANES), jnp.float32)
    zeros = (zero,) * (tracers * halves)
    lax.fori_loop(0, blocks, forward_block, zeros)
    if not first:
        above_copy.wait()

    def backward_block(i, later):
        b = blocks - 1 - i
        cells = part(flat, b, plane, rows)
        factors = part(above, b, rows)
        for u in reversed(range(unroll)):
            new = []
            for h in range(halves):
                factor = factors[pl.ds(u * rows + h * SUB, SUB), :]
                for t in range(tracers):
                    blk = pl.ds(u * plane + t * rows + h * SUB, SUB)
                    value = cells[blk, :] + factor * later[h * tracers + t]
                    cells[blk, :] = value
                    new.append(value)
            later = tuple(new)
        store(b).start()
        return later

    lax.fori_loop(0, blocks, backward_block, zeros)
    if first:
        for chunk in range(chunks):
            put_rims(flat, rows, levels, per_chunk, chunk, side_ref, 0, plane)
        put_rows(flat, rows, a_ref, b_ref, rows, 0, levels * tracers)
        keep.wait()
    for b in range(blocks):
        store(b).wait()


def row_offsets(count):
    return list(range(0, count - SUB, SUB)) + [count - SUB]


def pack(levels, group_rows, cap, kernel, columns, observed, errors, out, k_buf, c_buf, o_buf, e_buf, wide, out_buf, sems):
    lane = lane_iota()
    copies = [
        pltpu.make_async_copy(source, target, sems.at[i])
        for i, (source, target) in enumerate(
            ((columns, c_buf), (observed, o_buf), (errors, e_buf), (kernel, k_buf))
        )
    ]
    for copy in copies:
        copy.start()
    for copy in copies:
        copy.wait()
    per_level = columns.shape[0]
    groups = LANES // cap
    offsets = row_offsets(group_rows)
    padded = wide.shape[1] // groups
    together = wide.shape[0]

    def body(start, carry):
        for n in range(together):
            i = start * together + n
            one = pl.ds(i, 1)
            for g in range(groups):
                begin = g * group_rows
                count = min(group_rows, levels - begin)
                wide[n, pl.ds(g * padded, count), :] = k_buf[
                    pl.ds(i + per_level * begin, count, stride=per_level), :
                ]
            end = (groups - 1) * padded + levels - (groups - 1) * group_rows
            for m, row in enumerate((c_buf[one, :].astype(jnp.float32), o_buf[one, :], e_buf[one, :])):
                wide[n, pl.ds(end + m, 1), :] = row
            for m in range(end + 3, (groups - 1) * padded + group_rows):
                wide[n, pl.ds(m, 1), :] = jnp.zeros((1, LANES), jnp.float32)
        for n in range(together):
            i = start * together + n
            for j in range(groups):
                for m in offsets:
                    made = None
                    for g in range(groups):
                        piece = wide[n, pl.ds(g * padded + m, SUB), :]
                        if g != j:
                            piece = pltpu.roll(piece, (g - j) * cap % LANES, 1)
                        made = piece if made is None else jnp.where(lane >= g * cap, piece, made)
                    out_buf[pl.ds((i * groups + j) * group_rows + m, SUB), :] = made
        return carry

    if per_level == together:
        body(0, 0)
    else:
        lax.fori_loop(0, per_level // together, body, 0)
    done = pltpu.make_async_copy(out_buf, out, sems.at[4])
    done.start()
    done.wait()


def tracer_sum(block, concentration, out, buf, sems):
    levels, tracers, rows, cols = buf.shape

    def load(b):
        return pltpu.make_async_copy(
            concentration.at[pl.ds(b * block, block)], buf.at[pl.ds(b * block, block)], sems.at[b]
        )

    for b in range(levels // block):
        load(b).start()

    def body(b, carry):
        load(b).wait()
        for h in range(rows // SUB):
            tops, rests = [], []
            for k in range(block):
                part = jnp.sum(buf[b * block + k, :, pl.ds(h * SUB, SUB), :], axis=0)
                top = part.astype(jnp.bfloat16).astype(jnp.float32)
                tops.append(top)
                rests.append(part - top)
            at = pl.ds(pl.multiple_of(b * block * SUB, block * SUB), block * SUB)
            lanes = pl.ds(h * cols, cols)
            out[0, at, lanes] = jnp.concatenate(tops, axis=0).astype(jnp.bfloat16)
            out[1, at, lanes] = jnp.concatenate(rests, axis=0).astype(jnp.bfloat16)
        return carry

    lax.fori_loop(0, levels // block, body, 0)


def soundings(
    levels, rows, group_rows, cap, chunks, per_chunk, block,
    received, sums, forcing, side_ref, a_ref, b_ref, back_out, arrived, table, scaled, back, sem
):
    lane = lane_iota()
    parts, _, width = arrived.shape
    halves = rows // SUB
    keys = halves * LANES
    groups = LANES // cap

    def unpack(c, carry):
        part, col = c // (width // LANES), c % (width // LANES)
        for g in range(groups):
            for m in row_offsets(group_rows):
                made = None
                for p in range(groups):
                    piece = received[pl.ds((c * groups + p) * group_rows + m, SUB), :]
                    if p != g:
                        piece = pltpu.roll(piece, (p - g) * cap % LANES, 1)
                    made = piece if made is None else jnp.where(lane >= p * cap, piece, made)
                lanes = pl.ds(pl.multiple_of(col * LANES, LANES), LANES)
                arrived[part, pl.ds(g * group_rows + m, SUB), lanes] = made
        return carry

    lax.fori_loop(0, parts * width // LANES, unpack, 0)

    sub_index = lax.broadcasted_iota(jnp.int32, (SUB, width), 0)
    key_index = lax.broadcasted_iota(jnp.int32, (keys, width), 0)
    turned_index = lax.broadcasted_iota(jnp.int32, (LANES, keys), 1)

    def columns(j):
        return arrived[j, pl.ds(levels, 1), :].astype(jnp.int32)

    def key_of(col):
        return (col >> 10) * LANES + (col & (LANES - 1))

    def mask_of(j):
        return sub_index == ((columns(j) >> 7) & (SUB - 1))

    for j in range(parts):
        col = columns(j)
        key = key_of(col)
        look = jnp.where(key_index == key, 1.0, 0.0).astype(jnp.bfloat16)
        for c in range(width // LANES):
            piece = key[:, c * LANES : (c + 1) * LANES].astype(jnp.float32)
            across = jnp.broadcast_to(piece, (LANES, LANES)).T.astype(jnp.int32)
            across = jnp.concatenate([across] * halves, axis=1)
            table[j, pl.ds(c * LANES, LANES), :] = jnp.where(turned_index == across, 1.0, 0.0).astype(
                jnp.bfloat16
            )
        total = jnp.zeros((SUB, width), jnp.float32)
        for b in range(levels // block):
            blk = pl.ds(b * block * SUB, block * SUB)
            seen = jnp.dot(sums[0, blk, :], look, preferred_element_type=jnp.float32)
            seen += jnp.dot(sums[1, blk, :], look, preferred_element_type=jnp.float32)
            weight = arrived[j, pl.ds(b * block, block), :]
            for k in range(block):
                total += weight[k : k + 1, :] * seen[k * SUB : (k + 1) * SUB, :]
        modelled = jnp.sum(jnp.where(mask_of(j), total, 0.0), axis=0, keepdims=True)
        observed = arrived[j, pl.ds(levels + 1, 1), :]
        error = arrived[j, pl.ds(levels + 2, 1), :]
        residual = jnp.where(col >= 0, (modelled - observed) / error, 0.0)
        scaled[pl.ds(j, 1), :] = residual / error
        for i in range(width // cap):
            at = i * cap
            piece = residual[:, at // LANES * LANES : at // LANES * LANES + LANES]
            if at % LANES:
                piece = pltpu.roll(piece, LANES - at % LANES, 1)
            back[pl.ds(j * (width // cap) + i, 1), :] = piece

    leave = pltpu.make_async_copy(back, back_out, sem.at[0])
    leave.start()
    zeros = jnp.zeros((SUB, LANES), jnp.float32)
    forcing[pl.ds(0, SUB), :] = zeros
    forcing[pl.ds(levels * rows + SUB, SUB), :] = zeros
    for b in range(levels // block):
        total = jnp.zeros((block * SUB, keys), jnp.float32)
        for j in range(parts):
            weight = arrived[j, pl.ds(b * block, block), :] * scaled[pl.ds(j, 1), :]
            top = weight.astype(jnp.bfloat16).astype(jnp.float32)
            mask = mask_of(j)
            for part in (top, weight - top):
                spread = jnp.concatenate(
                    [jnp.where(mask, part[k : k + 1, :], 0.0) for k in range(block)], axis=0
                ).astype(jnp.bfloat16)
                total += jnp.dot(spread, table[j, :, :], preferred_element_type=jnp.float32)
        for k in range(block):
            for h in range(halves):
                forcing[pl.ds((b * block + k) * rows + (h + 1) * SUB, SUB), :] = total[
                    k * SUB : (k + 1) * SUB, h * LANES : (h + 1) * LANES
                ]

    for chunk in range(chunks):
        put_rims(forcing, SUB, levels, per_chunk, chunk, side_ref, 0, rows)
    put_rows(forcing, SUB, a_ref, b_ref, rows, 0, levels)
    leave.wait()


def unpack_residual(cap, arrived, out):
    lane = lax.broadcasted_iota(jnp.int32, (1, LANES), 1)
    groups = LANES // cap
    for row in range(out.shape[0]):
        made = None
        for g in range(groups):
            piece = arrived[pl.ds(row * groups + g, 1), :]
            if g:
                piece = pltpu.roll(piece, g * cap, 1)
            made = piece if made is None else jnp.where(lane >= g * cap, piece, made)
        out[pl.ds(row, 1), :] = made


def exchange(side_rim, a_rim, b_rim):
    lons, lats = lax.axis_size("lon"), lax.axis_size("lat")

    def partner(j, odd):
        other = j + 1 if j % 2 == odd else j - 1
        return other if 0 <= other < lats else j

    return (
        lax.ppermute(side_rim, "lon", [(i, (i + 1) % lons) for i in range(lons)]),
        lax.ppermute(side_rim, "lon", [((i + 1) % lons, i) for i in range(lons)]),
        lax.ppermute(a_rim, "lat", [(j, partner(j, 0)) for j in range(lats)]),
        lax.ppermute(b_rim, "lat", [(j, partner(j, 1)) for j in range(lats)]),
    )


def per_device(
    concentration, adjoint, wind_east, wind_north, mixing, sound_col, kernel, observed, obs_error
):
    levels, tracers, rows, cols = adjoint.shape
    bricks = lax.axis_size("lon") * lax.axis_size("lat")
    slots = sound_col.shape[2]
    cap = slots // bricks
    unroll = largest(levels, 8, 4, 3, 2, 1)
    chunks, per_chunk = rim_chunks(levels, unroll)
    plane = tracers * rows
    per_level = slots // LANES
    groups = LANES // cap
    group_rows = -(-(levels + 3) // groups)
    padded_rows = -(-group_rows // SUB) * SUB
    field_bytes = levels * plane * cols * 4
    dma = pltpu.SemaphoreType.DMA

    def flat(x):
        return x.reshape(-1, LANES)

    packed = call(
        functools.partial(pack, levels, group_rows, cap),
        [HBM] * 4, f32(bricks * group_rows, LANES), HBM,
        (
            vmem(levels * per_level, LANES), pltpu.VMEM((per_level, LANES), jnp.int32),
            vmem(per_level, LANES), vmem(per_level, LANES),
            vmem(largest(per_level, 8, 4, 2, 1), groups * padded_rows, LANES),
            vmem(bricks * group_rows, LANES), dma((5,)),
        ),
        4, 10, 800000, "pack",
    )(*(in_hbm(flat(x)) for x in (kernel, sound_col, observed, obs_error)))
    received = lax.all_to_all(
        packed.reshape(-1, 1, LANES), ("lon", "lat"), split_axis=0, concat_axis=0, tiled=True
    ).reshape(-1, LANES)

    field = adjoint.reshape(levels * tracers, rows, LANES)
    east, north, mix = (in_hbm(flat(x)) for x in (wind_east, wind_north, mixing))
    rims = call(
        functools.partial(first_rims, levels, tracers, rows, chunks, per_chunk),
        [HBM] * 3,
        (f32(chunks, plane + rows, LANES),) + (f32(levels * tracers + levels, LANES),) * 2,
        (VMEM,) * 3,
        (vmem(levels * plane, LANES), vmem(levels * rows, LANES), vmem(levels * rows, LANES), dma((chunks + 2,))),
        10, field_bytes, 2 * field_bytes, "first_rims",
    )(in_hbm(flat(adjoint)), east, north)
    start_rims = exchange(*rims)

    block = largest(levels, 24, 16, 8)
    sum_block = largest(levels, 12, 8)
    sums = call(
        functools.partial(tracer_sum, sum_block),
        [HBM], jax.ShapeDtypeStruct((2, levels * SUB, rows // SUB * cols), jnp.bfloat16), VMEM,
        (vmem(levels, tracers, rows, cols), dma((levels // sum_block,))),
        10, field_bytes // 4, field_bytes, "tracer_sum",
    )(concentration)

    width = largest(slots, 2 * LANES, LANES)
    parts = slots // width
    forcing, *rims, back = call(
        functools.partial(soundings, levels, rows, group_rows, cap, chunks, per_chunk, block),
        [VMEM] * 2,
        (
            f32(levels * rows + 2 * SUB, LANES), f32(chunks, rows, LANES), f32(levels, LANES), f32(levels, LANES),
            hbm(bricks, LANES),
        ),
        (VMEM,) * 4 + (HBM,),
        (
            vmem(parts, -(-groups * group_rows // SUB) * SUB, width),
            pltpu.VMEM((parts, width, rows // SUB * LANES), jnp.bfloat16),
            vmem(max(parts, SUB), width), vmem(bricks, LANES), dma((1,)),
        ),
        10, field_bytes * 8, field_bytes, "soundings",
    )(received, sums)
    forcing_rims = exchange(*rims)

    rim_shape, edge_shape = (chunks, plane, LANES), (2, levels * tracers, LANES)
    weight_shape = (8, levels * rows, LANES)
    weights, rim0, edges0 = call(
        functools.partial(coefficients, levels, tracers, rows, per_chunk, unroll),
        [HBM] * 3 + [VMEM] * 4,
        (f32(*weight_shape), f32(*rim_shape), f32(*edge_shape)),
        (VMEM,) * 3,
        (vmem(levels * rows, LANES),) * 3 + (dma((3,)),),
        4, field_bytes, field_bytes, "coefficients",
    )(east, north, mix, *start_rims)

    def advance(first, together, specs, operands, outs, out_specs, scratch):
        return call(
            functools.partial(step, levels, tracers, rows, chunks, per_chunk, together, first),
            specs, outs, out_specs,
            (vmem(levels * tracers + 2, rows, LANES), vmem(plane + rows, LANES))
            + scratch + (dma((2 * (levels // together) + 5,)),),
            16, field_bytes * 8, field_bytes * 2, "step",
        )(*operands)

    edge_rows = f32(levels * tracers, LANES)
    stepped, kept, *rims = advance(
        True, unroll, [HBM] + [VMEM] * 8, (in_hbm(field), weights, rim0, edges0, forcing, *forcing_rims),
        (hbm(*field.shape), hbm(*weight_shape), f32(*rim_shape), edge_rows, edge_rows), (HBM,) * 2 + (VMEM,) * 3,
        (vmem(chunks, rows, LANES), vmem(2, levels, LANES)),
    )
    (result,) = advance(
        False, largest(unroll, 4, 3, 2, 1), [HBM] * 2 + [ANY] * 4, (in_hbm(stepped), in_hbm(kept), *exchange(*rims)),
        (f32(*field.shape),), (HBM,),
        (vmem(*weight_shape),) + (vmem(*rim_shape),) * 2 + (vmem(levels * tracers, LANES),) * 2
        + (vmem(*rim_shape), vmem(*edge_shape)),
    )

    returned = lax.all_to_all(
        back.reshape(bricks, 1, LANES), ("lon", "lat"), split_axis=0, concat_axis=0, tiled=True
    )
    result, returned = lax.optimization_barrier((result, returned))
    residual = call(
        functools.partial(unpack_residual, cap), [VMEM], f32(per_level, LANES), VMEM, (), 2, 10, 10000, "residual",
    )(returned.reshape(bricks, LANES))
    return result.reshape(adjoint.shape), residual.reshape(sound_col.shape)


def solution(mesh):
    field = P(None, None, "lat", "lon")
    face = P(None, "lat", "lon")
    owned = P(None, ("lon", "lat"), None)
    return jax.shard_map(
        per_device,
        mesh=mesh,
        in_specs=(field, field, face, face, face, owned, owned, owned, owned),
        out_specs=(field, owned),
        check_vma=False,
    )
```

```python
import functools

import jax
import jax.numpy as jnp
from jax import lax
from jax.experimental import pallas as pl
from jax.experimental.pallas import tpu as pltpu
from jax.sharding import PartitionSpec as P

LANES = 128
SUB = 8
MIB = 1 << 20
ANY = pl.BlockSpec(memory_space=pl.ANY)
HBM = pl.BlockSpec(memory_space=pltpu.HBM)
VMEM = pl.BlockSpec(memory_space=pltpu.VMEM)


def rim_chunks(levels, unroll):
    per_chunk = 63 // unroll * unroll
    chunks = -(-levels // per_chunk)
    return chunks, -(-levels // (chunks * unroll)) * unroll


def lane_iota():
    return lax.broadcasted_iota(jnp.int32, (SUB, LANES), 1)


def sub_iota():
    return lax.broadcasted_iota(jnp.int32, (SUB, LANES), 0)


def largest(count, *choices):
    return next(u for u in choices if count % u == 0)


def in_hbm(x):
    return pltpu.with_memory_space_constraint(x, pltpu.HBM)


def hbm(*shape):
    return pltpu.HBM(shape, jnp.float32)


def f32(*shape):
    return jax.ShapeDtypeStruct(shape, jnp.float32)


def vmem(*shape):
    return pltpu.VMEM(shape, jnp.float32)


def call(body, ins, outs, out_specs, scratch, mib, flops, size, name):
    return pl.pallas_call(
        body,
        in_specs=ins,
        out_specs=out_specs,
        out_shape=outs,
        scratch_shapes=scratch,
        compiler_params=pltpu.CompilerParams(vmem_limit_bytes=mib * MIB),
        cost_estimate=pl.CostEstimate(flops=flops, bytes_accessed=size, transcendentals=0),
        name=name,
    )


def put_rims(field, offset, levels, per_chunk, chunk, out, first, plane):
    lane = lane_iota()
    group = largest(plane // SUB, 4, 2, 1)
    count = min(per_chunk, levels - chunk * per_chunk)

    def body(i, carry):
        r = pl.multiple_of(i * SUB * group, SUB * group)
        made = [jnp.zeros((SUB, LANES), jnp.float32)] * group
        for q in range(count):
            for g in range(group):
                at = pl.multiple_of((chunk * per_chunk + q) * plane + offset + r + g * SUB, SUB)
                turned = pltpu.roll(field[pl.ds(at, SUB), :], 2 * q + 2, 1)
                made[g] = jnp.where(lane >= 2 * q + 1, turned, made[g])
        for g in range(group):
            out[chunk, pl.ds(pl.multiple_of(first + r + g * SUB, SUB), SUB), :] = made[g]
        return carry

    lax.fori_loop(0, plane // SUB // group, body, 0)


def put_rows(field, offset, a_ref, b_ref, rows, begin, end):
    unroll = largest((end - begin) // SUB, 9, 8, 4, 2, 1)
    odd = lax.axis_index("lat") % 2
    in_a = (1 - odd) * (rows - 1)
    in_b = odd * (rows - 1)

    def body(i, carry):
        for u in range(unroll):
            start = pl.multiple_of(begin + (i * unroll + u) * SUB, SUB)
            at = start * rows + offset
            a_ref[pl.ds(start, SUB), :] = field[pl.ds(at + in_a, SUB, stride=rows), :]
            b_ref[pl.ds(start, SUB), :] = field[pl.ds(at + in_b, SUB, stride=rows), :]
        return carry

    lax.fori_loop(0, (end - begin) // SUB // unroll, body, 0)


def first_rims(levels, tracers, rows, chunks, per_chunk, field, east, north, side, a_ref, b_ref, f, e, n, sems):
    plane = tracers * rows
    wind_copies = [
        pltpu.make_async_copy(east, e, sems.at[chunks]),
        pltpu.make_async_copy(north, n, sems.at[chunks + 1]),
    ]
    copies = []
    for i in range(chunks):
        part = pl.ds(i * per_chunk * plane, min(per_chunk, levels - i * per_chunk) * plane)
        copies.append(pltpu.make_async_copy(field.at[part], f.at[part], sems.at[i]))
    for copy in wind_copies + copies:
        copy.start()
    wind_copies[0].wait()
    for i in range(chunks):
        put_rims(e, 0, levels, per_chunk, i, side, plane, rows)
    wind_copies[1].wait()
    winds = pl.ds(levels * tracers, levels)
    put_rows(n, 0, a_ref.at[winds], b_ref.at[winds], rows, 0, levels)
    for i in range(chunks):
        copies[i].wait()
        put_rims(f, 0, levels, per_chunk, i, side, 0, plane)
        put_rows(
            f, 0, a_ref, b_ref, rows, i * per_chunk * tracers, min((i + 1) * per_chunk, levels) * tracers
        )


def meet(rim, target, from_west, from_east, count):
    lane = lane_iota()
    for chunk in range(rim.shape[0]):
        for r in range(0, count, SUB):
            rows = pl.ds(r, SUB)
            turned = pltpu.roll(from_east[chunk, rows, :], LANES - 2, 1)
            rim[chunk, pl.ds(target + r, SUB), :] = jnp.where(lane % 2 == 1, from_west[chunk, rows, :], turned)


def pair(edges, target, from_a, from_b, count):
    even = jnp.full((SUB, LANES), lax.axis_index("lat"), jnp.int32) % 2 == 0
    repeat = largest(count // SUB, 9, 8, 4, 2, 1)

    def body(i, carry):
        for u in range(repeat):
            at = pl.multiple_of((i * repeat + u) * SUB, SUB)
            a, b = from_a[pl.ds(at, SUB), :], from_b[pl.ds(at, SUB), :]
            edges[0, pl.ds(target + at, SUB), :] = jnp.where(even, a, b)
            edges[1, pl.ds(target + at, SUB), :] = jnp.where(even, b, a)
        return carry

    lax.fori_loop(0, count // SUB // repeat, body, 0)


def coefficients(
    levels, tracers, rows, per_chunk, unroll, east, north, mixing, west0, east0, a0, b0, *refs
):
    weights, rim, edges, e_buf, n_buf, m_buf, sems = refs
    plane = tracers * rows
    halves = rows // SUB
    lane, sub = lane_iota(), sub_iota()
    copies = [
        pltpu.make_async_copy(source, target, sems.at[i])
        for i, (source, target) in enumerate(((east, e_buf), (north, n_buf), (mixing, m_buf)))
    ]
    for copy in copies:
        copy.start()
    meet(rim, 0, west0, east0, plane)
    pair(edges, 0, a0, b0, levels * tracers)
    for copy in copies:
        copy.wait()
    place = lax.axis_index("lat")
    even = jnp.full((1, LANES), place, jnp.int32) % 2 == 0
    south_flag = (place > 0).astype(jnp.float32)
    north_flag = (place < lax.axis_size("lat") - 1).astype(jnp.float32)
    north_mask = jnp.where(sub == SUB - 1, north_flag, 1.0)

    def level(k, pivots):
        chunk, q = k // per_chunk, k % per_chunk
        has_up = (k < levels - 1).astype(jnp.float32)
        new, edge = [], None
        for h in range(halves):
            blk = pl.ds(pl.multiple_of(k * rows + h * SUB, SUB), SUB)
            down, factor = pivots[h]
            up = m_buf[blk, :] * has_up
            inv = 1.0 / (1.0 + up + down - down * factor)
            factor = up * inv
            new.append((up, factor))
            e, n = e_buf[blk, :], n_buf[blk, :]
            side = pltpu.roll(west0[chunk, pl.ds(plane + h * SUB, SUB), :], LANES - 1 - 2 * q, 1)
            w_in = jnp.minimum(jnp.where(lane == 0, side, pltpu.roll(e, 1, 1)), 0.0)
            if h == 0:
                row = pl.ds(levels * tracers + k, 1)
                edge = jnp.where(even, b0[row, :], a0[row, :]) * south_flag
            s_in = jnp.minimum(jnp.where(sub == 0, edge, pltpu.roll(n, 1, 0)), 0.0)
            edge = n[SUB - 1 : SUB, :]
            e_out, n_out = jnp.maximum(e, 0.0), jnp.maximum(n, 0.0)
            from_n = n_out * inv
            if h == halves - 1:
                from_n = from_n * north_mask
            stay = (1.0 - e_out + w_in - n_out + s_in) * inv
            from_e, from_w = e_out * inv, -(w_in * inv)
            from_rim = jnp.where(lane == 0, from_w, jnp.where(lane == LANES - 1, from_e, 0.0))
            from_e = jnp.where(lane == LANES - 1, 0.0, from_e)
            from_w = jnp.where(lane == 0, 0.0, from_w)
            values = (stay, from_e, from_w, from_n, -(s_in * inv), from_rim, down * inv, factor)
            for i, value in enumerate(values):
                weights[i, blk, :] = value
        return tuple(new)

    def body(b, carry):
        for u in range(unroll):
            carry = level(b * unroll + u, carry)
        return carry

    zero = jnp.zeros((SUB, LANES), jnp.float32)
    lax.fori_loop(0, levels // unroll, body, ((zero, zero),) * halves)


def step(levels, tracers, rows, chunks, per_chunk, unroll, first, *refs):
    if first:
        field_in, weights, rim, edges, forcing, f_west, f_east, f_a, f_b = refs[:9]
        solved_ref, side_ref, a_ref, b_ref, rim_now, f_rim, f_edges, sems = refs[9:]
        field = solved_ref
    else:
        field, weights, west_in, east_in, a_in, b_in, out = refs[:7]
        solved_ref, rim_now, rim, edges, sems = refs[7:]

    plane = tracers * rows
    halves = rows // SUB
    lane, sub = lane_iota(), sub_iota()
    blocks = levels // unroll
    above = weights.at[weights.shape[0] - 1]

    def load(b):
        at = pl.ds(pl.multiple_of(b * unroll * plane, SUB), unroll * plane)
        return pltpu.make_async_copy(field_in.at[at], field.at[at], sems.at[b])

    def store(b):
        at = pl.ds(pl.multiple_of(b * unroll * plane, SUB), unroll * plane)
        return pltpu.make_async_copy(solved_ref.at[at], out.at[at], sems.at[b])

    if first:
        for b in range(blocks):
            load(b).start()
        meet(f_rim, 0, f_west, f_east, rows)
        pair(f_edges, 0, f_a, f_b, levels)
    else:
        meet(rim, 0, west_in, east_in, plane)
        pair(edges, 0, a_in, b_in, levels * tracers)

    def stencil(cells, here, side, edge, row, co):
        halfs = [cells[pl.ds(here + h * SUB, SUB), :] for h in range(halves)]
        ups = [pltpu.roll(half, SUB - 1, 0) for half in halfs] + [edge[0, pl.ds(row, 1), :]]
        downs = [edge[1, pl.ds(row, 1), :]] + [pltpu.roll(half, 1, 0) for half in halfs]
        values = []
        for h, cell in enumerate(halfs):
            n = jnp.where(sub == SUB - 1, ups[h + 1], ups[h])
            s = jnp.where(sub == 0, downs[h], downs[h + 1])
            c0, ce, cw, cn, cs, rims = co[h][:6]
            value = (c0 * cell + ce * pltpu.roll(cell, LANES - 1, 1)) + (cw * pltpu.roll(cell, 1, 1) + cn * n)
            values.append(value + (cs * s + rims * side(h)))
        return values

    def part(ref, b, size, offset=0):
        return ref.at[pl.ds(pl.multiple_of(b * unroll * size + offset, SUB), unroll * size)]

    def forward_block(b, solved):
        if first:
            load(b).wait()

        chunk, q = b * unroll // per_chunk, b * unroll % per_chunk
        turn = (LANES - 2 * q) % LANES
        for r in range(0, plane, SUB):
            rim_now[pl.ds(r, SUB), :] = pltpu.roll(rim[chunk, pl.ds(r, SUB), :], turn, 1)
        if first:
            for r in range(0, rows, SUB):
                rim_now[pl.ds(plane + r, SUB), :] = pltpu.roll(f_rim[chunk, pl.ds(r, SUB), :], turn, 1)

        def side(u, r):
            return lambda h: pltpu.roll(rim_now[pl.ds(r + h * SUB, SUB), :], LANES - 1 - 2 * u, 1)

        cells, solves = part(field, b, plane), part(solved_ref, b, plane)
        edge = edges.at[:, pl.ds(pl.multiple_of(b * unroll * tracers, SUB), unroll * tracers)]
        co_part = weights.at[:, pl.ds(pl.multiple_of(b * unroll * rows, SUB), unroll * rows)]
        if first:
            f_cells = part(forcing, b, rows, SUB)
            f_edge = f_edges.at[:, pl.ds(pl.multiple_of(b * unroll, SUB), unroll)]
        for u in range(unroll):
            co = [
                [co_part[i, pl.ds(u * rows + h * SUB, SUB), :] for i in range(weights.shape[0] - 1)]
                for h in range(halves)
            ]
            if first:
                extra = stencil(f_cells, u * rows, side(u, plane), f_edge, u, co)
            new = []
            for t in range(tracers):
                here = u * plane + t * rows
                values = stencil(cells, here, side(u, t * rows), edge, u * tracers + t, co)
                for h in range(halves):
                    value = values[h] + extra[h] if first else values[h]
                    value = value + co[h][6] * solved[t * halves + h]
                    new.append(value)
                    solves[pl.ds(here + h * SUB, SUB), :] = value
            solved = tuple(new)
        return solved

    zero = jnp.zeros((SUB, LANES), jnp.float32)
    zeros = (zero,) * (tracers * halves)
    lax.fori_loop(0, blocks, forward_block, zeros)

    def backward_block(i, later):
        b = blocks - 1 - i
        cells = part(solved_ref, b, plane)
        factors = part(above, b, rows)
        for u in reversed(range(unroll)):
            new = []
            for h in range(halves):
                factor = factors[pl.ds(u * rows + h * SUB, SUB), :]
                for t in range(tracers):
                    blk = pl.ds(u * plane + t * rows + h * SUB, SUB)
                    value = cells[blk, :] + factor * later[h * tracers + t]
                    cells[blk, :] = value
                    new.append(value)
            later = tuple(new)
        if not first:
            store(b).start()
        return later

    lax.fori_loop(0, blocks, backward_block, zeros)
    if first:
        for chunk in range(chunks):
            put_rims(solved_ref, 0, levels, per_chunk, chunk, side_ref, 0, plane)
        put_rows(solved_ref, 0, a_ref, b_ref, rows, 0, levels * tracers)
    else:
        for b in range(blocks):
            store(b).wait()


def row_offsets(count):
    return list(range(0, count - SUB, SUB)) + [count - SUB]


def pack(levels, group_rows, cap, kernel, columns, observed, errors, out, k_buf, c_buf, o_buf, e_buf, wide, out_buf, sems):
    lane = lane_iota()
    copies = [
        pltpu.make_async_copy(source, target, sems.at[i])
        for i, (source, target) in enumerate(
            ((columns, c_buf), (observed, o_buf), (errors, e_buf), (kernel, k_buf))
        )
    ]
    for copy in copies:
        copy.start()
    for copy in copies:
        copy.wait()
    per_level = columns.shape[0]
    groups = LANES // cap
    offsets = row_offsets(group_rows)
    padded = wide.shape[1] // groups
    together = wide.shape[0]

    def body(start, carry):
        for n in range(together):
            i = start * together + n
            one = pl.ds(i, 1)
            for g in range(groups):
                begin = g * group_rows
                count = min(group_rows, levels - begin)
                wide[n, pl.ds(g * padded, count), :] = k_buf[
                    pl.ds(i + per_level * begin, count, stride=per_level), :
                ]
            end = (groups - 1) * padded + levels - (groups - 1) * group_rows
            for m, row in enumerate((c_buf[one, :].astype(jnp.float32), o_buf[one, :], e_buf[one, :])):
                wide[n, pl.ds(end + m, 1), :] = row
            for m in range(end + 3, (groups - 1) * padded + group_rows):
                wide[n, pl.ds(m, 1), :] = jnp.zeros((1, LANES), jnp.float32)
        for n in range(together):
            i = start * together + n
            for j in range(groups):
                for m in offsets:
                    made = None
                    for g in range(groups):
                        piece = wide[n, pl.ds(g * padded + m, SUB), :]
                        if g != j:
                            piece = pltpu.roll(piece, (g - j) * cap % LANES, 1)
                        made = piece if made is None else jnp.where(lane >= g * cap, piece, made)
                    out_buf[pl.ds((i * groups + j) * group_rows + m, SUB), :] = made
        return carry

    if per_level == together:
        body(0, 0)
    else:
        lax.fori_loop(0, per_level // together, body, 0)
    done = pltpu.make_async_copy(out_buf, out, sems.at[4])
    done.start()
    done.wait()


def tracer_sum(block, concentration, out, buf, sems):
    levels, tracers, rows, cols = buf.shape

    def load(b):
        return pltpu.make_async_copy(
            concentration.at[pl.ds(b * block, block)], buf.at[pl.ds(b * block, block)], sems.at[b]
        )

    for b in range(levels // block):
        load(b).start()

    def body(b, carry):
        load(b).wait()
        for h in range(rows // SUB):
            tops, rests = [], []
            for k in range(block):
                part = jnp.sum(buf[b * block + k, :, pl.ds(h * SUB, SUB), :], axis=0)
                top = part.astype(jnp.bfloat16).astype(jnp.float32)
                tops.append(top)
                rests.append(part - top)
            at = pl.ds(pl.multiple_of(b * block * SUB, block * SUB), block * SUB)
            lanes = pl.ds(h * cols, cols)
            out[0, at, lanes] = jnp.concatenate(tops, axis=0).astype(jnp.bfloat16)
            out[1, at, lanes] = jnp.concatenate(rests, axis=0).astype(jnp.bfloat16)
        return carry

    lax.fori_loop(0, levels // block, body, 0)


def soundings(
    levels, rows, group_rows, cap, chunks, per_chunk, block,
    received, sums, forcing, side_ref, a_ref, b_ref, back_out, arrived, table, scaled, back, sem
):
    lane = lane_iota()
    parts, _, width = arrived.shape
    halves = rows // SUB
    keys = halves * LANES
    groups = LANES // cap

    def unpack(c, carry):
        part, col = c // (width // LANES), c % (width // LANES)
        for g in range(groups):
            for m in row_offsets(group_rows):
                made = None
                for p in range(groups):
                    piece = received[pl.ds((c * groups + p) * group_rows + m, SUB), :]
                    if p != g:
                        piece = pltpu.roll(piece, (p - g) * cap % LANES, 1)
                    made = piece if made is None else jnp.where(lane >= p * cap, piece, made)
                lanes = pl.ds(pl.multiple_of(col * LANES, LANES), LANES)
                arrived[part, pl.ds(g * group_rows + m, SUB), lanes] = made
        return carry

    lax.fori_loop(0, parts * width // LANES, unpack, 0)

    sub_index = lax.broadcasted_iota(jnp.int32, (SUB, width), 0)
    key_index = lax.broadcasted_iota(jnp.int32, (keys, width), 0)
    turned_index = lax.broadcasted_iota(jnp.int32, (LANES, keys), 1)

    def columns(j):
        return arrived[j, pl.ds(levels, 1), :].astype(jnp.int32)

    def key_of(col):
        return (col >> 10) * LANES + (col & (LANES - 1))

    def mask_of(j):
        return sub_index == ((columns(j) >> 7) & (SUB - 1))

    for j in range(parts):
        col = columns(j)
        key = key_of(col)
        look = jnp.where(key_index == key, 1.0, 0.0).astype(jnp.bfloat16)
        for c in range(width // LANES):
            piece = key[:, c * LANES : (c + 1) * LANES].astype(jnp.float32)
            across = jnp.broadcast_to(piece, (LANES, LANES)).T.astype(jnp.int32)
            across = jnp.concatenate([across] * halves, axis=1)
            table[j, pl.ds(c * LANES, LANES), :] = jnp.where(turned_index == across, 1.0, 0.0).astype(
                jnp.bfloat16
            )
        total = jnp.zeros((SUB, width), jnp.float32)
        for b in range(levels // block):
            blk = pl.ds(b * block * SUB, block * SUB)
            seen = jnp.dot(sums[0, blk, :], look, preferred_element_type=jnp.float32)
            seen += jnp.dot(sums[1, blk, :], look, preferred_element_type=jnp.float32)
            weight = arrived[j, pl.ds(b * block, block), :]
            for k in range(block):
                total += weight[k : k + 1, :] * seen[k * SUB : (k + 1) * SUB, :]
        modelled = jnp.sum(jnp.where(mask_of(j), total, 0.0), axis=0, keepdims=True)
        observed = arrived[j, pl.ds(levels + 1, 1), :]
        error = arrived[j, pl.ds(levels + 2, 1), :]
        residual = jnp.where(col >= 0, (modelled - observed) / error, 0.0)
        scaled[pl.ds(j, 1), :] = residual / error
        for i in range(width // cap):
            at = i * cap
            piece = residual[:, at // LANES * LANES : at // LANES * LANES + LANES]
            if at % LANES:
                piece = pltpu.roll(piece, LANES - at % LANES, 1)
            back[pl.ds(j * (width // cap) + i, 1), :] = piece

    leave = pltpu.make_async_copy(back, back_out, sem.at[0])
    leave.start()
    zeros = jnp.zeros((SUB, LANES), jnp.float32)
    forcing[pl.ds(0, SUB), :] = zeros
    forcing[pl.ds(levels * rows + SUB, SUB), :] = zeros
    for b in range(levels // block):
        total = jnp.zeros((block * SUB, keys), jnp.float32)
        for j in range(parts):
            weight = arrived[j, pl.ds(b * block, block), :] * scaled[pl.ds(j, 1), :]
            top = weight.astype(jnp.bfloat16).astype(jnp.float32)
            mask = mask_of(j)
            for part in (top, weight - top):
                spread = jnp.concatenate(
                    [jnp.where(mask, part[k : k + 1, :], 0.0) for k in range(block)], axis=0
                ).astype(jnp.bfloat16)
                total += jnp.dot(spread, table[j, :, :], preferred_element_type=jnp.float32)
        for k in range(block):
            for h in range(halves):
                forcing[pl.ds((b * block + k) * rows + (h + 1) * SUB, SUB), :] = total[
                    k * SUB : (k + 1) * SUB, h * LANES : (h + 1) * LANES
                ]

    for chunk in range(chunks):
        put_rims(forcing, SUB, levels, per_chunk, chunk, side_ref, 0, rows)
    put_rows(forcing, SUB, a_ref, b_ref, rows, 0, levels)
    leave.wait()


def unpack_residual(cap, arrived, out):
    lane = lax.broadcasted_iota(jnp.int32, (1, LANES), 1)
    groups = LANES // cap
    for row in range(out.shape[0]):
        made = None
        for g in range(groups):
            piece = arrived[pl.ds(row * groups + g, 1), :]
            if g:
                piece = pltpu.roll(piece, g * cap, 1)
            made = piece if made is None else jnp.where(lane >= g * cap, piece, made)
        out[pl.ds(row, 1), :] = made


def exchange(side_rim, a_rim, b_rim):
    lons, lats = lax.axis_size("lon"), lax.axis_size("lat")

    def partner(j, odd):
        other = j + 1 if j % 2 == odd else j - 1
        return other if 0 <= other < lats else j

    return (
        lax.ppermute(side_rim, "lon", [(i, (i + 1) % lons) for i in range(lons)]),
        lax.ppermute(side_rim, "lon", [((i + 1) % lons, i) for i in range(lons)]),
        lax.ppermute(a_rim, "lat", [(j, partner(j, 0)) for j in range(lats)]),
        lax.ppermute(b_rim, "lat", [(j, partner(j, 1)) for j in range(lats)]),
    )


def per_device(
    concentration, adjoint, wind_east, wind_north, mixing, sound_col, kernel, observed, obs_error
):
    levels, tracers, rows, cols = adjoint.shape
    bricks = lax.axis_size("lon") * lax.axis_size("lat")
    slots = sound_col.shape[2]
    cap = slots // bricks
    unroll = largest(levels, 8, 4, 3, 2, 1)
    chunks, per_chunk = rim_chunks(levels, unroll)
    plane = tracers * rows
    per_level = slots // LANES
    groups = LANES // cap
    group_rows = -(-(levels + 3) // groups)
    padded_rows = -(-group_rows // SUB) * SUB
    field_bytes = levels * plane * cols * 4
    dma = pltpu.SemaphoreType.DMA

    def flat(x):
        return x.reshape(-1, LANES)

    packed = call(
        functools.partial(pack, levels, group_rows, cap),
        [HBM] * 4, f32(bricks * group_rows, LANES), HBM,
        (
            vmem(levels * per_level, LANES), pltpu.VMEM((per_level, LANES), jnp.int32),
            vmem(per_level, LANES), vmem(per_level, LANES),
            vmem(largest(per_level, 8, 4, 2, 1), groups * padded_rows, LANES),
            vmem(bricks * group_rows, LANES), dma((5,)),
        ),
        4, 10, 800000, "pack",
    )(*(in_hbm(flat(x)) for x in (kernel, sound_col, observed, obs_error)))
    received = lax.all_to_all(
        packed.reshape(-1, 1, LANES), ("lon", "lat"), split_axis=0, concat_axis=0, tiled=True
    ).reshape(-1, LANES)

    east, north, mix = (in_hbm(flat(x)) for x in (wind_east, wind_north, mixing))
    rims = call(
        functools.partial(first_rims, levels, tracers, rows, chunks, per_chunk),
        [HBM] * 3,
        (f32(chunks, plane + rows, LANES),) + (f32(levels * tracers + levels, LANES),) * 2,
        (VMEM,) * 3,
        (vmem(levels * plane, LANES), vmem(levels * rows, LANES), vmem(levels * rows, LANES), dma((chunks + 2,))),
        10, field_bytes, 2 * field_bytes, "first_rims",
    )(in_hbm(flat(adjoint)), east, north)
    start_rims = exchange(*rims)

    block = largest(levels, 24, 16, 8)
    sum_block = largest(levels, 12, 8)
    sums = call(
        functools.partial(tracer_sum, sum_block),
        [HBM], jax.ShapeDtypeStruct((2, levels * SUB, rows // SUB * cols), jnp.bfloat16), VMEM,
        (vmem(levels, tracers, rows, cols), dma((levels // sum_block,))),
        10, field_bytes // 4, field_bytes, "tracer_sum",
    )(concentration)

    width = largest(slots, 2 * LANES, LANES)
    parts = slots // width
    forcing, *rims, back = call(
        functools.partial(soundings, levels, rows, group_rows, cap, chunks, per_chunk, block),
        [VMEM] * 2,
        (
            f32(levels * rows + 2 * SUB, LANES), f32(chunks, rows, LANES), f32(levels, LANES), f32(levels, LANES),
            hbm(bricks, LANES),
        ),
        (VMEM,) * 4 + (HBM,),
        (
            vmem(parts, -(-groups * group_rows // SUB) * SUB, width),
            pltpu.VMEM((parts, width, rows // SUB * LANES), jnp.bfloat16),
            vmem(max(parts, SUB), width), vmem(bricks, LANES), dma((1,)),
        ),
        10, field_bytes * 8, field_bytes, "soundings",
    )(received, sums)
    forcing_rims = exchange(*rims)

    rim_shape, edge_shape = (chunks, plane, LANES), (2, levels * tracers, LANES)
    weight_shape = (8, levels * rows, LANES)
    weights, rim0, edges0 = call(
        functools.partial(coefficients, levels, tracers, rows, per_chunk, unroll),
        [HBM] * 3 + [VMEM] * 4,
        (f32(*weight_shape), f32(*rim_shape), f32(*edge_shape)),
        (VMEM,) * 3,
        (vmem(levels * rows, LANES),) * 3 + (dma((3,)),),
        4, field_bytes, 8 * field_bytes, "coefficients",
    )(east, north, mix, *start_rims)

    def advance(first, specs, operands, outs, out_specs, scratch):
        return call(
            functools.partial(step, levels, tracers, rows, chunks, per_chunk, unroll, first),
            specs, outs, out_specs, scratch + (dma((levels // unroll,)),), 10, 1, 1, "step",
        )(*operands)

    edge_rows, whole = f32(levels * tracers, LANES), (levels * plane, LANES)
    stepped, *rims = advance(
        True, [HBM] + [VMEM] * 8, (in_hbm(flat(adjoint)), weights, rim0, edges0, forcing, *forcing_rims),
        (f32(*whole), f32(*rim_shape), edge_rows, edge_rows), (VMEM,) * 4,
        (vmem(plane + rows, LANES), vmem(chunks, rows, LANES), vmem(2, levels, LANES)),
    )
    (result,) = advance(
        False, [VMEM] * 6, (stepped, weights, *exchange(*rims)), (f32(*whole),), (HBM,),
        (vmem(*whole), vmem(plane, LANES), vmem(*rim_shape), vmem(*edge_shape)),
    )

    returned = lax.all_to_all(
        back.reshape(bricks, 1, LANES), ("lon", "lat"), split_axis=0, concat_axis=0, tiled=True
    )
    result, returned = lax.optimization_barrier((result, returned))
    residual = call(
        functools.partial(unpack_residual, cap), [VMEM], f32(per_level, LANES), VMEM, (), 2, 10, 10000, "residual",
    )(returned.reshape(bricks, LANES))
    return result.reshape(adjoint.shape), residual.reshape(sound_col.shape)


def solution(mesh):
    field = P(None, None, "lat", "lon")
    face = P(None, "lat", "lon")
    owned = P(None, ("lon", "lat"), None)
    return jax.shard_map(
        per_device,
        mesh=mesh,
        in_specs=(field, field, face, face, face, owned, owned, owned, owned),
        out_specs=(field, owned),
        check_vma=False,
    )
```

```python
import functools

import jax
import jax.numpy as jnp
from jax import lax
from jax.experimental import pallas as pl
from jax.experimental.pallas import tpu as pltpu
from jax.sharding import PartitionSpec as P

LANES = 128
SUB = 8
MIB = 1 << 20
ANY = pl.BlockSpec(memory_space=pl.ANY)
HBM = pl.BlockSpec(memory_space=pltpu.HBM)
VMEM = pl.BlockSpec(memory_space=pltpu.VMEM)


def rim_chunks(levels, unroll):
    per_chunk = 63 // unroll * unroll
    chunks = -(-levels // per_chunk)
    return chunks, -(-levels // (chunks * unroll)) * unroll


def lane_iota():
    return lax.broadcasted_iota(jnp.int32, (SUB, LANES), 1)


def sub_iota():
    return lax.broadcasted_iota(jnp.int32, (SUB, LANES), 0)


def largest(count, *choices):
    return next(u for u in choices if count % u == 0)


def in_hbm(x):
    return pltpu.with_memory_space_constraint(x, pltpu.HBM)


def hbm(*shape):
    return pltpu.HBM(shape, jnp.float32)


def f32(*shape):
    return jax.ShapeDtypeStruct(shape, jnp.float32)


def vmem(*shape):
    return pltpu.VMEM(shape, jnp.float32)


def call(body, ins, outs, out_specs, scratch, mib, flops, size, name):
    return pl.pallas_call(
        body,
        in_specs=ins,
        out_specs=out_specs,
        out_shape=outs,
        scratch_shapes=scratch,
        compiler_params=pltpu.CompilerParams(vmem_limit_bytes=mib * MIB),
        cost_estimate=pl.CostEstimate(flops=flops, bytes_accessed=size, transcendentals=0),
        name=name,
    )


def put_rims(field, offset, levels, per_chunk, chunk, out, first, plane):
    lane = lane_iota()
    group = largest(plane // SUB, 4, 2, 1)
    count = min(per_chunk, levels - chunk * per_chunk)

    def body(i, carry):
        r = pl.multiple_of(i * SUB * group, SUB * group)
        made = [jnp.zeros((SUB, LANES), jnp.float32)] * group
        for q in range(count):
            for g in range(group):
                at = pl.multiple_of((chunk * per_chunk + q) * plane + offset + r + g * SUB, SUB)
                turned = pltpu.roll(field[pl.ds(at, SUB), :], 2 * q + 2, 1)
                made[g] = jnp.where(lane >= 2 * q + 1, turned, made[g])
        for g in range(group):
            out[chunk, pl.ds(pl.multiple_of(first + r + g * SUB, SUB), SUB), :] = made[g]
        return carry

    lax.fori_loop(0, plane // SUB // group, body, 0)


def row_places(rows):
    odd = lax.axis_index("lat") % 2
    return (1 - odd) * (rows - 1), odd * (rows - 1)


def put_rows(field, offset, a_ref, b_ref, rows, begin, end):
    unroll = largest((end - begin) // SUB, 9, 8, 4, 2, 1)
    in_a, in_b = row_places(rows)

    def body(i, carry):
        for u in range(unroll):
            start = pl.multiple_of(begin + (i * unroll + u) * SUB, SUB)
            at = start * rows + offset
            a_ref[pl.ds(start, SUB), :] = field[pl.ds(at + in_a, SUB, stride=rows), :]
            b_ref[pl.ds(start, SUB), :] = field[pl.ds(at + in_b, SUB, stride=rows), :]
        return carry

    lax.fori_loop(0, (end - begin) // SUB // unroll, body, 0)


def first_rims(levels, tracers, rows, chunks, per_chunk, field, east, north, side, a_ref, b_ref, f, e, n, sems):
    plane = tracers * rows
    wind_copies = [
        pltpu.make_async_copy(east, e, sems.at[chunks]),
        pltpu.make_async_copy(north, n, sems.at[chunks + 1]),
    ]
    copies = []
    for i in range(chunks):
        part = pl.ds(i * per_chunk * plane, min(per_chunk, levels - i * per_chunk) * plane)
        copies.append(pltpu.make_async_copy(field.at[part], f.at[part], sems.at[i]))
    for copy in wind_copies + copies:
        copy.start()
    wind_copies[0].wait()
    for i in range(chunks):
        put_rims(e, 0, levels, per_chunk, i, side, plane, rows)
    wind_copies[1].wait()
    winds = pl.ds(levels * tracers, levels)
    put_rows(n, 0, a_ref.at[winds], b_ref.at[winds], rows, 0, levels)
    for i in range(chunks):
        copies[i].wait()
        put_rims(f, 0, levels, per_chunk, i, side, 0, plane)
        put_rows(
            f, 0, a_ref, b_ref, rows, i * per_chunk * tracers, min((i + 1) * per_chunk, levels) * tracers
        )


def meet(rim, target, from_west, from_east, count):
    lane = lane_iota()
    for chunk in range(rim.shape[0]):
        for r in range(0, count, SUB):
            rows = pl.ds(r, SUB)
            turned = pltpu.roll(from_east[chunk, rows, :], LANES - 2, 1)
            rim[chunk, pl.ds(target + r, SUB), :] = jnp.where(lane % 2 == 1, from_west[chunk, rows, :], turned)


def pair(edges, target, from_a, from_b, count):
    even = jnp.full((SUB, LANES), lax.axis_index("lat"), jnp.int32) % 2 == 0
    repeat = largest(count // SUB, 9, 8, 4, 2, 1)

    def body(i, carry):
        for u in range(repeat):
            at = pl.multiple_of((i * repeat + u) * SUB, SUB)
            a, b = from_a[pl.ds(at, SUB), :], from_b[pl.ds(at, SUB), :]
            edges[0, pl.ds(target + at, SUB), :] = jnp.where(even, a, b)
            edges[1, pl.ds(target + at, SUB), :] = jnp.where(even, b, a)
        return carry

    lax.fori_loop(0, count // SUB // repeat, body, 0)


def coefficients(
    levels, tracers, rows, per_chunk, unroll, east, north, mixing, west0, east0, a0, b0, *refs
):
    weights, rim, edges, e_buf, n_buf, m_buf, sems = refs
    plane = tracers * rows
    halves = rows // SUB
    lane, sub = lane_iota(), sub_iota()
    copies = [
        pltpu.make_async_copy(source, target, sems.at[i])
        for i, (source, target) in enumerate(((east, e_buf), (north, n_buf), (mixing, m_buf)))
    ]
    for copy in copies:
        copy.start()
    meet(rim, 0, west0, east0, plane)
    pair(edges, 0, a0, b0, levels * tracers)
    for copy in copies:
        copy.wait()
    place = lax.axis_index("lat")
    even = jnp.full((1, LANES), place, jnp.int32) % 2 == 0
    south_flag = (place > 0).astype(jnp.float32)
    north_flag = (place < lax.axis_size("lat") - 1).astype(jnp.float32)
    north_mask = jnp.where(sub == SUB - 1, north_flag, 1.0)

    def level(k, pivots):
        chunk, q = k // per_chunk, k % per_chunk
        has_up = (k < levels - 1).astype(jnp.float32)
        new, edge = [], None
        for h in range(halves):
            blk = pl.ds(pl.multiple_of(k * rows + h * SUB, SUB), SUB)
            down, factor = pivots[h]
            up = m_buf[blk, :] * has_up
            inv = 1.0 / (1.0 + up + down - down * factor)
            factor = up * inv
            new.append((up, factor))
            e, n = e_buf[blk, :], n_buf[blk, :]
            side = pltpu.roll(west0[chunk, pl.ds(plane + h * SUB, SUB), :], LANES - 1 - 2 * q, 1)
            w_in = jnp.minimum(jnp.where(lane == 0, side, pltpu.roll(e, 1, 1)), 0.0)
            if h == 0:
                row = pl.ds(levels * tracers + k, 1)
                edge = jnp.where(even, b0[row, :], a0[row, :]) * south_flag
            s_in = jnp.minimum(jnp.where(sub == 0, edge, pltpu.roll(n, 1, 0)), 0.0)
            edge = n[SUB - 1 : SUB, :]
            e_out, n_out = jnp.maximum(e, 0.0), jnp.maximum(n, 0.0)
            from_n = n_out * inv
            if h == halves - 1:
                from_n = from_n * north_mask
            stay = (1.0 - e_out + w_in - n_out + s_in) * inv
            from_e, from_w = e_out * inv, -(w_in * inv)
            from_rim = jnp.where(lane == 0, from_w, jnp.where(lane == LANES - 1, from_e, 0.0))
            from_e = jnp.where(lane == LANES - 1, 0.0, from_e)
            from_w = jnp.where(lane == 0, 0.0, from_w)
            values = (stay, from_e, from_w, from_n, -(s_in * inv), from_rim, down * inv, factor)
            for i, value in enumerate(values):
                weights[i, blk, :] = value
        return tuple(new)

    def body(b, carry):
        for u in range(unroll):
            carry = level(b * unroll + u, carry)
        return carry

    zero = jnp.zeros((SUB, LANES), jnp.float32)
    lax.fori_loop(0, levels // unroll, body, ((zero, zero),) * halves)


def step(levels, tracers, rows, chunks, per_chunk, unroll, first, *refs):
    if first:
        field, weights, rim, edges, forcing, f_west, f_east, f_a, f_b = refs[:9]
        out, weights_out, side_ref, a_ref, b_ref = refs[9:14]
        buf, rim_now, f_rim, f_edges, f_part, sems = refs[14:]
    else:
        field, weights_in, west_in, east_in, a_in, b_in, out = refs[:7]
        buf, rim_now, weights, rim, edges, sems = refs[7:]

    plane = tracers * rows
    halves = rows // SUB
    lane, sub = lane_iota(), sub_iota()
    blocks = levels // unroll
    flat = buf.reshape((levels * tracers + 2) * rows, LANES)

    def load(b):
        at = b * unroll * tracers
        return pltpu.make_async_copy(
            field.at[pl.ds(at, unroll * tracers)], buf.at[pl.ds(at + 1, unroll * tracers)], sems.at[b]
        )

    def store(b):
        at = b * unroll * tracers
        return pltpu.make_async_copy(
            buf.at[pl.ds(at + 1, unroll * tracers)], out.at[pl.ds(at, unroll * tracers)], sems.at[b]
        )

    last = 2 * blocks
    above = weights.at[weights.shape[0] - 1]
    if first:
        keep = pltpu.make_async_copy(weights, weights_out, sems.at[last])
        for b in range(blocks):
            load(b).start()
        keep.start()
        meet(f_rim, 0, f_west, f_east, rows)
        pair(f_edges, 0, f_a, f_b, levels)
    else:
        above_copy = pltpu.make_async_copy(weights_in.at[weights.shape[0] - 1], above, sems.at[last])
        def load_weights(b):
            planes, levels_of = pl.ds(0, weights.shape[0] - 1), pl.ds(b * unroll * rows, unroll * rows)
            return pltpu.make_async_copy(
                weights_in.at[planes, levels_of], weights.at[planes, levels_of], sems.at[blocks + b]
            )

        for b in range(blocks):
            load(b).start()
            load_weights(b).start()
        above_copy.start()
        meet(rim, 0, west_in, east_in, plane)
        pair(edges, 0, a_in, b_in, levels * tracers)

    def stencil(cells, here, side, edge, row, co):
        halfs = [cells[pl.ds(here + h * SUB, SUB), :] for h in range(halves)]
        ups = [pltpu.roll(half, SUB - 1, 0) for half in halfs] + [edge[0, pl.ds(row, 1), :]]
        downs = [edge[1, pl.ds(row, 1), :]] + [pltpu.roll(half, 1, 0) for half in halfs]
        values = []
        for h, cell in enumerate(halfs):
            n = jnp.where(sub == SUB - 1, ups[h + 1], ups[h])
            s = jnp.where(sub == 0, downs[h], downs[h + 1])
            c0, ce, cw, cn, cs, rims = co[h][:6]
            value = (c0 * cell + ce * pltpu.roll(cell, LANES - 1, 1)) + (cw * pltpu.roll(cell, 1, 1) + cn * n)
            values.append(value + (cs * s + rims * side(h)))
        return values

    def part(ref, b, size, offset=0):
        return ref.at[pl.ds(pl.multiple_of(b * unroll * size + offset, SUB), unroll * size)]

    def turned_rims(b, source, count):
        chunk, q = b * unroll // per_chunk, b * unroll % per_chunk
        for r in range(0, count, SUB):
            rim_now[pl.ds(r, SUB), :] = pltpu.roll(source[chunk, pl.ds(r, SUB), :], (LANES - 2 * q) % LANES, 1)

    def side(u, r):
        return lambda h: pltpu.roll(rim_now[pl.ds(r + h * SUB, SUB), :], LANES - 1 - 2 * u, 1)

    def weights_of(b):
        co_part = weights.at[:, pl.ds(pl.multiple_of(b * unroll * rows, SUB), unroll * rows)]
        return lambda u: [
            [co_part[i, pl.ds(u * rows + h * SUB, SUB), :] for i in range(weights.shape[0] - 1)]
            for h in range(halves)
        ]

    def forcing_block(b, carry):
        turned_rims(b, f_rim, rows)
        cells, co, parts = part(forcing, b, rows, SUB), weights_of(b), part(f_part, b, rows)
        edge = f_edges.at[:, pl.ds(pl.multiple_of(b * unroll, SUB), unroll)]
        for u in range(unroll):
            values = stencil(cells, u * rows, side(u, 0), edge, u, co(u))
            for h in range(halves):
                parts[pl.ds(u * rows + h * SUB, SUB), :] = values[h]
        return carry

    if first:
        lax.fori_loop(0, blocks, forcing_block, 0)

    def forward_block(b, solved):
        load(b).wait()
        if not first:
            load_weights(b).wait()
        turned_rims(b, rim, plane)
        cells, co_of = part(flat, b, plane, rows), weights_of(b)
        edge = edges.at[:, pl.ds(pl.multiple_of(b * unroll * tracers, SUB), unroll * tracers)]
        if first:
            extra = part(f_part, b, rows)
        for u in range(unroll):
            co = co_of(u)
            new = []
            for t in range(tracers):
                here = u * plane + t * rows
                values = stencil(cells, here, side(u, t * rows), edge, u * tracers + t, co)
                for h in range(halves):
                    value = values[h]
                    if first:
                        value = value + extra[pl.ds(u * rows + h * SUB, SUB), :]
                    value = value + co[h][6] * solved[t * halves + h]
                    new.append(value)
                    cells[pl.ds(here + h * SUB, SUB), :] = value
            solved = tuple(new)
        return solved

    zero = jnp.zeros((SUB, LANES), jnp.float32)
    zeros = (zero,) * (tracers * halves)
    lax.fori_loop(0, blocks, forward_block, zeros)
    if not first:
        above_copy.wait()

    def rims_of(b):
        cells = part(flat, b, plane, rows)
        chunk, q = b * unroll // per_chunk, b * unroll % per_chunk
        for r in range(0, plane, SUB):
            made = jnp.zeros((SUB, LANES), jnp.float32)
            for u in range(unroll):
                turned = pltpu.roll(cells[pl.ds(u * plane + r, SUB), :], 2 * u + 2, 1)
                made = jnp.where(lane >= 2 * u + 1, turned, made)
            made = pltpu.roll(made, 2 * q, 1)
            side_ref[chunk, pl.ds(r, SUB), :] = jnp.where(
                lane <= 2 * (q + unroll), made, side_ref[chunk, pl.ds(r, SUB), :]
            )
        begin = b * unroll * tracers
        for m in range(0, unroll * tracers, SUB):
            for target, at in zip((a_ref, b_ref), row_places(rows)):
                target[pl.ds(pl.multiple_of(begin + m, SUB), SUB), :] = flat[
                    pl.ds((begin + m + 1) * rows + at, SUB, stride=rows), :
                ]

    def backward_block(i, later):
        b = blocks - 1 - i
        if first:
            rims_of(jnp.minimum(b + 1, blocks - 1))
        cells = part(flat, b, plane, rows)
        factors = part(above, b, rows)
        for u in reversed(range(unroll)):
            new = []
            for h in range(halves):
                factor = factors[pl.ds(u * rows + h * SUB, SUB), :]
                for t in range(tracers):
                    blk = pl.ds(u * plane + t * rows + h * SUB, SUB)
                    value = cells[blk, :] + factor * later[h * tracers + t]
                    cells[blk, :] = value
                    new.append(value)
            later = tuple(new)
        store(b).start()
        return later

    if first:
        side_ref[...] = jnp.zeros(side_ref.shape, jnp.float32)
    lax.fori_loop(0, blocks, backward_block, zeros)
    if first:
        rims_of(0)
        keep.wait()
    for b in range(blocks):
        store(b).wait()


def row_offsets(count):
    return list(range(0, count - SUB, SUB)) + [count - SUB]


def pack(levels, group_rows, cap, kernel, columns, observed, errors, out, k_buf, c_buf, o_buf, e_buf, wide, out_buf, sems):
    lane = lane_iota()
    copies = [
        pltpu.make_async_copy(source, target, sems.at[i])
        for i, (source, target) in enumerate(
            ((columns, c_buf), (observed, o_buf), (errors, e_buf), (kernel, k_buf))
        )
    ]
    for copy in copies:
        copy.start()
    for copy in copies:
        copy.wait()
    per_level = columns.shape[0]
    groups = LANES // cap
    offsets = row_offsets(group_rows)
    padded = wide.shape[1] // groups
    together = wide.shape[0]

    def body(start, carry):
        for n in range(together):
            i = start * together + n
            one = pl.ds(i, 1)
            for g in range(groups):
                begin = g * group_rows
                count = min(group_rows, levels - begin)
                wide[n, pl.ds(g * padded, count), :] = k_buf[
                    pl.ds(i + per_level * begin, count, stride=per_level), :
                ]
            end = (groups - 1) * padded + levels - (groups - 1) * group_rows
            for m, row in enumerate((c_buf[one, :].astype(jnp.float32), o_buf[one, :], e_buf[one, :])):
                wide[n, pl.ds(end + m, 1), :] = row
            for m in range(end + 3, (groups - 1) * padded + group_rows):
                wide[n, pl.ds(m, 1), :] = jnp.zeros((1, LANES), jnp.float32)
        for n in range(together):
            i = start * together + n
            for j in range(groups):
                for m in offsets:
                    made = None
                    for g in range(groups):
                        piece = wide[n, pl.ds(g * padded + m, SUB), :]
                        if g != j:
                            piece = pltpu.roll(piece, (g - j) * cap % LANES, 1)
                        made = piece if made is None else jnp.where(lane >= g * cap, piece, made)
                    out_buf[pl.ds((i * groups + j) * group_rows + m, SUB), :] = made
        return carry

    if per_level == together:
        body(0, 0)
    else:
        lax.fori_loop(0, per_level // together, body, 0)
    done = pltpu.make_async_copy(out_buf, out, sems.at[4])
    done.start()
    done.wait()


def tracer_sum(block, concentration, out, buf, sems):
    levels, tracers, rows, cols = buf.shape

    def load(b):
        return pltpu.make_async_copy(
            concentration.at[pl.ds(b * block, block)], buf.at[pl.ds(b * block, block)], sems.at[b]
        )

    for b in range(levels // block):
        load(b).start()

    def body(b, carry):
        load(b).wait()
        for h in range(rows // SUB):
            tops, rests = [], []
            for k in range(block):
                part = jnp.sum(buf[b * block + k, :, pl.ds(h * SUB, SUB), :], axis=0)
                top = part.astype(jnp.bfloat16).astype(jnp.float32)
                tops.append(top)
                rests.append(part - top)
            at = pl.ds(pl.multiple_of(b * block * SUB, block * SUB), block * SUB)
            lanes = pl.ds(h * cols, cols)
            out[0, at, lanes] = jnp.concatenate(tops, axis=0).astype(jnp.bfloat16)
            out[1, at, lanes] = jnp.concatenate(rests, axis=0).astype(jnp.bfloat16)
        return carry

    lax.fori_loop(0, levels // block, body, 0)


def soundings(
    levels, rows, group_rows, cap, chunks, per_chunk, block,
    received, sums, forcing, side_ref, a_ref, b_ref, back_out, arrived, table, scaled, back, sem
):
    lane = lane_iota()
    parts, _, width = arrived.shape
    halves = rows // SUB
    keys = halves * LANES
    groups = LANES // cap

    def unpack(c, carry):
        part, col = c // (width // LANES), c % (width // LANES)
        for g in range(groups):
            for m in row_offsets(group_rows):
                made = None
                for p in range(groups):
                    piece = received[pl.ds((c * groups + p) * group_rows + m, SUB), :]
                    if p != g:
                        piece = pltpu.roll(piece, (p - g) * cap % LANES, 1)
                    made = piece if made is None else jnp.where(lane >= p * cap, piece, made)
                lanes = pl.ds(pl.multiple_of(col * LANES, LANES), LANES)
                arrived[part, pl.ds(g * group_rows + m, SUB), lanes] = made
        return carry

    lax.fori_loop(0, parts * width // LANES, unpack, 0)

    sub_index = lax.broadcasted_iota(jnp.int32, (SUB, width), 0)
    key_index = lax.broadcasted_iota(jnp.int32, (keys, width), 0)
    turned_index = lax.broadcasted_iota(jnp.int32, (LANES, keys), 1)

    def columns(j):
        return arrived[j, pl.ds(levels, 1), :].astype(jnp.int32)

    def key_of(col):
        return (col >> 10) * LANES + (col & (LANES - 1))

    def mask_of(j):
        return sub_index == ((columns(j) >> 7) & (SUB - 1))

    for j in range(parts):
        col = columns(j)
        key = key_of(col)
        look = jnp.where(key_index == key, 1.0, 0.0).astype(jnp.bfloat16)
        for c in range(width // LANES):
            piece = key[:, c * LANES : (c + 1) * LANES].astype(jnp.float32)
            across = jnp.broadcast_to(piece, (LANES, LANES)).T.astype(jnp.int32)
            across = jnp.concatenate([across] * halves, axis=1)
            table[j, pl.ds(c * LANES, LANES), :] = jnp.where(turned_index == across, 1.0, 0.0).astype(
                jnp.bfloat16
            )
        total = jnp.zeros((SUB, width), jnp.float32)
        for b in range(levels // block):
            blk = pl.ds(b * block * SUB, block * SUB)
            seen = jnp.dot(sums[0, blk, :], look, preferred_element_type=jnp.float32)
            seen += jnp.dot(sums[1, blk, :], look, preferred_element_type=jnp.float32)
            weight = arrived[j, pl.ds(b * block, block), :]
            for k in range(block):
                total += weight[k : k + 1, :] * seen[k * SUB : (k + 1) * SUB, :]
        modelled = jnp.sum(jnp.where(mask_of(j), total, 0.0), axis=0, keepdims=True)
        observed = arrived[j, pl.ds(levels + 1, 1), :]
        error = arrived[j, pl.ds(levels + 2, 1), :]
        residual = jnp.where(col >= 0, (modelled - observed) / error, 0.0)
        scaled[pl.ds(j, 1), :] = residual / error
        for i in range(width // cap):
            at = i * cap
            piece = residual[:, at // LANES * LANES : at // LANES * LANES + LANES]
            if at % LANES:
                piece = pltpu.roll(piece, LANES - at % LANES, 1)
            back[pl.ds(j * (width // cap) + i, 1), :] = piece

    leave = pltpu.make_async_copy(back, back_out, sem.at[0])
    leave.start()
    zeros = jnp.zeros((SUB, LANES), jnp.float32)
    forcing[pl.ds(0, SUB), :] = zeros
    forcing[pl.ds(levels * rows + SUB, SUB), :] = zeros
    for b in range(levels // block):
        total = jnp.zeros((block * SUB, keys), jnp.float32)
        for j in range(parts):
            weight = arrived[j, pl.ds(b * block, block), :] * scaled[pl.ds(j, 1), :]
            top = weight.astype(jnp.bfloat16).astype(jnp.float32)
            mask = mask_of(j)
            for part in (top, weight - top):
                spread = jnp.concatenate(
                    [jnp.where(mask, part[k : k + 1, :], 0.0) for k in range(block)], axis=0
                ).astype(jnp.bfloat16)
                total += jnp.dot(spread, table[j, :, :], preferred_element_type=jnp.float32)
        for k in range(block):
            for h in range(halves):
                forcing[pl.ds((b * block + k) * rows + (h + 1) * SUB, SUB), :] = total[
                    k * SUB : (k + 1) * SUB, h * LANES : (h + 1) * LANES
                ]

    for chunk in range(chunks):
        put_rims(forcing, SUB, levels, per_chunk, chunk, side_ref, 0, rows)
    put_rows(forcing, SUB, a_ref, b_ref, rows, 0, levels)
    leave.wait()


def unpack_residual(cap, arrived, out):
    lane = lax.broadcasted_iota(jnp.int32, (1, LANES), 1)
    groups = LANES // cap
    for row in range(out.shape[0]):
        made = None
        for g in range(groups):
            piece = arrived[pl.ds(row * groups + g, 1), :]
            if g:
                piece = pltpu.roll(piece, g * cap, 1)
            made = piece if made is None else jnp.where(lane >= g * cap, piece, made)
        out[pl.ds(row, 1), :] = made


def exchange(side_rim, a_rim, b_rim):
    lons, lats = lax.axis_size("lon"), lax.axis_size("lat")

    def partner(j, odd):
        other = j + 1 if j % 2 == odd else j - 1
        return other if 0 <= other < lats else j

    return (
        lax.ppermute(side_rim, "lon", [(i, (i + 1) % lons) for i in range(lons)]),
        lax.ppermute(side_rim, "lon", [((i + 1) % lons, i) for i in range(lons)]),
        lax.ppermute(a_rim, "lat", [(j, partner(j, 0)) for j in range(lats)]),
        lax.ppermute(b_rim, "lat", [(j, partner(j, 1)) for j in range(lats)]),
    )


def per_device(
    concentration, adjoint, wind_east, wind_north, mixing, sound_col, kernel, observed, obs_error
):
    levels, tracers, rows, cols = adjoint.shape
    bricks = lax.axis_size("lon") * lax.axis_size("lat")
    slots = sound_col.shape[2]
    cap = slots // bricks
    unroll = largest(levels, 8, 4, 3, 2, 1)
    chunks, per_chunk = rim_chunks(levels, unroll)
    plane = tracers * rows
    per_level = slots // LANES
    groups = LANES // cap
    group_rows = -(-(levels + 3) // groups)
    padded_rows = -(-group_rows // SUB) * SUB
    field_bytes = levels * plane * cols * 4
    dma = pltpu.SemaphoreType.DMA

    def flat(x):
        return x.reshape(-1, LANES)

    packed = call(
        functools.partial(pack, levels, group_rows, cap),
        [HBM] * 4, f32(bricks * group_rows, LANES), HBM,
        (
            vmem(levels * per_level, LANES), pltpu.VMEM((per_level, LANES), jnp.int32),
            vmem(per_level, LANES), vmem(per_level, LANES),
            vmem(largest(per_level, 8, 4, 2, 1), groups * padded_rows, LANES),
            vmem(bricks * group_rows, LANES), dma((5,)),
        ),
        4, 10, 800000, "pack",
    )(*(in_hbm(flat(x)) for x in (kernel, sound_col, observed, obs_error)))
    received = lax.all_to_all(
        packed.reshape(-1, 1, LANES), ("lon", "lat"), split_axis=0, concat_axis=0, tiled=True
    ).reshape(-1, LANES)

    field = adjoint.reshape(levels * tracers, rows, LANES)
    east, north, mix = (in_hbm(flat(x)) for x in (wind_east, wind_north, mixing))
    rims = call(
        functools.partial(first_rims, levels, tracers, rows, chunks, per_chunk),
        [HBM] * 3,
        (f32(chunks, plane + rows, LANES),) + (f32(levels * tracers + levels, LANES),) * 2,
        (VMEM,) * 3,
        (vmem(levels * plane, LANES), vmem(levels * rows, LANES), vmem(levels * rows, LANES), dma((chunks + 2,))),
        10, field_bytes, 2 * field_bytes, "first_rims",
    )(in_hbm(flat(adjoint)), east, north)
    start_rims = exchange(*rims)

    block = largest(levels, 24, 16, 8)
    sum_block = largest(levels, 12, 8)
    sums = call(
        functools.partial(tracer_sum, sum_block),
        [HBM], jax.ShapeDtypeStruct((2, levels * SUB, rows // SUB * cols), jnp.bfloat16), VMEM,
        (vmem(levels, tracers, rows, cols), dma((levels // sum_block,))),
        10, field_bytes // 4, field_bytes, "tracer_sum",
    )(concentration)

    width = largest(slots, 2 * LANES, LANES)
    parts = slots // width
    forcing, *rims, back = call(
        functools.partial(soundings, levels, rows, group_rows, cap, chunks, per_chunk, block),
        [VMEM] * 2,
        (
            f32(levels * rows + 2 * SUB, LANES), f32(chunks, rows, LANES), f32(levels, LANES), f32(levels, LANES),
            hbm(bricks, LANES),
        ),
        (VMEM,) * 4 + (HBM,),
        (
            vmem(parts, -(-groups * group_rows // SUB) * SUB, width),
            pltpu.VMEM((parts, width, rows // SUB * LANES), jnp.bfloat16),
            vmem(max(parts, SUB), width), vmem(bricks, LANES), dma((1,)),
        ),
        10, field_bytes * 8, field_bytes, "soundings",
    )(received, sums)
    forcing_rims = exchange(*rims)

    rim_shape, edge_shape = (chunks, plane, LANES), (2, levels * tracers, LANES)
    weight_shape = (8, levels * rows, LANES)
    weights, rim0, edges0 = call(
        functools.partial(coefficients, levels, tracers, rows, per_chunk, unroll),
        [HBM] * 3 + [VMEM] * 4,
        (f32(*weight_shape), f32(*rim_shape), f32(*edge_shape)),
        (VMEM,) * 3,
        (vmem(levels * rows, LANES),) * 3 + (dma((3,)),),
        4, field_bytes, field_bytes, "coefficients",
    )(east, north, mix, *start_rims)

    def advance(first, together, specs, operands, outs, out_specs, scratch):
        return call(
            functools.partial(step, levels, tracers, rows, chunks, per_chunk, together, first),
            specs, outs, out_specs,
            (vmem(levels * tracers + 2, rows, LANES), vmem(plane + rows, LANES))
            + scratch + (dma((2 * (levels // together) + 5,)),),
            16, field_bytes * 8, field_bytes * 2, "step",
        )(*operands)

    edge_rows = f32(levels * tracers, LANES)
    stepped, kept, *rims = advance(
        True, unroll, [HBM] + [VMEM] * 8, (in_hbm(field), weights, rim0, edges0, forcing, *forcing_rims),
        (hbm(*field.shape), hbm(*weight_shape), f32(*rim_shape), edge_rows, edge_rows), (HBM,) * 2 + (VMEM,) * 3,
        (vmem(chunks, rows, LANES), vmem(2, levels, LANES), vmem(levels * rows, LANES)),
    )
    (result,) = advance(
        False, unroll, [HBM] * 2 + [VMEM] * 4, (in_hbm(stepped), in_hbm(kept), *exchange(*rims)),
        (f32(*field.shape),), (HBM,),
        (vmem(*weight_shape), vmem(*rim_shape), vmem(*edge_shape)),
    )

    returned = lax.all_to_all(
        back.reshape(bricks, 1, LANES), ("lon", "lat"), split_axis=0, concat_axis=0, tiled=True
    )
    result, returned = lax.optimization_barrier((result, returned))
    residual = call(
        functools.partial(unpack_residual, cap), [VMEM], f32(per_level, LANES), VMEM, (), 2, 10, 10000, "residual",
    )(returned.reshape(bricks, LANES))
    return result.reshape(adjoint.shape), residual.reshape(sound_col.shape)


def solution(mesh):
    field = P(None, None, "lat", "lon")
    face = P(None, "lat", "lon")
    owned = P(None, ("lon", "lat"), None)
    return jax.shard_map(
        per_device,
        mesh=mesh,
        in_specs=(field, field, face, face, face, owned, owned, owned, owned),
        out_specs=(field, owned),
        check_vma=False,
    )
```

```python
import functools

import jax
import jax.numpy as jnp
from jax import lax
from jax.experimental import pallas as pl
from jax.experimental.pallas import tpu as pltpu
from jax.sharding import PartitionSpec as P

LANES = 128
SUB = 8
MIB = 1 << 20
ANY = pl.BlockSpec(memory_space=pl.ANY)
HBM = pl.BlockSpec(memory_space=pltpu.HBM)
VMEM = pl.BlockSpec(memory_space=pltpu.VMEM)


def rim_chunks(levels, unroll):
    per_chunk = 63 // unroll * unroll
    chunks = -(-levels // per_chunk)
    return chunks, -(-levels // (chunks * unroll)) * unroll


def lane_iota():
    return lax.broadcasted_iota(jnp.int32, (SUB, LANES), 1)


def sub_iota():
    return lax.broadcasted_iota(jnp.int32, (SUB, LANES), 0)


def largest(count, *choices):
    return next(u for u in choices if count % u == 0)


def in_hbm(x):
    return pltpu.with_memory_space_constraint(x, pltpu.HBM)


def hbm(*shape):
    return pltpu.HBM(shape, jnp.float32)


def f32(*shape):
    return jax.ShapeDtypeStruct(shape, jnp.float32)


def vmem(*shape):
    return pltpu.VMEM(shape, jnp.float32)


def call(body, ins, outs, out_specs, scratch, mib, flops, size, name):
    return pl.pallas_call(
        body,
        in_specs=ins,
        out_specs=out_specs,
        out_shape=outs,
        scratch_shapes=scratch,
        compiler_params=pltpu.CompilerParams(vmem_limit_bytes=mib * MIB),
        cost_estimate=pl.CostEstimate(flops=flops, bytes_accessed=size, transcendentals=0),
        name=name,
    )


def put_rims(field, offset, levels, per_chunk, chunk, out, first, plane, begin=0, end=None):
    lane = lane_iota()
    group = largest(plane // SUB, 4, 2, 1)
    count = min(per_chunk, levels - chunk * per_chunk)

    def body(i, carry):
        r = pl.multiple_of(i * SUB * group, SUB * group)
        made = [jnp.zeros((SUB, LANES), jnp.float32)] * group
        if begin:
            made = [
                out[chunk, pl.ds(pl.multiple_of(first + r + g * SUB, SUB), SUB), :] for g in range(group)
            ]
        for q in range(begin, count if end is None else end):
            for g in range(group):
                at = pl.multiple_of((chunk * per_chunk + q) * plane + offset + r + g * SUB, SUB)
                turned = pltpu.roll(field[pl.ds(at, SUB), :], 2 * q + 2, 1)
                made[g] = jnp.where(lane >= 2 * q + 1, turned, made[g])
        for g in range(group):
            out[chunk, pl.ds(pl.multiple_of(first + r + g * SUB, SUB), SUB), :] = made[g]
        return carry

    lax.fori_loop(0, plane // SUB // group, body, 0)


def row_places(rows):
    odd = lax.axis_index("lat") % 2
    return (1 - odd) * (rows - 1), odd * (rows - 1)


def put_rows(field, offset, a_ref, b_ref, rows, begin, end):
    unroll = largest((end - begin) // SUB, 9, 8, 4, 2, 1)
    in_a, in_b = row_places(rows)

    def body(i, carry):
        for u in range(unroll):
            start = pl.multiple_of(begin + (i * unroll + u) * SUB, SUB)
            at = start * rows + offset
            a_ref[pl.ds(start, SUB), :] = field[pl.ds(at + in_a, SUB, stride=rows), :]
            b_ref[pl.ds(start, SUB), :] = field[pl.ds(at + in_b, SUB, stride=rows), :]
        return carry

    lax.fori_loop(0, (end - begin) // SUB // unroll, body, 0)


def first_rims(levels, tracers, rows, chunks, per_chunk, field, east, north, side, a_ref, b_ref, f, e, n, sems):
    plane = tracers * rows
    wind_copies = [
        pltpu.make_async_copy(east, e, sems.at[2 * chunks]),
        pltpu.make_async_copy(north, n, sems.at[2 * chunks + 1]),
    ]
    pieces, copies = [], []
    for i in range(chunks):
        count = min(per_chunk, levels - i * per_chunk)
        for begin, end in ((0, count // 2), (count // 2, count)):
            pieces.append((i, begin, end))
            part = pl.ds((i * per_chunk + begin) * plane, (end - begin) * plane)
            copies.append(pltpu.make_async_copy(field.at[part], f.at[part], sems.at[len(copies)]))
    for copy in wind_copies + copies:
        copy.start()
    wind_copies[0].wait()
    for i in range(chunks):
        put_rims(e, 0, levels, per_chunk, i, side, plane, rows)
    wind_copies[1].wait()
    winds = pl.ds(levels * tracers, levels)
    put_rows(n, 0, a_ref.at[winds], b_ref.at[winds], rows, 0, levels)
    for copy, (i, begin, end) in zip(copies, pieces):
        copy.wait()
        put_rims(f, 0, levels, per_chunk, i, side, 0, plane, begin, end)
        at = i * per_chunk * tracers
        put_rows(f, 0, a_ref, b_ref, rows, at + begin * tracers, at + end * tracers)


def meet(rim, target, from_west, from_east, count):
    lane = lane_iota()
    for chunk in range(rim.shape[0]):
        for r in range(0, count, SUB):
            rows = pl.ds(r, SUB)
            turned = pltpu.roll(from_east[chunk, rows, :], LANES - 2, 1)
            rim[chunk, pl.ds(target + r, SUB), :] = jnp.where(lane % 2 == 1, from_west[chunk, rows, :], turned)


def pair(edges, target, from_a, from_b, count):
    even = jnp.full((SUB, LANES), lax.axis_index("lat"), jnp.int32) % 2 == 0
    repeat = largest(count // SUB, 9, 8, 4, 2, 1)

    def body(i, carry):
        for u in range(repeat):
            at = pl.multiple_of((i * repeat + u) * SUB, SUB)
            a, b = from_a[pl.ds(at, SUB), :], from_b[pl.ds(at, SUB), :]
            edges[0, pl.ds(target + at, SUB), :] = jnp.where(even, a, b)
            edges[1, pl.ds(target + at, SUB), :] = jnp.where(even, b, a)
        return carry

    lax.fori_loop(0, count // SUB // repeat, body, 0)


def coefficients(
    levels, tracers, rows, per_chunk, unroll, east, north, mixing, west0, east0, a0, b0, *refs
):
    weights, rim, edges, e_buf, n_buf, m_buf, sems = refs
    plane = tracers * rows
    halves = rows // SUB
    lane, sub = lane_iota(), sub_iota()
    copies = [
        pltpu.make_async_copy(source, target, sems.at[i])
        for i, (source, target) in enumerate(((east, e_buf), (north, n_buf), (mixing, m_buf)))
    ]
    for copy in copies:
        copy.start()
    meet(rim, 0, west0, east0, plane)
    pair(edges, 0, a0, b0, levels * tracers)
    for copy in copies:
        copy.wait()
    place = lax.axis_index("lat")
    even = jnp.full((1, LANES), place, jnp.int32) % 2 == 0
    south_flag = (place > 0).astype(jnp.float32)
    north_flag = (place < lax.axis_size("lat") - 1).astype(jnp.float32)
    north_mask = jnp.where(sub == SUB - 1, north_flag, 1.0)

    def level(k, pivots):
        chunk, q = k // per_chunk, k % per_chunk
        has_up = (k < levels - 1).astype(jnp.float32)
        new, edge = [], None
        for h in range(halves):
            blk = pl.ds(pl.multiple_of(k * rows + h * SUB, SUB), SUB)
            down, factor = pivots[h]
            up = m_buf[blk, :] * has_up
            inv = 1.0 / (1.0 + up + down - down * factor)
            factor = up * inv
            new.append((up, factor))
            e, n = e_buf[blk, :], n_buf[blk, :]
            side = pltpu.roll(west0[chunk, pl.ds(plane + h * SUB, SUB), :], LANES - 1 - 2 * q, 1)
            w_in = jnp.minimum(jnp.where(lane == 0, side, pltpu.roll(e, 1, 1)), 0.0)
            if h == 0:
                row = pl.ds(levels * tracers + k, 1)
                edge = jnp.where(even, b0[row, :], a0[row, :]) * south_flag
            s_in = jnp.minimum(jnp.where(sub == 0, edge, pltpu.roll(n, 1, 0)), 0.0)
            edge = n[SUB - 1 : SUB, :]
            e_out, n_out = jnp.maximum(e, 0.0), jnp.maximum(n, 0.0)
            from_n = n_out * inv
            if h == halves - 1:
                from_n = from_n * north_mask
            stay = (1.0 - e_out + w_in - n_out + s_in) * inv
            from_e, from_w = e_out * inv, -(w_in * inv)
            from_rim = jnp.where(lane == 0, from_w, jnp.where(lane == LANES - 1, from_e, 0.0))
            from_e = jnp.where(lane == LANES - 1, 0.0, from_e)
            from_w = jnp.where(lane == 0, 0.0, from_w)
            values = (stay, from_e, from_w, from_n, -(s_in * inv), from_rim, down * inv, factor)
            for i, value in enumerate(values):
                weights[i, blk, :] = value
        return tuple(new)

    def body(b, carry):
        for u in range(unroll):
            carry = level(b * unroll + u, carry)
        return carry

    zero = jnp.zeros((SUB, LANES), jnp.float32)
    lax.fori_loop(0, levels // unroll, body, ((zero, zero),) * halves)


def step(levels, tracers, rows, chunks, per_chunk, unroll, first, *refs):
    if first:
        field, weights, rim, edges, forcing, f_west, f_east, f_a, f_b = refs[:9]
        out, weights_out, side_ref, a_ref, b_ref = refs[9:14]
        buf, rim_now, f_rim, f_edges, sems = refs[14:]
    else:
        field, weights_in, west_in, east_in, a_in, b_in, out = refs[:7]
        buf, rim_now, weights, rim, edges, solved_buf, sems = refs[7:]

    plane = tracers * rows
    halves = rows // SUB
    lane, sub = lane_iota(), sub_iota()
    blocks = levels // unroll
    flat = buf.reshape((levels * tracers + 2) * rows, LANES)

    def load(b):
        at = b * unroll * tracers
        return pltpu.make_async_copy(
            field.at[pl.ds(at, unroll * tracers)], buf.at[pl.ds(at + 1, unroll * tracers)], sems.at[b]
        )

    if first:
        solved_buf, solved_at = buf, 1
        solved_ref = flat
    else:
        solved_at = 0
        solved_ref = solved_buf.reshape(levels * tracers * rows, LANES)

    def store(b):
        at = b * unroll * tracers
        return pltpu.make_async_copy(
            solved_buf.at[pl.ds(at + solved_at, unroll * tracers)], out.at[pl.ds(at, unroll * tracers)], sems.at[b]
        )

    last = 2 * blocks
    above = weights.at[weights.shape[0] - 1]
    if first:
        keep = pltpu.make_async_copy(weights, weights_out, sems.at[last])
        for b in range(blocks):
            load(b).start()
        keep.start()
        meet(f_rim, 0, f_west, f_east, rows)
        pair(f_edges, 0, f_a, f_b, levels)
    else:
        above_copy = pltpu.make_async_copy(weights_in.at[weights.shape[0] - 1], above, sems.at[last])
        def load_weights(b):
            planes, levels_of = pl.ds(0, weights.shape[0] - 1), pl.ds(b * unroll * rows, unroll * rows)
            return pltpu.make_async_copy(
                weights_in.at[planes, levels_of], weights.at[planes, levels_of], sems.at[blocks + b]
            )

        for b in range(blocks):
            load(b).start()
            load_weights(b).start()
        above_copy.start()
        meet(rim, 0, west_in, east_in, plane)
        pair(edges, 0, a_in, b_in, levels * tracers)

    def stencil(near, cells, here, side, edge, row, co, wanted=range(rows // SUB)):
        halfs = [cells[pl.ds(here + h * SUB, SUB), :] for h in range(halves)]
        values = []
        for h in wanted:
            cell = halfs[h]
            if h == halves - 1:
                n = jnp.where(sub == SUB - 1, edge[0, pl.ds(row, 1), :], pltpu.roll(cell, SUB - 1, 0))
            elif near is not None:
                n = near[0][pl.ds(near[1] + here + h * SUB + 1, SUB), :]
            else:
                n = jnp.where(sub == SUB - 1, pltpu.roll(halfs[h + 1], SUB - 1, 0), pltpu.roll(cell, SUB - 1, 0))
            if h == 0:
                s = jnp.where(sub == 0, edge[1, pl.ds(row, 1), :], pltpu.roll(cell, 1, 0))
            elif near is not None:
                s = near[0][pl.ds(near[1] + here + h * SUB - 1, SUB), :]
            else:
                s = jnp.where(sub == 0, pltpu.roll(halfs[h - 1], 1, 0), pltpu.roll(cell, 1, 0))
            c0, ce, cw, cn, cs, rims = co[h][:6]
            value = (c0 * cell + ce * pltpu.roll(cell, LANES - 1, 1)) + (cw * pltpu.roll(cell, 1, 1) + cn * n)
            values.append(value + (cs * s + rims * side(h)))
        return values

    def part(ref, b, size, offset=0):
        return ref.at[pl.ds(pl.multiple_of(b * unroll * size + offset, SUB), unroll * size)]

    def turned_rims(b, source, count, first_row):
        chunk, q = b * unroll // per_chunk, b * unroll % per_chunk
        for r in range(0, count, SUB):
            turned = pltpu.roll(source[chunk, pl.ds(r, SUB), :], (LANES - 2 * q) % LANES, 1)
            rim_now[pl.ds(first_row + r, SUB), :] = turned

    def side(u, r):
        return lambda h: pltpu.roll(rim_now[pl.ds(r + h * SUB, SUB), :], LANES - 1 - 2 * u, 1)

    def weights_of(b):
        co_part = weights.at[:, pl.ds(pl.multiple_of(b * unroll * rows, SUB), unroll * rows)]
        return lambda u: [
            [co_part[i, pl.ds(u * rows + h * SUB, SUB), :] for i in range(weights.shape[0] - 1)]
            for h in range(halves)
        ]

    def forward_block(b, solved):
        load(b).wait()
        if not first:
            load_weights(b).wait()
        turned_rims(b, rim, plane, 0)
        cells, co_of = part(flat, b, plane, rows), weights_of(b)
        edge = edges.at[:, pl.ds(pl.multiple_of(b * unroll * tracers, SUB), unroll * tracers)]
        if first:
            turned_rims(b, f_rim, rows, plane)
            f_cells = part(forcing, b, rows, SUB)
            f_edge = f_edges.at[:, pl.ds(pl.multiple_of(b * unroll, SUB), unroll)]
        else:
            solves = part(solved_ref, b, plane)
        for u in range(unroll):
            co = co_of(u)
            new = []
            if first:
                extra = stencil((forcing, b * unroll * rows + SUB), f_cells, u * rows, side(u, plane), f_edge, u, co)
                for t in range(tracers):
                    here = u * plane + t * rows
                    near = (flat, b * unroll * plane + rows)
                    values = stencil(near, cells, here, side(u, t * rows), edge, u * tracers + t, co)
                    for h in range(halves):
                        value = values[h] + extra[h] + co[h][6] * solved[h * tracers + t]
                        new.append(value)
                        cells[pl.ds(here + h * SUB, SUB), :] = value
                solved = tuple(new[t * halves + h] for h in range(halves) for t in range(tracers))
            else:
                for h in range(halves):
                    for t in range(tracers):
                        here = u * plane + t * rows
                        (value,) = stencil(
                            None, cells, here, side(u, t * rows), edge, u * tracers + t, co, (h,)
                        )
                        value = value + co[h][6] * solved[h * tracers + t]
                        new.append(value)
                        solves[pl.ds(here + h * SUB, SUB), :] = value
                solved = tuple(new)
        return solved

    zero = jnp.zeros((SUB, LANES), jnp.float32)
    zeros = (zero,) * (tracers * halves)
    lax.fori_loop(0, blocks, forward_block, zeros)
    if not first:
        above_copy.wait()

    def backward_block(i, later):
        b = blocks - 1 - i
        cells = part(solved_ref, b, plane, solved_at * rows)
        factors = part(above, b, rows)
        for u in reversed(range(unroll)):
            new = []
            for h in range(halves):
                factor = factors[pl.ds(u * rows + h * SUB, SUB), :]
                for t in range(tracers):
                    blk = pl.ds(u * plane + t * rows + h * SUB, SUB)
                    value = cells[blk, :] + factor * later[h * tracers + t]
                    cells[blk, :] = value
                    new.append(value)
            later = tuple(new)
        store(b).start()
        return later

    lax.fori_loop(0, blocks, backward_block, zeros)
    if first:
        for chunk in range(chunks):
            put_rims(flat, rows, levels, per_chunk, chunk, side_ref, 0, plane)
        put_rows(flat, rows, a_ref, b_ref, rows, 0, levels * tracers)
        keep.wait()
    for b in range(blocks):
        store(b).wait()


def row_offsets(count):
    return list(range(0, count - SUB, SUB)) + [count - SUB]


def pack(levels, group_rows, cap, kernel, columns, observed, errors, out, k_buf, c_buf, o_buf, e_buf, wide, out_buf, sems):
    lane = lane_iota()
    copies = [
        pltpu.make_async_copy(source, target, sems.at[i])
        for i, (source, target) in enumerate(
            ((columns, c_buf), (observed, o_buf), (errors, e_buf), (kernel, k_buf))
        )
    ]
    for copy in copies:
        copy.start()
    for copy in copies:
        copy.wait()
    per_level = columns.shape[0]
    groups = LANES // cap
    offsets = row_offsets(group_rows)
    padded = wide.shape[1] // groups
    together = wide.shape[0]

    def body(start, carry):
        for n in range(together):
            i = start * together + n
            one = pl.ds(i, 1)
            for g in range(groups):
                begin = g * group_rows
                count = min(group_rows, levels - begin)
                wide[n, pl.ds(g * padded, count), :] = k_buf[
                    pl.ds(i + per_level * begin, count, stride=per_level), :
                ]
            end = (groups - 1) * padded + levels - (groups - 1) * group_rows
            for m, row in enumerate((c_buf[one, :].astype(jnp.float32), o_buf[one, :], e_buf[one, :])):
                wide[n, pl.ds(end + m, 1), :] = row
            for m in range(end + 3, (groups - 1) * padded + group_rows):
                wide[n, pl.ds(m, 1), :] = jnp.zeros((1, LANES), jnp.float32)
        for n in range(together):
            i = start * together + n
            for j in range(groups):
                for m in offsets:
                    made = None
                    for g in range(groups):
                        piece = wide[n, pl.ds(g * padded + m, SUB), :]
                        if g != j:
                            piece = pltpu.roll(piece, (g - j) * cap % LANES, 1)
                        made = piece if made is None else jnp.where(lane >= g * cap, piece, made)
                    out_buf[pl.ds((i * groups + j) * group_rows + m, SUB), :] = made
        return carry

    if per_level == together:
        body(0, 0)
    else:
        lax.fori_loop(0, per_level // together, body, 0)
    done = pltpu.make_async_copy(out_buf, out, sems.at[4])
    done.start()
    done.wait()


def tracer_sum(block, concentration, out, buf, sems):
    levels, tracers, rows, cols = buf.shape

    def load(b):
        return pltpu.make_async_copy(
            concentration.at[pl.ds(b * block, block)], buf.at[pl.ds(b * block, block)], sems.at[b]
        )

    for b in range(levels // block):
        load(b).start()

    def body(b, carry):
        load(b).wait()
        for h in range(rows // SUB):
            tops, rests = [], []
            for k in range(block):
                part = jnp.sum(buf[b * block + k, :, pl.ds(h * SUB, SUB), :], axis=0)
                top = part.astype(jnp.bfloat16).astype(jnp.float32)
                tops.append(top)
                rests.append(part - top)
            at = pl.ds(pl.multiple_of(b * block * SUB, block * SUB), block * SUB)
            lanes = pl.ds(h * cols, cols)
            out[0, at, lanes] = jnp.concatenate(tops, axis=0).astype(jnp.bfloat16)
            out[1, at, lanes] = jnp.concatenate(rests, axis=0).astype(jnp.bfloat16)
        return carry

    lax.fori_loop(0, levels // block, body, 0)


def soundings(
    levels, rows, group_rows, cap, chunks, per_chunk, block,
    received, sums, forcing, side_ref, a_ref, b_ref, back_out, arrived, table, scaled, back, sem
):
    lane = lane_iota()
    parts, _, width = arrived.shape
    halves = rows // SUB
    keys = halves * LANES
    groups = LANES // cap

    def unpack_one(c):
        part, col = c // (width // LANES), c % (width // LANES)
        for g in range(groups):
            for m in row_offsets(group_rows):
                made = None
                for p in range(groups):
                    piece = received[pl.ds((c * groups + p) * group_rows + m, SUB), :]
                    if p != g:
                        piece = pltpu.roll(piece, (p - g) * cap % LANES, 1)
                    made = piece if made is None else jnp.where(lane >= p * cap, piece, made)
                lanes = pl.ds(pl.multiple_of(col * LANES, LANES), LANES)
                arrived[part, pl.ds(g * group_rows + m, SUB), lanes] = made

    at_once = largest(parts * width // LANES, 4, 2, 1)

    def unpack(i, carry):
        for n in range(at_once):
            unpack_one(i * at_once + n)
        return carry

    lax.fori_loop(0, parts * width // LANES // at_once, unpack, 0)

    sub_index = lax.broadcasted_iota(jnp.int32, (SUB, width), 0)
    key_index = lax.broadcasted_iota(jnp.int32, (keys, width), 0)
    turned_index = lax.broadcasted_iota(jnp.int32, (LANES, keys), 1)

    def columns(j):
        return arrived[j, pl.ds(levels, 1), :].astype(jnp.int32)

    def key_of(col):
        return (col >> 10) * LANES + (col & (LANES - 1))

    def mask_of(j):
        return sub_index == ((columns(j) >> 7) & (SUB - 1))

    for j in range(parts):
        col = columns(j)
        key = key_of(col)
        look = jnp.where(key_index == key, 1.0, 0.0).astype(jnp.bfloat16)
        for c in range(width // LANES):
            piece = key[:, c * LANES : (c + 1) * LANES].astype(jnp.float32)
            across = jnp.broadcast_to(piece, (LANES, LANES)).T.astype(jnp.int32)
            across = jnp.concatenate([across] * halves, axis=1)
            table[j, pl.ds(c * LANES, LANES), :] = jnp.where(turned_index == across, 1.0, 0.0).astype(
                jnp.bfloat16
            )
        total = jnp.zeros((SUB, width), jnp.float32)
        for b in range(levels // block):
            blk = pl.ds(b * block * SUB, block * SUB)
            seen = jnp.dot(sums[0, blk, :], look, preferred_element_type=jnp.float32)
            seen += jnp.dot(sums[1, blk, :], look, preferred_element_type=jnp.float32)
            weight = arrived[j, pl.ds(b * block, block), :]
            for k in range(block):
                total += weight[k : k + 1, :] * seen[k * SUB : (k + 1) * SUB, :]
        modelled = jnp.sum(jnp.where(mask_of(j), total, 0.0), axis=0, keepdims=True)
        observed = arrived[j, pl.ds(levels + 1, 1), :]
        error = arrived[j, pl.ds(levels + 2, 1), :]
        residual = jnp.where(col >= 0, (modelled - observed) / error, 0.0)
        scaled[pl.ds(j, 1), :] = residual / error
        for i in range(width // cap):
            at = i * cap
            piece = residual[:, at // LANES * LANES : at // LANES * LANES + LANES]
            if at % LANES:
                piece = pltpu.roll(piece, LANES - at % LANES, 1)
            back[pl.ds(j * (width // cap) + i, 1), :] = piece

    leave = pltpu.make_async_copy(back, back_out, sem.at[0])
    leave.start()
    zeros = jnp.zeros((SUB, LANES), jnp.float32)
    forcing[pl.ds(0, SUB), :] = zeros
    forcing[pl.ds(levels * rows + SUB, SUB), :] = zeros
    for b in range(levels // block):
        total = jnp.zeros((block * SUB, keys), jnp.float32)
        for j in range(parts):
            weight = arrived[j, pl.ds(b * block, block), :] * scaled[pl.ds(j, 1), :]
            top = weight.astype(jnp.bfloat16).astype(jnp.float32)
            mask = mask_of(j)
            for part in (top, weight - top):
                spread = jnp.concatenate(
                    [jnp.where(mask, part[k : k + 1, :], 0.0) for k in range(block)], axis=0
                ).astype(jnp.bfloat16)
                total += jnp.dot(spread, table[j, :, :], preferred_element_type=jnp.float32)
        for k in range(block):
            for h in range(halves):
                forcing[pl.ds((b * block + k) * rows + (h + 1) * SUB, SUB), :] = total[
                    k * SUB : (k + 1) * SUB, h * LANES : (h + 1) * LANES
                ]

    for chunk in range(chunks):
        put_rims(forcing, SUB, levels, per_chunk, chunk, side_ref, 0, rows)
    put_rows(forcing, SUB, a_ref, b_ref, rows, 0, levels)
    leave.wait()


def unpack_residual(cap, arrived, out):
    lane = lax.broadcasted_iota(jnp.int32, (1, LANES), 1)
    groups = LANES // cap
    for row in range(out.shape[0]):
        made = None
        for g in range(groups):
            piece = arrived[pl.ds(row * groups + g, 1), :]
            if g:
                piece = pltpu.roll(piece, g * cap, 1)
            made = piece if made is None else jnp.where(lane >= g * cap, piece, made)
        out[pl.ds(row, 1), :] = made


def exchange(side_rim, a_rim, b_rim):
    lons, lats = lax.axis_size("lon"), lax.axis_size("lat")

    def partner(j, odd):
        other = j + 1 if j % 2 == odd else j - 1
        return other if 0 <= other < lats else j

    return (
        lax.ppermute(side_rim, "lon", [(i, (i + 1) % lons) for i in range(lons)]),
        lax.ppermute(side_rim, "lon", [((i + 1) % lons, i) for i in range(lons)]),
        lax.ppermute(a_rim, "lat", [(j, partner(j, 0)) for j in range(lats)]),
        lax.ppermute(b_rim, "lat", [(j, partner(j, 1)) for j in range(lats)]),
    )


def per_device(
    concentration, adjoint, wind_east, wind_north, mixing, sound_col, kernel, observed, obs_error
):
    levels, tracers, rows, cols = adjoint.shape
    bricks = lax.axis_size("lon") * lax.axis_size("lat")
    slots = sound_col.shape[2]
    cap = slots // bricks
    unroll = largest(levels, 8, 4, 3, 2, 1)
    chunks, per_chunk = rim_chunks(levels, unroll)
    plane = tracers * rows
    per_level = slots // LANES
    groups = LANES // cap
    group_rows = -(-(levels + 3) // groups)
    padded_rows = -(-group_rows // SUB) * SUB
    field_bytes = levels * plane * cols * 4
    dma = pltpu.SemaphoreType.DMA

    def flat(x):
        return x.reshape(-1, LANES)

    packed = call(
        functools.partial(pack, levels, group_rows, cap),
        [HBM] * 4, f32(bricks * group_rows, LANES), HBM,
        (
            vmem(levels * per_level, LANES), pltpu.VMEM((per_level, LANES), jnp.int32),
            vmem(per_level, LANES), vmem(per_level, LANES),
            vmem(largest(per_level, 8, 4, 2, 1), groups * padded_rows, LANES),
            vmem(bricks * group_rows, LANES), dma((5,)),
        ),
        4, 10, 800000, "pack",
    )(*(in_hbm(flat(x)) for x in (kernel, sound_col, observed, obs_error)))
    received = lax.all_to_all(
        packed.reshape(-1, 1, LANES), ("lon", "lat"), split_axis=0, concat_axis=0, tiled=True
    ).reshape(-1, LANES)

    field = adjoint.reshape(levels * tracers, rows, LANES)
    east, north, mix = (in_hbm(flat(x)) for x in (wind_east, wind_north, mixing))
    rims = call(
        functools.partial(first_rims, levels, tracers, rows, chunks, per_chunk),
        [HBM] * 3,
        (f32(chunks, plane + rows, LANES),) + (f32(levels * tracers + levels, LANES),) * 2,
        (VMEM,) * 3,
        (vmem(levels * plane, LANES), vmem(levels * rows, LANES), vmem(levels * rows, LANES), dma((2 * chunks + 2,))),
        10, field_bytes, 2 * field_bytes, "first_rims",
    )(in_hbm(flat(adjoint)), east, north)
    start_rims = exchange(*rims)

    block = largest(levels, 24, 16, 8)
    sum_block = largest(levels, 12, 8)
    sums = call(
        functools.partial(tracer_sum, sum_block),
        [HBM], jax.ShapeDtypeStruct((2, levels * SUB, rows // SUB * cols), jnp.bfloat16), VMEM,
        (vmem(levels, tracers, rows, cols), dma((levels // sum_block,))),
        10, field_bytes // 4, field_bytes, "tracer_sum",
    )(concentration)

    width = largest(slots, 2 * LANES, LANES)
    parts = slots // width
    forcing, *rims, back = call(
        functools.partial(soundings, levels, rows, group_rows, cap, chunks, per_chunk, block),
        [VMEM] * 2,
        (
            f32(levels * rows + 2 * SUB, LANES), f32(chunks, rows, LANES), f32(levels, LANES), f32(levels, LANES),
            hbm(bricks, LANES),
        ),
        (VMEM,) * 4 + (HBM,),
        (
            vmem(parts, -(-groups * group_rows // SUB) * SUB, width),
            pltpu.VMEM((parts, width, rows // SUB * LANES), jnp.bfloat16),
            vmem(max(parts, SUB), width), vmem(bricks, LANES), dma((1,)),
        ),
        10, field_bytes * 8, field_bytes, "soundings",
    )(received, sums)
    forcing_rims = exchange(*rims)

    rim_shape, edge_shape = (chunks, plane, LANES), (2, levels * tracers, LANES)
    weight_shape = (8, levels * rows, LANES)
    weights, rim0, edges0 = call(
        functools.partial(coefficients, levels, tracers, rows, per_chunk, unroll),
        [HBM] * 3 + [VMEM] * 4,
        (f32(*weight_shape), f32(*rim_shape), f32(*edge_shape)),
        (VMEM,) * 3,
        (vmem(levels * rows, LANES),) * 3 + (dma((3,)),),
        4, field_bytes, field_bytes, "coefficients",
    )(east, north, mix, *start_rims)

    def advance(first, together, specs, operands, outs, out_specs, scratch):
        return call(
            functools.partial(step, levels, tracers, rows, chunks, per_chunk, together, first),
            specs, outs, out_specs,
            (vmem(levels * tracers + 2, rows, LANES), vmem(plane + rows, LANES))
            + scratch + (dma((2 * (levels // together) + 5,)),),
            22, field_bytes * 8, field_bytes * 2, "step",
        )(*operands)

    edge_rows = f32(levels * tracers, LANES)
    stepped, kept, *rims = advance(
        True, unroll, [HBM] + [VMEM] * 8, (in_hbm(field), weights, rim0, edges0, forcing, *forcing_rims),
        (hbm(*field.shape), hbm(*weight_shape), f32(*rim_shape), edge_rows, edge_rows), (HBM,) * 2 + (VMEM,) * 3,
        (vmem(chunks, rows, LANES), vmem(2, levels, LANES)),
    )
    (result,) = advance(
        False, unroll, [HBM] * 2 + [VMEM] * 4, (in_hbm(stepped), in_hbm(kept), *exchange(*rims)),
        (f32(*field.shape),), (HBM,),
        (vmem(*weight_shape), vmem(*rim_shape), vmem(*edge_shape), vmem(levels * tracers, rows, LANES)),
    )

    returned = lax.all_to_all(
        back.reshape(bricks, 1, LANES), ("lon", "lat"), split_axis=0, concat_axis=0, tiled=True
    )
    result, returned = lax.optimization_barrier((result, returned))
    residual = call(
        functools.partial(unpack_residual, cap), [VMEM], f32(per_level, LANES), VMEM, (), 2, 10, 10000, "residual",
    )(returned.reshape(bricks, LANES))
    return result.reshape(adjoint.shape), residual.reshape(sound_col.shape)


def solution(mesh):
    field = P(None, None, "lat", "lon")
    face = P(None, "lat", "lon")
    owned = P(None, ("lon", "lat"), None)
    return jax.shard_map(
        per_device,
        mesh=mesh,
        in_specs=(field, field, face, face, face, owned, owned, owned, owned),
        out_specs=(field, owned),
        check_vma=False,
    )
```

```python
import functools

import jax
import jax.numpy as jnp
from jax import lax
from jax.experimental import pallas as pl
from jax.experimental.pallas import tpu as pltpu
from jax.sharding import PartitionSpec as P

LANES = 128
SUB = 8
MIB = 1 << 20
ANY = pl.BlockSpec(memory_space=pl.ANY)
HBM = pl.BlockSpec(memory_space=pltpu.HBM)
VMEM = pl.BlockSpec(memory_space=pltpu.VMEM)


def rim_chunks(levels, unroll):
    per_chunk = 63 // unroll * unroll
    chunks = -(-levels // per_chunk)
    return chunks, -(-levels // (chunks * unroll)) * unroll


def lane_iota():
    return lax.broadcasted_iota(jnp.int32, (SUB, LANES), 1)


def sub_iota():
    return lax.broadcasted_iota(jnp.int32, (SUB, LANES), 0)


def largest(count, *choices):
    return next(u for u in choices if count % u == 0)


def in_hbm(x):
    return pltpu.with_memory_space_constraint(x, pltpu.HBM)


def hbm(*shape):
    return pltpu.HBM(shape, jnp.float32)


def f32(*shape):
    return jax.ShapeDtypeStruct(shape, jnp.float32)


def vmem(*shape):
    return pltpu.VMEM(shape, jnp.float32)


def call(body, ins, outs, out_specs, scratch, mib, flops, size, name):
    return pl.pallas_call(
        body,
        in_specs=ins,
        out_specs=out_specs,
        out_shape=outs,
        scratch_shapes=scratch,
        compiler_params=pltpu.CompilerParams(vmem_limit_bytes=mib * MIB),
        cost_estimate=pl.CostEstimate(flops=flops, bytes_accessed=size, transcendentals=0),
        name=name,
    )


def put_rims(field, offset, levels, per_chunk, chunk, out, first, plane, begin=0, end=None):
    lane = lane_iota()
    group = largest(plane // SUB, 4, 2, 1)
    count = min(per_chunk, levels - chunk * per_chunk)

    def body(i, carry):
        r = pl.multiple_of(i * SUB * group, SUB * group)
        made = [jnp.zeros((SUB, LANES), jnp.float32)] * group
        if begin:
            made = [
                out[chunk, pl.ds(pl.multiple_of(first + r + g * SUB, SUB), SUB), :] for g in range(group)
            ]
        for q in range(begin, count if end is None else end):
            for g in range(group):
                at = pl.multiple_of((chunk * per_chunk + q) * plane + offset + r + g * SUB, SUB)
                turned = pltpu.roll(field[pl.ds(at, SUB), :], 2 * q + 2, 1)
                made[g] = jnp.where(lane >= 2 * q + 1, turned, made[g])
        for g in range(group):
            out[chunk, pl.ds(pl.multiple_of(first + r + g * SUB, SUB), SUB), :] = made[g]
        return carry

    lax.fori_loop(0, plane // SUB // group, body, 0)


def row_places(rows):
    odd = lax.axis_index("lat") % 2
    return (1 - odd) * (rows - 1), odd * (rows - 1)


def put_rows(field, offset, a_ref, b_ref, rows, begin, end):
    unroll = largest((end - begin) // SUB, 9, 8, 4, 2, 1)
    in_a, in_b = row_places(rows)

    def body(i, carry):
        for u in range(unroll):
            start = pl.multiple_of(begin + (i * unroll + u) * SUB, SUB)
            at = start * rows + offset
            a_ref[pl.ds(start, SUB), :] = field[pl.ds(at + in_a, SUB, stride=rows), :]
            b_ref[pl.ds(start, SUB), :] = field[pl.ds(at + in_b, SUB, stride=rows), :]
        return carry

    lax.fori_loop(0, (end - begin) // SUB // unroll, body, 0)


def first_rims(levels, tracers, rows, chunks, per_chunk, field, east, north, side, a_ref, b_ref, f, e, n, sems):
    plane = tracers * rows
    wind_copies = [
        pltpu.make_async_copy(east, e, sems.at[2 * chunks]),
        pltpu.make_async_copy(north, n, sems.at[2 * chunks + 1]),
    ]
    pieces, copies = [], []
    for i in range(chunks):
        count = min(per_chunk, levels - i * per_chunk)
        for begin, end in ((0, count // 2), (count // 2, count)):
            pieces.append((i, begin, end))
            part = pl.ds((i * per_chunk + begin) * plane, (end - begin) * plane)
            copies.append(pltpu.make_async_copy(field.at[part], f.at[part], sems.at[len(copies)]))
    for copy in wind_copies + copies:
        copy.start()
    wind_copies[0].wait()
    for i in range(chunks):
        put_rims(e, 0, levels, per_chunk, i, side, plane, rows)
    wind_copies[1].wait()
    winds = pl.ds(levels * tracers, levels)
    put_rows(n, 0, a_ref.at[winds], b_ref.at[winds], rows, 0, levels)
    for copy, (i, begin, end) in zip(copies, pieces):
        copy.wait()
        put_rims(f, 0, levels, per_chunk, i, side, 0, plane, begin, end)
        at = i * per_chunk * tracers
        put_rows(f, 0, a_ref, b_ref, rows, at + begin * tracers, at + end * tracers)


def meet(rim, target, from_west, from_east, count):
    lane = lane_iota()
    for chunk in range(rim.shape[0]):
        for r in range(0, count, SUB):
            rows = pl.ds(r, SUB)
            turned = pltpu.roll(from_east[chunk, rows, :], LANES - 2, 1)
            rim[chunk, pl.ds(target + r, SUB), :] = jnp.where(lane % 2 == 1, from_west[chunk, rows, :], turned)


def pair(edges, target, from_a, from_b, count):
    even = jnp.full((SUB, LANES), lax.axis_index("lat"), jnp.int32) % 2 == 0
    repeat = largest(count // SUB, 9, 8, 4, 2, 1)

    def body(i, carry):
        for u in range(repeat):
            at = pl.multiple_of((i * repeat + u) * SUB, SUB)
            a, b = from_a[pl.ds(at, SUB), :], from_b[pl.ds(at, SUB), :]
            edges[0, pl.ds(target + at, SUB), :] = jnp.where(even, a, b)
            edges[1, pl.ds(target + at, SUB), :] = jnp.where(even, b, a)
        return carry

    lax.fori_loop(0, count // SUB // repeat, body, 0)


def coefficients(
    levels, tracers, rows, per_chunk, unroll, east, north, mixing, west0, east0, a0, b0, *refs
):
    weights, rim, edges, e_buf, n_buf, m_buf, sems = refs
    plane = tracers * rows
    halves = rows // SUB
    lane, sub = lane_iota(), sub_iota()
    blocks = levels // unroll

    def load(b):
        at = pl.ds(pl.multiple_of(b * unroll * rows, SUB), unroll * rows)
        return [
            pltpu.make_async_copy(source.at[at], target.at[at], sems.at[i, b])
            for i, (source, target) in enumerate(((mixing, m_buf), (east, e_buf), (north, n_buf)))
        ]

    for b in range(blocks):
        for copy in load(b):
            copy.start()
    meet(rim, 0, west0, east0, plane)
    pair(edges, 0, a0, b0, levels * tracers)
    place = lax.axis_index("lat")
    even = jnp.full((1, LANES), place, jnp.int32) % 2 == 0
    south_flag = (place > 0).astype(jnp.float32)
    north_flag = (place < lax.axis_size("lat") - 1).astype(jnp.float32)
    north_mask = jnp.where(sub == SUB - 1, north_flag, 1.0)

    def level(k, pivots):
        chunk, q = k // per_chunk, k % per_chunk
        has_up = (k < levels - 1).astype(jnp.float32)
        new, edge = [], None
        for h in range(halves):
            blk = pl.ds(pl.multiple_of(k * rows + h * SUB, SUB), SUB)
            down, factor = pivots[h]
            up = m_buf[blk, :] * has_up
            inv = 1.0 / (1.0 + up + down - down * factor)
            factor = up * inv
            new.append((up, factor))
            e, n = e_buf[blk, :], n_buf[blk, :]
            side = pltpu.roll(west0[chunk, pl.ds(plane + h * SUB, SUB), :], LANES - 1 - 2 * q, 1)
            w_in = jnp.minimum(jnp.where(lane == 0, side, pltpu.roll(e, 1, 1)), 0.0)
            if h == 0:
                row = pl.ds(levels * tracers + k, 1)
                edge = jnp.where(even, b0[row, :], a0[row, :]) * south_flag
            s_in = jnp.minimum(jnp.where(sub == 0, edge, pltpu.roll(n, 1, 0)), 0.0)
            edge = n[SUB - 1 : SUB, :]
            e_out, n_out = jnp.maximum(e, 0.0), jnp.maximum(n, 0.0)
            from_n = n_out * inv
            if h == halves - 1:
                from_n = from_n * north_mask
            stay = (1.0 - e_out + w_in - n_out + s_in) * inv
            from_e, from_w = e_out * inv, -(w_in * inv)
            values = (stay, from_e, from_w, from_n, -(s_in * inv), down * inv, factor)
            for i, value in enumerate(values):
                weights[i, blk, :] = value
        return tuple(new)

    def body(b, carry):
        for copy in load(b):
            copy.wait()
        for u in range(unroll):
            carry = level(b * unroll + u, carry)
        return carry

    zero = jnp.zeros((SUB, LANES), jnp.float32)
    lax.fori_loop(0, blocks, body, ((zero, zero),) * halves)


def step(levels, tracers, rows, chunks, per_chunk, unroll, first, *refs):
    if first:
        field, weights, rim, edges, forcing, f_west, f_east, f_a, f_b = refs[:9]
        out, weights_out, side_ref, a_ref, b_ref = refs[9:14]
        buf, rim_now, f_rim, f_edges, sems = refs[14:]
    else:
        field, weights_in, west_in, east_in, a_in, b_in, out = refs[:7]
        buf, rim_now, weights, rim, edges, solved_buf, sems = refs[7:]

    plane = tracers * rows
    halves = rows // SUB
    lane, sub = lane_iota(), sub_iota()
    blocks = levels // unroll
    flat = buf.reshape((levels * tracers + 2) * rows, LANES)

    def load(b):
        at = b * unroll * tracers
        return pltpu.make_async_copy(
            field.at[pl.ds(at, unroll * tracers)], buf.at[pl.ds(at + 1, unroll * tracers)], sems.at[b]
        )

    if first:
        solved_buf, solved_at = buf, 1
        solved_ref = flat
    else:
        solved_at = 0
        solved_ref = solved_buf.reshape(levels * tracers * rows, LANES)

    def store(b):
        at = b * unroll * tracers
        return pltpu.make_async_copy(
            solved_buf.at[pl.ds(at + solved_at, unroll * tracers)], out.at[pl.ds(at, unroll * tracers)], sems.at[b]
        )

    last = 2 * blocks
    above = weights.at[weights.shape[0] - 1]
    if first:
        keep = pltpu.make_async_copy(weights, weights_out, sems.at[last])
        for b in range(blocks):
            load(b).start()
        keep.start()
        meet(f_rim, 0, f_west, f_east, rows)
        pair(f_edges, 0, f_a, f_b, levels)
    else:
        above_copy = pltpu.make_async_copy(weights_in.at[weights.shape[0] - 1], above, sems.at[last])
        def load_weights(b):
            planes, levels_of = pl.ds(0, weights.shape[0] - 1), pl.ds(b * unroll * rows, unroll * rows)
            return pltpu.make_async_copy(
                weights_in.at[planes, levels_of], weights.at[planes, levels_of], sems.at[blocks + b]
            )

        for b in range(blocks):
            load(b).start()
            load_weights(b).start()
        above_copy.start()
        meet(rim, 0, west_in, east_in, plane)
        pair(edges, 0, a_in, b_in, levels * tracers)

    def stencil(near, cells, here, side, edge, row, co, wanted=range(rows // SUB)):
        halfs = [cells[pl.ds(here + h * SUB, SUB), :] for h in range(halves)]
        values = []
        for h in wanted:
            cell = halfs[h]
            if h == halves - 1:
                n = jnp.where(sub == SUB - 1, edge[0, pl.ds(row, 1), :], pltpu.roll(cell, SUB - 1, 0))
            elif near is not None:
                n = near[0][pl.ds(near[1] + here + h * SUB + 1, SUB), :]
            else:
                n = jnp.where(sub == SUB - 1, pltpu.roll(halfs[h + 1], SUB - 1, 0), pltpu.roll(cell, SUB - 1, 0))
            if h == 0:
                s = jnp.where(sub == 0, edge[1, pl.ds(row, 1), :], pltpu.roll(cell, 1, 0))
            elif near is not None:
                s = near[0][pl.ds(near[1] + here + h * SUB - 1, SUB), :]
            else:
                s = jnp.where(sub == 0, pltpu.roll(halfs[h - 1], 1, 0), pltpu.roll(cell, 1, 0))
            c0, ce, cw, cn, cs, rims = co[h][:6]
            value = (c0 * cell + ce * pltpu.roll(cell, LANES - 1, 1)) + (cw * pltpu.roll(cell, 1, 1) + cn * n)
            values.append(value + (cs * s + rims * side(h)))
        return values

    def part(ref, b, size, offset=0):
        return ref.at[pl.ds(pl.multiple_of(b * unroll * size + offset, SUB), unroll * size)]

    def turned_rims(b, source, count, first_row):
        chunk, q = b * unroll // per_chunk, b * unroll % per_chunk
        for r in range(0, count, SUB):
            turned = pltpu.roll(source[chunk, pl.ds(r, SUB), :], (LANES - 2 * q) % LANES, 1)
            rim_now[pl.ds(first_row + r, SUB), :] = turned

    def side(u, r):
        return lambda h: pltpu.roll(rim_now[pl.ds(r + h * SUB, SUB), :], LANES - 1 - 2 * u, 1)

    def weights_of(b):
        co_part = weights.at[:, pl.ds(pl.multiple_of(b * unroll * rows, SUB), unroll * rows)]

        def one(u, h):
            c0, ce, cw, cn, cs, a = (
                co_part[i, pl.ds(u * rows + h * SUB, SUB), :] for i in range(weights.shape[0] - 1)
            )
            first_col, last_col = lane == 0, lane == LANES - 1
            rims = jnp.where(first_col, cw, jnp.where(last_col, ce, 0.0))
            return c0, jnp.where(last_col, 0.0, ce), jnp.where(first_col, 0.0, cw), cn, cs, rims, a

        return lambda u: [one(u, h) for h in range(halves)]

    def forward_block(b, solved):
        load(b).wait()
        if not first:
            load_weights(b).wait()
        turned_rims(b, rim, plane, 0)
        cells, co_of = part(flat, b, plane, rows), weights_of(b)
        edge = edges.at[:, pl.ds(pl.multiple_of(b * unroll * tracers, SUB), unroll * tracers)]
        if first:
            turned_rims(b, f_rim, rows, plane)
            f_cells = part(forcing, b, rows, SUB)
            f_edge = f_edges.at[:, pl.ds(pl.multiple_of(b * unroll, SUB), unroll)]
        else:
            solves = part(solved_ref, b, plane)
        for u in range(unroll):
            co = co_of(u)
            new = []
            if first:
                extra = stencil((forcing, b * unroll * rows + SUB), f_cells, u * rows, side(u, plane), f_edge, u, co)
                for t in range(tracers):
                    here = u * plane + t * rows
                    near = (flat, b * unroll * plane + rows)
                    values = stencil(near, cells, here, side(u, t * rows), edge, u * tracers + t, co)
                    for h in range(halves):
                        value = values[h] + extra[h] + co[h][6] * solved[h * tracers + t]
                        new.append(value)
                        cells[pl.ds(here + h * SUB, SUB), :] = value
                solved = tuple(new[t * halves + h] for h in range(halves) for t in range(tracers))
            else:
                for h in range(halves):
                    for t in range(tracers):
                        here = u * plane + t * rows
                        (value,) = stencil(
                            None, cells, here, side(u, t * rows), edge, u * tracers + t, co, (h,)
                        )
                        value = value + co[h][6] * solved[h * tracers + t]
                        new.append(value)
                        solves[pl.ds(here + h * SUB, SUB), :] = value
                solved = tuple(new)
        return solved

    zero = jnp.zeros((SUB, LANES), jnp.float32)
    zeros = (zero,) * (tracers * halves)
    lax.fori_loop(0, blocks, forward_block, zeros)
    if not first:
        above_copy.wait()

    def backward_block(i, later):
        b = blocks - 1 - i
        cells = part(solved_ref, b, plane, solved_at * rows)
        factors = part(above, b, rows)
        for u in reversed(range(unroll)):
            new = []
            for h in range(halves):
                factor = factors[pl.ds(u * rows + h * SUB, SUB), :]
                for t in range(tracers):
                    blk = pl.ds(u * plane + t * rows + h * SUB, SUB)
                    value = cells[blk, :] + factor * later[h * tracers + t]
                    cells[blk, :] = value
                    new.append(value)
            later = tuple(new)
        store(b).start()
        return later

    lax.fori_loop(0, blocks, backward_block, zeros)
    if first:
        for chunk in range(chunks):
            put_rims(flat, rows, levels, per_chunk, chunk, side_ref, 0, plane)
        put_rows(flat, rows, a_ref, b_ref, rows, 0, levels * tracers)
        keep.wait()
    for b in range(blocks):
        store(b).wait()


def row_offsets(count):
    return list(range(0, count - SUB, SUB)) + [count - SUB]


def pack(levels, group_rows, cap, kernel, columns, observed, errors, out, k_buf, c_buf, o_buf, e_buf, wide, out_buf, sems):
    lane = lane_iota()
    copies = [
        pltpu.make_async_copy(source, target, sems.at[i])
        for i, (source, target) in enumerate(
            ((columns, c_buf), (observed, o_buf), (errors, e_buf), (kernel, k_buf))
        )
    ]
    for copy in copies:
        copy.start()
    for copy in copies:
        copy.wait()
    per_level = columns.shape[0]
    groups = LANES // cap
    offsets = row_offsets(group_rows)
    padded = wide.shape[1] // groups
    together = wide.shape[0]

    def body(start, carry):
        for n in range(together):
            i = start * together + n
            one = pl.ds(i, 1)
            for g in range(groups):
                begin = g * group_rows
                count = min(group_rows, levels - begin)
                wide[n, pl.ds(g * padded, count), :] = k_buf[
                    pl.ds(i + per_level * begin, count, stride=per_level), :
                ]
            end = (groups - 1) * padded + levels - (groups - 1) * group_rows
            for m, row in enumerate((c_buf[one, :].astype(jnp.float32), o_buf[one, :], e_buf[one, :])):
                wide[n, pl.ds(end + m, 1), :] = row
            for m in range(end + 3, (groups - 1) * padded + group_rows):
                wide[n, pl.ds(m, 1), :] = jnp.zeros((1, LANES), jnp.float32)
        for n in range(together):
            i = start * together + n
            for j in range(groups):
                for m in offsets:
                    made = None
                    for g in range(groups):
                        piece = wide[n, pl.ds(g * padded + m, SUB), :]
                        if g != j:
                            piece = pltpu.roll(piece, (g - j) * cap % LANES, 1)
                        made = piece if made is None else jnp.where(lane >= g * cap, piece, made)
                    out_buf[pl.ds((i * groups + j) * group_rows + m, SUB), :] = made
        return carry

    if per_level == together:
        body(0, 0)
    else:
        lax.fori_loop(0, per_level // together, body, 0)
    done = pltpu.make_async_copy(out_buf, out, sems.at[4])
    done.start()
    done.wait()


def tracer_sum(block, concentration, out, buf, sems):
    levels, tracers, rows, cols = buf.shape

    def load(b):
        return pltpu.make_async_copy(
            concentration.at[pl.ds(b * block, block)], buf.at[pl.ds(b * block, block)], sems.at[b]
        )

    for b in range(levels // block):
        load(b).start()

    def body(b, carry):
        load(b).wait()
        for h in range(rows // SUB):
            tops, rests = [], []
            for k in range(block):
                part = jnp.sum(buf[b * block + k, :, pl.ds(h * SUB, SUB), :], axis=0)
                top = part.astype(jnp.bfloat16).astype(jnp.float32)
                tops.append(top)
                rests.append(part - top)
            at = pl.ds(pl.multiple_of(b * block * SUB, block * SUB), block * SUB)
            lanes = pl.ds(h * cols, cols)
            out[0, at, lanes] = jnp.concatenate(tops, axis=0).astype(jnp.bfloat16)
            out[1, at, lanes] = jnp.concatenate(rests, axis=0).astype(jnp.bfloat16)
        return carry

    lax.fori_loop(0, levels // block, body, 0)


def soundings(
    levels, rows, group_rows, cap, chunks, per_chunk, block,
    received, sums, forcing, side_ref, a_ref, b_ref, back_out, arrived, table, scaled, back, sem
):
    lane = lane_iota()
    parts, _, width = arrived.shape
    halves = rows // SUB
    keys = halves * LANES
    groups = LANES // cap

    def unpack_one(c):
        part, col = c // (width // LANES), c % (width // LANES)
        for g in range(groups):
            for m in row_offsets(group_rows):
                made = None
                for p in range(groups):
                    piece = received[pl.ds((c * groups + p) * group_rows + m, SUB), :]
                    if p != g:
                        piece = pltpu.roll(piece, (p - g) * cap % LANES, 1)
                    made = piece if made is None else jnp.where(lane >= p * cap, piece, made)
                lanes = pl.ds(pl.multiple_of(col * LANES, LANES), LANES)
                arrived[part, pl.ds(g * group_rows + m, SUB), lanes] = made

    at_once = largest(parts * width // LANES, 4, 2, 1)

    def unpack(i, carry):
        for n in range(at_once):
            unpack_one(i * at_once + n)
        return carry

    lax.fori_loop(0, parts * width // LANES // at_once, unpack, 0)

    sub_index = lax.broadcasted_iota(jnp.int32, (SUB, width), 0)
    key_index = lax.broadcasted_iota(jnp.int32, (keys, width), 0)
    turned_index = lax.broadcasted_iota(jnp.int32, (LANES, keys), 1)

    def columns(j):
        return arrived[j, pl.ds(levels, 1), :].astype(jnp.int32)

    def key_of(col):
        return (col >> 10) * LANES + (col & (LANES - 1))

    def mask_of(j):
        return sub_index == ((columns(j) >> 7) & (SUB - 1))

    for j in range(parts):
        col = columns(j)
        key = key_of(col)
        look = jnp.where(key_index == key, 1.0, 0.0).astype(jnp.bfloat16)
        for c in range(width // LANES):
            piece = key[:, c * LANES : (c + 1) * LANES].astype(jnp.float32)
            across = jnp.broadcast_to(piece, (LANES, LANES)).T.astype(jnp.int32)
            across = jnp.concatenate([across] * halves, axis=1)
            table[j, pl.ds(c * LANES, LANES), :] = jnp.where(turned_index == across, 1.0, 0.0).astype(
                jnp.bfloat16
            )
        total = jnp.zeros((SUB, width), jnp.float32)
        for b in range(levels // block):
            blk = pl.ds(b * block * SUB, block * SUB)
            seen = jnp.dot(sums[0, blk, :], look, preferred_element_type=jnp.float32)
            seen += jnp.dot(sums[1, blk, :], look, preferred_element_type=jnp.float32)
            weight = arrived[j, pl.ds(b * block, block), :]
            for k in range(block):
                total += weight[k : k + 1, :] * seen[k * SUB : (k + 1) * SUB, :]
        modelled = jnp.sum(jnp.where(mask_of(j), total, 0.0), axis=0, keepdims=True)
        observed = arrived[j, pl.ds(levels + 1, 1), :]
        error = arrived[j, pl.ds(levels + 2, 1), :]
        residual = jnp.where(col >= 0, (modelled - observed) / error, 0.0)
        scaled[pl.ds(j, 1), :] = residual / error
        for i in range(width // cap):
            at = i * cap
            piece = residual[:, at // LANES * LANES : at // LANES * LANES + LANES]
            if at % LANES:
                piece = pltpu.roll(piece, LANES - at % LANES, 1)
            back[pl.ds(j * (width // cap) + i, 1), :] = piece

    leave = pltpu.make_async_copy(back, back_out, sem.at[0])
    leave.start()
    zeros = jnp.zeros((SUB, LANES), jnp.float32)
    forcing[pl.ds(0, SUB), :] = zeros
    forcing[pl.ds(levels * rows + SUB, SUB), :] = zeros
    for b in range(levels // block):
        total = jnp.zeros((block * SUB, keys), jnp.float32)
        for j in range(parts):
            weight = arrived[j, pl.ds(b * block, block), :] * scaled[pl.ds(j, 1), :]
            top = weight.astype(jnp.bfloat16).astype(jnp.float32)
            mask = mask_of(j)
            for part in (top, weight - top):
                spread = jnp.concatenate(
                    [jnp.where(mask, part[k : k + 1, :], 0.0) for k in range(block)], axis=0
                ).astype(jnp.bfloat16)
                total += jnp.dot(spread, table[j, :, :], preferred_element_type=jnp.float32)
        for k in range(block):
            for h in range(halves):
                forcing[pl.ds((b * block + k) * rows + (h + 1) * SUB, SUB), :] = total[
                    k * SUB : (k + 1) * SUB, h * LANES : (h + 1) * LANES
                ]

    for chunk in range(chunks):
        put_rims(forcing, SUB, levels, per_chunk, chunk, side_ref, 0, rows)
    put_rows(forcing, SUB, a_ref, b_ref, rows, 0, levels)
    leave.wait()


def unpack_residual(cap, arrived, out):
    lane = lax.broadcasted_iota(jnp.int32, (1, LANES), 1)
    groups = LANES // cap
    for row in range(out.shape[0]):
        made = None
        for g in range(groups):
            piece = arrived[pl.ds(row * groups + g, 1), :]
            if g:
                piece = pltpu.roll(piece, g * cap, 1)
            made = piece if made is None else jnp.where(lane >= g * cap, piece, made)
        out[pl.ds(row, 1), :] = made


def exchange(side_rim, a_rim, b_rim):
    lons, lats = lax.axis_size("lon"), lax.axis_size("lat")

    def partner(j, odd):
        other = j + 1 if j % 2 == odd else j - 1
        return other if 0 <= other < lats else j

    return (
        lax.ppermute(side_rim, "lon", [(i, (i + 1) % lons) for i in range(lons)]),
        lax.ppermute(side_rim, "lon", [((i + 1) % lons, i) for i in range(lons)]),
        lax.ppermute(a_rim, "lat", [(j, partner(j, 0)) for j in range(lats)]),
        lax.ppermute(b_rim, "lat", [(j, partner(j, 1)) for j in range(lats)]),
    )


def per_device(
    concentration, adjoint, wind_east, wind_north, mixing, sound_col, kernel, observed, obs_error
):
    levels, tracers, rows, cols = adjoint.shape
    bricks = lax.axis_size("lon") * lax.axis_size("lat")
    slots = sound_col.shape[2]
    cap = slots // bricks
    unroll = largest(levels, 8, 4, 3, 2, 1)
    chunks, per_chunk = rim_chunks(levels, unroll)
    plane = tracers * rows
    per_level = slots // LANES
    groups = LANES // cap
    group_rows = -(-(levels + 3) // groups)
    padded_rows = -(-group_rows // SUB) * SUB
    field_bytes = levels * plane * cols * 4
    dma = pltpu.SemaphoreType.DMA

    def flat(x):
        return x.reshape(-1, LANES)

    packed = call(
        functools.partial(pack, levels, group_rows, cap),
        [HBM] * 4, f32(bricks * group_rows, LANES), HBM,
        (
            vmem(levels * per_level, LANES), pltpu.VMEM((per_level, LANES), jnp.int32),
            vmem(per_level, LANES), vmem(per_level, LANES),
            vmem(largest(per_level, 8, 4, 2, 1), groups * padded_rows, LANES),
            vmem(bricks * group_rows, LANES), dma((5,)),
        ),
        4, 10, 800000, "pack",
    )(*(in_hbm(flat(x)) for x in (kernel, sound_col, observed, obs_error)))
    received = lax.all_to_all(
        packed.reshape(-1, 1, LANES), ("lon", "lat"), split_axis=0, concat_axis=0, tiled=True
    ).reshape(-1, LANES)

    field = adjoint.reshape(levels * tracers, rows, LANES)
    east, north, mix = (in_hbm(flat(x)) for x in (wind_east, wind_north, mixing))
    rims = call(
        functools.partial(first_rims, levels, tracers, rows, chunks, per_chunk),
        [HBM] * 3,
        (f32(chunks, plane + rows, LANES),) + (f32(levels * tracers + levels, LANES),) * 2,
        (VMEM,) * 3,
        (vmem(levels * plane, LANES), vmem(levels * rows, LANES), vmem(levels * rows, LANES), dma((2 * chunks + 2,))),
        10, field_bytes, 2 * field_bytes, "first_rims",
    )(in_hbm(flat(adjoint)), east, north)
    start_rims = exchange(*rims)

    block = largest(levels, 24, 16, 8)
    sum_block = largest(levels, 12, 8)
    sums = call(
        functools.partial(tracer_sum, sum_block),
        [HBM], jax.ShapeDtypeStruct((2, levels * SUB, rows // SUB * cols), jnp.bfloat16), VMEM,
        (vmem(levels, tracers, rows, cols), dma((levels // sum_block,))),
        10, field_bytes // 4, field_bytes, "tracer_sum",
    )(concentration)

    width = largest(slots, 2 * LANES, LANES)
    parts = slots // width
    forcing, *rims, back = call(
        functools.partial(soundings, levels, rows, group_rows, cap, chunks, per_chunk, block),
        [VMEM] * 2,
        (
            f32(levels * rows + 2 * SUB, LANES), f32(chunks, rows, LANES), f32(levels, LANES), f32(levels, LANES),
            hbm(bricks, LANES),
        ),
        (VMEM,) * 4 + (HBM,),
        (
            vmem(parts, -(-groups * group_rows // SUB) * SUB, width),
            pltpu.VMEM((parts, width, rows // SUB * LANES), jnp.bfloat16),
            vmem(max(parts, SUB), width), vmem(bricks, LANES), dma((1,)),
        ),
        10, field_bytes * 8, field_bytes, "soundings",
    )(received, sums)
    forcing_rims = exchange(*rims)

    rim_shape, edge_shape = (chunks, plane, LANES), (2, levels * tracers, LANES)
    weight_shape = (7, levels * rows, LANES)
    weights, rim0, edges0 = call(
        functools.partial(coefficients, levels, tracers, rows, per_chunk, unroll),
        [HBM] * 3 + [VMEM] * 4,
        (f32(*weight_shape), f32(*rim_shape), f32(*edge_shape)),
        (VMEM,) * 3,
        (vmem(levels * rows, LANES),) * 3 + (dma((3, levels // unroll)),),
        4, field_bytes, field_bytes, "coefficients",
    )(east, north, mix, *start_rims)

    def advance(first, together, specs, operands, outs, out_specs, scratch):
        return call(
            functools.partial(step, levels, tracers, rows, chunks, per_chunk, together, first),
            specs, outs, out_specs,
            (vmem(levels * tracers + 2, rows, LANES), vmem(plane + rows, LANES))
            + scratch + (dma((2 * (levels // together) + 5,)),),
            22, field_bytes * 8, field_bytes * 2, "step",
        )(*operands)

    edge_rows = f32(levels * tracers, LANES)
    stepped, kept, *rims = advance(
        True, unroll, [HBM] + [VMEM] * 8, (in_hbm(field), weights, rim0, edges0, forcing, *forcing_rims),
        (hbm(*field.shape), hbm(*weight_shape), f32(*rim_shape), edge_rows, edge_rows), (HBM,) * 2 + (VMEM,) * 3,
        (vmem(chunks, rows, LANES), vmem(2, levels, LANES)),
    )
    (result,) = advance(
        False, unroll, [HBM] * 2 + [VMEM] * 4, (in_hbm(stepped), in_hbm(kept), *exchange(*rims)),
        (f32(*field.shape),), (HBM,),
        (vmem(*weight_shape), vmem(*rim_shape), vmem(*edge_shape), vmem(levels * tracers, rows, LANES)),
    )

    returned = lax.all_to_all(
        back.reshape(bricks, 1, LANES), ("lon", "lat"), split_axis=0, concat_axis=0, tiled=True
    )
    result, returned = lax.optimization_barrier((result, returned))
    residual = call(
        functools.partial(unpack_residual, cap), [VMEM], f32(per_level, LANES), VMEM, (), 2, 10, 10000, "residual",
    )(returned.reshape(bricks, LANES))
    return result.reshape(adjoint.shape), residual.reshape(sound_col.shape)


def solution(mesh):
    field = P(None, None, "lat", "lon")
    face = P(None, "lat", "lon")
    owned = P(None, ("lon", "lat"), None)
    return jax.shard_map(
        per_device,
        mesh=mesh,
        in_specs=(field, field, face, face, face, owned, owned, owned, owned),
        out_specs=(field, owned),
        check_vma=False,
    )
```

```python
import functools

import jax
import jax.numpy as jnp
from jax import lax
from jax.experimental import pallas as pl
from jax.experimental.pallas import tpu as pltpu
from jax.sharding import PartitionSpec as P

LANES = 128
SUB = 8
MIB = 1 << 20
ANY = pl.BlockSpec(memory_space=pl.ANY)
HBM = pl.BlockSpec(memory_space=pltpu.HBM)
VMEM = pl.BlockSpec(memory_space=pltpu.VMEM)


def rim_chunks(levels, unroll):
    per_chunk = 63 // unroll * unroll
    chunks = -(-levels // per_chunk)
    return chunks, -(-levels // (chunks * unroll)) * unroll


def lane_iota():
    return lax.broadcasted_iota(jnp.int32, (SUB, LANES), 1)


def sub_iota():
    return lax.broadcasted_iota(jnp.int32, (SUB, LANES), 0)


def largest(count, *choices):
    return next(u for u in choices if count % u == 0)


def in_hbm(x):
    return pltpu.with_memory_space_constraint(x, pltpu.HBM)


def hbm(*shape):
    return pltpu.HBM(shape, jnp.float32)


def f32(*shape):
    return jax.ShapeDtypeStruct(shape, jnp.float32)


def vmem(*shape):
    return pltpu.VMEM(shape, jnp.float32)


def call(body, ins, outs, out_specs, scratch, mib, flops, size, name):
    return pl.pallas_call(
        body,
        in_specs=ins,
        out_specs=out_specs,
        out_shape=outs,
        scratch_shapes=scratch,
        compiler_params=pltpu.CompilerParams(vmem_limit_bytes=mib * MIB),
        cost_estimate=pl.CostEstimate(flops=flops, bytes_accessed=size, transcendentals=0),
        name=name,
    )


def put_rims(field, offset, levels, per_chunk, chunk, out, first, plane, begin=0, end=None):
    lane = lane_iota()
    group = largest(plane // SUB, 16, 8, 4, 2, 1)
    count = min(per_chunk, levels - chunk * per_chunk)

    def body(i, carry):
        r = pl.multiple_of(i * SUB * group, SUB * group)
        made = [jnp.zeros((SUB, LANES), jnp.float32)] * group
        if begin:
            made = [
                out[chunk, pl.ds(pl.multiple_of(first + r + g * SUB, SUB), SUB), :] for g in range(group)
            ]
        for q in range(begin, count if end is None else end):
            for g in range(group):
                at = pl.multiple_of((chunk * per_chunk + q) * plane + offset + r + g * SUB, SUB)
                turned = pltpu.roll(field[pl.ds(at, SUB), :], 2 * q + 2, 1)
                made[g] = jnp.where(lane >= 2 * q + 1, turned, made[g])
        for g in range(group):
            out[chunk, pl.ds(pl.multiple_of(first + r + g * SUB, SUB), SUB), :] = made[g]
        return carry

    lax.fori_loop(0, plane // SUB // group, body, 0)


def row_places(rows):
    odd = lax.axis_index("lat") % 2
    return (1 - odd) * (rows - 1), odd * (rows - 1)


def put_rows(field, offset, a_ref, b_ref, rows, begin, end, places=None):
    unroll = largest((end - begin) // SUB, 9, 8, 4, 2, 1)
    in_a, in_b = places or row_places(rows)

    def body(i, carry):
        for u in range(unroll):
            start = pl.multiple_of(begin + (i * unroll + u) * SUB, SUB)
            at = start * rows + offset
            a_ref[pl.ds(start, SUB), :] = field[pl.ds(at + in_a, SUB, stride=rows), :]
            b_ref[pl.ds(start, SUB), :] = field[pl.ds(at + in_b, SUB, stride=rows), :]
        return carry

    lax.fori_loop(0, (end - begin) // SUB // unroll, body, 0)


def first_rims(levels, tracers, rows, chunks, per_chunk, field, east, north, side, a_ref, b_ref, f, e, n, sems):
    plane = tracers * rows
    wind_copies = [
        pltpu.make_async_copy(east, e, sems.at[2 * chunks]),
        pltpu.make_async_copy(north, n, sems.at[2 * chunks + 1]),
    ]
    pieces, copies = [], []
    for i in range(chunks):
        count = min(per_chunk, levels - i * per_chunk)
        for begin, end in ((0, count // 2), (count // 2, count)):
            pieces.append((i, begin, end))
            part = pl.ds((i * per_chunk + begin) * plane, (end - begin) * plane)
            copies.append(pltpu.make_async_copy(field.at[part], f.at[part], sems.at[len(copies)]))
    for copy in wind_copies + copies:
        copy.start()
    wind_copies[0].wait()
    for i in range(chunks):
        put_rims(e, 0, levels, per_chunk, i, side, plane, rows)
    wind_copies[1].wait()
    winds = pl.ds(levels * tracers, levels)
    put_rows(n, 0, a_ref.at[winds], b_ref.at[winds], rows, 0, levels)
    for copy, (i, begin, end) in zip(copies, pieces):
        copy.wait()
        put_rims(f, 0, levels, per_chunk, i, side, 0, plane, begin, end)
        at = i * per_chunk * tracers
        put_rows(f, 0, a_ref, b_ref, rows, at + begin * tracers, at + end * tracers)


def meet(rim, target, from_west, from_east, count):
    lane = lane_iota()
    for chunk in range(rim.shape[0]):
        for r in range(0, count, SUB):
            rows = pl.ds(r, SUB)
            turned = pltpu.roll(from_east[chunk, rows, :], LANES - 2, 1)
            rim[chunk, pl.ds(target + r, SUB), :] = jnp.where(lane % 2 == 1, from_west[chunk, rows, :], turned)


def pair(edges, target, from_a, from_b, count):
    even = jnp.full((SUB, LANES), lax.axis_index("lat"), jnp.int32) % 2 == 0
    repeat = largest(count // SUB, 9, 8, 4, 2, 1)

    def body(i, carry):
        for u in range(repeat):
            at = pl.multiple_of((i * repeat + u) * SUB, SUB)
            a, b = from_a[pl.ds(at, SUB), :], from_b[pl.ds(at, SUB), :]
            edges[0, pl.ds(target + at, SUB), :] = jnp.where(even, a, b)
            edges[1, pl.ds(target + at, SUB), :] = jnp.where(even, b, a)
        return carry

    lax.fori_loop(0, count // SUB // repeat, body, 0)


def coefficients(
    levels, tracers, rows, per_chunk, unroll, east, north, mixing, west0, east0, a0, b0, *refs
):
    weights, rim, edges, e_buf, n_buf, m_buf, sems = refs
    plane = tracers * rows
    halves = rows // SUB
    lane, sub = lane_iota(), sub_iota()
    blocks = levels // unroll

    def load(b):
        at = pl.ds(pl.multiple_of(b * unroll * rows, SUB), unroll * rows)
        return [
            pltpu.make_async_copy(source.at[at], target.at[at], sems.at[i, b])
            for i, (source, target) in enumerate(((mixing, m_buf), (east, e_buf), (north, n_buf)))
        ]

    for b in range(blocks):
        for copy in load(b):
            copy.start()
    meet(rim, 0, west0, east0, plane)
    pair(edges, 0, a0, b0, levels * tracers)
    place = lax.axis_index("lat")
    even = jnp.full((1, LANES), place, jnp.int32) % 2 == 0
    south_flag = (place > 0).astype(jnp.float32)
    north_flag = (place < lax.axis_size("lat") - 1).astype(jnp.float32)
    north_mask = jnp.where(sub == SUB - 1, north_flag, 1.0)

    def level(k, pivots):
        chunk, q = k // per_chunk, k % per_chunk
        has_up = (k < levels - 1).astype(jnp.float32)
        new, edge = [], None
        for h in range(halves):
            blk = pl.ds(pl.multiple_of(k * rows + h * SUB, SUB), SUB)
            down, factor = pivots[h]
            up = m_buf[blk, :] * has_up
            inv = 1.0 / (1.0 + up + down - down * factor)
            factor = up * inv
            new.append((up, factor))
            e, n = e_buf[blk, :], n_buf[blk, :]
            side = pltpu.roll(west0[chunk, pl.ds(plane + h * SUB, SUB), :], LANES - 1 - 2 * q, 1)
            w_in = jnp.minimum(jnp.where(lane == 0, side, pltpu.roll(e, 1, 1)), 0.0)
            if h == 0:
                row = pl.ds(levels * tracers + k, 1)
                edge = jnp.where(even, b0[row, :], a0[row, :]) * south_flag
            s_in = jnp.minimum(jnp.where(sub == 0, edge, pltpu.roll(n, 1, 0)), 0.0)
            edge = n[SUB - 1 : SUB, :]
            e_out, n_out = jnp.maximum(e, 0.0), jnp.maximum(n, 0.0)
            from_n = n_out * inv
            if h == halves - 1:
                from_n = from_n * north_mask
            stay = (1.0 - e_out + w_in - n_out + s_in) * inv
            from_e, from_w = e_out * inv, -(w_in * inv)
            values = (stay, from_e, from_w, from_n, -(s_in * inv), down * inv, factor)
            for i, value in enumerate(values):
                weights[i, blk, :] = value
        return tuple(new)

    def body(b, carry):
        for copy in load(b):
            copy.wait()
        for u in range(unroll):
            carry = level(b * unroll + u, carry)
        return carry

    zero = jnp.zeros((SUB, LANES), jnp.float32)
    lax.fori_loop(0, blocks, body, ((zero, zero),) * halves)


def step(levels, tracers, rows, chunks, per_chunk, unroll, first, *refs):
    if first:
        field, weights, rim, edges, forcing, f_west, f_east, f_north, f_south = refs[:9]
        out, weights_out, side_ref, a_ref, b_ref = refs[9:14]
        buf, rim_now, f_rim, f_edges, sems = refs[14:]
    else:
        field, weights_in, west_in, east_in, a_in, b_in, out = refs[:7]
        buf, rim_now, weights, rim, edges, solved_buf, sems = refs[7:]

    plane = tracers * rows
    halves = rows // SUB
    lane, sub = lane_iota(), sub_iota()
    blocks = levels // unroll
    flat = buf.reshape((levels * tracers + 2) * rows, LANES)

    def load(b):
        at = b * unroll * tracers
        return pltpu.make_async_copy(
            field.at[pl.ds(at, unroll * tracers)], buf.at[pl.ds(at + 1, unroll * tracers)], sems.at[b]
        )

    if first:
        solved_buf, solved_at = buf, 1
        solved_ref = flat
    else:
        solved_at = 0
        solved_ref = solved_buf.reshape(levels * tracers * rows, LANES)

    def store(b):
        at = b * unroll * tracers
        return pltpu.make_async_copy(
            solved_buf.at[pl.ds(at + solved_at, unroll * tracers)], out.at[pl.ds(at, unroll * tracers)], sems.at[b]
        )

    last = 2 * blocks
    above = weights.at[weights.shape[0] - 1]
    if first:
        keep = pltpu.make_async_copy(weights, weights_out, sems.at[last])
        for b in range(blocks):
            load(b).start()
        keep.start()
        meet(f_rim, 0, f_west, f_east, rows)
        f_edges[0] = f_north[...]
        f_edges[1] = f_south[...]
    else:
        above_copy = pltpu.make_async_copy(weights_in.at[weights.shape[0] - 1], above, sems.at[last])
        def load_weights(b):
            planes, levels_of = pl.ds(0, weights.shape[0] - 1), pl.ds(b * unroll * rows, unroll * rows)
            return pltpu.make_async_copy(
                weights_in.at[planes, levels_of], weights.at[planes, levels_of], sems.at[blocks + b]
            )

        for b in range(blocks):
            load(b).start()
            load_weights(b).start()
        above_copy.start()
        meet(rim, 0, west_in, east_in, plane)
        pair(edges, 0, a_in, b_in, levels * tracers)

    def stencil(near, cells, here, side, edge, row, co, wanted=range(rows // SUB)):
        halfs = [cells[pl.ds(here + h * SUB, SUB), :] for h in range(halves)]
        values = []
        for h in wanted:
            cell = halfs[h]
            if h == halves - 1:
                n = jnp.where(sub == SUB - 1, edge[0, pl.ds(row, 1), :], pltpu.roll(cell, SUB - 1, 0))
            elif near is not None:
                n = near[0][pl.ds(near[1] + here + h * SUB + 1, SUB), :]
            else:
                n = jnp.where(sub == SUB - 1, pltpu.roll(halfs[h + 1], SUB - 1, 0), pltpu.roll(cell, SUB - 1, 0))
            if h == 0:
                s = jnp.where(sub == 0, edge[1, pl.ds(row, 1), :], pltpu.roll(cell, 1, 0))
            elif near is not None:
                s = near[0][pl.ds(near[1] + here + h * SUB - 1, SUB), :]
            else:
                s = jnp.where(sub == 0, pltpu.roll(halfs[h - 1], 1, 0), pltpu.roll(cell, 1, 0))
            c0, ce, cw, cn, cs, rims = co[h][:6]
            value = (c0 * cell + ce * pltpu.roll(cell, LANES - 1, 1)) + (cw * pltpu.roll(cell, 1, 1) + cn * n)
            values.append(value + (cs * s + rims * side(h)))
        return values

    def part(ref, b, size, offset=0):
        return ref.at[pl.ds(pl.multiple_of(b * unroll * size + offset, SUB), unroll * size)]

    def turned_rims(b, source, count, first_row):
        chunk, q = b * unroll // per_chunk, b * unroll % per_chunk
        for r in range(0, count, SUB):
            turned = pltpu.roll(source[chunk, pl.ds(r, SUB), :], (LANES - 2 * q) % LANES, 1)
            rim_now[pl.ds(first_row + r, SUB), :] = turned

    def side(u, r):
        return lambda h: pltpu.roll(rim_now[pl.ds(r + h * SUB, SUB), :], LANES - 1 - 2 * u, 1)

    def weights_of(b):
        co_part = weights.at[:, pl.ds(pl.multiple_of(b * unroll * rows, SUB), unroll * rows)]

        def one(u, h):
            c0, ce, cw, cn, cs, a = (
                co_part[i, pl.ds(u * rows + h * SUB, SUB), :] for i in range(weights.shape[0] - 1)
            )
            first_col, last_col = lane == 0, lane == LANES - 1
            rims = jnp.where(first_col, cw, jnp.where(last_col, ce, 0.0))
            return c0, jnp.where(last_col, 0.0, ce), jnp.where(first_col, 0.0, cw), cn, cs, rims, a

        return lambda u: [one(u, h) for h in range(halves)]

    def forward_block(b, solved):
        load(b).wait()
        if not first:
            load_weights(b).wait()
        turned_rims(b, rim, plane, 0)
        cells, co_of = part(flat, b, plane, rows), weights_of(b)
        edge = edges.at[:, pl.ds(pl.multiple_of(b * unroll * tracers, SUB), unroll * tracers)]
        if first:
            turned_rims(b, f_rim, rows, plane)
            f_cells = part(forcing, b, rows, SUB)
            f_edge = f_edges.at[:, pl.ds(pl.multiple_of(b * unroll, SUB), unroll)]
        else:
            solves = part(solved_ref, b, plane)
        for u in range(unroll):
            co = co_of(u)
            new = []
            if first:
                extra = stencil((forcing, b * unroll * rows + SUB), f_cells, u * rows, side(u, plane), f_edge, u, co)
                for t in range(tracers):
                    here = u * plane + t * rows
                    near = (flat, b * unroll * plane + rows)
                    values = stencil(near, cells, here, side(u, t * rows), edge, u * tracers + t, co)
                    for h in range(halves):
                        value = values[h] + extra[h] + co[h][6] * solved[h * tracers + t]
                        new.append(value)
                        cells[pl.ds(here + h * SUB, SUB), :] = value
                solved = tuple(new[t * halves + h] for h in range(halves) for t in range(tracers))
            else:
                for h in range(halves):
                    for t in range(tracers):
                        here = u * plane + t * rows
                        (value,) = stencil(
                            None, cells, here, side(u, t * rows), edge, u * tracers + t, co, (h,)
                        )
                        value = value + co[h][6] * solved[h * tracers + t]
                        new.append(value)
                        solves[pl.ds(here + h * SUB, SUB), :] = value
                solved = tuple(new)
        return solved

    zero = jnp.zeros((SUB, LANES), jnp.float32)
    zeros = (zero,) * (tracers * halves)
    lax.fori_loop(0, blocks, forward_block, zeros)
    if not first:
        above_copy.wait()

    def backward_block(i, later):
        b = blocks - 1 - i
        cells = part(solved_ref, b, plane, solved_at * rows)
        factors = part(above, b, rows)
        for u in reversed(range(unroll)):
            new = []
            for h in range(halves):
                factor = factors[pl.ds(u * rows + h * SUB, SUB), :]
                for t in range(tracers):
                    blk = pl.ds(u * plane + t * rows + h * SUB, SUB)
                    value = cells[blk, :] + factor * later[h * tracers + t]
                    cells[blk, :] = value
                    new.append(value)
            later = tuple(new)
        store(b).start()
        return later

    lax.fori_loop(0, blocks, backward_block, zeros)
    if first:
        for chunk in range(chunks):
            put_rims(flat, rows, levels, per_chunk, chunk, side_ref, 0, plane)
        put_rows(flat, rows, a_ref, b_ref, rows, 0, levels * tracers)
        keep.wait()
    for b in range(blocks):
        store(b).wait()


def row_offsets(count):
    return list(range(0, count - SUB, SUB)) + [count - SUB]


def pack(levels, group_rows, cap, kernel, columns, observed, errors, out, k_buf, c_buf, o_buf, e_buf, wide, out_buf, sems):
    lane = lane_iota()
    copies = [
        pltpu.make_async_copy(source, target, sems.at[i])
        for i, (source, target) in enumerate(
            ((columns, c_buf), (observed, o_buf), (errors, e_buf), (kernel, k_buf))
        )
    ]
    for copy in copies:
        copy.start()
    for copy in copies:
        copy.wait()
    per_level = columns.shape[0]
    groups = LANES // cap
    offsets = row_offsets(group_rows)
    padded = wide.shape[1] // groups
    together = wide.shape[0]

    def body(start, carry):
        for n in range(together):
            i = start * together + n
            one = pl.ds(i, 1)
            for g in range(groups):
                begin = g * group_rows
                count = min(group_rows, levels - begin)
                wide[n, pl.ds(g * padded, count), :] = k_buf[
                    pl.ds(i + per_level * begin, count, stride=per_level), :
                ]
            end = (groups - 1) * padded + levels - (groups - 1) * group_rows
            for m, row in enumerate((c_buf[one, :].astype(jnp.float32), o_buf[one, :], e_buf[one, :])):
                wide[n, pl.ds(end + m, 1), :] = row
            for m in range(end + 3, (groups - 1) * padded + group_rows):
                wide[n, pl.ds(m, 1), :] = jnp.zeros((1, LANES), jnp.float32)
        for n in range(together):
            i = start * together + n
            for j in range(groups):
                for m in offsets:
                    made = None
                    for g in range(groups):
                        piece = wide[n, pl.ds(g * padded + m, SUB), :]
                        if g != j:
                            piece = pltpu.roll(piece, (g - j) * cap % LANES, 1)
                        made = piece if made is None else jnp.where(lane >= g * cap, piece, made)
                    out_buf[pl.ds((i * groups + j) * group_rows + m, SUB), :] = made
        return carry

    if per_level == together:
        body(0, 0)
    else:
        lax.fori_loop(0, per_level // together, body, 0)
    done = pltpu.make_async_copy(out_buf, out, sems.at[4])
    done.start()
    done.wait()


def tracer_sum(block, concentration, out, buf, sems):
    levels, tracers, rows, cols = buf.shape

    def load(b):
        return pltpu.make_async_copy(
            concentration.at[pl.ds(b * block, block)], buf.at[pl.ds(b * block, block)], sems.at[b]
        )

    for b in range(levels // block):
        load(b).start()

    def body(b, carry):
        load(b).wait()
        for h in range(rows // SUB):
            tops, rests = [], []
            for k in range(block):
                part = jnp.sum(buf[b * block + k, :, pl.ds(h * SUB, SUB), :], axis=0)
                top = part.astype(jnp.bfloat16).astype(jnp.float32)
                tops.append(top)
                rests.append(part - top)
            at = pl.ds(pl.multiple_of(b * block * SUB, block * SUB), block * SUB)
            lanes = pl.ds(h * cols, cols)
            out[0, at, lanes] = jnp.concatenate(tops, axis=0).astype(jnp.bfloat16)
            out[1, at, lanes] = jnp.concatenate(rests, axis=0).astype(jnp.bfloat16)
        return carry

    lax.fori_loop(0, levels // block, body, 0)


def soundings(
    levels, rows, group_rows, cap, chunks, per_chunk, block,
    received, sums, forcing, side_ref, a_ref, b_ref, back_out, arrived, table, scaled, back, sem
):
    lane = lane_iota()
    parts, _, width = arrived.shape
    halves = rows // SUB
    keys = halves * LANES
    groups = LANES // cap

    def unpack_one(c):
        part, col = c // (width // LANES), c % (width // LANES)
        for g in range(groups):
            for m in row_offsets(group_rows):
                made = None
                for p in range(groups):
                    piece = received[pl.ds((c * groups + p) * group_rows + m, SUB), :]
                    if p != g:
                        piece = pltpu.roll(piece, (p - g) * cap % LANES, 1)
                    made = piece if made is None else jnp.where(lane >= p * cap, piece, made)
                lanes = pl.ds(pl.multiple_of(col * LANES, LANES), LANES)
                arrived[part, pl.ds(g * group_rows + m, SUB), lanes] = made

    at_once = largest(parts * width // LANES, 4, 2, 1)

    def unpack(i, carry):
        for n in range(at_once):
            unpack_one(i * at_once + n)
        return carry

    lax.fori_loop(0, parts * width // LANES // at_once, unpack, 0)

    sub_index = lax.broadcasted_iota(jnp.int32, (SUB, width), 0)
    key_index = lax.broadcasted_iota(jnp.int32, (keys, width), 0)
    turned_index = lax.broadcasted_iota(jnp.int32, (LANES, keys), 1)

    def columns(j):
        return arrived[j, pl.ds(levels, 1), :].astype(jnp.int32)

    def key_of(col):
        return (col >> 10) * LANES + (col & (LANES - 1))

    def mask_of(j):
        return sub_index == ((columns(j) >> 7) & (SUB - 1))

    for j in range(parts):
        col = columns(j)
        key = key_of(col)
        look = jnp.where(key_index == key, 1.0, 0.0).astype(jnp.bfloat16)
        for c in range(width // LANES):
            piece = key[:, c * LANES : (c + 1) * LANES].astype(jnp.float32)
            across = jnp.broadcast_to(piece, (LANES, LANES)).T.astype(jnp.int32)
            across = jnp.concatenate([across] * halves, axis=1)
            table[j, pl.ds(c * LANES, LANES), :] = jnp.where(turned_index == across, 1.0, 0.0).astype(
                jnp.bfloat16
            )
        total = jnp.zeros((SUB, width), jnp.float32)
        for b in range(levels // block):
            blk = pl.ds(b * block * SUB, block * SUB)
            seen = jnp.dot(sums[0, blk, :], look, preferred_element_type=jnp.float32)
            seen += jnp.dot(sums[1, blk, :], look, preferred_element_type=jnp.float32)
            weight = arrived[j, pl.ds(b * block, block), :]
            for k in range(block):
                total += weight[k : k + 1, :] * seen[k * SUB : (k + 1) * SUB, :]
        modelled = jnp.sum(jnp.where(mask_of(j), total, 0.0), axis=0, keepdims=True)
        observed = arrived[j, pl.ds(levels + 1, 1), :]
        error = arrived[j, pl.ds(levels + 2, 1), :]
        residual = jnp.where(col >= 0, (modelled - observed) / error, 0.0)
        scaled[pl.ds(j, 1), :] = residual / error
        for i in range(width // cap):
            at = i * cap
            piece = residual[:, at // LANES * LANES : at // LANES * LANES + LANES]
            if at % LANES:
                piece = pltpu.roll(piece, LANES - at % LANES, 1)
            back[pl.ds(j * (width // cap) + i, 1), :] = piece

    leave = pltpu.make_async_copy(back, back_out, sem.at[0])
    leave.start()
    zeros = jnp.zeros((SUB, LANES), jnp.float32)
    forcing[pl.ds(0, SUB), :] = zeros
    forcing[pl.ds(levels * rows + SUB, SUB), :] = zeros
    for b in range(levels // block):
        total = jnp.zeros((block * SUB, keys), jnp.float32)
        for j in range(parts):
            weight = arrived[j, pl.ds(b * block, block), :] * scaled[pl.ds(j, 1), :]
            top = weight.astype(jnp.bfloat16).astype(jnp.float32)
            mask = mask_of(j)
            for part in (top, weight - top):
                spread = jnp.concatenate(
                    [jnp.where(mask, part[k : k + 1, :], 0.0) for k in range(block)], axis=0
                ).astype(jnp.bfloat16)
                total += jnp.dot(spread, table[j, :, :], preferred_element_type=jnp.float32)
        for k in range(block):
            for h in range(halves):
                forcing[pl.ds((b * block + k) * rows + (h + 1) * SUB, SUB), :] = total[
                    k * SUB : (k + 1) * SUB, h * LANES : (h + 1) * LANES
                ]

    for chunk in range(chunks):
        put_rims(forcing, SUB, levels, per_chunk, chunk, side_ref, 0, rows)
    put_rows(forcing, SUB, a_ref, b_ref, rows, 0, levels, (0, rows - 1))
    leave.wait()


def unpack_residual(cap, arrived, out):
    lane = lax.broadcasted_iota(jnp.int32, (1, LANES), 1)
    groups = LANES // cap
    for row in range(out.shape[0]):
        made = None
        for g in range(groups):
            piece = arrived[pl.ds(row * groups + g, 1), :]
            if g:
                piece = pltpu.roll(piece, g * cap, 1)
            made = piece if made is None else jnp.where(lane >= g * cap, piece, made)
        out[pl.ds(row, 1), :] = made


def turn(value, axis, by):
    count = lax.axis_size(axis)
    return lax.ppermute(value, axis, [(i, (i + by) % count) for i in range(count)])


def exchange(side_rim, a_rim, b_rim):
    lats = lax.axis_size("lat")

    def partner(j, odd):
        other = j + 1 if j % 2 == odd else j - 1
        return other if 0 <= other < lats else j

    return (
        turn(side_rim, "lon", 1),
        turn(side_rim, "lon", -1),
        lax.ppermute(a_rim, "lat", [(j, partner(j, 0)) for j in range(lats)]),
        lax.ppermute(b_rim, "lat", [(j, partner(j, 1)) for j in range(lats)]),
    )


def exchange_small(side_rim, first_rows, last_rows):
    return (
        turn(side_rim, "lon", 1),
        turn(side_rim, "lon", -1),
        turn(first_rows, "lat", -1),
        turn(last_rows, "lat", 1),
    )


def per_device(
    concentration, adjoint, wind_east, wind_north, mixing, sound_col, kernel, observed, obs_error
):
    levels, tracers, rows, cols = adjoint.shape
    bricks = lax.axis_size("lon") * lax.axis_size("lat")
    slots = sound_col.shape[2]
    cap = slots // bricks
    unroll = largest(levels, 8, 4, 3, 2, 1)
    chunks, per_chunk = rim_chunks(levels, unroll)
    plane = tracers * rows
    per_level = slots // LANES
    groups = LANES // cap
    group_rows = -(-(levels + 3) // groups)
    padded_rows = -(-group_rows // SUB) * SUB
    field_bytes = levels * plane * cols * 4
    dma = pltpu.SemaphoreType.DMA

    def flat(x):
        return x.reshape(-1, LANES)

    packed = call(
        functools.partial(pack, levels, group_rows, cap),
        [HBM] * 4, f32(bricks * group_rows, LANES), HBM,
        (
            vmem(levels * per_level, LANES), pltpu.VMEM((per_level, LANES), jnp.int32),
            vmem(per_level, LANES), vmem(per_level, LANES),
            vmem(largest(per_level, 8, 4, 2, 1), groups * padded_rows, LANES),
            vmem(bricks * group_rows, LANES), dma((5,)),
        ),
        4, 10, 800000, "pack",
    )(*(in_hbm(flat(x)) for x in (kernel, sound_col, observed, obs_error)))
    received = lax.all_to_all(
        packed.reshape(-1, 1, LANES), ("lon", "lat"), split_axis=0, concat_axis=0, tiled=True
    ).reshape(-1, LANES)

    field = adjoint.reshape(levels * tracers, rows, LANES)
    east, north, mix = (in_hbm(flat(x)) for x in (wind_east, wind_north, mixing))
    rims = call(
        functools.partial(first_rims, levels, tracers, rows, chunks, per_chunk),
        [HBM] * 3,
        (f32(chunks, plane + rows, LANES),) + (f32(levels * tracers + levels, LANES),) * 2,
        (VMEM,) * 3,
        (vmem(levels * plane, LANES), vmem(levels * rows, LANES), vmem(levels * rows, LANES), dma((2 * chunks + 2,))),
        10, field_bytes, 2 * field_bytes, "first_rims",
    )(in_hbm(flat(adjoint)), east, north)
    start_rims = exchange(*rims)

    block = largest(levels, 24, 16, 8)
    sum_block = largest(levels, 12, 8)
    sums = call(
        functools.partial(tracer_sum, sum_block),
        [HBM], jax.ShapeDtypeStruct((2, levels * SUB, rows // SUB * cols), jnp.bfloat16), VMEM,
        (vmem(levels, tracers, rows, cols), dma((levels // sum_block,))),
        10, field_bytes // 4, field_bytes, "tracer_sum",
    )(concentration)

    width = largest(slots, 2 * LANES, LANES)
    parts = slots // width
    forcing, *rims, back = call(
        functools.partial(soundings, levels, rows, group_rows, cap, chunks, per_chunk, block),
        [VMEM] * 2,
        (
            f32(levels * rows + 2 * SUB, LANES), f32(chunks, rows, LANES), f32(levels, LANES), f32(levels, LANES),
            hbm(bricks, LANES),
        ),
        (VMEM,) * 4 + (HBM,),
        (
            vmem(parts, -(-groups * group_rows // SUB) * SUB, width),
            pltpu.VMEM((parts, width, rows // SUB * LANES), jnp.bfloat16),
            vmem(max(parts, SUB), width), vmem(bricks, LANES), dma((1,)),
        ),
        10, field_bytes * 8, field_bytes, "soundings",
    )(received, sums)
    forcing_rims = exchange_small(*rims)

    rim_shape, edge_shape = (chunks, plane, LANES), (2, levels * tracers, LANES)
    weight_shape = (7, levels * rows, LANES)
    weights, rim0, edges0 = call(
        functools.partial(coefficients, levels, tracers, rows, per_chunk, unroll),
        [HBM] * 3 + [VMEM] * 4,
        (f32(*weight_shape), f32(*rim_shape), f32(*edge_shape)),
        (VMEM,) * 3,
        (vmem(levels * rows, LANES),) * 3 + (dma((3, levels // unroll)),),
        4, field_bytes, field_bytes, "coefficients",
    )(east, north, mix, *start_rims)

    def advance(first, together, specs, operands, outs, out_specs, scratch):
        return call(
            functools.partial(step, levels, tracers, rows, chunks, per_chunk, together, first),
            specs, outs, out_specs,
            (vmem(levels * tracers + 2, rows, LANES), vmem(plane + rows, LANES))
            + scratch + (dma((2 * (levels // together) + 5,)),),
            22, field_bytes * 8, field_bytes * 2, "step",
        )(*operands)

    edge_rows = f32(levels * tracers, LANES)
    stepped, kept, *rims = advance(
        True, unroll, [HBM] + [VMEM] * 8, (in_hbm(field), weights, rim0, edges0, forcing, *forcing_rims),
        (hbm(*field.shape), hbm(*weight_shape), f32(*rim_shape), edge_rows, edge_rows), (HBM,) * 2 + (VMEM,) * 3,
        (vmem(chunks, rows, LANES), vmem(2, levels, LANES)),
    )
    (result,) = advance(
        False, unroll, [HBM] * 2 + [VMEM] * 4, (in_hbm(stepped), in_hbm(kept), *exchange(*rims)),
        (f32(*field.shape),), (HBM,),
        (vmem(*weight_shape), vmem(*rim_shape), vmem(*edge_shape), vmem(levels * tracers, rows, LANES)),
    )

    returned = lax.all_to_all(
        back.reshape(bricks, 1, LANES), ("lon", "lat"), split_axis=0, concat_axis=0, tiled=True
    )
    result, returned = lax.optimization_barrier((result, returned))
    residual = call(
        functools.partial(unpack_residual, cap), [VMEM], f32(per_level, LANES), VMEM, (), 2, 10, 10000, "residual",
    )(returned.reshape(bricks, LANES))
    return result.reshape(adjoint.shape), residual.reshape(sound_col.shape)


def solution(mesh):
    field = P(None, None, "lat", "lon")
    face = P(None, "lat", "lon")
    owned = P(None, ("lon", "lat"), None)
    return jax.shard_map(
        per_device,
        mesh=mesh,
        in_specs=(field, field, face, face, face, owned, owned, owned, owned),
        out_specs=(field, owned),
        check_vma=False,
    )
```

```python
import functools

import jax
import jax.numpy as jnp
from jax import lax
from jax.experimental import pallas as pl
from jax.experimental.pallas import tpu as pltpu
from jax.sharding import PartitionSpec as P

LANES = 128
SUB = 8
MIB = 1 << 20
ANY = pl.BlockSpec(memory_space=pl.ANY)
HBM = pl.BlockSpec(memory_space=pltpu.HBM)
VMEM = pl.BlockSpec(memory_space=pltpu.VMEM)


def rim_chunks(levels, unroll):
    per_chunk = 63 // unroll * unroll
    chunks = -(-levels // per_chunk)
    return chunks, -(-levels // (chunks * unroll)) * unroll


def lane_iota():
    return lax.broadcasted_iota(jnp.int32, (SUB, LANES), 1)


def sub_iota():
    return lax.broadcasted_iota(jnp.int32, (SUB, LANES), 0)


def largest(count, *choices):
    return next(u for u in choices if count % u == 0)


def in_hbm(x):
    return pltpu.with_memory_space_constraint(x, pltpu.HBM)


def hbm(*shape):
    return pltpu.HBM(shape, jnp.float32)


def f32(*shape):
    return jax.ShapeDtypeStruct(shape, jnp.float32)


def vmem(*shape):
    return pltpu.VMEM(shape, jnp.float32)


def call(body, ins, outs, out_specs, scratch, mib, flops, size, name):
    return pl.pallas_call(
        body,
        in_specs=ins,
        out_specs=out_specs,
        out_shape=outs,
        scratch_shapes=scratch,
        compiler_params=pltpu.CompilerParams(vmem_limit_bytes=mib * MIB),
        cost_estimate=pl.CostEstimate(flops=flops, bytes_accessed=size, transcendentals=0),
        name=name,
    )


def put_rims(field, offset, levels, per_chunk, chunk, out, first, plane, begin=0, end=None):
    lane = lane_iota()
    group = largest(plane // SUB, 16, 8, 4, 2, 1)
    count = min(per_chunk, levels - chunk * per_chunk)

    def body(i, carry):
        r = pl.multiple_of(i * SUB * group, SUB * group)
        made = [jnp.zeros((SUB, LANES), jnp.float32)] * group
        if begin:
            made = [
                out[chunk, pl.ds(pl.multiple_of(first + r + g * SUB, SUB), SUB), :] for g in range(group)
            ]
        for q in range(begin, count if end is None else end):
            for g in range(group):
                at = pl.multiple_of((chunk * per_chunk + q) * plane + offset + r + g * SUB, SUB)
                turned = pltpu.roll(field[pl.ds(at, SUB), :], 2 * q + 2, 1)
                made[g] = jnp.where(lane >= 2 * q + 1, turned, made[g])
        for g in range(group):
            out[chunk, pl.ds(pl.multiple_of(first + r + g * SUB, SUB), SUB), :] = made[g]
        return carry

    lax.fori_loop(0, plane // SUB // group, body, 0)


def row_places(rows):
    odd = lax.axis_index("lat") % 2
    return (1 - odd) * (rows - 1), odd * (rows - 1)


def put_rows(field, offset, a_ref, b_ref, rows, begin, end, places=None):
    unroll = largest((end - begin) // SUB, 9, 8, 4, 2, 1)
    in_a, in_b = places or row_places(rows)

    def body(i, carry):
        for u in range(unroll):
            start = pl.multiple_of(begin + (i * unroll + u) * SUB, SUB)
            at = start * rows + offset
            a_ref[pl.ds(start, SUB), :] = field[pl.ds(at + in_a, SUB, stride=rows), :]
            b_ref[pl.ds(start, SUB), :] = field[pl.ds(at + in_b, SUB, stride=rows), :]
        return carry

    lax.fori_loop(0, (end - begin) // SUB // unroll, body, 0)


def first_rims(levels, tracers, rows, chunks, per_chunk, field, east, north, side, a_ref, b_ref, f, e, n, sems):
    plane = tracers * rows
    wind_copies = [
        pltpu.make_async_copy(east, e, sems.at[2 * chunks]),
        pltpu.make_async_copy(north, n, sems.at[2 * chunks + 1]),
    ]
    pieces, copies = [], []
    for i in range(chunks):
        count = min(per_chunk, levels - i * per_chunk)
        for begin, end in ((0, count // 2), (count // 2, count)):
            pieces.append((i, begin, end))
            part = pl.ds((i * per_chunk + begin) * plane, (end - begin) * plane)
            copies.append(pltpu.make_async_copy(field.at[part], f.at[part], sems.at[len(copies)]))
    for copy in wind_copies + copies:
        copy.start()
    wind_copies[0].wait()
    for i in range(chunks):
        put_rims(e, 0, levels, per_chunk, i, side, plane, rows)
    wind_copies[1].wait()
    winds = pl.ds(levels * tracers, levels)
    put_rows(n, 0, a_ref.at[winds], b_ref.at[winds], rows, 0, levels)
    for copy, (i, begin, end) in zip(copies, pieces):
        copy.wait()
        put_rims(f, 0, levels, per_chunk, i, side, 0, plane, begin, end)
        at = i * per_chunk * tracers
        put_rows(f, 0, a_ref, b_ref, rows, at + begin * tracers, at + end * tracers)


def meet(rim, target, from_west, from_east, count):
    lane = lane_iota()
    for chunk in range(rim.shape[0]):
        for r in range(0, count, SUB):
            rows = pl.ds(r, SUB)
            turned = pltpu.roll(from_east[chunk, rows, :], LANES - 2, 1)
            rim[chunk, pl.ds(target + r, SUB), :] = jnp.where(lane % 2 == 1, from_west[chunk, rows, :], turned)


def pair(edges, target, from_a, from_b, count):
    even = jnp.full((SUB, LANES), lax.axis_index("lat"), jnp.int32) % 2 == 0
    repeat = largest(count // SUB, 9, 8, 4, 2, 1)

    def body(i, carry):
        for u in range(repeat):
            at = pl.multiple_of((i * repeat + u) * SUB, SUB)
            a, b = from_a[pl.ds(at, SUB), :], from_b[pl.ds(at, SUB), :]
            edges[0, pl.ds(target + at, SUB), :] = jnp.where(even, a, b)
            edges[1, pl.ds(target + at, SUB), :] = jnp.where(even, b, a)
        return carry

    lax.fori_loop(0, count // SUB // repeat, body, 0)


def coefficients(
    levels, tracers, rows, per_chunk, unroll, east, north, mixing, west0, east0, a0, b0, *refs
):
    weights, rim, edges, e_buf, n_buf, m_buf, sems = refs
    plane = tracers * rows
    halves = rows // SUB
    lane, sub = lane_iota(), sub_iota()
    blocks = levels // unroll

    def load(b):
        at = pl.ds(pl.multiple_of(b * unroll * rows, SUB), unroll * rows)
        return [
            pltpu.make_async_copy(source.at[at], target.at[at], sems.at[i, b])
            for i, (source, target) in enumerate(((mixing, m_buf), (east, e_buf), (north, n_buf)))
        ]

    for b in range(blocks):
        for copy in load(b):
            copy.start()
    meet(rim, 0, west0, east0, plane)
    pair(edges, 0, a0, b0, levels * tracers)
    place = lax.axis_index("lat")
    even = jnp.full((1, LANES), place, jnp.int32) % 2 == 0
    south_flag = (place > 0).astype(jnp.float32)
    north_flag = (place < lax.axis_size("lat") - 1).astype(jnp.float32)
    north_mask = jnp.where(sub == SUB - 1, north_flag, 1.0)

    def level(k, pivots):
        chunk, q = k // per_chunk, k % per_chunk
        has_up = (k < levels - 1).astype(jnp.float32)
        new, edge = [], None
        for h in range(halves):
            blk = pl.ds(pl.multiple_of(k * rows + h * SUB, SUB), SUB)
            down, factor = pivots[h]
            up = m_buf[blk, :] * has_up
            inv = 1.0 / (1.0 + up + down - down * factor)
            factor = up * inv
            new.append((up, factor))
            e, n = e_buf[blk, :], n_buf[blk, :]
            side = pltpu.roll(west0[chunk, pl.ds(plane + h * SUB, SUB), :], LANES - 1 - 2 * q, 1)
            w_in = jnp.minimum(jnp.where(lane == 0, side, pltpu.roll(e, 1, 1)), 0.0)
            if h == 0:
                row = pl.ds(levels * tracers + k, 1)
                edge = jnp.where(even, b0[row, :], a0[row, :]) * south_flag
            s_in = jnp.minimum(jnp.where(sub == 0, edge, pltpu.roll(n, 1, 0)), 0.0)
            edge = n[SUB - 1 : SUB, :]
            e_out, n_out = jnp.maximum(e, 0.0), jnp.maximum(n, 0.0)
            from_n = n_out * inv
            if h == halves - 1:
                from_n = from_n * north_mask
            stay = (1.0 - e_out + w_in - n_out + s_in) * inv
            from_e, from_w = e_out * inv, -(w_in * inv)
            values = (stay, from_e, from_w, from_n, -(s_in * inv), down * inv, factor)
            for i, value in enumerate(values):
                weights[i, blk, :] = value
        return tuple(new)

    def body(b, carry):
        for copy in load(b):
            copy.wait()
        for u in range(unroll):
            carry = level(b * unroll + u, carry)
        return carry

    zero = jnp.zeros((SUB, LANES), jnp.float32)
    lax.fori_loop(0, blocks, body, ((zero, zero),) * halves)


def step(levels, tracers, rows, chunks, per_chunk, unroll, first, *refs):
    if first:
        field, weights, rim, edges, forcing, f_west, f_east, f_north, f_south = refs[:9]
        out, weights_out, side_ref, a_ref, b_ref = refs[9:14]
        buf, rim_now, f_rim, f_edges, sems = refs[14:]
    else:
        field, weights_in, west_in, east_in, a_in, b_in, out = refs[:7]
        buf, rim_now, weights, rim, edges, solved_buf, sems = refs[7:]

    plane = tracers * rows
    halves = rows // SUB
    lane, sub = lane_iota(), sub_iota()
    blocks = levels // unroll
    flat = buf.reshape((levels * tracers + 2) * rows, LANES)

    def load(b):
        at = b * unroll * tracers
        return pltpu.make_async_copy(
            field.at[pl.ds(at, unroll * tracers)], buf.at[pl.ds(at + 1, unroll * tracers)], sems.at[b]
        )

    if first:
        solved_buf, solved_at = buf, 1
        solved_ref = flat
    else:
        solved_at = 0
        solved_ref = solved_buf.reshape(levels * tracers * rows, LANES)

    def store(b):
        at = b * unroll * tracers
        return pltpu.make_async_copy(
            solved_buf.at[pl.ds(at + solved_at, unroll * tracers)], out.at[pl.ds(at, unroll * tracers)], sems.at[b]
        )

    last = 2 * blocks
    above = weights.at[weights.shape[0] - 1]
    if first:
        keep = pltpu.make_async_copy(weights, weights_out, sems.at[last])
        for b in range(blocks):
            load(b).start()
        keep.start()
        meet(f_rim, 0, f_west, f_east, rows)
        f_edges[0] = f_north[...]
        f_edges[1] = f_south[...]
    else:
        above_copy = pltpu.make_async_copy(weights_in.at[weights.shape[0] - 1], above, sems.at[last])
        def load_weights(b):
            planes, levels_of = pl.ds(0, weights.shape[0] - 1), pl.ds(b * unroll * rows, unroll * rows)
            return pltpu.make_async_copy(
                weights_in.at[planes, levels_of], weights.at[planes, levels_of], sems.at[blocks + b]
            )

        for b in range(blocks):
            load(b).start()
            load_weights(b).start()
        above_copy.start()
        meet(rim, 0, west_in, east_in, plane)
        pair(edges, 0, a_in, b_in, levels * tracers)

    def stencil(near, cells, here, side, edge, row, co, wanted=range(rows // SUB)):
        halfs = [cells[pl.ds(here + h * SUB, SUB), :] for h in range(halves)]
        values = []
        for h in wanted:
            cell = halfs[h]
            if h == halves - 1:
                n = jnp.where(sub == SUB - 1, edge[0, pl.ds(row, 1), :], pltpu.roll(cell, SUB - 1, 0))
            elif near is not None:
                n = near[0][pl.ds(near[1] + here + h * SUB + 1, SUB), :]
            else:
                n = jnp.where(sub == SUB - 1, pltpu.roll(halfs[h + 1], SUB - 1, 0), pltpu.roll(cell, SUB - 1, 0))
            if h == 0:
                s = jnp.where(sub == 0, edge[1, pl.ds(row, 1), :], pltpu.roll(cell, 1, 0))
            elif near is not None:
                s = near[0][pl.ds(near[1] + here + h * SUB - 1, SUB), :]
            else:
                s = jnp.where(sub == 0, pltpu.roll(halfs[h - 1], 1, 0), pltpu.roll(cell, 1, 0))
            c0, ce, cw, cn, cs, rims = co[h][:6]
            value = (c0 * cell + ce * pltpu.roll(cell, LANES - 1, 1)) + (cw * pltpu.roll(cell, 1, 1) + cn * n)
            values.append(value + (cs * s + rims * side(h)))
        return values

    def part(ref, b, size, offset=0):
        return ref.at[pl.ds(pl.multiple_of(b * unroll * size + offset, SUB), unroll * size)]

    def turned_rims(b, source, count, first_row):
        chunk, q = b * unroll // per_chunk, b * unroll % per_chunk
        for r in range(0, count, SUB):
            turned = pltpu.roll(source[chunk, pl.ds(r, SUB), :], (LANES - 2 * q) % LANES, 1)
            rim_now[pl.ds(first_row + r, SUB), :] = turned

    def side(u, r):
        return lambda h: pltpu.roll(rim_now[pl.ds(r + h * SUB, SUB), :], LANES - 1 - 2 * u, 1)

    def weights_of(b):
        co_part = weights.at[:, pl.ds(pl.multiple_of(b * unroll * rows, SUB), unroll * rows)]

        def one(u, h):
            c0, ce, cw, cn, cs, a = (
                co_part[i, pl.ds(u * rows + h * SUB, SUB), :] for i in range(weights.shape[0] - 1)
            )
            first_col, last_col = lane == 0, lane == LANES - 1
            rims = jnp.where(first_col, cw, jnp.where(last_col, ce, 0.0))
            return c0, jnp.where(last_col, 0.0, ce), jnp.where(first_col, 0.0, cw), cn, cs, rims, a

        return lambda u: [one(u, h) for h in range(halves)]

    def forward_block(b, solved):
        load(b).wait()
        if not first:
            load_weights(b).wait()
        turned_rims(b, rim, plane, 0)
        cells, co_of = part(flat, b, plane, rows), weights_of(b)
        edge = edges.at[:, pl.ds(pl.multiple_of(b * unroll * tracers, SUB), unroll * tracers)]
        if first:
            turned_rims(b, f_rim, rows, plane)
            f_cells = part(forcing, b, rows, SUB)
            f_edge = f_edges.at[:, pl.ds(pl.multiple_of(b * unroll, SUB), unroll)]
        else:
            solves = part(solved_ref, b, plane)
        for u in range(unroll):
            co = co_of(u)
            new = []
            if first:
                extra = stencil((forcing, b * unroll * rows + SUB), f_cells, u * rows, side(u, plane), f_edge, u, co)
                for t in range(tracers):
                    here = u * plane + t * rows
                    near = (flat, b * unroll * plane + rows)
                    values = stencil(near, cells, here, side(u, t * rows), edge, u * tracers + t, co)
                    for h in range(halves):
                        value = values[h] + extra[h] + co[h][6] * solved[h * tracers + t]
                        new.append(value)
                        cells[pl.ds(here + h * SUB, SUB), :] = value
                solved = tuple(new[t * halves + h] for h in range(halves) for t in range(tracers))
            else:
                for h in range(halves):
                    for t in range(tracers):
                        here = u * plane + t * rows
                        (value,) = stencil(
                            None, cells, here, side(u, t * rows), edge, u * tracers + t, co, (h,)
                        )
                        value = value + co[h][6] * solved[h * tracers + t]
                        new.append(value)
                        solves[pl.ds(here + h * SUB, SUB), :] = value
                solved = tuple(new)
        return solved

    zero = jnp.zeros((SUB, LANES), jnp.float32)
    zeros = (zero,) * (tracers * halves)
    lax.fori_loop(0, blocks, forward_block, zeros)
    if not first:
        above_copy.wait()

    def backward_block(i, later):
        b = blocks - 1 - i
        cells = part(solved_ref, b, plane, solved_at * rows)
        factors = part(above, b, rows)
        for u in reversed(range(unroll)):
            new = []
            for h in range(halves):
                factor = factors[pl.ds(u * rows + h * SUB, SUB), :]
                for t in range(tracers):
                    blk = pl.ds(u * plane + t * rows + h * SUB, SUB)
                    value = cells[blk, :] + factor * later[h * tracers + t]
                    cells[blk, :] = value
                    new.append(value)
            later = tuple(new)
        store(b).start()
        return later

    lax.fori_loop(0, blocks, backward_block, zeros)
    if first:
        for chunk in range(chunks):
            put_rims(flat, rows, levels, per_chunk, chunk, side_ref, 0, plane)
        put_rows(flat, rows, a_ref, b_ref, rows, 0, levels * tracers)
        keep.wait()
    for b in range(blocks):
        store(b).wait()


def row_offsets(count):
    return list(range(0, count - SUB, SUB)) + [count - SUB]


def pack(levels, group_rows, cap, kernel, columns, observed, errors, out, k_buf, c_buf, o_buf, e_buf, wide, out_buf, sems):
    lane = lane_iota()
    copies = [
        pltpu.make_async_copy(source, target, sems.at[i])
        for i, (source, target) in enumerate(
            ((columns, c_buf), (observed, o_buf), (errors, e_buf), (kernel, k_buf))
        )
    ]
    for copy in copies:
        copy.start()
    for copy in copies:
        copy.wait()
    per_level = columns.shape[0]
    groups = LANES // cap
    offsets = row_offsets(group_rows)
    padded = wide.shape[1] // groups
    together = wide.shape[0]

    def body(start, carry):
        for n in range(together):
            i = start * together + n
            one = pl.ds(i, 1)
            for g in range(groups):
                begin = g * group_rows
                count = min(group_rows, levels - begin)
                wide[n, pl.ds(g * padded, count), :] = k_buf[
                    pl.ds(i + per_level * begin, count, stride=per_level), :
                ]
            end = (groups - 1) * padded + levels - (groups - 1) * group_rows
            for m, row in enumerate((c_buf[one, :].astype(jnp.float32), o_buf[one, :], e_buf[one, :])):
                wide[n, pl.ds(end + m, 1), :] = row
            for m in range(end + 3, (groups - 1) * padded + group_rows):
                wide[n, pl.ds(m, 1), :] = jnp.zeros((1, LANES), jnp.float32)
        for n in range(together):
            i = start * together + n
            for j in range(groups):
                for m in offsets:
                    made = None
                    for g in range(groups):
                        piece = wide[n, pl.ds(g * padded + m, SUB), :]
                        if g != j:
                            piece = pltpu.roll(piece, (g - j) * cap % LANES, 1)
                        made = piece if made is None else jnp.where(lane >= g * cap, piece, made)
                    out_buf[pl.ds((i * groups + j) * group_rows + m, SUB), :] = made
        return carry

    if per_level == together:
        body(0, 0)
    else:
        lax.fori_loop(0, per_level // together, body, 0)
    done = pltpu.make_async_copy(out_buf, out, sems.at[4])
    done.start()
    done.wait()


def tracer_sum(block, concentration, out, buf, sems):
    levels, tracers, rows, cols = buf.shape

    def load(b):
        return pltpu.make_async_copy(
            concentration.at[pl.ds(b * block, block)], buf.at[pl.ds(b * block, block)], sems.at[b]
        )

    for b in range(levels // block):
        load(b).start()

    def body(b, carry):
        load(b).wait()
        for h in range(rows // SUB):
            tops, rests = [], []
            for k in range(block):
                part = jnp.sum(buf[b * block + k, :, pl.ds(h * SUB, SUB), :], axis=0)
                top = part.astype(jnp.bfloat16).astype(jnp.float32)
                tops.append(top)
                rests.append(part - top)
            at = pl.ds(pl.multiple_of(b * block * SUB, 2 * SUB), block * SUB)
            rest_at = pl.ds(pl.multiple_of((levels + b * block) * SUB, 2 * SUB), block * SUB)
            lanes = pl.ds(h * cols, cols)
            out[at, lanes] = jnp.concatenate(tops, axis=0).astype(jnp.bfloat16)
            out[rest_at, lanes] = jnp.concatenate(rests, axis=0).astype(jnp.bfloat16)
        return carry

    lax.fori_loop(0, levels // block, body, 0)


def soundings(
    levels, rows, group_rows, cap, chunks, per_chunk, block,
    received, sums, forcing, side_ref, a_ref, b_ref, back_out,
    arrived, table, scaled, back, seen, spread, gathered, sem
):
    lane = lane_iota()
    parts, _, width = arrived.shape
    halves = rows // SUB
    keys = halves * LANES
    groups = LANES // cap

    def unpack_one(c):
        part, col = c // (width // LANES), c % (width // LANES)
        for g in range(groups):
            for m in row_offsets(group_rows):
                made = None
                for p in range(groups):
                    piece = received[pl.ds((c * groups + p) * group_rows + m, SUB), :]
                    if p != g:
                        piece = pltpu.roll(piece, (p - g) * cap % LANES, 1)
                    made = piece if made is None else jnp.where(lane >= p * cap, piece, made)
                lanes = pl.ds(pl.multiple_of(col * LANES, LANES), LANES)
                arrived[part, pl.ds(g * group_rows + m, SUB), lanes] = made

    at_once = largest(parts * width // LANES, 4, 2, 1)

    def unpack(i, carry):
        for n in range(at_once):
            unpack_one(i * at_once + n)
        return carry

    lax.fori_loop(0, parts * width // LANES // at_once, unpack, 0)

    sub_index = lax.broadcasted_iota(jnp.int32, (SUB, width), 0)
    key_index = lax.broadcasted_iota(jnp.int32, (keys, width), 0)
    turned_index = lax.broadcasted_iota(jnp.int32, (LANES, keys), 1)

    def columns(j):
        return arrived[j, pl.ds(levels, 1), :].astype(jnp.int32)

    def key_of(col):
        return (col >> 10) * LANES + (col & (LANES - 1))

    def mask_of(j):
        return sub_index == ((columns(j) >> 7) & (SUB - 1))

    for j in range(parts):
        col = columns(j)
        key = key_of(col)
        look = jnp.where(key_index == key, 1.0, 0.0).astype(jnp.bfloat16)
        for c in range(width // LANES):
            piece = key[:, c * LANES : (c + 1) * LANES].astype(jnp.float32)
            across = jnp.broadcast_to(piece, (LANES, LANES)).T.astype(jnp.int32)
            across = jnp.concatenate([across] * halves, axis=1)
            table[j, pl.ds(c * LANES, LANES), :] = jnp.where(turned_index == across, 1.0, 0.0).astype(
                jnp.bfloat16
            )
        total = jnp.zeros((SUB, width), jnp.float32)
        seen[...] = jnp.dot(sums[...], look, preferred_element_type=jnp.float32)
        for k in range(levels):
            at = k * SUB
            both = seen[pl.ds(at, SUB), :] + seen[pl.ds(levels * SUB + at, SUB), :]
            total += arrived[j, pl.ds(k, 1), :] * both
        modelled = jnp.sum(jnp.where(mask_of(j), total, 0.0), axis=0, keepdims=True)
        observed = arrived[j, pl.ds(levels + 1, 1), :]
        error = arrived[j, pl.ds(levels + 2, 1), :]
        residual = jnp.where(col >= 0, (modelled - observed) / error, 0.0)
        scaled[pl.ds(j, 1), :] = residual / error
        for i in range(width // cap):
            at = i * cap
            piece = residual[:, at // LANES * LANES : at // LANES * LANES + LANES]
            if at % LANES:
                piece = pltpu.roll(piece, LANES - at % LANES, 1)
            back[pl.ds(j * (width // cap) + i, 1), :] = piece

    leave = pltpu.make_async_copy(back, back_out, sem.at[0])
    leave.start()
    zeros = jnp.zeros((SUB, LANES), jnp.float32)
    forcing[pl.ds(0, SUB), :] = zeros
    forcing[pl.ds(levels * rows + SUB, SUB), :] = zeros
    for j in range(parts):
        mask = mask_of(j)
        for b in range(levels // block):
            weight = arrived[j, pl.ds(b * block, block), :] * scaled[pl.ds(j, 1), :]
            top = weight.astype(jnp.bfloat16).astype(jnp.float32)
            for first_row, part in ((0, top), (levels * SUB, weight - top)):
                spread[pl.ds(first_row + b * block * SUB, block * SUB), :] = jnp.concatenate(
                    [jnp.where(mask, part[k : k + 1, :], 0.0) for k in range(block)], axis=0
                ).astype(jnp.bfloat16)
        made = jnp.dot(spread[...], table[j, :, :], preferred_element_type=jnp.float32)
        made = made[: levels * SUB, :] + made[levels * SUB :, :]
        gathered[...] = made if j == 0 else gathered[...] + made
    for k in range(levels):
        for h in range(halves):
            forcing[pl.ds(k * rows + (h + 1) * SUB, SUB), :] = gathered[
                pl.ds(k * SUB, SUB), pl.ds(h * LANES, LANES)
            ]

    for chunk in range(chunks):
        put_rims(forcing, SUB, levels, per_chunk, chunk, side_ref, 0, rows)
    put_rows(forcing, SUB, a_ref, b_ref, rows, 0, levels, (0, rows - 1))
    leave.wait()


def unpack_residual(cap, arrived, out):
    lane = lax.broadcasted_iota(jnp.int32, (1, LANES), 1)
    groups = LANES // cap
    for row in range(out.shape[0]):
        made = None
        for g in range(groups):
            piece = arrived[pl.ds(row * groups + g, 1), :]
            if g:
                piece = pltpu.roll(piece, g * cap, 1)
            made = piece if made is None else jnp.where(lane >= g * cap, piece, made)
        out[pl.ds(row, 1), :] = made


def turn(value, axis, by):
    count = lax.axis_size(axis)
    return lax.ppermute(value, axis, [(i, (i + by) % count) for i in range(count)])


def exchange(side_rim, a_rim, b_rim):
    lats = lax.axis_size("lat")

    def partner(j, odd):
        other = j + 1 if j % 2 == odd else j - 1
        return other if 0 <= other < lats else j

    return (
        turn(side_rim, "lon", 1),
        turn(side_rim, "lon", -1),
        lax.ppermute(a_rim, "lat", [(j, partner(j, 0)) for j in range(lats)]),
        lax.ppermute(b_rim, "lat", [(j, partner(j, 1)) for j in range(lats)]),
    )


def exchange_small(side_rim, first_rows, last_rows):
    return (
        turn(side_rim, "lon", 1),
        turn(side_rim, "lon", -1),
        turn(first_rows, "lat", -1),
        turn(last_rows, "lat", 1),
    )


def per_device(
    concentration, adjoint, wind_east, wind_north, mixing, sound_col, kernel, observed, obs_error
):
    levels, tracers, rows, cols = adjoint.shape
    bricks = lax.axis_size("lon") * lax.axis_size("lat")
    slots = sound_col.shape[2]
    cap = slots // bricks
    unroll = largest(levels, 8, 4, 3, 2, 1)
    chunks, per_chunk = rim_chunks(levels, unroll)
    plane = tracers * rows
    per_level = slots // LANES
    groups = LANES // cap
    group_rows = -(-(levels + 3) // groups)
    padded_rows = -(-group_rows // SUB) * SUB
    field_bytes = levels * plane * cols * 4
    dma = pltpu.SemaphoreType.DMA

    def flat(x):
        return x.reshape(-1, LANES)

    packed = call(
        functools.partial(pack, levels, group_rows, cap),
        [HBM] * 4, f32(bricks * group_rows, LANES), HBM,
        (
            vmem(levels * per_level, LANES), pltpu.VMEM((per_level, LANES), jnp.int32),
            vmem(per_level, LANES), vmem(per_level, LANES),
            vmem(largest(per_level, 8, 4, 2, 1), groups * padded_rows, LANES),
            vmem(bricks * group_rows, LANES), dma((5,)),
        ),
        4, 10, 800000, "pack",
    )(*(in_hbm(flat(x)) for x in (kernel, sound_col, observed, obs_error)))
    received = lax.all_to_all(
        packed.reshape(-1, 1, LANES), ("lon", "lat"), split_axis=0, concat_axis=0, tiled=True
    ).reshape(-1, LANES)

    field = adjoint.reshape(levels * tracers, rows, LANES)
    east, north, mix = (in_hbm(flat(x)) for x in (wind_east, wind_north, mixing))
    rims = call(
        functools.partial(first_rims, levels, tracers, rows, chunks, per_chunk),
        [HBM] * 3,
        (f32(chunks, plane + rows, LANES),) + (f32(levels * tracers + levels, LANES),) * 2,
        (VMEM,) * 3,
        (vmem(levels * plane, LANES), vmem(levels * rows, LANES), vmem(levels * rows, LANES), dma((2 * chunks + 2,))),
        10, field_bytes, 2 * field_bytes, "first_rims",
    )(in_hbm(flat(adjoint)), east, north)
    start_rims = exchange(*rims)

    block = largest(levels, 24, 16, 8)
    sum_block = largest(levels, 12, 8)
    sums = call(
        functools.partial(tracer_sum, sum_block),
        [HBM], jax.ShapeDtypeStruct((2 * levels * SUB, rows // SUB * cols), jnp.bfloat16), VMEM,
        (vmem(levels, tracers, rows, cols), dma((levels // sum_block,))),
        10, field_bytes // 4, field_bytes, "tracer_sum",
    )(concentration)

    width = largest(slots, 2 * LANES, LANES)
    parts = slots // width
    forcing, *rims, back = call(
        functools.partial(soundings, levels, rows, group_rows, cap, chunks, per_chunk, block),
        [VMEM] * 2,
        (
            f32(levels * rows + 2 * SUB, LANES), f32(chunks, rows, LANES), f32(levels, LANES), f32(levels, LANES),
            hbm(bricks, LANES),
        ),
        (VMEM,) * 4 + (HBM,),
        (
            vmem(parts, -(-groups * group_rows // SUB) * SUB, width),
            pltpu.VMEM((parts, width, rows // SUB * LANES), jnp.bfloat16),
            vmem(max(parts, SUB), width), vmem(bricks, LANES),
            vmem(2 * levels * SUB, width), pltpu.VMEM((2 * levels * SUB, width), jnp.bfloat16),
            vmem(levels * SUB, rows // SUB * LANES), dma((1,)),
        ),
        16, field_bytes * 8, field_bytes, "soundings",
    )(received, sums)
    forcing_rims = exchange_small(*rims)

    rim_shape, edge_shape = (chunks, plane, LANES), (2, levels * tracers, LANES)
    weight_shape = (7, levels * rows, LANES)
    weights, rim0, edges0 = call(
        functools.partial(coefficients, levels, tracers, rows, per_chunk, unroll),
        [HBM] * 3 + [VMEM] * 4,
        (f32(*weight_shape), f32(*rim_shape), f32(*edge_shape)),
        (VMEM,) * 3,
        (vmem(levels * rows, LANES),) * 3 + (dma((3, levels // unroll)),),
        4, field_bytes, field_bytes, "coefficients",
    )(east, north, mix, *start_rims)

    def advance(first, together, specs, operands, outs, out_specs, scratch):
        return call(
            functools.partial(step, levels, tracers, rows, chunks, per_chunk, together, first),
            specs, outs, out_specs,
            (vmem(levels * tracers + 2, rows, LANES), vmem(plane + rows, LANES))
            + scratch + (dma((2 * (levels // together) + 5,)),),
            22, field_bytes * 8, field_bytes * 2, "step",
        )(*operands)

    edge_rows = f32(levels * tracers, LANES)
    stepped, kept, *rims = advance(
        True, unroll, [HBM] + [VMEM] * 8, (in_hbm(field), weights, rim0, edges0, forcing, *forcing_rims),
        (hbm(*field.shape), hbm(*weight_shape), f32(*rim_shape), edge_rows, edge_rows), (HBM,) * 2 + (VMEM,) * 3,
        (vmem(chunks, rows, LANES), vmem(2, levels, LANES)),
    )
    (result,) = advance(
        False, largest(unroll, 4, 3, 2, 1), [HBM] * 2 + [VMEM] * 4, (in_hbm(stepped), in_hbm(kept), *exchange(*rims)),
        (f32(*field.shape),), (HBM,),
        (vmem(*weight_shape), vmem(*rim_shape), vmem(*edge_shape), vmem(levels * tracers, rows, LANES)),
    )

    returned = lax.all_to_all(
        back.reshape(bricks, 1, LANES), ("lon", "lat"), split_axis=0, concat_axis=0, tiled=True
    )
    result, returned = lax.optimization_barrier((result, returned))
    residual = call(
        functools.partial(unpack_residual, cap), [VMEM], f32(per_level, LANES), VMEM, (), 2, 10, 10000, "residual",
    )(returned.reshape(bricks, LANES))
    return result.reshape(adjoint.shape), residual.reshape(sound_col.shape)


def solution(mesh):
    field = P(None, None, "lat", "lon")
    face = P(None, "lat", "lon")
    owned = P(None, ("lon", "lat"), None)
    return jax.shard_map(
        per_device,
        mesh=mesh,
        in_specs=(field, field, face, face, face, owned, owned, owned, owned),
        out_specs=(field, owned),
        check_vma=False,
    )
```

```python
import functools

import jax
import jax.numpy as jnp
from jax import lax
from jax.experimental import pallas as pl
from jax.experimental.pallas import tpu as pltpu
from jax.sharding import PartitionSpec as P

LANES = 128
SUB = 8
MIB = 1 << 20
ANY = pl.BlockSpec(memory_space=pl.ANY)
HBM = pl.BlockSpec(memory_space=pltpu.HBM)
VMEM = pl.BlockSpec(memory_space=pltpu.VMEM)


def rim_chunks(levels, unroll):
    per_chunk = 63 // unroll * unroll
    chunks = -(-levels // per_chunk)
    return chunks, -(-levels // (chunks * unroll)) * unroll


def lane_iota():
    return lax.broadcasted_iota(jnp.int32, (SUB, LANES), 1)


def sub_iota():
    return lax.broadcasted_iota(jnp.int32, (SUB, LANES), 0)


def largest(count, *choices):
    return next(u for u in choices if count % u == 0)


def in_hbm(x):
    return pltpu.with_memory_space_constraint(x, pltpu.HBM)


def hbm(*shape):
    return pltpu.HBM(shape, jnp.float32)


def f32(*shape):
    return jax.ShapeDtypeStruct(shape, jnp.float32)


def vmem(*shape):
    return pltpu.VMEM(shape, jnp.float32)


def call(body, ins, outs, out_specs, scratch, mib, flops, size, name):
    return pl.pallas_call(
        body,
        in_specs=ins,
        out_specs=out_specs,
        out_shape=outs,
        scratch_shapes=scratch,
        compiler_params=pltpu.CompilerParams(vmem_limit_bytes=mib * MIB),
        cost_estimate=pl.CostEstimate(flops=flops, bytes_accessed=size, transcendentals=0),
        name=name,
    )


def put_rims(field, offset, levels, per_chunk, chunk, out, first, plane, begin=0, end=None):
    lane = lane_iota()
    group = largest(plane // SUB, 16, 8, 4, 2, 1)
    count = min(per_chunk, levels - chunk * per_chunk)

    def body(i, carry):
        r = pl.multiple_of(i * SUB * group, SUB * group)
        made = [jnp.zeros((SUB, LANES), jnp.float32)] * group
        if begin:
            made = [
                out[chunk, pl.ds(pl.multiple_of(first + r + g * SUB, SUB), SUB), :] for g in range(group)
            ]
        for q in range(begin, count if end is None else end):
            for g in range(group):
                at = pl.multiple_of((chunk * per_chunk + q) * plane + offset + r + g * SUB, SUB)
                turned = pltpu.roll(field[pl.ds(at, SUB), :], 2 * q + 2, 1)
                made[g] = jnp.where(lane >= 2 * q + 1, turned, made[g])
        for g in range(group):
            out[chunk, pl.ds(pl.multiple_of(first + r + g * SUB, SUB), SUB), :] = made[g]
        return carry

    lax.fori_loop(0, plane // SUB // group, body, 0)


def row_places(rows):
    odd = lax.axis_index("lat") % 2
    return (1 - odd) * (rows - 1), odd * (rows - 1)


def put_rows(field, offset, a_ref, b_ref, rows, begin, end, places=None):
    unroll = largest((end - begin) // SUB, 9, 8, 4, 2, 1)
    in_a, in_b = places or row_places(rows)

    def body(i, carry):
        for u in range(unroll):
            start = pl.multiple_of(begin + (i * unroll + u) * SUB, SUB)
            at = start * rows + offset
            a_ref[pl.ds(start, SUB), :] = field[pl.ds(at + in_a, SUB, stride=rows), :]
            b_ref[pl.ds(start, SUB), :] = field[pl.ds(at + in_b, SUB, stride=rows), :]
        return carry

    lax.fori_loop(0, (end - begin) // SUB // unroll, body, 0)


def first_rims(levels, tracers, rows, chunks, per_chunk, field, east, north, side, a_ref, b_ref, f, e, n, sems):
    plane = tracers * rows
    wind_copies = [
        pltpu.make_async_copy(east, e, sems.at[2 * chunks]),
        pltpu.make_async_copy(north, n, sems.at[2 * chunks + 1]),
    ]
    pieces, copies = [], []
    for i in range(chunks):
        count = min(per_chunk, levels - i * per_chunk)
        for begin, end in ((0, count // 2), (count // 2, count)):
            pieces.append((i, begin, end))
            part = pl.ds((i * per_chunk + begin) * plane, (end - begin) * plane)
            copies.append(pltpu.make_async_copy(field.at[part], f.at[part], sems.at[len(copies)]))
    for copy in wind_copies + copies:
        copy.start()
    wind_copies[0].wait()
    for i in range(chunks):
        put_rims(e, 0, levels, per_chunk, i, side, plane, rows)
    wind_copies[1].wait()
    winds = pl.ds(levels * tracers, levels)
    put_rows(n, 0, a_ref.at[winds], b_ref.at[winds], rows, 0, levels)
    for copy, (i, begin, end) in zip(copies, pieces):
        copy.wait()
        put_rims(f, 0, levels, per_chunk, i, side, 0, plane, begin, end)
        at = i * per_chunk * tracers
        put_rows(f, 0, a_ref, b_ref, rows, at + begin * tracers, at + end * tracers)


def meet(rim, target, from_west, from_east, count):
    lane = lane_iota()
    for chunk in range(rim.shape[0]):
        for r in range(0, count, SUB):
            rows = pl.ds(r, SUB)
            turned = pltpu.roll(from_east[chunk, rows, :], LANES - 2, 1)
            rim[chunk, pl.ds(target + r, SUB), :] = jnp.where(lane % 2 == 1, from_west[chunk, rows, :], turned)


def pair(edges, target, from_a, from_b, count):
    even = jnp.full((SUB, LANES), lax.axis_index("lat"), jnp.int32) % 2 == 0
    repeat = largest(count // SUB, 9, 8, 4, 2, 1)

    def body(i, carry):
        for u in range(repeat):
            at = pl.multiple_of((i * repeat + u) * SUB, SUB)
            a, b = from_a[pl.ds(at, SUB), :], from_b[pl.ds(at, SUB), :]
            edges[0, pl.ds(target + at, SUB), :] = jnp.where(even, a, b)
            edges[1, pl.ds(target + at, SUB), :] = jnp.where(even, b, a)
        return carry

    lax.fori_loop(0, count // SUB // repeat, body, 0)


def coefficients(
    levels, tracers, rows, per_chunk, unroll, east, north, mixing, west0, east0, a0, b0, *refs
):
    weights, rim, edges, e_buf, n_buf, m_buf, sems = refs
    plane = tracers * rows
    halves = rows // SUB
    lane, sub = lane_iota(), sub_iota()
    blocks = levels // unroll

    def load(b):
        at = pl.ds(pl.multiple_of(b * unroll * rows, SUB), unroll * rows)
        return [
            pltpu.make_async_copy(source.at[at], target.at[at], sems.at[i, b])
            for i, (source, target) in enumerate(((mixing, m_buf), (east, e_buf), (north, n_buf)))
        ]

    for b in range(blocks):
        for copy in load(b):
            copy.start()
    meet(rim, 0, west0, east0, plane)
    pair(edges, 0, a0, b0, levels * tracers)
    place = lax.axis_index("lat")
    even = jnp.full((1, LANES), place, jnp.int32) % 2 == 0
    south_flag = (place > 0).astype(jnp.float32)
    north_flag = (place < lax.axis_size("lat") - 1).astype(jnp.float32)
    north_mask = jnp.where(sub == SUB - 1, north_flag, 1.0)

    def level(k, pivots):
        chunk, q = k // per_chunk, k % per_chunk
        has_up = (k < levels - 1).astype(jnp.float32)
        new, edge = [], None
        for h in range(halves):
            blk = pl.ds(pl.multiple_of(k * rows + h * SUB, SUB), SUB)
            down, factor = pivots[h]
            up = m_buf[blk, :] * has_up
            inv = 1.0 / (1.0 + up + down - down * factor)
            factor = up * inv
            new.append((up, factor))
            e, n = e_buf[blk, :], n_buf[blk, :]
            side = pltpu.roll(west0[chunk, pl.ds(plane + h * SUB, SUB), :], LANES - 1 - 2 * q, 1)
            w_in = jnp.minimum(jnp.where(lane == 0, side, pltpu.roll(e, 1, 1)), 0.0)
            if h == 0:
                row = pl.ds(levels * tracers + k, 1)
                edge = jnp.where(even, b0[row, :], a0[row, :]) * south_flag
            s_in = jnp.minimum(jnp.where(sub == 0, edge, pltpu.roll(n, 1, 0)), 0.0)
            edge = n[SUB - 1 : SUB, :]
            e_out, n_out = jnp.maximum(e, 0.0), jnp.maximum(n, 0.0)
            from_n = n_out * inv
            if h == halves - 1:
                from_n = from_n * north_mask
            stay = (1.0 - e_out + w_in - n_out + s_in) * inv
            from_e, from_w = e_out * inv, -(w_in * inv)
            values = (stay, from_e, from_w, from_n, -(s_in * inv), down * inv, factor)
            for i, value in enumerate(values):
                weights[i, blk, :] = value
        return tuple(new)

    def body(b, carry):
        for copy in load(b):
            copy.wait()
        for u in range(unroll):
            carry = level(b * unroll + u, carry)
        return carry

    zero = jnp.zeros((SUB, LANES), jnp.float32)
    lax.fori_loop(0, blocks, body, ((zero, zero),) * halves)


def step(levels, tracers, rows, chunks, per_chunk, unroll, first, *refs):
    if first:
        field, weights, rim, edges, forcing, f_west, f_east, f_north, f_south = refs[:9]
        out, weights_out, side_ref, a_ref, b_ref = refs[9:14]
        buf, rim_now, f_rim, f_edges, sems = refs[14:]
    else:
        field, weights_in, west_in, east_in, a_in, b_in, out = refs[:7]
        buf, rim_now, weights, rim, edges, solved_buf, sems = refs[7:]

    plane = tracers * rows
    halves = rows // SUB
    lane, sub = lane_iota(), sub_iota()
    blocks = levels // unroll
    flat = buf.reshape((levels * tracers + 2) * rows, LANES)

    def load(b):
        at = b * unroll * tracers
        return pltpu.make_async_copy(
            field.at[pl.ds(at, unroll * tracers)], buf.at[pl.ds(at + 1, unroll * tracers)], sems.at[b]
        )

    if first:
        solved_buf, solved_at = buf, 1
        solved_ref = flat
    else:
        solved_at = 0
        solved_ref = solved_buf.reshape(levels * tracers * rows, LANES)

    def store(b):
        at = b * unroll * tracers
        return pltpu.make_async_copy(
            solved_buf.at[pl.ds(at + solved_at, unroll * tracers)], out.at[pl.ds(at, unroll * tracers)], sems.at[b]
        )

    last = 2 * blocks
    above = weights.at[weights.shape[0] - 1]
    if first:
        keep = pltpu.make_async_copy(weights, weights_out, sems.at[last])
        for b in range(blocks):
            load(b).start()
        keep.start()
        meet(f_rim, 0, f_west, f_east, rows)
        f_edges[0] = f_north[...]
        f_edges[1] = f_south[...]
    else:
        above_copy = pltpu.make_async_copy(weights_in.at[weights.shape[0] - 1], above, sems.at[last])
        def load_weights(b):
            planes, levels_of = pl.ds(0, weights.shape[0] - 1), pl.ds(b * unroll * rows, unroll * rows)
            return pltpu.make_async_copy(
                weights_in.at[planes, levels_of], weights.at[planes, levels_of], sems.at[blocks + b]
            )

        for b in range(blocks):
            load(b).start()
            load_weights(b).start()
        above_copy.start()
        meet(rim, 0, west_in, east_in, plane)
        pair(edges, 0, a_in, b_in, levels * tracers)

    def stencil(near, cells, here, side, edge, row, co, wanted=range(rows // SUB)):
        halfs = [cells[pl.ds(here + h * SUB, SUB), :] for h in range(halves)]
        values = []
        for h in wanted:
            cell = halfs[h]
            if h == halves - 1:
                n = jnp.where(sub == SUB - 1, edge[0, pl.ds(row, 1), :], pltpu.roll(cell, SUB - 1, 0))
            elif near is not None:
                n = near[0][pl.ds(near[1] + here + h * SUB + 1, SUB), :]
            else:
                n = jnp.where(sub == SUB - 1, pltpu.roll(halfs[h + 1], SUB - 1, 0), pltpu.roll(cell, SUB - 1, 0))
            if h == 0:
                s = jnp.where(sub == 0, edge[1, pl.ds(row, 1), :], pltpu.roll(cell, 1, 0))
            elif near is not None:
                s = near[0][pl.ds(near[1] + here + h * SUB - 1, SUB), :]
            else:
                s = jnp.where(sub == 0, pltpu.roll(halfs[h - 1], 1, 0), pltpu.roll(cell, 1, 0))
            c0, ce, cw, cn, cs, rims = co[h][:6]
            value = (c0 * cell + ce * pltpu.roll(cell, LANES - 1, 1)) + (cw * pltpu.roll(cell, 1, 1) + cn * n)
            values.append(value + (cs * s + rims * side(h)))
        return values

    def part(ref, b, size, offset=0):
        return ref.at[pl.ds(pl.multiple_of(b * unroll * size + offset, SUB), unroll * size)]

    def in_turn(body, carry):
        group = rim_now.shape[0]

        def turn_of(i, carry):
            for n in range(group):
                carry = body(i * group + n, n, carry)
            return carry

        return lax.fori_loop(0, blocks // group, turn_of, carry)

    def turned_rims(b, n, source, count, first_row):
        chunk, q = b * unroll // per_chunk, b * unroll % per_chunk
        for r in range(0, count, SUB):
            turned = pltpu.roll(source[chunk, pl.ds(r, SUB), :], (LANES - 2 * q) % LANES, 1)
            rim_now[n, pl.ds(first_row + r, SUB), :] = turned

    def side(n, u, r):
        return lambda h: pltpu.roll(rim_now[n, pl.ds(r + h * SUB, SUB), :], LANES - 1 - 2 * u, 1)

    def weights_of(b):
        co_part = weights.at[:, pl.ds(pl.multiple_of(b * unroll * rows, SUB), unroll * rows)]

        def one(u, h):
            c0, ce, cw, cn, cs, a = (
                co_part[i, pl.ds(u * rows + h * SUB, SUB), :] for i in range(weights.shape[0] - 1)
            )
            first_col, last_col = lane == 0, lane == LANES - 1
            rims = jnp.where(first_col, cw, jnp.where(last_col, ce, 0.0))
            return c0, jnp.where(last_col, 0.0, ce), jnp.where(first_col, 0.0, cw), cn, cs, rims, a

        return lambda u: [one(u, h) for h in range(halves)]

    def forward_block(b, n, solved):
        load(b).wait()
        if not first:
            load_weights(b).wait()
        turned_rims(b, n, rim, plane, 0)
        cells, co_of = part(flat, b, plane, rows), weights_of(b)
        edge = edges.at[:, pl.ds(pl.multiple_of(b * unroll * tracers, SUB), unroll * tracers)]
        if first:
            turned_rims(b, n, f_rim, rows, plane)
            f_cells = part(forcing, b, rows, SUB)
            f_edge = f_edges.at[:, pl.ds(pl.multiple_of(b * unroll, SUB), unroll)]
        else:
            solves = part(solved_ref, b, plane)
        for u in range(unroll):
            co = co_of(u)
            new = []
            if first:
                extra = stencil((forcing, b * unroll * rows + SUB), f_cells, u * rows, side(n, u, plane), f_edge, u, co)
                for t in range(tracers):
                    here = u * plane + t * rows
                    near = (flat, b * unroll * plane + rows)
                    values = stencil(near, cells, here, side(n, u, t * rows), edge, u * tracers + t, co)
                    for h in range(halves):
                        value = values[h] + extra[h] + co[h][6] * solved[h * tracers + t]
                        new.append(value)
                        cells[pl.ds(here + h * SUB, SUB), :] = value
                solved = tuple(new[t * halves + h] for h in range(halves) for t in range(tracers))
            else:
                for h in range(halves):
                    for t in range(tracers):
                        here = u * plane + t * rows
                        (value,) = stencil(
                            None, cells, here, side(n, u, t * rows), edge, u * tracers + t, co, (h,)
                        )
                        value = value + co[h][6] * solved[h * tracers + t]
                        new.append(value)
                        solves[pl.ds(here + h * SUB, SUB), :] = value
                solved = tuple(new)
        return solved

    zero = jnp.zeros((SUB, LANES), jnp.float32)
    zeros = (zero,) * (tracers * halves)
    in_turn(forward_block, zeros)
    if not first:
        above_copy.wait()

    def backward_block(i, n, later):
        b = blocks - 1 - i
        cells = part(solved_ref, b, plane, solved_at * rows)
        factors = part(above, b, rows)
        for u in reversed(range(unroll)):
            new = []
            for h in range(halves):
                factor = factors[pl.ds(u * rows + h * SUB, SUB), :]
                for t in range(tracers):
                    blk = pl.ds(u * plane + t * rows + h * SUB, SUB)
                    value = cells[blk, :] + factor * later[h * tracers + t]
                    cells[blk, :] = value
                    new.append(value)
            later = tuple(new)
        store(b).start()
        return later

    in_turn(backward_block, zeros)
    if first:
        for chunk in range(chunks):
            put_rims(flat, rows, levels, per_chunk, chunk, side_ref, 0, plane)
        put_rows(flat, rows, a_ref, b_ref, rows, 0, levels * tracers)
        keep.wait()
    for b in range(blocks):
        store(b).wait()


def row_offsets(count):
    return list(range(0, count - SUB, SUB)) + [count - SUB]


def pack(levels, group_rows, cap, kernel, columns, observed, errors, out, k_buf, c_buf, o_buf, e_buf, wide, out_buf, sems):
    lane = lane_iota()
    copies = [
        pltpu.make_async_copy(source, target, sems.at[i])
        for i, (source, target) in enumerate(
            ((columns, c_buf), (observed, o_buf), (errors, e_buf), (kernel, k_buf))
        )
    ]
    for copy in copies:
        copy.start()
    for copy in copies:
        copy.wait()
    per_level = columns.shape[0]
    groups = LANES // cap
    offsets = row_offsets(group_rows)
    padded = wide.shape[1] // groups
    together = wide.shape[0]

    def body(start, carry):
        for n in range(together):
            i = start * together + n
            one = pl.ds(i, 1)
            for g in range(groups):
                begin = g * group_rows
                count = min(group_rows, levels - begin)
                wide[n, pl.ds(g * padded, count), :] = k_buf[
                    pl.ds(i + per_level * begin, count, stride=per_level), :
                ]
            end = (groups - 1) * padded + levels - (groups - 1) * group_rows
            for m, row in enumerate((c_buf[one, :].astype(jnp.float32), o_buf[one, :], e_buf[one, :])):
                wide[n, pl.ds(end + m, 1), :] = row
            for m in range(end + 3, (groups - 1) * padded + group_rows):
                wide[n, pl.ds(m, 1), :] = jnp.zeros((1, LANES), jnp.float32)
        for n in range(together):
            i = start * together + n
            for j in range(groups):
                for m in offsets:
                    made = None
                    for g in range(groups):
                        piece = wide[n, pl.ds(g * padded + m, SUB), :]
                        if g != j:
                            piece = pltpu.roll(piece, (g - j) * cap % LANES, 1)
                        made = piece if made is None else jnp.where(lane >= g * cap, piece, made)
                    out_buf[pl.ds((i * groups + j) * group_rows + m, SUB), :] = made
        return carry

    if per_level == together:
        body(0, 0)
    else:
        lax.fori_loop(0, per_level // together, body, 0)
    done = pltpu.make_async_copy(out_buf, out, sems.at[4])
    done.start()
    done.wait()


def tracer_sum(block, concentration, out, buf, sems):
    levels, tracers, rows, cols = buf.shape

    def load(b):
        return pltpu.make_async_copy(
            concentration.at[pl.ds(b * block, block)], buf.at[pl.ds(b * block, block)], sems.at[b]
        )

    for b in range(levels // block):
        load(b).start()

    def body(b, carry):
        load(b).wait()
        for h in range(rows // SUB):
            tops, rests = [], []
            for k in range(block):
                part = jnp.sum(buf[b * block + k, :, pl.ds(h * SUB, SUB), :], axis=0)
                top = part.astype(jnp.bfloat16).astype(jnp.float32)
                tops.append(top)
                rests.append(part - top)
            at = pl.ds(pl.multiple_of(b * block * SUB, block * SUB), block * SUB)
            lanes = pl.ds(h * cols, cols)
            out[0, at, lanes] = jnp.concatenate(tops, axis=0).astype(jnp.bfloat16)
            out[1, at, lanes] = jnp.concatenate(rests, axis=0).astype(jnp.bfloat16)
        return carry

    lax.fori_loop(0, levels // block, body, 0)


def soundings(
    levels, rows, group_rows, cap, chunks, per_chunk, block,
    received, sums, forcing, side_ref, a_ref, b_ref, back_out, arrived, table, scaled, back, sem
):
    lane = lane_iota()
    parts, _, width = arrived.shape
    halves = rows // SUB
    keys = halves * LANES
    groups = LANES // cap

    def unpack_one(c):
        part, col = c // (width // LANES), c % (width // LANES)
        for g in range(groups):
            for m in row_offsets(group_rows):
                made = None
                for p in range(groups):
                    piece = received[pl.ds((c * groups + p) * group_rows + m, SUB), :]
                    if p != g:
                        piece = pltpu.roll(piece, (p - g) * cap % LANES, 1)
                    made = piece if made is None else jnp.where(lane >= p * cap, piece, made)
                lanes = pl.ds(pl.multiple_of(col * LANES, LANES), LANES)
                arrived[part, pl.ds(g * group_rows + m, SUB), lanes] = made

    at_once = largest(parts * width // LANES, 4, 2, 1)

    def unpack(i, carry):
        for n in range(at_once):
            unpack_one(i * at_once + n)
        return carry

    lax.fori_loop(0, parts * width // LANES // at_once, unpack, 0)

    sub_index = lax.broadcasted_iota(jnp.int32, (SUB, width), 0)
    key_index = lax.broadcasted_iota(jnp.int32, (keys, width), 0)
    turned_index = lax.broadcasted_iota(jnp.int32, (LANES, keys), 1)

    def columns(j):
        return arrived[j, pl.ds(levels, 1), :].astype(jnp.int32)

    def key_of(col):
        return (col >> 10) * LANES + (col & (LANES - 1))

    def mask_of(j):
        return sub_index == ((columns(j) >> 7) & (SUB - 1))

    for j in range(parts):
        col = columns(j)
        key = key_of(col)
        look = jnp.where(key_index == key, 1.0, 0.0).astype(jnp.bfloat16)
        for c in range(width // LANES):
            piece = key[:, c * LANES : (c + 1) * LANES].astype(jnp.float32)
            across = jnp.broadcast_to(piece, (LANES, LANES)).T.astype(jnp.int32)
            across = jnp.concatenate([across] * halves, axis=1)
            table[j, pl.ds(c * LANES, LANES), :] = jnp.where(turned_index == across, 1.0, 0.0).astype(
                jnp.bfloat16
            )
        total = jnp.zeros((SUB, width), jnp.float32)
        for b in range(levels // block):
            blk = pl.ds(b * block * SUB, block * SUB)
            seen = jnp.dot(sums[0, blk, :], look, preferred_element_type=jnp.float32)
            seen += jnp.dot(sums[1, blk, :], look, preferred_element_type=jnp.float32)
            weight = arrived[j, pl.ds(b * block, block), :]
            for k in range(block):
                total += weight[k : k + 1, :] * seen[k * SUB : (k + 1) * SUB, :]
        modelled = jnp.sum(jnp.where(mask_of(j), total, 0.0), axis=0, keepdims=True)
        observed = arrived[j, pl.ds(levels + 1, 1), :]
        error = arrived[j, pl.ds(levels + 2, 1), :]
        residual = jnp.where(col >= 0, (modelled - observed) / error, 0.0)
        scaled[pl.ds(j, 1), :] = residual / error
        for i in range(width // cap):
            at = i * cap
            piece = residual[:, at // LANES * LANES : at // LANES * LANES + LANES]
            if at % LANES:
                piece = pltpu.roll(piece, LANES - at % LANES, 1)
            back[pl.ds(j * (width // cap) + i, 1), :] = piece

    leave = pltpu.make_async_copy(back, back_out, sem.at[0])
    leave.start()
    zeros = jnp.zeros((SUB, LANES), jnp.float32)
    forcing[pl.ds(0, SUB), :] = zeros
    forcing[pl.ds(levels * rows + SUB, SUB), :] = zeros
    for b in range(levels // block):
        total = jnp.zeros((block * SUB, keys), jnp.float32)
        for j in range(parts):
            weight = arrived[j, pl.ds(b * block, block), :] * scaled[pl.ds(j, 1), :]
            top = weight.astype(jnp.bfloat16).astype(jnp.float32)
            mask = mask_of(j)
            for part in (top, weight - top):
                spread = jnp.concatenate(
                    [jnp.where(mask, part[k : k + 1, :], 0.0) for k in range(block)], axis=0
                ).astype(jnp.bfloat16)
                total += jnp.dot(spread, table[j, :, :], preferred_element_type=jnp.float32)
        for k in range(block):
            for h in range(halves):
                forcing[pl.ds((b * block + k) * rows + (h + 1) * SUB, SUB), :] = total[
                    k * SUB : (k + 1) * SUB, h * LANES : (h + 1) * LANES
                ]

    for chunk in range(chunks):
        put_rims(forcing, SUB, levels, per_chunk, chunk, side_ref, 0, rows)
    put_rows(forcing, SUB, a_ref, b_ref, rows, 0, levels, (0, rows - 1))
    leave.wait()


def unpack_residual(cap, arrived, out):
    lane = lax.broadcasted_iota(jnp.int32, (1, LANES), 1)
    groups = LANES // cap
    for row in range(out.shape[0]):
        made = None
        for g in range(groups):
            piece = arrived[pl.ds(row * groups + g, 1), :]
            if g:
                piece = pltpu.roll(piece, g * cap, 1)
            made = piece if made is None else jnp.where(lane >= g * cap, piece, made)
        out[pl.ds(row, 1), :] = made


def turn(value, axis, by):
    count = lax.axis_size(axis)
    return lax.ppermute(value, axis, [(i, (i + by) % count) for i in range(count)])


def exchange(side_rim, a_rim, b_rim):
    lats = lax.axis_size("lat")

    def partner(j, odd):
        other = j + 1 if j % 2 == odd else j - 1
        return other if 0 <= other < lats else j

    return (
        turn(side_rim, "lon", 1),
        turn(side_rim, "lon", -1),
        lax.ppermute(a_rim, "lat", [(j, partner(j, 0)) for j in range(lats)]),
        lax.ppermute(b_rim, "lat", [(j, partner(j, 1)) for j in range(lats)]),
    )


def exchange_small(side_rim, first_rows, last_rows):
    return (
        turn(side_rim, "lon", 1),
        turn(side_rim, "lon", -1),
        turn(first_rows, "lat", -1),
        turn(last_rows, "lat", 1),
    )


def per_device(
    concentration, adjoint, wind_east, wind_north, mixing, sound_col, kernel, observed, obs_error
):
    levels, tracers, rows, cols = adjoint.shape
    bricks = lax.axis_size("lon") * lax.axis_size("lat")
    slots = sound_col.shape[2]
    cap = slots // bricks
    unroll = largest(levels, 8, 4, 3, 2, 1)
    chunks, per_chunk = rim_chunks(levels, unroll)
    plane = tracers * rows
    per_level = slots // LANES
    groups = LANES // cap
    group_rows = -(-(levels + 3) // groups)
    padded_rows = -(-group_rows // SUB) * SUB
    field_bytes = levels * plane * cols * 4
    dma = pltpu.SemaphoreType.DMA

    def flat(x):
        return x.reshape(-1, LANES)

    packed = call(
        functools.partial(pack, levels, group_rows, cap),
        [HBM] * 4, f32(bricks * group_rows, LANES), HBM,
        (
            vmem(levels * per_level, LANES), pltpu.VMEM((per_level, LANES), jnp.int32),
            vmem(per_level, LANES), vmem(per_level, LANES),
            vmem(largest(per_level, 8, 4, 2, 1), groups * padded_rows, LANES),
            vmem(bricks * group_rows, LANES), dma((5,)),
        ),
        4, 10, 800000, "pack",
    )(*(in_hbm(flat(x)) for x in (kernel, sound_col, observed, obs_error)))
    received = lax.all_to_all(
        packed.reshape(-1, 1, LANES), ("lon", "lat"), split_axis=0, concat_axis=0, tiled=True
    ).reshape(-1, LANES)

    field = adjoint.reshape(levels * tracers, rows, LANES)
    east, north, mix = (in_hbm(flat(x)) for x in (wind_east, wind_north, mixing))
    rims = call(
        functools.partial(first_rims, levels, tracers, rows, chunks, per_chunk),
        [HBM] * 3,
        (f32(chunks, plane + rows, LANES),) + (f32(levels * tracers + levels, LANES),) * 2,
        (VMEM,) * 3,
        (vmem(levels * plane, LANES), vmem(levels * rows, LANES), vmem(levels * rows, LANES), dma((2 * chunks + 2,))),
        10, field_bytes, 2 * field_bytes, "first_rims",
    )(in_hbm(flat(adjoint)), east, north)
    start_rims = exchange(*rims)

    block = largest(levels, 24, 16, 8)
    sum_block = largest(levels, 12, 8)
    sums = call(
        functools.partial(tracer_sum, sum_block),
        [HBM], jax.ShapeDtypeStruct((2, levels * SUB, rows // SUB * cols), jnp.bfloat16), VMEM,
        (vmem(levels, tracers, rows, cols), dma((levels // sum_block,))),
        10, field_bytes // 4, field_bytes, "tracer_sum",
    )(concentration)

    width = largest(slots, 2 * LANES, LANES)
    parts = slots // width
    forcing, *rims, back = call(
        functools.partial(soundings, levels, rows, group_rows, cap, chunks, per_chunk, block),
        [VMEM] * 2,
        (
            f32(levels * rows + 2 * SUB, LANES), f32(chunks, rows, LANES), f32(levels, LANES), f32(levels, LANES),
            hbm(bricks, LANES),
        ),
        (VMEM,) * 4 + (HBM,),
        (
            vmem(parts, -(-groups * group_rows // SUB) * SUB, width),
            pltpu.VMEM((parts, width, rows // SUB * LANES), jnp.bfloat16),
            vmem(max(parts, SUB), width), vmem(bricks, LANES), dma((1,)),
        ),
        10, field_bytes * 8, field_bytes, "soundings",
    )(received, sums)
    forcing_rims = exchange_small(*rims)

    rim_shape, edge_shape = (chunks, plane, LANES), (2, levels * tracers, LANES)
    weight_shape = (7, levels * rows, LANES)
    weights, rim0, edges0 = call(
        functools.partial(coefficients, levels, tracers, rows, per_chunk, unroll),
        [HBM] * 3 + [VMEM] * 4,
        (f32(*weight_shape), f32(*rim_shape), f32(*edge_shape)),
        (VMEM,) * 3,
        (vmem(levels * rows, LANES),) * 3 + (dma((3, levels // unroll)),),
        4, field_bytes, field_bytes, "coefficients",
    )(east, north, mix, *start_rims)

    def advance(first, together, specs, operands, outs, out_specs, scratch):
        return call(
            functools.partial(step, levels, tracers, rows, chunks, per_chunk, together, first),
            specs, outs, out_specs,
            (vmem(levels * tracers + 2, rows, LANES), vmem(largest(levels // together, 3, 2, 1), plane + rows, LANES))
            + scratch + (dma((2 * (levels // together) + 5,)),),
            22, field_bytes * 8, field_bytes * 2, "step",
        )(*operands)

    edge_rows = f32(levels * tracers, LANES)
    stepped, kept, *rims = advance(
        True, unroll, [HBM] + [VMEM] * 8, (in_hbm(field), weights, rim0, edges0, forcing, *forcing_rims),
        (hbm(*field.shape), hbm(*weight_shape), f32(*rim_shape), edge_rows, edge_rows), (HBM,) * 2 + (VMEM,) * 3,
        (vmem(chunks, rows, LANES), vmem(2, levels, LANES)),
    )
    (result,) = advance(
        False, unroll, [HBM] * 2 + [VMEM] * 4, (in_hbm(stepped), in_hbm(kept), *exchange(*rims)),
        (f32(*field.shape),), (HBM,),
        (vmem(*weight_shape), vmem(*rim_shape), vmem(*edge_shape), vmem(levels * tracers, rows, LANES)),
    )

    returned = lax.all_to_all(
        back.reshape(bricks, 1, LANES), ("lon", "lat"), split_axis=0, concat_axis=0, tiled=True
    )
    result, returned = lax.optimization_barrier((result, returned))
    residual = call(
        functools.partial(unpack_residual, cap), [VMEM], f32(per_level, LANES), VMEM, (), 2, 10, 10000, "residual",
    )(returned.reshape(bricks, LANES))
    return result.reshape(adjoint.shape), residual.reshape(sound_col.shape)


def solution(mesh):
    field = P(None, None, "lat", "lon")
    face = P(None, "lat", "lon")
    owned = P(None, ("lon", "lat"), None)
    return jax.shard_map(
        per_device,
        mesh=mesh,
        in_specs=(field, field, face, face, face, owned, owned, owned, owned),
        out_specs=(field, owned),
        check_vma=False,
    )
```
